32 devices in a mesh: rows: 16 (over z, y, core), ch: 2 (over x).
Axes of the slice: x: 2, y: 2, z: 4, core: 2. Of those that a mesh axis runs over, the one named last changes fastest.
Arguments:
- images: bfloat16 [4, 256, 64, 96], P(None, 'rows', None, 'ch'), may hold values from -6 to 6
- valid_h: int32 [4, 4], replicated, may hold values from 48 to 64
- valid_w: int32 [4, 4], replicated, may hold values from 32 to 64
- kernel_one: bfloat16 [3, 3, 96, 192], P(None, None, None, 'ch'), may hold values from -0.21875 to 0.21875
- kernel_two: bfloat16 [3, 3, 192, 192], P(None, None, None, 'ch'), may hold values from -0.15625 to 0.15625
- kernel_skip: bfloat16 [96, 192], P(None, 'ch'), may hold values from -0.625 to 0.625
- bias_one: bfloat16 [192], P('ch'), may hold values from -3 to 3
- bias_two: bfloat16 [192], P('ch'), may hold values from -3 to 3
- vector_one: float32 [192], P('ch'), may hold values from -6 to 6
- vector_two: float32 [192], P('ch'), may hold values from -6 to 6
- vector_skip: float32 [192], P('ch'), may hold values from -6 to 6
- cotangent: bfloat16 [4, 128, 32, 192], P(None, 'rows', None, 'ch'), may hold values from -6 to 6
Outputs:
- block_output: bfloat16 [4, 128, 32, 192], P(None, 'rows', None, 'ch')
- input_grad: bfloat16 [4, 256, 64, 96], P(None, 'rows', None, 'ch')
- grad_kernel_one: float32 [3, 3, 96, 192], P(None, None, None, 'ch')
- grad_kernel_two: float32 [3, 3, 192, 192], P(None, None, None, 'ch')
- grad_kernel_skip: float32 [96, 192], P(None, 'ch')
- grad_bias_one: float32 [192], P('ch')
- grad_bias_two: float32 [192], P('ch')
The draws below stay inside these ranges and needn't reach their ends.
All inputs are finite; a program needn't handle non-finite values.
Results may differ from the reference program's by a relative error of at most 0.0056.
The reference program's roundings to bfloat16 on the way count: a program that leaves them out, or rounds other values in their place, can miss the bound.
Values may be sent and summed in bfloat16 or wider, within the bound.
A program may use at most 128 MiB of HBM per device.

```python
from functools import partial
import jax
import jax.numpy as jnp
from jax import lax

C_IN = 96
C_OUT = 192
IMG = 64
MB = 4
IMAGES = 4
ROWS = 256
SHIFT = 40


def plant(entries, own_key, smallest, largest):
    place = [jax.random.randint(jax.random.fold_in(own_key, axis), (), 0, length) for axis, length in enumerate(entries.shape)]
    widest = entries.shape.index(max(entries.shape))
    beside = place[:widest] + [(place[widest] + 1) % entries.shape[widest]] + place[widest + 1:]
    return entries.at[tuple(place)].set(smallest).at[tuple(beside)].set(largest)


def level_of(own_key, dims, pieces, low, high):
    factor_of = 1.0
    for axis_at, blocks in pieces:
        heights = jax.random.uniform(jax.random.fold_in(jax.random.fold_in(own_key, 6), axis_at), (blocks,), jnp.float32, low / len(pieces), high / len(pieces))
        factor_of = factor_of * jnp.repeat(jnp.exp(heights), dims[axis_at] // blocks).reshape((-1,) + (1,) * (len(dims) - 1 - axis_at))
    return factor_of


def gaussian(own_key, dims, spread, limit, cuts=(), dtype=jnp.bfloat16):
    factor_of = level_of(own_key, dims, cuts, -0.22, 0.18) if cuts else 1.0
    values = jax.random.normal(own_key, dims, jnp.float32) * spread * factor_of
    return jnp.minimum(jnp.maximum(values, -limit), limit).astype(dtype)


def setup_inputs(seed: int = 0) -> dict:
    streams_of = jax.random.split(jax.random.key(seed), 13)
    images = gaussian(streams_of[0], (MB, ROWS, IMG, C_IN), 1.0, 6.0, ((1, 16), (3, 2)))
    valid_h = plant(jax.random.randint(streams_of[1], (MB, IMAGES), IMG - IMG // 4, IMG + 1), jax.random.fold_in(streams_of[1], 1), IMG - IMG // 4, IMG).astype(jnp.int32)
    valid_w = plant(jax.random.randint(streams_of[2], (MB, IMAGES), IMG // 2, IMG + 1), jax.random.fold_in(streams_of[2], 1), IMG // 2, IMG).astype(jnp.int32)
    kernel_one = gaussian(streams_of[3], (3, 3, C_IN, C_OUT), (9 * C_IN) ** -0.5, 0.21875, ((3, 2),))
    kernel_two = gaussian(streams_of[4], (3, 3, C_OUT, C_OUT), (9 * C_OUT) ** -0.5, 0.15625, ((3, 2),))
    kernel_skip = gaussian(streams_of[5], (C_IN, C_OUT), C_IN ** -0.5, 0.625, ((1, 2),))
    bias_one = gaussian(streams_of[6], (C_OUT,), 0.5, 3.0, ((0, 2),))
    bias_two = gaussian(streams_of[7], (C_OUT,), 0.5, 3.0, ((0, 2),))
    vector_one = gaussian(streams_of[8], (C_OUT,), 1.0, 6.0, ((0, 2),), jnp.float32)
    vector_two = gaussian(streams_of[9], (C_OUT,), 1.0, 6.0, ((0, 2),), jnp.float32)
    vector_skip = gaussian(streams_of[10], (C_OUT,), 1.0, 6.0, ((0, 2),), jnp.float32)
    cotangent = gaussian(streams_of[11], (MB, ROWS // 2, IMG // 2, C_OUT), 1.0, 6.0, ((1, 16), (3, 2)))
    return dict(images=images, valid_h=valid_h, valid_w=valid_w, kernel_one=kernel_one, kernel_two=kernel_two, kernel_skip=kernel_skip, bias_one=bias_one, bias_two=bias_two, vector_one=vector_one, vector_two=vector_two, vector_skip=vector_skip, cotangent=cotangent)


EPS = 1e-06
HIGH = lax.Precision.HIGHEST

@jax.custom_vjp
def low(v):
    return lax.optimization_barrier(v.astype(jnp.bfloat16)).astype(jnp.float32)

@jax.custom_vjp
def low_back(v):
    return v

def low_keep(v):
    return (low(v), None)

def low_pass(kept, grad):
    return (grad,)

def back_keep(v):
    return (v, None)

def back_low(kept, grad):
    return (low(grad),)
low.defvjp(low_keep, low_pass)
low_back.defvjp(back_keep, back_low)

def conv_same(inputs, kernel):
    return lax.conv_general_dilated(inputs, kernel, (1, 1), 'SAME', dimension_numbers=('NHWC', 'HWIO', 'NHWC'), precision=HIGH)

def power_step(kernel, vector):
    left = jnp.einsum('hwio,o->hwi', kernel, vector, precision=HIGH)
    left = left * lax.rsqrt(jnp.sum(left * left) + EPS)
    image = jnp.einsum('hwio,hwi->o', kernel, left, precision=HIGH)
    right = image * lax.rsqrt(jnp.sum(image * image) + EPS)
    return (right, left)

def normalized(kernel, right, left):
    sigma = jnp.sum(right * jnp.einsum('hwio,hwi->o', kernel, left, precision=HIGH))
    return low(kernel / sigma)

def block_forward(mask, spectra, inputs, kernel_one, kernel_two, kernel_skip, bias_one, bias_two):
    act_in = low(jax.nn.silu(inputs) * mask)
    pre_one = low_back(conv_same(act_in, normalized(kernel_one, spectra[0][0], spectra[0][1])) + bias_one)
    act_one = low(jax.nn.silu(pre_one) * mask)
    main = conv_same(act_one, normalized(kernel_two, spectra[1][0], spectra[1][1])) + bias_two
    skip_term = conv_same(inputs * mask, normalized(kernel_skip, spectra[2][0], spectra[2][1]))
    total = main + skip_term
    return lax.optimization_barrier(jnp.mean(total.reshape(IMAGES, IMG // 2, 2, IMG // 2, 2, C_OUT), axis=(2, 4)))

def reference(images, valid_h, valid_w, kernel_one, kernel_two, kernel_skip, bias_one, bias_two, vector_one, vector_two, vector_skip, cotangent):
    kern_one = kernel_one.astype(jnp.float32)
    kern_two = kernel_two.astype(jnp.float32)
    kern_skip = kernel_skip.astype(jnp.float32).reshape(1, 1, C_IN, C_OUT)
    bias_first = bias_one.astype(jnp.float32)
    bias_second = bias_two.astype(jnp.float32)
    spectra = (power_step(kern_one, vector_one), power_step(kern_two, vector_two), power_step(kern_skip, vector_skip))
    places = jnp.arange(IMG)
    outputs = []
    in_grads = []
    totals = None
    for micro in range(MB):
        row_ok = places[None, :, None] < valid_h[micro][:, None, None]
        col_ok = places[None, None, :] < valid_w[micro][:, None, None]
        mask = (row_ok & col_ok).astype(jnp.float32)[..., None]
        rolled = jnp.roll(images[micro].astype(jnp.float32), -SHIFT, axis=0)
        inputs = rolled.reshape(IMAGES, IMG, IMG, C_IN)
        forward = partial(block_forward, mask, spectra)
        result, pullback = jax.vjp(forward, inputs, kern_one, kern_two, kern_skip, bias_first, bias_second)
        out_rows = jnp.roll(cotangent[micro].astype(jnp.float32), -(SHIFT // 2), axis=0)
        out_grad = out_rows.reshape(IMAGES, IMG // 2, IMG // 2, C_OUT)
        grads = pullback(out_grad)
        placed_out = jnp.roll(result.reshape(IMAGES * IMG // 2, IMG // 2, C_OUT), SHIFT // 2, axis=0)
        outputs.append(placed_out.astype(jnp.bfloat16))
        placed_grad = jnp.roll(grads[0].reshape(IMAGES * IMG, IMG, C_IN), SHIFT, axis=0)
        in_grads.append(placed_grad.astype(jnp.bfloat16))
        if totals is None:
            totals = grads[1:]
        else:
            totals = tuple((acc + new for acc, new in zip(totals, grads[1:])))
    return (jnp.stack(outputs), jnp.stack(in_grads), totals[0], totals[1], totals[2].reshape(C_IN, C_OUT), totals[3], totals[4])
```

```python
import functools

import jax
import jax.numpy as jnp
from jax import lax
from jax.experimental import pallas as pl
from jax.experimental.pallas import tpu as pltpu
from jax.sharding import PartitionSpec as P

IMG = 64
SHIFT = 40


EPS = 1e-06
HIGH = lax.Precision.HIGHEST


def extended(cells, sides, width):
    for axis, dim in sides:
        count = lax.axis_size(axis)
        head = lax.slice_in_dim(cells, 0, width, axis=dim)
        tail = lax.slice_in_dim(cells, cells.shape[dim] - width, cells.shape[dim], axis=dim)
        cells = jnp.concatenate(
            [
                lax.ppermute(tail, axis, [(i, (i + 1) % count) for i in range(count)]),
                cells,
                lax.ppermute(head, axis, [((i + 1) % count, i) for i in range(count)]),
            ],
            axis=dim,
        )
    return cells


def conv_rows(rim, kernel, taps):
    slab_rows = taps.shape[1]
    result = None
    for row_tap in range(3):
        part = lax.conv_general_dilated(
            rim[None, row_tap : row_tap + slab_rows],
            kernel[row_tap : row_tap + 1],
            (1, 1),
            ((0, 0), (1, 1)),
            dimension_numbers=("NHWC", "HWIO", "NHWC"),
            preferred_element_type=jnp.float32,
        )
        part = part[0] * taps[row_tap][:, None, None]
        result = part if result is None else result + part
    return result


def flipped(kernel):
    return jnp.transpose(kernel[::-1, ::-1], (0, 1, 3, 2))


def kernel_taps(rim, grad, taps_low):
    slab_rows = grad.shape[0]
    width = grad.shape[1]
    padded = jnp.pad(rim, ((0, 0), (1, 1), (0, 0)))
    stacked = []
    for row_tap in range(3):
        kept_grad = grad * taps_low[row_tap][:, None, None]
        line = []
        for col_tap in range(3):
            window = padded[row_tap : row_tap + slab_rows, col_tap : col_tap + width]
            line.append(
                jnp.einsum("rci,rco->io", window, kept_grad, preferred_element_type=jnp.float32)
            )
        stacked.append(jnp.stack(line))
    return jnp.stack(stacked)


def silu_slope(value):
    gate = jax.nn.sigmoid(value)
    return gate + value * gate * (1.0 - gate)


def shards(
    images,
    valid_h,
    valid_w,
    kernel_one,
    kernel_two,
    kernel_skip,
    bias_one,
    bias_two,
    vector_one,
    vector_two,
    vector_skip,
    cotangent,
):
    micros, rows_dev, width, in_local = images.shape
    out_local = kernel_one.shape[3]
    count_images = valid_h.shape[1]
    total_rows = rows_dev * lax.axis_size("rows")
    slab_start = lax.axis_index("rows") * rows_dev
    rim_global = slab_start - 1 + jnp.arange(rows_dev + 2, dtype=jnp.int32)
    placed = jnp.mod(rim_global - SHIFT, total_rows)
    image_of = placed // IMG
    row_of = placed % IMG
    taps = jnp.stack(
        [image_of[tap : tap + rows_dev] == image_of[1 : rows_dev + 1] for tap in range(3)]
    ).astype(jnp.float32)
    taps_low = taps.astype(jnp.bfloat16)
    owner = image_of[:, None] == jnp.arange(count_images, dtype=jnp.int32)[None, :]
    columns = jnp.arange(width)
    kern_one = kernel_one.astype(jnp.float32)
    kern_two = kernel_two.astype(jnp.float32)
    kern_skip = kernel_skip.astype(jnp.float32).reshape(1, 1, -1, out_local)
    part_one = jnp.einsum("hwio,o->hwi", kern_one, vector_one, precision=HIGH)
    part_two = jnp.einsum("hwio,o->hwi", kern_two, vector_two, precision=HIGH)
    part_skip = jnp.einsum("hwio,o->hwi", kern_skip, vector_skip, precision=HIGH)
    left_one, left_two, left_skip = lax.psum((part_one, part_two, part_skip), "ch")
    left_one = left_one * lax.rsqrt(jnp.sum(left_one * left_one) + EPS)
    left_two = left_two * lax.rsqrt(jnp.sum(left_two * left_two) + EPS)
    left_skip = left_skip * lax.rsqrt(jnp.sum(left_skip * left_skip) + EPS)
    image_one = jnp.einsum("hwio,hwi->o", kern_one, left_one, precision=HIGH)
    image_two = jnp.einsum("hwio,hwi->o", kern_two, left_two, precision=HIGH)
    image_skip = jnp.einsum("hwio,hwi->o", kern_skip, left_skip, precision=HIGH)
    square_one, square_two, square_skip = lax.psum(
        (
            jnp.sum(image_one * image_one),
            jnp.sum(image_two * image_two),
            jnp.sum(image_skip * image_skip),
        ),
        "ch",
    )
    scale_one = lax.rsqrt(square_one + EPS)
    scale_two = lax.rsqrt(square_two + EPS)
    scale_skip = lax.rsqrt(square_skip + EPS)
    right_one = image_one * scale_one
    right_two = image_two * scale_two
    right_skip = image_skip * scale_skip
    sigma_one = square_one * scale_one
    sigma_two = square_two * scale_two
    sigma_skip = square_skip * scale_skip
    eff_one = (kern_one / sigma_one).astype(jnp.bfloat16)
    eff_two = (kern_two / sigma_two).astype(jnp.bfloat16)
    eff_skip_full = (kern_skip / sigma_skip).astype(jnp.bfloat16)
    eff_skip = eff_skip_full[0, 0]
    bias_first = bias_one.astype(jnp.float32)
    bias_second = bias_two.astype(jnp.float32)
    back_two = flipped(eff_two)
    back_one = flipped(eff_one)
    outputs = []
    in_grads = []
    totals = None
    for micro in range(micros):
        height_rows = jnp.sum(jnp.where(owner, valid_h[micro][None, :], 0), axis=1)
        width_rows = jnp.sum(jnp.where(owner, valid_w[micro][None, :], 0), axis=1)
        mask_rim = (
            (row_of < height_rows)[:, None] & (columns[None, :] < width_rows[:, None])
        ).astype(jnp.float32)[:, :, None]
        mask_in = mask_rim[1:-1]
        input_rim = extended(images[micro], (("rows", 0),), 1)
        gathered = lax.all_gather(input_rim, "ch", axis=2, tiled=True)
        masked_rim = gathered * mask_rim.astype(jnp.bfloat16)
        act_in = jax.nn.silu(masked_rim.astype(jnp.float32)).astype(jnp.bfloat16)
        pre_one = conv_rows(act_in, eff_one, taps) + bias_first
        act_one = (jax.nn.silu(pre_one) * mask_in).astype(jnp.bfloat16)
        hidden_rim = extended(act_one, (("rows", 0),), 1)
        hidden_all = lax.all_gather(hidden_rim, "ch", axis=2, tiled=True)
        skip_in = masked_rim[1:-1]
        total = conv_rows(hidden_all, eff_two, taps) + bias_second
        total = total + jnp.einsum(
            "rci,io->rco", skip_in, eff_skip, preferred_element_type=jnp.float32
        )
        pooled = jnp.mean(total.reshape(rows_dev // 2, 2, width // 2, 2, out_local), axis=(1, 3))
        outputs.append(pooled.astype(jnp.bfloat16))
        quarter = cotangent[micro] * 0.25
        grad_total = jnp.broadcast_to(
            quarter[:, None, :, None, :], (rows_dev // 2, 2, width // 2, 2, out_local)
        ).reshape(rows_dev, width, out_local)
        grad_rim = extended(grad_total, (("rows", 0),), 1)
        partial_hidden = conv_rows(grad_rim, back_two, taps)
        grad_act_one = lax.psum_scatter(partial_hidden, "ch", scatter_dimension=2, tiled=True)
        grad_pre_one = (grad_act_one * mask_in * silu_slope(pre_one)).astype(jnp.bfloat16)
        pre_rim = extended(grad_pre_one, (("rows", 0),), 1)
        partial_act = conv_rows(pre_rim, back_one, taps)
        partial_skip = jnp.einsum(
            "rco,io->rci", grad_total, eff_skip, preferred_element_type=jnp.float32
        )
        grad_act_in, grad_skip_in = (
            lax.psum_scatter(partial_act, "ch", scatter_dimension=2, tiled=True),
            lax.psum_scatter(partial_skip, "ch", scatter_dimension=2, tiled=True),
        )
        own_input = images[micro].astype(jnp.float32)
        in_grads.append(
            (mask_in * (silu_slope(own_input) * grad_act_in + grad_skip_in)).astype(jnp.bfloat16)
        )
        grad_one = kernel_taps(act_in, grad_pre_one, taps_low)
        grad_two = kernel_taps(hidden_all, grad_total, taps_low)
        grad_skip = jnp.einsum(
            "rci,rco->io", skip_in, grad_total, preferred_element_type=jnp.float32
        )
        grad_first = jnp.sum(grad_pre_one.astype(jnp.float32), axis=(0, 1))
        grad_second = jnp.sum(grad_total.astype(jnp.float32), axis=(0, 1))
        current = (grad_one, grad_two, grad_skip, grad_first, grad_second)
        if totals is None:
            totals = current
        else:
            totals = tuple((acc + new for acc, new in zip(totals, current)))
    summed = lax.psum((totals[0], totals[1], totals[2], totals[3], totals[4]), "rows")
    sum_one, sum_two, sum_skip, sum_first, sum_second = summed
    sum_skip = sum_skip.reshape(1, 1, -1, out_local)
    dot_one, dot_two, dot_skip = lax.psum(
        (jnp.sum(sum_one * kern_one), jnp.sum(sum_two * kern_two), jnp.sum(sum_skip * kern_skip)),
        "ch",
    )
    final_one = (
        sum_one / sigma_one - dot_one / (sigma_one * sigma_one) * left_one[..., None] * right_one
    )
    final_two = (
        sum_two / sigma_two - dot_two / (sigma_two * sigma_two) * left_two[..., None] * right_two
    )
    final_skip = (
        sum_skip / sigma_skip
        - dot_skip / (sigma_skip * sigma_skip) * left_skip[..., None] * right_skip
    )
    return (
        jnp.stack(outputs),
        jnp.stack(in_grads),
        final_one,
        final_two,
        final_skip[0, 0],
        sum_first,
        sum_second,
    )


F32 = jnp.float32
BF16 = jnp.bfloat16
MESH = pl.DeviceIdType.MESH
TILE = 128
NT = (((1,), (1,)), ((), ()))
TN = (((0,), (0,)), ((), ()))
NN = (((1,), (0,)), ((), ()))


def fits(n_rows, n_ch, arrays):
    images, kernel_one = arrays[0], arrays[3]
    micros, rows_dev, width, in_local = images.shape
    out_local = kernel_one.shape[3]
    return (
        n_ch == 2
        and micros % 2 == 0
        and n_rows % 2 == 0
        and n_rows >= 4
        and rows_dev % 8 == 0
        and SHIFT % rows_dev == rows_dev // 2
        and IMG % rows_dev == 0
        and 2 * width == TILE
        and in_local % 16 == 0
        and 2 * in_local < TILE
        and out_local % 32 == 0
        and TILE < 2 * out_local <= 2 * TILE
    )


def dot(left, right, dims=NN):
    return lax.dot_general(left, right, dims, preferred_element_type=F32)


def iota(shape, dim):
    return lax.broadcasted_iota(jnp.int32, shape, dim)


def pieces(row):
    first = row.astype(BF16).astype(F32)
    rest = row - first
    second = rest.astype(BF16).astype(F32)
    third = rest - second
    at = iota((16, row.shape[1]), 0)
    zero = jnp.zeros((16, row.shape[1]), F32)
    stacked = jnp.where(at == 0, first, jnp.where(at == 1, second, jnp.where(at == 2, third, zero)))
    return stacked.astype(BF16)


def total(value):
    return jnp.sum(jnp.sum(value, axis=0, keepdims=True), axis=1, keepdims=True)


def power(vector_row, kernel):
    left = jnp.sum(dot(pieces(vector_row), kernel, NT), axis=0, keepdims=True)
    left = left * lax.rsqrt(total(left * left) + EPS)
    image = jnp.sum(dot(pieces(left), kernel), axis=0, keepdims=True)
    square = total(image * image)
    scale = lax.rsqrt(square + EPS)
    return left, image * scale, square * scale


def slope(value):
    gate = 1.0 / (1.0 + jnp.exp(-value))
    return gate + value * gate * (1.0 - gate)


def fused_kernel(names, n_rows, dims, *refs):
    micros, rows, width, ci, co, lanes_two, lanes_one = dims
    ref = dict(zip(names, refs))
    half = width // 2
    per = micros // 2
    pairs = rows // 2
    cut = rows // 2
    seg_slots = cut + 3
    seg_out = cut + 1
    pairs_a = cut // 2 + 1
    n_chips = n_rows // 2
    cin, cout = 2 * ci, 2 * co
    op = 2 * TILE
    total_rows = rows * n_rows

    img, cot = ref["img"], ref["cot"]
    ssem, rsem = ref["ssem"], ref["rsem"]
    me = lax.axis_index("rows")
    c = lax.axis_index("ch")
    o = 1 - c
    core = lax.rem(me, 2)
    mate = me + 1 - 2 * core
    chip = me // 2
    up = lax.rem(me + n_rows - 1, n_rows)
    down = lax.rem(me + 1, n_rows)
    my_id = c * n_chips + chip
    far = []
    for delta in range(1, 2 * n_chips):
        other = lax.rem(my_id + delta, 2 * n_chips)
        far.append((2 * lax.rem(other, n_chips) + core, other // n_chips))
    near = [(me, o), (mate, c), (up, c), (up, o), (down, c), (down, o)]

    barrier = pltpu.get_barrier_semaphore()
    for device in near + far:
        pl.semaphore_signal(barrier, inc=1, device_id=device, device_id_type=MESH)

    count = [0]

    def remote(src, dst, device):
        at = count[0]
        count[0] += 1
        return pltpu.make_async_remote_copy(
            src_ref=src,
            dst_ref=dst,
            send_sem=ssem.at[at],
            recv_sem=rsem.at[at],
            device_id=device,
            device_id_type=MESH,
        )

    imgr, sendp = ref["imgr"], ref["sendp"]

    def pack(p, carry):
        for j in range(per):
            for mine in (True, False):
                m = (c if mine else o) * per + j
                pair = jnp.concatenate([img[m, 2 * p], img[m, 2 * p + 1]], axis=1)
                if mine:
                    imgr[j, c, p + 1] = pair
                else:
                    sendp[j, p] = pair
        return carry

    lax.fori_loop(0, pairs, pack, 0)
    vec = ref["vec"]
    vec[c] = jnp.zeros(vec.shape[1:], F32)
    for i, name in enumerate(("q1", "q2", "q0", "b1", "b2")):
        vec[c, i : i + 1, 0:co] = ref[name][...].astype(F32)

    pl.semaphore_wait(barrier, len(near) + len(far))

    k1h, k2h, k0h, cotr = ref["k1h"], ref["k2h"], ref["k0h"], ref["cotr"]
    k1, k2, k0 = ref["k1"], ref["k2"], ref["k0"]
    n1, n2 = k1.shape[0] // 2, k2.shape[0] // 2
    part1, part2 = pl.ds(core * n1, n1), pl.ds(core * n2, n2)
    sends = []

    def begin(*args):
        copy = remote(*args)
        copy.start()
        sends.append(copy)
        return copy

    k1_x = begin(k1.at[part1], k1h.at[part1], (me, o))
    vec_x = begin(vec.at[c], vec.at[c], (me, o))
    img_x = [begin(sendp.at[j], imgr.at[j, c, pl.ds(1, pairs)], (me, o)) for j in range(per)]
    mine_c, mine_o = pl.ds(c * per, per), pl.ds(o * per, per)
    img_halo = [
        begin(imgr.at[:, c, 1], imgr.at[:, c, pairs + 1], (up, c)),
        begin(sendp.at[:, 0], imgr.at[:, c, pairs + 1], (up, o)),
        begin(imgr.at[:, c, pairs], imgr.at[:, c, 0], (down, c)),
        begin(sendp.at[:, pairs - 1], imgr.at[:, c, 0], (down, o)),
    ]
    cot_x = begin(cot.at[mine_o], cotr.at[:, c, pl.ds(1, pairs)], (me, o))
    cot_halo = [
        begin(cot.at[mine_c, 0], cotr.at[:, c, pairs + 1], (up, c)),
        begin(cot.at[mine_o, 0], cotr.at[:, c, pairs + 1], (up, o)),
        begin(cot.at[mine_c, pairs - 1], cotr.at[:, c, 0], (down, c)),
        begin(cot.at[mine_o, pairs - 1], cotr.at[:, c, 0], (down, o)),
    ]
    k2_x = begin(k2.at[part2], k2h.at[part2], (me, o))
    k0_x = begin(k0, k0h, (me, o))

    perm_in, perm_x = ref["perm_in"], ref["perm_x"]
    shape = (8 * half, TILE)
    at, lane = iota(shape, 0), iota(shape, 1)
    column = 2 * lax.rem(at, half) + lax.rem(at // half, 4) - 1
    hit = (lane - at // (4 * half) * width == column) & (column >= 0) & (column < width)
    perm_in[...] = jnp.where(hit, 1.0, 0.0).astype(BF16)
    shape = (4 * half, TILE)
    at, lane = iota(shape, 0), iota(shape, 1)
    source = at // (2 * half) * width + 2 * lax.rem(at, half) + lax.rem(at // half, 2)
    perm_x[0 : 4 * half] = jnp.where(lane == source, 1.0, 0.0).astype(BF16)
    shape = (half, TILE)
    at, lane = iota(shape, 0), iota(shape, 1)
    perm_x[4 * half : 5 * half] = jnp.where(lax.rem(lane, width) // 2 == at, 1.0, 0.0).astype(BF16)

    def rem_pos(value, by):
        return lax.rem(lax.rem(value, by) + by, by)

    first_a = rem_pos(me * rows - SHIFT, total_rows)
    first_b = rem_pos(me * rows + cut - SHIFT, total_rows)
    base = [lax.rem(first_a, IMG), lax.rem(first_b, IMG) - cut]
    image_a, image_b = first_a // IMG, first_b // IMG
    keep = jnp.where(base[1] < 0, 0.0, 1.0).astype(F32)
    vh, vw = ref["vh"], ref["vw"]
    high = [[vh[c * per + j, image] for image in (image_a, image_b)] for j in range(per)]
    wide = [[vw[c * per + j, image] for image in (image_a, image_b)] for j in range(per)]

    w1, w2, w0 = ref["w1"], ref["w2"], ref["w0"]

    def place(dst, row, own_part, other_part, padded):
        size = own_part.shape[0]
        first = jnp.where(c == 0, own_part, other_part)
        second = jnp.where(c == 0, other_part, own_part)
        line = jnp.concatenate([first, second, jnp.zeros((size, op - cout), BF16)], axis=1)
        dst[pl.ds(row, size), :] = line
        if padded > size:
            dst[pl.ds(row + size, padded - size), :] = jnp.zeros((padded - size, op), BF16)

    vec_x.wait_recv()

    def row_of(i):
        return jnp.concatenate(
            [vec[0, i : i + 1, 0:co], vec[1, i : i + 1, 0:co], jnp.zeros((1, op - cout), F32)], axis=1
        )

    k1_x.wait_recv()
    k1_m = begin(k1h.at[part1], k1h.at[part1], (mate, c))
    k1_m.wait_recv()
    for tap in range(9):
        rows_at = slice(tap * cin, (tap + 1) * cin)
        place(w1, tap * TILE, k1[rows_at], k1h[rows_at], TILE)
    left1, right1, sigma1 = power(row_of(0), w1[...])
    scale1 = 1.0 / sigma1
    bias1 = row_of(3)
    bias2 = row_of(4)
    left1_ref = ref["left1"]
    left1_ref[0:1] = left1

    for copy in img_x + img_halo:
        copy.wait_recv()
    b_in, xp, xb = ref["b_in"], ref["xp"], ref["xb"]
    ones = jnp.where(iota((TILE - cin, TILE), 0) == 0, 1.0, 0.0).astype(F32)

    def prepare(p, carry):
        seg = (p >= pairs_a).astype(jnp.int32)
        lane = iota((1, TILE), 1)
        row = 2 * p - 2 + lane // width
        column = lax.rem(lane, width)
        acts, plain = [], []
        for j in range(per):
            first = jnp.where(seg == 0, base[0], base[1])
            tall = jnp.where(seg == 0, high[j][0], high[j][1])
            broad = jnp.where(seg == 0, wide[j][0], wide[j][1])
            mask = jnp.where((first + row < tall) & (column < broad), 1.0, 0.0)
            x = jnp.concatenate([imgr[j, 0, p], imgr[j, 1, p]], axis=0).astype(F32) * mask
            act = x / (1.0 + jnp.exp(-x))
            acts += [act.astype(BF16), ones.astype(BF16)]
            plain += [x.astype(BF16), ones.astype(BF16)]
        spread = dot(perm_in[...], jnp.concatenate(acts, axis=0), NT).astype(BF16)
        slot = 2 * p + 2 * seg
        for j in range(per):
            for a in range(2):
                for t in range(4):
                    b_in[j, slot + a, :, t * TILE : (t + 1) * TILE] = spread[
                        (4 * a + t) * half : (4 * a + t + 1) * half, j * TILE : (j + 1) * TILE
                    ]
        spread = dot(perm_x[...], jnp.concatenate(plain, axis=0), NT).astype(BF16)
        for j in range(per):
            part = spread[:, j * TILE : (j + 1) * TILE]
            xp[j, p] = part[0 : 4 * half]
            xb[j, p] = part[4 * half : 5 * half]
        return carry

    lax.fori_loop(0, pairs + 2, prepare, 0)
    for j in range(per):
        b_in[j, seg_slots - 1] = (b_in[j, seg_slots + 1].astype(F32) * keep).astype(BF16)
        b_in[j, seg_slots] = (b_in[j, seg_slots - 2].astype(F32) * keep).astype(BF16)

    raw1, grad1 = ref["raw1"], ref["grad1"]

    def conv_one(step, carry):
        j, seg = step // 2, lax.rem(step, 2)
        parts = []
        for b in range(2):
            taps = [
                b_in[j, pl.ds(seg * seg_slots + u, seg_out), :, b * TILE : (b + 3) * TILE].reshape(
                    seg_out * half, 3 * TILE
                )
                for u in range(3)
            ]
            parts.append(jnp.concatenate(taps, axis=1))
        result = dot(jnp.concatenate(parts, axis=0), w1[...])
        for b in range(2):
            raw1[j, b, pl.ds(seg * seg_out, seg_out)] = result[
                b * seg_out * half : (b + 1) * seg_out * half
            ].reshape(seg_out, half, op)
        return carry

    lax.fori_loop(0, 2 * per, conv_one, 0)

    cols = ref["cols"]
    pixel = iota((half, op), 0)

    def activate(step, carry):
        j, i = step // (2 * seg_out), lax.rem(step, 2 * seg_out)
        seg = (i >= seg_out).astype(jnp.int32)
        first = jnp.where(seg == 0, base[0], base[1])
        tall = jnp.where(seg == 0, jnp.where(j == 0, high[0][0], high[1][0]), jnp.where(j == 0, high[0][1], high[1][1]))
        broad = jnp.where(seg == 0, jnp.where(j == 0, wide[0][0], wide[1][0]), jnp.where(j == 0, wide[0][1], wide[1][1]))
        broad = jnp.where(first + i - 1 < tall, broad, 0)
        acts = []
        for b in range(2):
            pre = raw1[j, b, i] * scale1 + bias1
            gate = 1.0 / (1.0 + jnp.exp(-pre))
            mask = 2 * pixel + b < broad
            lift = pre * gate
            grad1[j, b, i] = jnp.where(mask, gate + lift * (1.0 - gate), 0.0)
            acts.append(jnp.where(mask, lift, 0.0).astype(BF16).astype(F32))
        even, odd = acts
        before = jnp.where(pixel == 0, 0.0, pltpu.roll(odd, 1, 0))
        after = jnp.where(pixel == half - 1, 0.0, pltpu.roll(even, half - 1, 0))
        cols[j, 0, i] = before + even
        cols[j, 1, i] = even + odd
        cols[j, 2, i] = odd + after
        return carry

    lax.fori_loop(0, 2 * per * seg_out, activate, 0)

    box = ref["box"]

    def boxes(step, carry):
        j, i = step // pairs, lax.rem(step, pairs)
        above = jnp.where(i == cut // 2, keep, 1.0)
        below = jnp.where(i == cut // 2 - 1, keep, 1.0)
        for w in range(3):
            lines = [cols[j, w, 2 * i + k] for k in range(4)]
            for u in range(3):
                one, two = lines[u], lines[u + 1]
                if u == 0:
                    one = one * above
                if u == 2:
                    two = two * below
                tap = 3 * u + w
                box[j, i, :, tap * op : (tap + 1) * op] = (one + two).astype(BF16)
        return carry

    lax.fori_loop(0, per * pairs, boxes, 0)

    cot_x.wait_recv()
    for copy in cot_halo:
        copy.wait_recv()
    quart = ref["quart"]

    def quarter(step, carry):
        j, i = step // (pairs + 2), lax.rem(step, pairs + 2)
        inner = jnp.minimum(jnp.maximum(i - 1, 0), pairs - 1)
        own = jnp.where((i == 0) | (i == pairs + 1), cotr[j, c, i], cot[c * per + j, inner])
        other = cotr[j, o, i]
        first = jnp.where(c == 0, own, other)
        second = jnp.where(c == 0, other, own)
        line = jnp.concatenate([first, second, jnp.zeros((half, op - cout), BF16)], axis=1)
        quart[j, i] = (line.astype(F32) * 0.25).astype(BF16)
        return carry

    lax.fori_loop(0, per * (pairs + 2), quarter, 0)
    own_px = pairs * half

    def owned(j):
        return quart[j, 1 : pairs + 1].reshape(own_px, op)

    wire2, wire1 = ref["wire2"], ref["wire1"]
    acc2 = ref["acc2"]
    acc0 = ref["acc0"]
    for j in range(per):
        given = owned(j)[:, 0:cout]
        value = dot(given, box[j].reshape(own_px, 9 * op), TN)
        skip = dot(given, xb[j, 1 : pairs + 1].reshape(own_px, TILE), TN)
        acc2[...] = value if j == 0 else acc2[...] + value
        acc0[...] = skip if j == 0 else acc0[...] + skip
    spare = lanes_two - 9 * cout - cin
    for ch in range(2):
        rows_at = slice(ch * co, (ch + 1) * co)
        parts = [acc2[rows_at, tap * op : tap * op + cout] for tap in range(9)]
        parts += [acc0[rows_at, 0:cin], jnp.zeros((co, spare), F32)]
        wire2[ch] = jnp.concatenate(parts, axis=1).astype(BF16)

    half_rows = co // 2
    kept_rows = pl.ds(core * half_rows, half_rows)
    mate_rows = pl.ds((1 - core) * half_rows, half_rows)

    def sum_mate(wire, got):
        return begin(wire.at[:, mate_rows], got, (mate, c))

    def sum_far(copy, wire, got, shares, landing, mine):
        copy.wait_recv()
        share = shares.shape[-1]
        for ch in range(2):
            value = wire[ch, kept_rows].astype(F32) + got[ch].astype(F32)
            for chip_at in range(n_chips):
                shares[ch, chip_at] = value[:, chip_at * share : (chip_at + 1) * share].astype(BF16)
                @pl.when(my_id == ch * n_chips + chip_at)
                def _():
                    mine[...] = value[:, chip_at * share : (chip_at + 1) * share]
        copies = []
        for delta in range(1, 2 * n_chips):
            other = lax.rem(my_id + delta, 2 * n_chips)
            copies.append(
                begin(shares.at[other // n_chips, lax.rem(other, n_chips)], landing.at[delta - 1], far[delta - 1])
            )
        return copies

    def gather_far(copies, landing, mine, result):
        value = mine[...]
        for delta in range(1, 2 * n_chips):
            copies[delta - 1].wait_recv()
            value = value + landing[delta - 1].astype(F32)
        share = value.shape[1]
        result[chip, kept_rows] = value.astype(BF16)
        back = []
        for delta in range(1, n_chips):
            other = lax.rem(chip + delta, n_chips)
            back.append(
                begin(result.at[chip, kept_rows], result.at[chip, kept_rows], (2 * other + core, c))
            )
        return back

    def gather_mate(copies, result):
        for copy in copies:
            copy.wait_recv()
        return begin(result.at[:, kept_rows], result.at[:, kept_rows], (mate, c))

    sum2 = sum_mate(wire2, ref["got2"])

    k2_x.wait_recv()
    k2_m = begin(k2h.at[part2], k2h.at[part2], (mate, c))
    k0_x.wait_recv()
    place(w0, 0, k0[...], k0h[...], TILE)
    k2_m.wait_recv()
    for tap in range(9):
        rows_at = slice(tap * cout, (tap + 1) * cout)
        place(w2, tap * op, k2[rows_at], k2h[rows_at], op)
    left2, right2, sigma2 = power(row_of(1), w2[...])
    left0, right0, sigma0 = power(row_of(2), w0[...])
    scale2, scale0 = 1.0 / sigma2, 1.0 / sigma0
    left2_ref, left0_ref = ref["left2"], ref["left0"]
    left2_ref[0:1] = left2
    left0_ref[0:1] = left0

    taps_sum = ref["taps_sum"]
    spot = iota(((pairs + 2) * half, op), 0)
    at_left = lax.rem(spot, half) == 0
    at_right = lax.rem(spot, half) == half - 1
    all_px = (pairs + 2) * half
    g_pre = ref["g_pre"]
    dot1 = jnp.zeros((half, op), F32)
    for j in range(per):
        given = quart[j].reshape(all_px, op)
        for u in range(3):
            t0, t1, t2 = [
                dot(given, w2[(3 * u + w) * op : (3 * u + w + 1) * op], NT) for w in range(3)
            ]
            even = t0 + t1 + jnp.where(at_left, 0.0, pltpu.roll(t2, 1, 0))
            odd = t1 + t2 + jnp.where(at_right, 0.0, pltpu.roll(t0, all_px - 1, 0))
            taps_sum[u, 0] = even.reshape(pairs + 2, half, op)
            taps_sum[u, 1] = odd.reshape(pairs + 2, half, op)

        def back_rows(i, carry):
            hold = jnp.where(i == cut // 2, keep, 1.0)
            for b in range(2):
                upper, lower = taps_sum[2, b, i], taps_sum[0, b, i + 1]
                even = lower + taps_sum[1, b, i + 1] + hold * upper
                odd = taps_sum[1, b, i] + upper + hold * lower
                even = (even * scale2 * grad1[j, b, 2 * i + 1]).astype(BF16)
                odd = (odd * scale2 * grad1[j, b, 2 * i]).astype(BF16)
                g_pre[j, b, 2 * i + 1] = even
                g_pre[j, b, 2 * i] = odd
                own_even = jnp.where(i < pairs, 1.0, 0.0)
                own_odd = jnp.where(i > 0, 1.0, 0.0)
                carry = carry + own_even * even.astype(F32) * raw1[j, b, 2 * i + 1]
                carry = carry + own_odd * odd.astype(F32) * raw1[j, b, 2 * i]
            return carry

        dot1 = lax.fori_loop(0, pairs + 1, back_rows, dot1)

    out_b, send_b, got_b = ref["out_b"], ref["send_b"], ref["got_b"]
    dot2 = jnp.zeros((1, op), F32)
    dot0 = jnp.zeros((1, op), F32)
    for j in range(per):
        main = dot(box[j].reshape(own_px, 9 * op), w2[...])
        skip = dot(xb[j, 1 : pairs + 1].reshape(own_px, TILE), w0[...])
        given = owned(j).astype(F32)
        dot2 = dot2 + jnp.sum(given * main, axis=0, keepdims=True)
        dot0 = dot0 + jnp.sum(given * skip, axis=0, keepdims=True)
        value = (main * scale2 + skip * scale0) * 0.25 + bias2
        value = value.astype(BF16)
        first, second = value[:, 0:co], value[:, co:cout]
        out_b[c * per + j] = jnp.where(c == 0, first, second).reshape(pairs, half, co)
        send_b[j] = jnp.where(c == 0, second, first).reshape(pairs, half, co)
    out_x = begin(send_b, got_b, (me, o))

    far2 = sum_far(sum2, wire2, ref["got2"], ref["shares2"], ref["landing2"], ref["mine2"])

    acc1 = ref["acc1"]

    def kernel_one_grad(step, carry):
        j, seg = step // 2, lax.rem(step, 2)
        value = None
        for b in range(2):
            given = g_pre[j, b, pl.ds(seg * cut + 1, cut)].reshape(cut * half, op)[:, 0:cout]
            taps = [
                b_in[j, pl.ds(seg * (cut + 2) + 1 + u, cut), :, b * TILE : (b + 3) * TILE].reshape(
                    cut * half, 3 * TILE
                )
                for u in range(3)
            ]
            part = dot(given, jnp.concatenate(taps, axis=1), TN)
            value = part if value is None else value + part
        acc1[...] = acc1[...] + value
        return carry

    acc1[...] = jnp.zeros_like(acc1)
    lax.fori_loop(0, 2 * per, kernel_one_grad, 0)
    spare = lanes_one - 9 * cin - 10
    dots = [total(dot1), total(dot2), total(dot0)]

    def pair_of(column):
        high_part = column.astype(BF16).astype(F32)
        return [high_part, column - high_part]

    for ch in range(2):
        rows_at = slice(ch * co, (ch + 1) * co)
        parts = [acc1[rows_at, tap * TILE : tap * TILE + cin] for tap in range(9)]
        parts += pair_of(acc1[rows_at, 4 * TILE + cin : 4 * TILE + cin + 1])
        parts += pair_of(acc0[rows_at, cin : cin + 1])
        for value in dots:
            parts += pair_of(jnp.broadcast_to(value, (co, 1)))
        parts.append(jnp.zeros((co, spare), F32))
        wire1[ch] = jnp.concatenate(parts, axis=1).astype(BF16)
    sum1 = sum_mate(wire1, ref["got1"])

    taps_in, skip_back = ref["taps_in"], ref["skip_back"]
    pixel_in = iota((half, TILE), 0)
    out_g, send_g, got_g = ref["out_g"], ref["send_g"], ref["got_g"]
    far1 = None
    back2 = None
    for j in range(per):
        skip_back[...] = (dot(owned(j), w0[...], NT) * scale0).reshape(pairs, half, TILE)

        def tap_products(step, carry):
            b, part = step // 2, lax.rem(step, 2)
            given = g_pre[j, b, pl.ds(part * seg_out, seg_out)].reshape(seg_out * half, op)
            taps_in[b, pl.ds(part * seg_out, seg_out)] = dot(given, w1[...], NT).reshape(
                seg_out, half, 9 * TILE
            )
            return carry

        lax.fori_loop(0, 4, tap_products, 0)

        def input_rows(p, carry):
            lines = []
            for a in range(2):
                r = 2 * p + a
                hold_up = jnp.where(r == cut - 1, keep, 1.0)
                hold_down = jnp.where(r == cut, keep, 1.0)

                def column_sum(w, s):
                    def of(u, row):
                        at = (3 * u + w) * TILE
                        return taps_in[s, row, :, at : at + TILE]

                    return of(0, r + 2) * hold_up + of(1, r + 1) + of(2, r) * hold_down

                before = pltpu.roll(column_sum(2, 1), 1, 0)
                after = pltpu.roll(column_sum(0, 0), half - 1, 0)
                even = column_sum(0, 1) + column_sum(1, 0) + jnp.where(pixel_in == 0, 0.0, before)
                odd = column_sum(1, 1) + column_sum(2, 0) + jnp.where(pixel_in == half - 1, 0.0, after)
                seg = (r >= cut).astype(jnp.int32)
                first = jnp.where(seg == 0, base[0], base[1])
                tall = jnp.where(seg == 0, high[j][0], high[j][1])
                broad = jnp.where(seg == 0, wide[j][0], wide[j][1])
                broad = jnp.where(first + r < tall, broad, 0)
                for b, value in ((0, even), (1, odd)):
                    at = (2 * a + b) * half
                    x = xp[j, p + 1, at : at + half].astype(F32)
                    mask = 2 * pixel_in + b < broad
                    value = slope(x) * (value * scale1) + skip_back[p]
                    lines.append(jnp.where(mask, value, 0.0).astype(BF16))
            line = dot(jnp.concatenate(lines, axis=0), perm_x[0 : 4 * half], TN).astype(BF16)
            own = jnp.where(c == 0, line[0:ci], line[ci:cin])
            other = jnp.where(c == 0, line[ci:cin], line[0:ci])
            out_g[c * per + j, 2 * p] = own[:, 0:width]
            out_g[c * per + j, 2 * p + 1] = own[:, width:TILE]
            send_g[j, p] = other
            return carry

        lax.fori_loop(0, pairs, input_rows, 0)
        copy = begin(send_g.at[j], got_g.at[j], (me, o))
        if j == 0:
            grad_x = [copy]
            far1 = sum_far(sum1, wire1, ref["got1"], ref["shares1"], ref["landing1"], ref["mine1"])
            back2 = gather_far(far2, ref["landing2"], ref["mine2"], ref["result2"])
        else:
            grad_x.append(copy)

    last2 = gather_mate(back2, ref["result2"])
    back1 = gather_far(far1, ref["landing1"], ref["mine1"], ref["result1"])
    out_x.wait_recv()
    out_b[mine_o] = got_b[...].reshape(per, pairs, half, co)

    def unpack(p, carry):
        for j in range(per):
            out_g[o * per + j, 2 * p] = got_g[j, p, :, 0:width]
            out_g[o * per + j, 2 * p + 1] = got_g[j, p, :, width:TILE]
        return carry

    for copy in grad_x:
        copy.wait_recv()
    lax.fori_loop(0, pairs, unpack, 0)

    last1 = gather_mate(back1, ref["result1"])

    def own_half(row):
        return jnp.where(c == 0, row[:, 0:co], row[:, co:cout])

    def column_of(row):
        row = jnp.concatenate([own_half(row), jnp.zeros((1, TILE - co), F32)], axis=1)
        return jnp.transpose(jnp.broadcast_to(row, (TILE, TILE)))[0:co]

    def compact(row, size, padded):
        return jnp.concatenate([row[:, t * padded : t * padded + size] for t in range(9)], axis=1)

    def lines_of(result):
        share = result.shape[2]
        return [result[chip_at, :, 0:share].astype(F32) for chip_at in range(n_chips)]

    last1.wait_recv()
    flat1 = jnp.concatenate(lines_of(ref["result1"]), axis=1)
    extra = flat1[:, 9 * cin : 9 * cin + 10]
    dot_values = [extra[0:1, 4 + 2 * i : 5 + 2 * i] + extra[0:1, 5 + 2 * i : 6 + 2 * i] for i in range(3)]
    biases = jnp.concatenate([extra, jnp.zeros((co, TILE - 10), F32)], axis=1)
    biases = jnp.transpose(jnp.concatenate([biases, jnp.zeros((TILE - co, TILE), F32)], axis=0))
    ref["out_b1"][...] = biases[0:1, 0:co] + biases[1:2, 0:co]
    ref["out_b2"][...] = biases[2:3, 0:co] + biases[3:4, 0:co]

    def finish(flat, left, right, scale, value, out):
        columns = column_of(right) * (value * scale * scale)
        size = flat.shape[1]
        for at in range(0, size, TILE):
            some = min(TILE, size - at)
            part = flat[:, at : at + some] * scale - columns[:, 0:some] * left[:, at : at + some]
            if some < TILE:
                part = jnp.concatenate([part, jnp.zeros((co, TILE - some), F32)], axis=1)
            part = jnp.concatenate([part, jnp.zeros((TILE - co, TILE), F32)], axis=0)
            out[at : at + some] = jnp.transpose(part)[0:some, 0:co]

    finish(flat1[:, 0 : 9 * cin], compact(left1_ref[0:1], cin, TILE), right1, scale1, dot_values[0], ref["out_k1"])
    last2.wait_recv()
    flat2 = jnp.concatenate(lines_of(ref["result2"]), axis=1)
    finish(flat2[:, 0 : 9 * cout], compact(left2_ref[0:1], cout, op), right2, scale2, dot_values[1], ref["out_k2"])
    finish(flat2[:, 9 * cout : 9 * cout + cin], left0_ref[0:1, 0:cin], right0, scale0, dot_values[2], ref["out_k0"])

    for copy in sends:
        copy.wait_send()


def fused(n_rows, arrays):
    (images, valid_h, valid_w, kernel_one, kernel_two, kernel_skip, bias_one, bias_two,
     vector_one, vector_two, vector_skip, cotangent) = arrays
    micros, rows, width, ci = images.shape
    co = kernel_one.shape[3]
    per, pairs, half = micros // 2, rows // 2, width // 2
    op = 2 * TILE
    n_chips = n_rows // 2
    cin, cout = 2 * ci, 2 * co
    step = TILE * n_chips
    lanes_two = -(-(9 * cout + cin) // step) * step
    lanes_one = -(-(9 * cin + 10) // step) * step
    seg_out = rows // 2 + 1
    inputs = {
        "vh": valid_h,
        "vw": valid_w,
        "img": jnp.transpose(images, (0, 1, 3, 2)),
        "k1": kernel_one.reshape(9 * cin, co),
        "k2": kernel_two.reshape(9 * cout, co),
        "k0": kernel_skip,
        "b1": bias_one.reshape(1, co),
        "b2": bias_two.reshape(1, co),
        "q1": vector_one.reshape(1, co),
        "q2": vector_two.reshape(1, co),
        "q0": vector_skip.reshape(1, co),
        "cot": cotangent,
    }
    outputs = {
        "out_b": jax.ShapeDtypeStruct(cotangent.shape, BF16),
        "out_g": jax.ShapeDtypeStruct((micros, rows, ci, width), BF16),
        "out_k1": jax.ShapeDtypeStruct((9 * cin, co), F32),
        "out_k2": jax.ShapeDtypeStruct((9 * cout, co), F32),
        "out_k0": jax.ShapeDtypeStruct((cin, co), F32),
        "out_b1": jax.ShapeDtypeStruct((1, co), F32),
        "out_b2": jax.ShapeDtypeStruct((1, co), F32),
    }
    vm = pltpu.VMEM
    scratch = {
        "imgr": vm((per, 2, pairs + 2, ci, TILE), BF16),
        "sendp": vm((per, pairs, ci, TILE), BF16),
        "vec": vm((2, 8, TILE), F32),
        "k1h": vm((9 * cin, co), BF16),
        "k2h": vm((9 * cout, co), BF16),
        "k0h": vm((cin, co), BF16),
        "cotr": vm((per, 2, pairs + 2, half, co), BF16),
        "perm_in": vm((8 * half, TILE), BF16),
        "perm_x": vm((5 * half, TILE), BF16),
        "w1": vm((9 * TILE, op), BF16),
        "w2": vm((9 * op, op), BF16),
        "w0": vm((TILE, op), BF16),
        "left1": vm((8, 9 * TILE), F32),
        "left2": vm((8, 9 * op), F32),
        "left0": vm((8, TILE), F32),
        "b_in": vm((per, 2 * (rows // 2 + 3), half, 4 * TILE), BF16),
        "xp": vm((per, pairs + 2, 4 * half, TILE), BF16),
        "xb": vm((per, pairs + 2, half, TILE), BF16),
        "raw1": vm((per, 2, 2 * seg_out, half, op), F32),
        "grad1": vm((per, 2, 2 * seg_out, half, op), F32),
        "cols": vm((per, 3, 2 * seg_out, half, op), F32),
        "box": vm((per, pairs, half, 9 * op), BF16),
        "quart": vm((per, pairs + 2, half, op), BF16),
        "acc2": vm((cout, 9 * op), F32),
        "acc0": vm((cout, TILE), F32),
        "acc1": vm((cout, 9 * TILE), F32),
        "taps_sum": vm((3, 2, pairs + 2, half, op), F32),
        "g_pre": vm((per, 2, 2 * seg_out, half, op), BF16),
        "taps_in": vm((2, 2 * seg_out, half, 9 * TILE), F32),
        "skip_back": vm((pairs, half, TILE), F32),
        "send_b": vm((per, pairs, half, co), BF16),
        "got_b": vm((per, pairs, half, co), BF16),
        "send_g": vm((per, pairs, ci, TILE), BF16),
        "got_g": vm((per, pairs, ci, TILE), BF16),
    }
    for name, lanes in (("1", lanes_one), ("2", lanes_two)):
        share = lanes // n_chips
        scratch["wire" + name] = vm((2, co, lanes), BF16)
        scratch["got" + name] = vm((2, co // 2, lanes), BF16)
        scratch["shares" + name] = vm((2, n_chips, co // 2, share), BF16)
        scratch["landing" + name] = vm((2 * n_chips - 1, co // 2, share), BF16)
        scratch["mine" + name] = vm((co // 2, share), F32)
        scratch["result" + name] = vm((n_chips, co, share), BF16)
    copies = 18 + per * 2 + 2 * (1 + 2 * n_chips - 1 + n_chips - 1 + 1)
    scratch["ssem"] = pltpu.SemaphoreType.DMA((copies,))
    scratch["rsem"] = pltpu.SemaphoreType.DMA((copies,))
    names = list(inputs) + list(outputs) + list(scratch)
    dims = (micros, rows, width, ci, co, lanes_two, lanes_one)
    smem = pl.BlockSpec(memory_space=pltpu.SMEM)
    vmem = pl.BlockSpec(memory_space=pltpu.VMEM)
    results = pl.pallas_call(
        functools.partial(fused_kernel, names, n_rows, dims),
        out_shape=list(outputs.values()),
        in_specs=[smem, smem] + [vmem] * (len(inputs) - 2),
        out_specs=[vmem] * len(outputs),
        scratch_shapes=list(scratch.values()),
        compiler_params=pltpu.CompilerParams(
            collective_id=0, has_side_effects=True, vmem_limit_bytes=60 * 1024 * 1024
        ),
        name="down_block",
    )(*inputs.values())
    out_b, out_g, out_k1, out_k2, out_k0, out_b1, out_b2 = results
    return (
        out_b,
        jnp.transpose(out_g, (0, 1, 3, 2)),
        out_k1.reshape(3, 3, cin, co),
        out_k2.reshape(3, 3, cout, co),
        out_k0,
        out_b1.reshape(co),
        out_b2.reshape(co),
    )


def solution(mesh):
    in_specs = (
        P(None, "rows", None, "ch"),
        P(),
        P(),
        P(None, None, None, "ch"),
        P(None, None, None, "ch"),
        P(None, "ch"),
        P("ch"),
        P("ch"),
        P("ch"),
        P("ch"),
        P("ch"),
        P(None, "rows", None, "ch"),
    )
    out_specs = (
        P(None, "rows", None, "ch"),
        P(None, "rows", None, "ch"),
        P(None, None, None, "ch"),
        P(None, None, None, "ch"),
        P(None, "ch"),
        P("ch"),
        P("ch"),
    )

    def step(*arrays):
        if fits(mesh.shape["rows"], mesh.shape["ch"], arrays):
            return fused(mesh.shape["rows"], arrays)
        return shards(*arrays)

    return jax.shard_map(step, mesh=mesh, in_specs=in_specs, out_specs=out_specs, check_vma=False)
```

```python
import functools

import jax
import jax.numpy as jnp
from jax import lax
from jax.experimental import pallas as pl
from jax.experimental.pallas import tpu as pltpu
from jax.sharding import PartitionSpec as P

IMG = 64
SHIFT = 40


EPS = 1e-06
HIGH = lax.Precision.HIGHEST


def extended(cells, sides, width):
    for axis, dim in sides:
        count = lax.axis_size(axis)
        head = lax.slice_in_dim(cells, 0, width, axis=dim)
        tail = lax.slice_in_dim(cells, cells.shape[dim] - width, cells.shape[dim], axis=dim)
        cells = jnp.concatenate(
            [
                lax.ppermute(tail, axis, [(i, (i + 1) % count) for i in range(count)]),
                cells,
                lax.ppermute(head, axis, [((i + 1) % count, i) for i in range(count)]),
            ],
            axis=dim,
        )
    return cells


def conv_rows(rim, kernel, taps):
    slab_rows = taps.shape[1]
    result = None
    for row_tap in range(3):
        part = lax.conv_general_dilated(
            rim[None, row_tap : row_tap + slab_rows],
            kernel[row_tap : row_tap + 1],
            (1, 1),
            ((0, 0), (1, 1)),
            dimension_numbers=("NHWC", "HWIO", "NHWC"),
            preferred_element_type=jnp.float32,
        )
        part = part[0] * taps[row_tap][:, None, None]
        result = part if result is None else result + part
    return result


def flipped(kernel):
    return jnp.transpose(kernel[::-1, ::-1], (0, 1, 3, 2))


def kernel_taps(rim, grad, taps_low):
    slab_rows = grad.shape[0]
    width = grad.shape[1]
    padded = jnp.pad(rim, ((0, 0), (1, 1), (0, 0)))
    stacked = []
    for row_tap in range(3):
        kept_grad = grad * taps_low[row_tap][:, None, None]
        line = []
        for col_tap in range(3):
            window = padded[row_tap : row_tap + slab_rows, col_tap : col_tap + width]
            line.append(
                jnp.einsum("rci,rco->io", window, kept_grad, preferred_element_type=jnp.float32)
            )
        stacked.append(jnp.stack(line))
    return jnp.stack(stacked)


def silu_slope(value):
    gate = jax.nn.sigmoid(value)
    return gate + value * gate * (1.0 - gate)


def shards(
    images,
    valid_h,
    valid_w,
    kernel_one,
    kernel_two,
    kernel_skip,
    bias_one,
    bias_two,
    vector_one,
    vector_two,
    vector_skip,
    cotangent,
):
    micros, rows_dev, width, in_local = images.shape
    out_local = kernel_one.shape[3]
    count_images = valid_h.shape[1]
    total_rows = rows_dev * lax.axis_size("rows")
    slab_start = lax.axis_index("rows") * rows_dev
    rim_global = slab_start - 1 + jnp.arange(rows_dev + 2, dtype=jnp.int32)
    placed = jnp.mod(rim_global - SHIFT, total_rows)
    image_of = placed // IMG
    row_of = placed % IMG
    taps = jnp.stack(
        [image_of[tap : tap + rows_dev] == image_of[1 : rows_dev + 1] for tap in range(3)]
    ).astype(jnp.float32)
    taps_low = taps.astype(jnp.bfloat16)
    owner = image_of[:, None] == jnp.arange(count_images, dtype=jnp.int32)[None, :]
    columns = jnp.arange(width)
    kern_one = kernel_one.astype(jnp.float32)
    kern_two = kernel_two.astype(jnp.float32)
    kern_skip = kernel_skip.astype(jnp.float32).reshape(1, 1, -1, out_local)
    part_one = jnp.einsum("hwio,o->hwi", kern_one, vector_one, precision=HIGH)
    part_two = jnp.einsum("hwio,o->hwi", kern_two, vector_two, precision=HIGH)
    part_skip = jnp.einsum("hwio,o->hwi", kern_skip, vector_skip, precision=HIGH)
    left_one, left_two, left_skip = lax.psum((part_one, part_two, part_skip), "ch")
    left_one = left_one * lax.rsqrt(jnp.sum(left_one * left_one) + EPS)
    left_two = left_two * lax.rsqrt(jnp.sum(left_two * left_two) + EPS)
    left_skip = left_skip * lax.rsqrt(jnp.sum(left_skip * left_skip) + EPS)
    image_one = jnp.einsum("hwio,hwi->o", kern_one, left_one, precision=HIGH)
    image_two = jnp.einsum("hwio,hwi->o", kern_two, left_two, precision=HIGH)
    image_skip = jnp.einsum("hwio,hwi->o", kern_skip, left_skip, precision=HIGH)
    square_one, square_two, square_skip = lax.psum(
        (
            jnp.sum(image_one * image_one),
            jnp.sum(image_two * image_two),
            jnp.sum(image_skip * image_skip),
        ),
        "ch",
    )
    scale_one = lax.rsqrt(square_one + EPS)
    scale_two = lax.rsqrt(square_two + EPS)
    scale_skip = lax.rsqrt(square_skip + EPS)
    right_one = image_one * scale_one
    right_two = image_two * scale_two
    right_skip = image_skip * scale_skip
    sigma_one = square_one * scale_one
    sigma_two = square_two * scale_two
    sigma_skip = square_skip * scale_skip
    eff_one = (kern_one / sigma_one).astype(jnp.bfloat16)
    eff_two = (kern_two / sigma_two).astype(jnp.bfloat16)
    eff_skip_full = (kern_skip / sigma_skip).astype(jnp.bfloat16)
    eff_skip = eff_skip_full[0, 0]
    bias_first = bias_one.astype(jnp.float32)
    bias_second = bias_two.astype(jnp.float32)
    back_two = flipped(eff_two)
    back_one = flipped(eff_one)
    outputs = []
    in_grads = []
    totals = None
    for micro in range(micros):
        height_rows = jnp.sum(jnp.where(owner, valid_h[micro][None, :], 0), axis=1)
        width_rows = jnp.sum(jnp.where(owner, valid_w[micro][None, :], 0), axis=1)
        mask_rim = (
            (row_of < height_rows)[:, None] & (columns[None, :] < width_rows[:, None])
        ).astype(jnp.float32)[:, :, None]
        mask_in = mask_rim[1:-1]
        input_rim = extended(images[micro], (("rows", 0),), 1)
        gathered = lax.all_gather(input_rim, "ch", axis=2, tiled=True)
        masked_rim = gathered * mask_rim.astype(jnp.bfloat16)
        act_in = jax.nn.silu(masked_rim.astype(jnp.float32)).astype(jnp.bfloat16)
        pre_one = conv_rows(act_in, eff_one, taps) + bias_first
        act_one = (jax.nn.silu(pre_one) * mask_in).astype(jnp.bfloat16)
        hidden_rim = extended(act_one, (("rows", 0),), 1)
        hidden_all = lax.all_gather(hidden_rim, "ch", axis=2, tiled=True)
        skip_in = masked_rim[1:-1]
        total = conv_rows(hidden_all, eff_two, taps) + bias_second
        total = total + jnp.einsum(
            "rci,io->rco", skip_in, eff_skip, preferred_element_type=jnp.float32
        )
        pooled = jnp.mean(total.reshape(rows_dev // 2, 2, width // 2, 2, out_local), axis=(1, 3))
        outputs.append(pooled.astype(jnp.bfloat16))
        quarter = cotangent[micro] * 0.25
        grad_total = jnp.broadcast_to(
            quarter[:, None, :, None, :], (rows_dev // 2, 2, width // 2, 2, out_local)
        ).reshape(rows_dev, width, out_local)
        grad_rim = extended(grad_total, (("rows", 0),), 1)
        partial_hidden = conv_rows(grad_rim, back_two, taps)
        grad_act_one = lax.psum_scatter(partial_hidden, "ch", scatter_dimension=2, tiled=True)
        grad_pre_one = (grad_act_one * mask_in * silu_slope(pre_one)).astype(jnp.bfloat16)
        pre_rim = extended(grad_pre_one, (("rows", 0),), 1)
        partial_act = conv_rows(pre_rim, back_one, taps)
        partial_skip = jnp.einsum(
            "rco,io->rci", grad_total, eff_skip, preferred_element_type=jnp.float32
        )
        grad_act_in, grad_skip_in = (
            lax.psum_scatter(partial_act, "ch", scatter_dimension=2, tiled=True),
            lax.psum_scatter(partial_skip, "ch", scatter_dimension=2, tiled=True),
        )
        own_input = images[micro].astype(jnp.float32)
        in_grads.append(
            (mask_in * (silu_slope(own_input) * grad_act_in + grad_skip_in)).astype(jnp.bfloat16)
        )
        grad_one = kernel_taps(act_in, grad_pre_one, taps_low)
        grad_two = kernel_taps(hidden_all, grad_total, taps_low)
        grad_skip = jnp.einsum(
            "rci,rco->io", skip_in, grad_total, preferred_element_type=jnp.float32
        )
        grad_first = jnp.sum(grad_pre_one.astype(jnp.float32), axis=(0, 1))
        grad_second = jnp.sum(grad_total.astype(jnp.float32), axis=(0, 1))
        current = (grad_one, grad_two, grad_skip, grad_first, grad_second)
        if totals is None:
            totals = current
        else:
            totals = tuple((acc + new for acc, new in zip(totals, current)))
    summed = lax.psum((totals[0], totals[1], totals[2], totals[3], totals[4]), "rows")
    sum_one, sum_two, sum_skip, sum_first, sum_second = summed
    sum_skip = sum_skip.reshape(1, 1, -1, out_local)
    dot_one, dot_two, dot_skip = lax.psum(
        (jnp.sum(sum_one * kern_one), jnp.sum(sum_two * kern_two), jnp.sum(sum_skip * kern_skip)),
        "ch",
    )
    final_one = (
        sum_one / sigma_one - dot_one / (sigma_one * sigma_one) * left_one[..., None] * right_one
    )
    final_two = (
        sum_two / sigma_two - dot_two / (sigma_two * sigma_two) * left_two[..., None] * right_two
    )
    final_skip = (
        sum_skip / sigma_skip
        - dot_skip / (sigma_skip * sigma_skip) * left_skip[..., None] * right_skip
    )
    return (
        jnp.stack(outputs),
        jnp.stack(in_grads),
        final_one,
        final_two,
        final_skip[0, 0],
        sum_first,
        sum_second,
    )


F32 = jnp.float32
BF16 = jnp.bfloat16
MESH = pl.DeviceIdType.MESH
TILE = 128
NT = (((1,), (1,)), ((), ()))
TN = (((0,), (0,)), ((), ()))
NN = (((1,), (0,)), ((), ()))


def fits(n_rows, n_ch, arrays):
    images, kernel_one = arrays[0], arrays[3]
    micros, rows_dev, width, in_local = images.shape
    out_local = kernel_one.shape[3]
    return (
        n_ch == 2
        and micros % 2 == 0
        and n_rows % 2 == 0
        and n_rows >= 4
        and rows_dev % 8 == 0
        and SHIFT % rows_dev == rows_dev // 2
        and IMG % rows_dev == 0
        and 2 * width == TILE
        and in_local % 16 == 0
        and 2 * in_local < TILE
        and out_local % 32 == 0
        and TILE < 2 * out_local <= 2 * TILE
    )


def dot(left, right, dims=NN):
    return lax.dot_general(left, right, dims, preferred_element_type=F32)


def iota(shape, dim):
    return lax.broadcasted_iota(jnp.int32, shape, dim)


def pieces(row):
    first = row.astype(BF16).astype(F32)
    rest = row - first
    second = rest.astype(BF16).astype(F32)
    third = rest - second
    at = iota((16, row.shape[1]), 0)
    zero = jnp.zeros((16, row.shape[1]), F32)
    stacked = jnp.where(at == 0, first, jnp.where(at == 1, second, jnp.where(at == 2, third, zero)))
    return stacked.astype(BF16)


def total(value):
    return jnp.sum(jnp.sum(value, axis=0, keepdims=True), axis=1, keepdims=True)


def power(vector_row, kernel):
    left = jnp.sum(dot(pieces(vector_row), kernel, NT), axis=0, keepdims=True)
    left = left * lax.rsqrt(total(left * left) + EPS)
    image = jnp.sum(dot(pieces(left), kernel), axis=0, keepdims=True)
    square = total(image * image)
    scale = lax.rsqrt(square + EPS)
    return left, image * scale, square * scale


def slope(value):
    gate = 1.0 / (1.0 + jnp.exp(-value))
    return gate + value * gate * (1.0 - gate)


def fused_kernel(names, n_rows, dims, *refs):
    micros, rows, width, ci, co, lanes_two, lanes_one, bits, share1, share2 = dims
    ref = dict(zip(names, refs))
    half = width // 2
    per = micros // 2
    pairs = rows // 2
    cut = rows // 2
    seg_slots = cut + 3
    seg_out = cut + 1
    pairs_a = cut // 2 + 1
    n_chips = n_rows // 2
    cin, cout = 2 * ci, 2 * co
    op = 2 * TILE
    total_rows = rows * n_rows
    own_px = pairs * half
    all_px = (pairs + 2) * half

    ssem, rsem, lsem = ref["ssem"], ref["rsem"], ref["lsem"]
    me = lax.axis_index("rows")
    c = lax.axis_index("ch")
    o = 1 - c
    core = lax.rem(me, 2)
    mate = me + 1 - 2 * core
    chip = me // 2
    up = lax.rem(me + n_rows - 1, n_rows)
    down = lax.rem(me + 1, n_rows)
    my_id = c * n_chips + chip
    far = []
    for delta in range(1, 2 * n_chips):
        other = lax.rem(my_id + delta, 2 * n_chips)
        far.append((2 * lax.rem(other, n_chips) + core, other // n_chips))
    near = [(me, o), (mate, c), (up, c), (up, o), (down, c), (down, o)]

    barrier = pltpu.get_barrier_semaphore()
    for device in near + far:
        pl.semaphore_signal(barrier, inc=1, device_id=device, device_id_type=MESH)

    count = [0]
    sends = []

    def remote(src, dst, device):
        at = count[0]
        count[0] += 1
        return pltpu.make_async_remote_copy(
            src_ref=src,
            dst_ref=dst,
            send_sem=ssem.at[at],
            recv_sem=rsem.at[at],
            device_id=device,
            device_id_type=MESH,
        )

    def begin(*args):
        copy = remote(*args)
        copy.start()
        sends.append(copy)
        return copy

    img, cot, k10, k2 = ref["img_v"], ref["cot_v"], ref["k10_v"], ref["k2_v"]
    n1, n2 = 9 * cin, 9 * cout
    loads = []
    for i, (src, dst) in enumerate(
        [
            (ref["img"], img),
            (ref["k1"], k10.at[0:n1]),
            (ref["k0"], k10.at[n1 : n1 + cin]),
            (ref["k2"], k2.at[0:n2]),
            (ref["cot"], cot),
        ]
    ):
        load = pltpu.make_async_copy(src, dst, lsem.at[i])
        load.start()
        loads.append(load)

    perm_in, perm_x = ref["perm_in"], ref["perm_x"]
    shape = (8 * half, TILE)
    at, lane = iota(shape, 0), iota(shape, 1)
    column = 2 * lax.rem(at, half) + lax.rem(at // half, 4) - 1
    hit = (lane - at // (4 * half) * width == column) & (column >= 0) & (column < width)
    perm_in[...] = jnp.where(hit, 1.0, 0.0).astype(BF16)
    shape = (4 * half, TILE)
    at, lane = iota(shape, 0), iota(shape, 1)
    source = at // (2 * half) * width + 2 * lax.rem(at, half) + lax.rem(at // half, 2)
    perm_x[0 : 4 * half] = jnp.where(lane == source, 1.0, 0.0).astype(BF16)
    shape = (half, TILE)
    at, lane = iota(shape, 0), iota(shape, 1)
    perm_x[4 * half : 5 * half] = jnp.where(lax.rem(lane, width) // 2 == at, 1.0, 0.0).astype(BF16)

    def rem_pos(value, by):
        return lax.rem(lax.rem(value, by) + by, by)

    first_a = rem_pos(me * rows - SHIFT, total_rows)
    first_b = rem_pos(me * rows + cut - SHIFT, total_rows)
    base = [lax.rem(first_a, IMG), lax.rem(first_b, IMG) - cut]
    image_a, image_b = first_a // IMG, first_b // IMG
    keep = jnp.where(base[1] < 0, 0.0, 1.0).astype(F32)
    vh, vw = ref["vh"], ref["vw"]
    high = [[vh[c * per + j, image] for image in (image_a, image_b)] for j in range(per)]
    wide = [[vw[c * per + j, image] for image in (image_a, image_b)] for j in range(per)]

    def choose(seg, two):
        return jnp.where(seg == 0, two[0], two[1])

    vec = ref["vec"]
    vec[c] = jnp.zeros(vec.shape[1:], F32)
    for i, name in enumerate(("q1", "q2", "q0", "b1", "b2")):
        vec[c, i : i + 1, 0:co] = ref[name][...].astype(F32)

    imgr, sendp = ref["imgr"], ref["sendp"]
    loads[0].wait()
    for j in range(per):
        for mine in (False, True):

            def pack(p, carry, j=j, mine=mine):
                m = (c if mine else o) * per + j
                pair = jnp.concatenate([img[m, 2 * p], img[m, 2 * p + 1]], axis=1)
                if mine:
                    imgr[j, c, p + 1] = pair
                else:
                    sendp[j, p] = pair
                return carry

            lax.fori_loop(0, pairs, pack, 0, unroll=4)
    for load in loads[1:]:
        load.wait()

    pl.semaphore_wait(barrier, len(near) + len(far))

    k10h, k2h, cotr = ref["k10h"], ref["k2h"], ref["cotr"]
    spots = [core] + [lax.rem(me // 2**b, 2) for b in range(1, bits)]
    mates = [mate] + [me + 2**b * (1 - 2 * spots[b]) for b in range(1, bits)]

    def piece(rows_each, level, depth):
        first = 0
        for b in range(depth - level):
            first = first * 2 + spots[b]
        return pl.ds(first * (2**level * rows_each), 2**level * rows_each)

    class Shared:
        def __init__(self, own, got, rows_each, depth):
            self.got, self.rows_each, self.depth, self.level = got, rows_each, depth, 0
            at = piece(rows_each, 0, depth)
            self.copy = begin(own.at[at], got.at[at], (me, o))

        def turn(self):
            self.copy.wait_recv()
            if self.level < self.depth:
                at = piece(self.rows_each, self.level, self.depth)
                device = (mates[self.depth - 1 - self.level], c)
                self.copy = begin(self.got.at[at], self.got.at[at], device)
            self.level += 1

    mine_c, mine_o = pl.ds(c * per, per), pl.ds(o * per, per)
    img_x, img_halo = [], []

    def send_image(j):
        img_x.append(begin(sendp.at[j], imgr.at[j, c, pl.ds(1, pairs)], (me, o)))
        img_halo.append(
            [
                begin(sendp.at[j, 0], imgr.at[j, c, pairs + 1], (up, o)),
                begin(sendp.at[j, pairs - 1], imgr.at[j, c, 0], (down, o)),
                begin(imgr.at[j, c, 1], imgr.at[j, c, pairs + 1], (up, c)),
                begin(imgr.at[j, c, pairs], imgr.at[j, c, 0], (down, c)),
            ]
        )

    vec_x = begin(vec.at[c], vec.at[c], (me, o))
    one = Shared(k10, k10h, share1, 2)
    send_image(0)
    two = Shared(k2, k2h, share2, bits)
    for j in range(1, per):
        send_image(j)
    cot_x = begin(cot.at[mine_o], cotr.at[:, c, pl.ds(1, pairs)], (me, o))
    cot_halo = [
        begin(cot.at[mine_o, 0], cotr.at[:, c, pairs + 1], (up, o)),
        begin(cot.at[mine_o, pairs - 1], cotr.at[:, c, 0], (down, o)),
        begin(cot.at[mine_c, 0], cotr.at[:, c, pairs + 1], (up, c)),
        begin(cot.at[mine_c, pairs - 1], cotr.at[:, c, 0], (down, c)),
    ]

    w1, w2, w0 = ref["w1"], ref["w2"], ref["w0"]

    def place(dst, row, own_part, other_part, padded):
        size = own_part.shape[0]
        first = jnp.where(c == 0, own_part, other_part)
        second = jnp.where(c == 0, other_part, own_part)
        line = jnp.concatenate([first, second, jnp.zeros((size, op - cout), BF16)], axis=1)
        dst[pl.ds(row, size), :] = line
        if padded > size:
            dst[pl.ds(row + size, padded - size), :] = jnp.zeros((padded - size, op), BF16)

    def row_of(i):
        return jnp.concatenate(
            [vec[0, i : i + 1, 0:co], vec[1, i : i + 1, 0:co], jnp.zeros((1, op - cout), F32)], axis=1
        )

    b_in, xp, xb = ref["b_in"], ref["xp"], ref["xb"]
    ones = jnp.where(iota((TILE - cin, TILE), 0) == 0, 1.0, 0.0).astype(BF16)

    def prepare(j):
        img_x[j].wait_recv()
        for copy in img_halo[j]:
            copy.wait_recv()

        def two_pairs(step, carry):
            lane = iota((1, TILE), 1)
            column = lax.rem(lane, width)
            acts, plain, slots = [], [], []
            for k in range(2):
                p = 2 * step + k
                seg = (p >= pairs_a).astype(jnp.int32)
                row = 2 * p - 2 + lane // width
                mask = jnp.where(
                    (choose(seg, base) + row < choose(seg, high[j])) & (column < choose(seg, wide[j])), 1.0, 0.0
                )
                x = jnp.concatenate([imgr[j, 0, p], imgr[j, 1, p]], axis=0).astype(F32) * mask
                act = x / (1.0 + jnp.exp(-x))
                acts += [act.astype(BF16), ones]
                plain += [x.astype(BF16), ones]
                slots.append(2 * p + 2 * seg)
            spread = dot(perm_in[...], jnp.concatenate(acts, axis=0), NT).astype(BF16)
            for k in range(2):
                for a in range(2):
                    for t in range(4):
                        b_in[j, slots[k] + a, :, t * TILE : (t + 1) * TILE] = spread[
                            (4 * a + t) * half : (4 * a + t + 1) * half, k * TILE : (k + 1) * TILE
                        ]
            spread = dot(perm_x[...], jnp.concatenate(plain, axis=0), NT).astype(BF16)
            for k in range(2):
                part = spread[:, k * TILE : (k + 1) * TILE]
                xp[j, 2 * step + k] = part[0 : 4 * half]
                xb[j, 2 * step + k] = part[4 * half : 5 * half]
            return carry

        lax.fori_loop(0, (pairs + 2) // 2, two_pairs, 0, unroll=True)
        b_in[j, seg_slots - 1] = (b_in[j, seg_slots + 1].astype(F32) * keep).astype(BF16)
        b_in[j, seg_slots] = (b_in[j, seg_slots - 2].astype(F32) * keep).astype(BF16)

    raw1, grad1 = ref["raw1"], ref["grad1"]

    def conv_one(j):
        def segment(seg, carry):
            parts = []
            for b in range(2):
                taps = [
                    b_in[j, pl.ds(seg * seg_slots + u, seg_out), :, b * TILE : (b + 3) * TILE].reshape(
                        seg_out * half, 3 * TILE
                    )
                    for u in range(3)
                ]
                parts.append(jnp.concatenate(taps, axis=1))
            result = dot(jnp.concatenate(parts, axis=0), w1[...])
            for b in range(2):
                raw1[j, b, pl.ds(seg * seg_out, seg_out)] = result[
                    b * seg_out * half : (b + 1) * seg_out * half
                ].reshape(seg_out, half, op)
            return carry

        lax.fori_loop(0, 2, segment, 0)

    cols = ref["cols"]
    pixel = iota((half, op), 0)

    def activate(j):
        def line(i, carry):
            seg = (i >= seg_out).astype(jnp.int32)
            broad = jnp.where(choose(seg, base) + i - 1 < choose(seg, high[j]), choose(seg, wide[j]), 0)
            acts = []
            for b in range(2):
                pre = raw1[j, b, i] * scale1 + bias1
                gate = 1.0 / (1.0 + jnp.exp(-pre))
                mask = 2 * pixel + b < broad
                lift = pre * gate
                grad1[j, b, i] = jnp.where(mask, gate + lift * (1.0 - gate), 0.0)
                acts.append(jnp.where(mask, lift, 0.0).astype(BF16).astype(F32))
            even, odd = acts
            before = jnp.where(pixel == 0, 0.0, pltpu.roll(odd, 1, 0))
            after = jnp.where(pixel == half - 1, 0.0, pltpu.roll(even, half - 1, 0))
            cols[j, 0, i] = before + even
            cols[j, 1, i] = even + odd
            cols[j, 2, i] = odd + after
            return carry

        lax.fori_loop(0, 2 * seg_out, line, 0, unroll=2)

    box = ref["box"]

    def boxes(j):
        def line(i, carry):
            above = jnp.where(i == cut // 2, keep, 1.0)
            below = jnp.where(i == cut // 2 - 1, keep, 1.0)
            for w in range(3):
                lines = [cols[j, w, 2 * i + k] for k in range(4)]
                for u in range(3):
                    upper, lower = lines[u], lines[u + 1]
                    if u == 0:
                        upper = upper * above
                    if u == 2:
                        lower = lower * below
                    tap = 3 * u + w
                    box[j, i, :, tap * op : (tap + 1) * op] = (upper + lower).astype(BF16)
            return carry

        lax.fori_loop(0, pairs, line, 0, unroll=2)

    quart = ref["quart"]

    def quarter(j):
        def put(i, own, other):
            first = jnp.where(c == 0, own, other)
            second = jnp.where(c == 0, other, own)
            line = jnp.concatenate([first, second, jnp.zeros((half, op - cout), BF16)], axis=1)
            quart[j, i] = (line.astype(F32) * 0.25).astype(BF16)

        def inner(i, carry):
            put(i + 1, cot[c * per + j, i], cotr[j, o, i + 1])
            return carry

        lax.fori_loop(0, pairs, inner, 0, unroll=4)
        for i in (0, pairs + 1):
            put(i, cotr[j, c, i], cotr[j, o, i])

    def owned(j):
        return quart[j, 1 : pairs + 1].reshape(own_px, op)

    wire2, wire1 = ref["wire2"], ref["wire1"]
    half_rows = co // 2
    kept_rows = pl.ds(core * half_rows, half_rows)
    mate_rows = pl.ds((1 - core) * half_rows, half_rows)

    def sum_mate(wire, got):
        return begin(wire.at[:, mate_rows], got, (mate, c))

    def sum_far(copy, wire, got, shares, landing, mine):
        copy.wait_recv()
        share = shares.shape[-1]
        for ch in range(2):
            value = wire[ch, kept_rows].astype(F32) + got[ch].astype(F32)
            for chip_at in range(n_chips):
                part = value[:, chip_at * share : (chip_at + 1) * share]
                shares[ch, chip_at] = part.astype(BF16)

                @pl.when(my_id == ch * n_chips + chip_at)
                def _():
                    mine[...] = part

        copies = []
        for delta in range(1, 2 * n_chips):
            other = lax.rem(my_id + delta, 2 * n_chips)
            copies.append(
                begin(shares.at[other // n_chips, lax.rem(other, n_chips)], landing.at[delta - 1], far[delta - 1])
            )
        return copies

    def gather_far(copies, landing, mine, result):
        value = mine[...]
        for delta in range(1, 2 * n_chips):
            copies[delta - 1].wait_recv()
            value = value + landing[delta - 1].astype(F32)
        result[chip, kept_rows] = value.astype(BF16)
        back = []
        for delta in range(1, n_chips):
            other = lax.rem(chip + delta, n_chips)
            back.append(
                begin(result.at[chip, kept_rows], result.at[chip, kept_rows], (2 * other + core, c))
            )
        return back

    def gather_mate(copies, result):
        for copy in copies:
            copy.wait_recv()
        return begin(result.at[:, kept_rows], result.at[:, kept_rows], (mate, c))

    one.turn()
    prepare(0)
    one.turn()
    two.turn()
    one.turn()
    vec_x.wait_recv()
    for tap in range(9):
        rows_at = slice(tap * cin, (tap + 1) * cin)
        place(w1, tap * TILE, k10[rows_at], k10h[rows_at], TILE)
    rows_at = slice(n1, n1 + cin)
    place(w0, 0, k10[rows_at], k10h[rows_at], TILE)
    left1, right1, sigma1 = power(row_of(0), w1[...])
    left0, right0, sigma0 = power(row_of(2), w0[...])
    scale1, scale0 = 1.0 / sigma1, 1.0 / sigma0
    bias1, bias2 = row_of(3), row_of(4)
    left1_ref, left2_ref, left0_ref = ref["left1"], ref["left2"], ref["left0"]
    left1_ref[0:1] = left1
    left0_ref[0:1] = left0
    conv_one(0)
    activate(0)
    two.turn()
    boxes(0)
    for j in range(1, per):
        prepare(j)
        conv_one(j)
        if j == 1:
            two.turn()
        activate(j)
        boxes(j)
    cot_x.wait_recv()
    for copy in cot_halo:
        copy.wait_recv()
    for j in range(per):
        quarter(j)

    acc0 = ref["acc0"]
    given = jnp.concatenate([owned(j) for j in range(per)], axis=0)[:, 0:cout]
    value = dot(given, box[...].reshape(per * own_px, 9 * op), TN)
    skip = dot(given, xb[:, 1 : pairs + 1].reshape(per * own_px, TILE), TN)
    acc0[...] = skip
    spare = lanes_two - 9 * cout - cin
    for ch in range(2):
        rows_at = slice(ch * co, (ch + 1) * co)
        parts = [value[rows_at, tap * op : tap * op + cout] for tap in range(9)]
        parts += [skip[rows_at, 0:cin], jnp.zeros((co, spare), F32)]
        wire2[ch] = jnp.concatenate(parts, axis=1).astype(BF16)
    sum2 = sum_mate(wire2, ref["got2"])

    for turn in range(two.level, bits + 1):
        two.turn()
    for tap in range(9):
        rows_at = slice(tap * cout, (tap + 1) * cout)
        place(w2, tap * op, k2[rows_at], k2h[rows_at], op)
    left2, right2, sigma2 = power(row_of(1), w2[...])
    scale2 = 1.0 / sigma2
    left2_ref[0:1] = left2

    taps_sum = ref["taps_sum"]
    spot = iota((all_px, op), 0)
    at_left = lax.rem(spot, half) == 0
    at_right = lax.rem(spot, half) == half - 1
    g_pre = ref["g_pre"]

    def back_two(j, dot1):
        given = quart[j].reshape(all_px, op)
        for u in range(3):
            t0, t1, t2 = [
                dot(given, w2[(3 * u + w) * op : (3 * u + w + 1) * op], NT) for w in range(3)
            ]
            even = t0 + t1 + jnp.where(at_left, 0.0, pltpu.roll(t2, 1, 0))
            odd = t1 + t2 + jnp.where(at_right, 0.0, pltpu.roll(t0, all_px - 1, 0))
            taps_sum[u, 0] = even.reshape(pairs + 2, half, op)
            taps_sum[u, 1] = odd.reshape(pairs + 2, half, op)

        def line(i, carry):
            hold = jnp.where(i == cut // 2, keep, 1.0)
            own_even = jnp.where(i < pairs, 1.0, 0.0)
            own_odd = jnp.where(i > 0, 1.0, 0.0)
            for b in range(2):
                upper, lower = taps_sum[2, b, i], taps_sum[0, b, i + 1]
                even = lower + taps_sum[1, b, i + 1] + hold * upper
                odd = taps_sum[1, b, i] + upper + hold * lower
                even = (even * scale2 * grad1[j, b, 2 * i + 1]).astype(BF16)
                odd = (odd * scale2 * grad1[j, b, 2 * i]).astype(BF16)
                g_pre[j, b, 2 * i + 1] = even
                g_pre[j, b, 2 * i] = odd
                carry = carry + own_even * even.astype(F32) * raw1[j, b, 2 * i + 1]
                carry = carry + own_odd * odd.astype(F32) * raw1[j, b, 2 * i]
            return carry

        return lax.fori_loop(0, pairs + 1, line, dot1, unroll=3)

    dot1 = back_two(0, jnp.zeros((half, op), F32))
    far2 = sum_far(sum2, wire2, ref["got2"], ref["shares2"], ref["landing2"], ref["mine2"])
    for j in range(1, per):
        dot1 = back_two(j, dot1)

    out_b, send_b, got_b = ref["out_b"], ref["send_b"], ref["got_b"]
    dot2 = jnp.zeros((1, op), F32)
    dot0 = jnp.zeros((1, op), F32)
    for j in range(per):
        main = dot(box[j].reshape(own_px, 9 * op), w2[...])
        skip = dot(xb[j, 1 : pairs + 1].reshape(own_px, TILE), w0[...])
        given = owned(j).astype(F32)
        dot2 = dot2 + jnp.sum(given * main, axis=0, keepdims=True)
        dot0 = dot0 + jnp.sum(given * skip, axis=0, keepdims=True)
        value = (main * scale2 + skip * scale0) * 0.25 + bias2
        value = value.astype(BF16)
        first, second = value[:, 0:co], value[:, co:cout]
        out_b[c * per + j] = jnp.where(c == 0, first, second).reshape(pairs, half, co)
        send_b[j] = jnp.where(c == 0, second, first).reshape(pairs, half, co)

    acc1 = ref["acc1"]

    def kernel_one_grad(step, carry):
        j, seg = step // 2, lax.rem(step, 2)
        value = None
        for b in range(2):
            given = g_pre[j, b, pl.ds(seg * cut + 1, cut)].reshape(cut * half, op)[:, 0:cout]
            taps = [
                b_in[j, pl.ds(seg * (cut + 2) + 1 + u, cut), :, b * TILE : (b + 3) * TILE].reshape(
                    cut * half, 3 * TILE
                )
                for u in range(3)
            ]
            part = dot(given, jnp.concatenate(taps, axis=1), TN)
            value = part if value is None else value + part
        acc1[...] = acc1[...] + value
        return carry

    acc1[...] = jnp.zeros_like(acc1)
    lax.fori_loop(0, 2 * per, kernel_one_grad, 0)
    spare = lanes_one - 9 * cin - 10
    dots = [total(dot1), total(dot2), total(dot0)]

    def pair_of(column):
        high_part = column.astype(BF16).astype(F32)
        return [high_part, column - high_part]

    for ch in range(2):
        rows_at = slice(ch * co, (ch + 1) * co)
        parts = [acc1[rows_at, tap * TILE : tap * TILE + cin] for tap in range(9)]
        parts += pair_of(acc1[rows_at, 4 * TILE + cin : 4 * TILE + cin + 1])
        parts += pair_of(acc0[rows_at, cin : cin + 1])
        for value in dots:
            parts += pair_of(jnp.broadcast_to(value, (co, 1)))
        parts.append(jnp.zeros((co, spare), F32))
        wire1[ch] = jnp.concatenate(parts, axis=1).astype(BF16)
    sum1 = sum_mate(wire1, ref["got1"])
    out_x = begin(send_b, got_b, (me, o))

    taps_in, skip_back = ref["taps_in"], ref["skip_back"]
    pixel_in = iota((half, TILE), 0)
    out_g, send_g, got_g = ref["out_g"], ref["send_g"], ref["got_g"]

    def back_products(j):
        skip_back[...] = (dot(owned(j), w0[...], NT) * scale0).reshape(pairs, half, TILE)

        def some(step, carry):
            b, part = step // 2, lax.rem(step, 2)
            given = g_pre[j, b, pl.ds(part * seg_out, seg_out)].reshape(seg_out * half, op)
            taps_in[b, pl.ds(part * seg_out, seg_out)] = dot(given, w1[...], NT).reshape(
                seg_out, half, 9 * TILE
            )
            return carry

        lax.fori_loop(0, 4, some, 0)

    def input_rows(j):
        def two_rows(p, carry):
            lines = []
            for a in range(2):
                r = 2 * p + a
                hold_up = jnp.where(r == cut - 1, keep, 1.0)
                hold_down = jnp.where(r == cut, keep, 1.0)

                def column_sum(w, s):
                    def of(u, row):
                        at = (3 * u + w) * TILE
                        return taps_in[s, row, :, at : at + TILE]

                    return of(0, r + 2) * hold_up + of(1, r + 1) + of(2, r) * hold_down

                before = pltpu.roll(column_sum(2, 1), 1, 0)
                after = pltpu.roll(column_sum(0, 0), half - 1, 0)
                even = column_sum(0, 1) + column_sum(1, 0) + jnp.where(pixel_in == 0, 0.0, before)
                odd = column_sum(1, 1) + column_sum(2, 0) + jnp.where(pixel_in == half - 1, 0.0, after)
                seg = (r >= cut).astype(jnp.int32)
                broad = jnp.where(choose(seg, base) + r < choose(seg, high[j]), choose(seg, wide[j]), 0)
                for b, value in ((0, even), (1, odd)):
                    at = (2 * a + b) * half
                    x = xp[j, p + 1, at : at + half].astype(F32)
                    mask = 2 * pixel_in + b < broad
                    value = slope(x) * (value * scale1) + skip_back[p]
                    lines.append(jnp.where(mask, value, 0.0).astype(BF16))
            line = dot(jnp.concatenate(lines, axis=0), perm_x[0 : 4 * half], TN).astype(BF16)
            own = jnp.where(c == 0, line[0:ci], line[ci:cin])
            other = jnp.where(c == 0, line[ci:cin], line[0:ci])
            out_g[c * per + j, 2 * p] = own[:, 0:width]
            out_g[c * per + j, 2 * p + 1] = own[:, width:TILE]
            send_g[j, p] = other
            return carry

        lax.fori_loop(0, pairs, two_rows, 0, unroll=4)
        return begin(send_g.at[j], got_g.at[j], (me, o))

    def unpack(j):
        def line(p, carry):
            out_g[o * per + j, 2 * p] = got_g[j, p, :, 0:width]
            out_g[o * per + j, 2 * p + 1] = got_g[j, p, :, width:TILE]
            return carry

        grad_x[j].wait_recv()
        lax.fori_loop(0, pairs, line, 0, unroll=4)

    back_products(0)
    far1 = sum_far(sum1, wire1, ref["got1"], ref["shares1"], ref["landing1"], ref["mine1"])
    grad_x = [input_rows(0)]
    back2 = gather_far(far2, ref["landing2"], ref["mine2"], ref["result2"])
    for j in range(1, per):
        back_products(j)
        grad_x.append(input_rows(j))

    def own_half(row):
        return jnp.where(c == 0, row[:, 0:co], row[:, co:cout])

    def column_of(row):
        row = jnp.concatenate([own_half(row), jnp.zeros((1, TILE - co), F32)], axis=1)
        return jnp.transpose(jnp.broadcast_to(row, (TILE, TILE)))[0:co]

    def compact(row, size, padded):
        return jnp.concatenate([row[:, t * padded : t * padded + size] for t in range(9)], axis=1)

    def turned(part, out, at):
        some = part.shape[1]
        if some < TILE:
            part = jnp.concatenate([part, jnp.zeros((co, TILE - some), F32)], axis=1)
        part = jnp.concatenate([part, jnp.zeros((TILE - co, TILE), F32)], axis=0)
        out[at : at + some] = jnp.transpose(part)[0:some, 0:co]

    def outer(left, right, out):
        columns = column_of(right)
        for at in range(0, left.shape[1], TILE):
            some = min(TILE, left.shape[1] - at)
            turned(columns[:, 0:some] * left[:, at : at + some], out, at)

    def flat_of(result):
        return jnp.concatenate([result[at].astype(F32) for at in range(n_chips)], axis=1)

    corr1, corr2, corr0 = ref["corr1"], ref["corr2"], ref["corr0"]
    outer(compact(left1_ref[0:1], cin, TILE), right1 * (scale1 * scale1), corr1)
    outer(compact(left2_ref[0:1], cout, op), right2 * (scale2 * scale2), corr2)
    outer(left0_ref[0:1, 0:cin], right0 * (scale0 * scale0), corr0)
    back1 = gather_far(far1, ref["landing1"], ref["mine1"], ref["result1"])
    last2 = gather_mate(back2, ref["result2"])
    out_x.wait_recv()
    out_b[mine_o] = got_b[...]
    unpack(0)
    last2.wait_recv()
    flat2 = flat_of(ref["result2"])
    out_k1, out_k2, out_k0 = ref["out_k1"], ref["out_k2"], ref["out_k0"]
    for at in range(0, n2, TILE):
        turned(flat2[:, at : min(at + TILE, n2)] * scale2, out_k2, at)
    turned(flat2[:, n2 : n2 + cin] * scale0, out_k0, 0)
    last1 = gather_mate(back1, ref["result1"])
    for j in range(1, per):
        unpack(j)
    last1.wait_recv()
    flat1 = flat_of(ref["result1"])
    extra = flat1[:, n1 : n1 + 10]
    dot_values = [extra[0:1, 4 + 2 * i : 5 + 2 * i] + extra[0:1, 5 + 2 * i : 6 + 2 * i] for i in range(3)]
    biases = jnp.concatenate([extra, jnp.zeros((co, TILE - 10), F32)], axis=1)
    biases = jnp.transpose(jnp.concatenate([biases, jnp.zeros((TILE - co, TILE), F32)], axis=0))
    ref["out_b1"][...] = biases[0:1, 0:co] + biases[1:2, 0:co]
    ref["out_b2"][...] = biases[2:3, 0:co] + biases[3:4, 0:co]
    for at in range(0, n1, TILE):
        turned(flat1[:, at : min(at + TILE, n1)] * scale1, out_k1, at)
    for out, corr, value in ((out_k1, corr1, 0), (out_k2, corr2, 1), (out_k0, corr0, 2)):
        out[...] = out[...] - corr[...] * dot_values[value]

    for copy in sends:
        copy.wait_send()


def hand_over(arrays):
    number = len(arrays)

    def copy_all(*refs):
        sem = refs[-1]
        copies = [pltpu.make_async_copy(refs[i], refs[number + i], sem.at[i]) for i in range(number)]
        for copy in copies:
            copy.start()
        for copy in copies:
            copy.wait()

    return pl.pallas_call(
        copy_all,
        out_shape=[jax.ShapeDtypeStruct(a.shape, a.dtype) for a in arrays],
        in_specs=[pl.BlockSpec(memory_space=pltpu.VMEM)] * number,
        out_specs=[pl.BlockSpec(memory_space=pl.ANY)] * number,
        scratch_shapes=[pltpu.SemaphoreType.DMA((number,))],
        name="hand_over",
    )(*[pltpu.with_memory_space_constraint(a, pltpu.VMEM) for a in arrays])


def fused(n_rows, arrays):
    (images, valid_h, valid_w, kernel_one, kernel_two, kernel_skip, bias_one, bias_two,
     vector_one, vector_two, vector_skip, cotangent) = arrays
    micros, rows, width, ci = images.shape
    co = kernel_one.shape[3]
    per, pairs, half = micros // 2, rows // 2, width // 2
    op = 2 * TILE
    n_chips = n_rows // 2
    cin, cout = 2 * ci, 2 * co
    step = TILE * n_chips
    lanes_two = -(-(9 * cout + cin) // step) * step
    lanes_one = -(-(9 * cin + 10) // step) * step
    seg_out = rows // 2 + 1
    bits = 3 if n_rows % 8 == 0 else 2
    share1 = -(-(10 * cin) // 64) * 16
    share2 = -(-(9 * cout) // (16 * 2**bits)) * 16
    inputs = {
        "vh": valid_h,
        "vw": valid_w,
        "img": jnp.transpose(images, (0, 1, 3, 2)),
        "k1": kernel_one.reshape(9 * cin, co),
        "k2": kernel_two.reshape(9 * cout, co),
        "k0": kernel_skip,
        "b1": bias_one.reshape(1, co),
        "b2": bias_two.reshape(1, co),
        "q1": vector_one.reshape(1, co),
        "q2": vector_two.reshape(1, co),
        "q0": vector_skip.reshape(1, co),
        "cot": cotangent,
    }
    outputs = {
        "out_b": jax.ShapeDtypeStruct(cotangent.shape, BF16),
        "out_g": jax.ShapeDtypeStruct((micros, rows, ci, width), BF16),
        "out_k1": jax.ShapeDtypeStruct((9 * cin, co), F32),
        "out_k2": jax.ShapeDtypeStruct((9 * cout, co), F32),
        "out_k0": jax.ShapeDtypeStruct((cin, co), F32),
        "out_b1": jax.ShapeDtypeStruct((1, co), F32),
        "out_b2": jax.ShapeDtypeStruct((1, co), F32),
    }
    vm = pltpu.VMEM
    scratch = {
        "img_v": vm((micros, rows, ci, width), BF16),
        "cot_v": vm(cotangent.shape, BF16),
        "k10_v": vm((4 * share1, co), BF16),
        "k2_v": vm((2**bits * share2, co), BF16),
        "k10h": vm((4 * share1, co), BF16),
        "k2h": vm((2**bits * share2, co), BF16),
        "imgr": vm((per, 2, pairs + 2, ci, TILE), BF16),
        "sendp": vm((per, pairs, ci, TILE), BF16),
        "vec": vm((2, 8, TILE), F32),
        "cotr": vm((per, 2, pairs + 2, half, co), BF16),
        "perm_in": vm((8 * half, TILE), BF16),
        "perm_x": vm((5 * half, TILE), BF16),
        "w1": vm((9 * TILE, op), BF16),
        "w2": vm((9 * op, op), BF16),
        "w0": vm((TILE, op), BF16),
        "left1": vm((8, 9 * TILE), F32),
        "left2": vm((8, 9 * op), F32),
        "left0": vm((8, TILE), F32),
        "b_in": vm((per, 2 * (rows // 2 + 3), half, 4 * TILE), BF16),
        "xp": vm((per, pairs + 2, 4 * half, TILE), BF16),
        "xb": vm((per, pairs + 2, half, TILE), BF16),
        "raw1": vm((per, 2, 2 * seg_out, half, op), F32),
        "grad1": vm((per, 2, 2 * seg_out, half, op), F32),
        "cols": vm((per, 3, 2 * seg_out, half, op), F32),
        "box": vm((per, pairs, half, 9 * op), BF16),
        "quart": vm((per, pairs + 2, half, op), BF16),
        "acc0": vm((cout, TILE), F32),
        "acc1": vm((cout, 9 * TILE), F32),
        "taps_sum": vm((3, 2, pairs + 2, half, op), F32),
        "g_pre": vm((per, 2, 2 * seg_out, half, op), BF16),
        "taps_in": vm((2, 2 * seg_out, half, 9 * TILE), F32),
        "skip_back": vm((pairs, half, TILE), F32),
        "send_b": vm((per, pairs, half, co), BF16),
        "got_b": vm((per, pairs, half, co), BF16),
        "send_g": vm((per, pairs, ci, TILE), BF16),
        "got_g": vm((per, pairs, ci, TILE), BF16),
    }
    for name, size in (("corr1", 9 * cin), ("corr2", 9 * cout), ("corr0", cin)):
        scratch[name] = vm((size, co), F32)
    for name, lanes in (("1", lanes_one), ("2", lanes_two)):
        share = lanes // n_chips
        scratch["wire" + name] = vm((2, co, lanes), BF16)
        scratch["got" + name] = vm((2, co // 2, lanes), BF16)
        scratch["shares" + name] = vm((2, n_chips, co // 2, share), BF16)
        scratch["landing" + name] = vm((2 * n_chips - 1, co // 2, share), BF16)
        scratch["mine" + name] = vm((co // 2, share), F32)
        scratch["result" + name] = vm((n_chips, co, share), BF16)
    copies = 12 + bits + 6 * per + 2 * (1 + 2 * n_chips - 1 + n_chips - 1 + 1)
    scratch["lsem"] = pltpu.SemaphoreType.DMA((5,))
    scratch["ssem"] = pltpu.SemaphoreType.DMA((copies,))
    scratch["rsem"] = pltpu.SemaphoreType.DMA((copies,))
    names = list(inputs) + list(outputs) + list(scratch)
    dims = (micros, rows, width, ci, co, lanes_two, lanes_one, bits, share1, share2)
    smem = pl.BlockSpec(memory_space=pltpu.SMEM)
    vmem = pl.BlockSpec(memory_space=pltpu.VMEM)
    hbm = pl.BlockSpec(memory_space=pltpu.HBM)
    large = ("img", "k1", "k2", "k0", "cot")
    small = ("b1", "b2", "q1", "q2", "q0")
    results = pl.pallas_call(
        functools.partial(fused_kernel, names, n_rows, dims),
        out_shape=[pltpu.VMEM(a.shape, a.dtype) for a in outputs.values()],
        in_specs=[smem, smem] + [vmem if n in small else hbm for n in list(inputs)[2:]],
        out_specs=[vmem] * len(outputs),
        scratch_shapes=list(scratch.values()),
        compiler_params=pltpu.CompilerParams(
            collective_id=0, has_side_effects=True, vmem_limit_bytes=48 * 1024 * 1024
        ),
        name="down_block",
    )(*[pltpu.with_memory_space_constraint(a, pltpu.HBM) if n in large else a for n, a in inputs.items()])
    out_b, out_g, out_k1, out_k2, out_k0, out_b1, out_b2 = hand_over(results)
    return (
        out_b,
        jnp.transpose(out_g, (0, 1, 3, 2)),
        out_k1.reshape(3, 3, cin, co),
        out_k2.reshape(3, 3, cout, co),
        out_k0,
        out_b1.reshape(co),
        out_b2.reshape(co),
    )


def solution(mesh):
    in_specs = (
        P(None, "rows", None, "ch"),
        P(),
        P(),
        P(None, None, None, "ch"),
        P(None, None, None, "ch"),
        P(None, "ch"),
        P("ch"),
        P("ch"),
        P("ch"),
        P("ch"),
        P("ch"),
        P(None, "rows", None, "ch"),
    )
    out_specs = (
        P(None, "rows", None, "ch"),
        P(None, "rows", None, "ch"),
        P(None, None, None, "ch"),
        P(None, None, None, "ch"),
        P(None, "ch"),
        P("ch"),
        P("ch"),
    )

    def step(*arrays):
        if fits(mesh.shape["rows"], mesh.shape["ch"], arrays):
            return fused(mesh.shape["rows"], arrays)
        return shards(*arrays)

    return jax.shard_map(step, mesh=mesh, in_specs=in_specs, out_specs=out_specs, check_vma=False)
```

```python
import functools

import jax
import jax.numpy as jnp
from jax import lax
from jax.experimental import pallas as pl
from jax.experimental.pallas import tpu as pltpu
from jax.sharding import PartitionSpec as P

IMG = 64
SHIFT = 40


EPS = 1e-06
HIGH = lax.Precision.HIGHEST


def extended(cells, sides, width):
    for axis, dim in sides:
        count = lax.axis_size(axis)
        head = lax.slice_in_dim(cells, 0, width, axis=dim)
        tail = lax.slice_in_dim(cells, cells.shape[dim] - width, cells.shape[dim], axis=dim)
        cells = jnp.concatenate(
            [
                lax.ppermute(tail, axis, [(i, (i + 1) % count) for i in range(count)]),
                cells,
                lax.ppermute(head, axis, [((i + 1) % count, i) for i in range(count)]),
            ],
            axis=dim,
        )
    return cells


def conv_rows(rim, kernel, taps):
    slab_rows = taps.shape[1]
    result = None
    for row_tap in range(3):
        part = lax.conv_general_dilated(
            rim[None, row_tap : row_tap + slab_rows],
            kernel[row_tap : row_tap + 1],
            (1, 1),
            ((0, 0), (1, 1)),
            dimension_numbers=("NHWC", "HWIO", "NHWC"),
            preferred_element_type=jnp.float32,
        )
        part = part[0] * taps[row_tap][:, None, None]
        result = part if result is None else result + part
    return result


def flipped(kernel):
    return jnp.transpose(kernel[::-1, ::-1], (0, 1, 3, 2))


def kernel_taps(rim, grad, taps_low):
    slab_rows = grad.shape[0]
    width = grad.shape[1]
    padded = jnp.pad(rim, ((0, 0), (1, 1), (0, 0)))
    stacked = []
    for row_tap in range(3):
        kept_grad = grad * taps_low[row_tap][:, None, None]
        line = []
        for col_tap in range(3):
            window = padded[row_tap : row_tap + slab_rows, col_tap : col_tap + width]
            line.append(
                jnp.einsum("rci,rco->io", window, kept_grad, preferred_element_type=jnp.float32)
            )
        stacked.append(jnp.stack(line))
    return jnp.stack(stacked)


def silu_slope(value):
    gate = jax.nn.sigmoid(value)
    return gate + value * gate * (1.0 - gate)


def shards(
    images,
    valid_h,
    valid_w,
    kernel_one,
    kernel_two,
    kernel_skip,
    bias_one,
    bias_two,
    vector_one,
    vector_two,
    vector_skip,
    cotangent,
):
    micros, rows_dev, width, in_local = images.shape
    out_local = kernel_one.shape[3]
    count_images = valid_h.shape[1]
    total_rows = rows_dev * lax.axis_size("rows")
    slab_start = lax.axis_index("rows") * rows_dev
    rim_global = slab_start - 1 + jnp.arange(rows_dev + 2, dtype=jnp.int32)
    placed = jnp.mod(rim_global - SHIFT, total_rows)
    image_of = placed // IMG
    row_of = placed % IMG
    taps = jnp.stack(
        [image_of[tap : tap + rows_dev] == image_of[1 : rows_dev + 1] for tap in range(3)]
    ).astype(jnp.float32)
    taps_low = taps.astype(jnp.bfloat16)
    owner = image_of[:, None] == jnp.arange(count_images, dtype=jnp.int32)[None, :]
    columns = jnp.arange(width)
    kern_one = kernel_one.astype(jnp.float32)
    kern_two = kernel_two.astype(jnp.float32)
    kern_skip = kernel_skip.astype(jnp.float32).reshape(1, 1, -1, out_local)
    part_one = jnp.einsum("hwio,o->hwi", kern_one, vector_one, precision=HIGH)
    part_two = jnp.einsum("hwio,o->hwi", kern_two, vector_two, precision=HIGH)
    part_skip = jnp.einsum("hwio,o->hwi", kern_skip, vector_skip, precision=HIGH)
    left_one, left_two, left_skip = lax.psum((part_one, part_two, part_skip), "ch")
    left_one = left_one * lax.rsqrt(jnp.sum(left_one * left_one) + EPS)
    left_two = left_two * lax.rsqrt(jnp.sum(left_two * left_two) + EPS)
    left_skip = left_skip * lax.rsqrt(jnp.sum(left_skip * left_skip) + EPS)
    image_one = jnp.einsum("hwio,hwi->o", kern_one, left_one, precision=HIGH)
    image_two = jnp.einsum("hwio,hwi->o", kern_two, left_two, precision=HIGH)
    image_skip = jnp.einsum("hwio,hwi->o", kern_skip, left_skip, precision=HIGH)
    square_one, square_two, square_skip = lax.psum(
        (
            jnp.sum(image_one * image_one),
            jnp.sum(image_two * image_two),
            jnp.sum(image_skip * image_skip),
        ),
        "ch",
    )
    scale_one = lax.rsqrt(square_one + EPS)
    scale_two = lax.rsqrt(square_two + EPS)
    scale_skip = lax.rsqrt(square_skip + EPS)
    right_one = image_one * scale_one
    right_two = image_two * scale_two
    right_skip = image_skip * scale_skip
    sigma_one = square_one * scale_one
    sigma_two = square_two * scale_two
    sigma_skip = square_skip * scale_skip
    eff_one = (kern_one / sigma_one).astype(jnp.bfloat16)
    eff_two = (kern_two / sigma_two).astype(jnp.bfloat16)
    eff_skip_full = (kern_skip / sigma_skip).astype(jnp.bfloat16)
    eff_skip = eff_skip_full[0, 0]
    bias_first = bias_one.astype(jnp.float32)
    bias_second = bias_two.astype(jnp.float32)
    back_two = flipped(eff_two)
    back_one = flipped(eff_one)
    outputs = []
    in_grads = []
    totals = None
    for micro in range(micros):
        height_rows = jnp.sum(jnp.where(owner, valid_h[micro][None, :], 0), axis=1)
        width_rows = jnp.sum(jnp.where(owner, valid_w[micro][None, :], 0), axis=1)
        mask_rim = (
            (row_of < height_rows)[:, None] & (columns[None, :] < width_rows[:, None])
        ).astype(jnp.float32)[:, :, None]
        mask_in = mask_rim[1:-1]
        input_rim = extended(images[micro], (("rows", 0),), 1)
        gathered = lax.all_gather(input_rim, "ch", axis=2, tiled=True)
        masked_rim = gathered * mask_rim.astype(jnp.bfloat16)
        act_in = jax.nn.silu(masked_rim.astype(jnp.float32)).astype(jnp.bfloat16)
        pre_one = conv_rows(act_in, eff_one, taps) + bias_first
        act_one = (jax.nn.silu(pre_one) * mask_in).astype(jnp.bfloat16)
        hidden_rim = extended(act_one, (("rows", 0),), 1)
        hidden_all = lax.all_gather(hidden_rim, "ch", axis=2, tiled=True)
        skip_in = masked_rim[1:-1]
        total = conv_rows(hidden_all, eff_two, taps) + bias_second
        total = total + jnp.einsum(
            "rci,io->rco", skip_in, eff_skip, preferred_element_type=jnp.float32
        )
        pooled = jnp.mean(total.reshape(rows_dev // 2, 2, width // 2, 2, out_local), axis=(1, 3))
        outputs.append(pooled.astype(jnp.bfloat16))
        quarter = cotangent[micro] * 0.25
        grad_total = jnp.broadcast_to(
            quarter[:, None, :, None, :], (rows_dev // 2, 2, width // 2, 2, out_local)
        ).reshape(rows_dev, width, out_local)
        grad_rim = extended(grad_total, (("rows", 0),), 1)
        partial_hidden = conv_rows(grad_rim, back_two, taps)
        grad_act_one = lax.psum_scatter(partial_hidden, "ch", scatter_dimension=2, tiled=True)
        grad_pre_one = (grad_act_one * mask_in * silu_slope(pre_one)).astype(jnp.bfloat16)
        pre_rim = extended(grad_pre_one, (("rows", 0),), 1)
        partial_act = conv_rows(pre_rim, back_one, taps)
        partial_skip = jnp.einsum(
            "rco,io->rci", grad_total, eff_skip, preferred_element_type=jnp.float32
        )
        grad_act_in, grad_skip_in = (
            lax.psum_scatter(partial_act, "ch", scatter_dimension=2, tiled=True),
            lax.psum_scatter(partial_skip, "ch", scatter_dimension=2, tiled=True),
        )
        own_input = images[micro].astype(jnp.float32)
        in_grads.append(
            (mask_in * (silu_slope(own_input) * grad_act_in + grad_skip_in)).astype(jnp.bfloat16)
        )
        grad_one = kernel_taps(act_in, grad_pre_one, taps_low)
        grad_two = kernel_taps(hidden_all, grad_total, taps_low)
        grad_skip = jnp.einsum(
            "rci,rco->io", skip_in, grad_total, preferred_element_type=jnp.float32
        )
        grad_first = jnp.sum(grad_pre_one.astype(jnp.float32), axis=(0, 1))
        grad_second = jnp.sum(grad_total.astype(jnp.float32), axis=(0, 1))
        current = (grad_one, grad_two, grad_skip, grad_first, grad_second)
        if totals is None:
            totals = current
        else:
            totals = tuple((acc + new for acc, new in zip(totals, current)))
    summed = lax.psum((totals[0], totals[1], totals[2], totals[3], totals[4]), "rows")
    sum_one, sum_two, sum_skip, sum_first, sum_second = summed
    sum_skip = sum_skip.reshape(1, 1, -1, out_local)
    dot_one, dot_two, dot_skip = lax.psum(
        (jnp.sum(sum_one * kern_one), jnp.sum(sum_two * kern_two), jnp.sum(sum_skip * kern_skip)),
        "ch",
    )
    final_one = (
        sum_one / sigma_one - dot_one / (sigma_one * sigma_one) * left_one[..., None] * right_one
    )
    final_two = (
        sum_two / sigma_two - dot_two / (sigma_two * sigma_two) * left_two[..., None] * right_two
    )
    final_skip = (
        sum_skip / sigma_skip
        - dot_skip / (sigma_skip * sigma_skip) * left_skip[..., None] * right_skip
    )
    return (
        jnp.stack(outputs),
        jnp.stack(in_grads),
        final_one,
        final_two,
        final_skip[0, 0],
        sum_first,
        sum_second,
    )


F32 = jnp.float32
BF16 = jnp.bfloat16
MESH = pl.DeviceIdType.MESH
TILE = 128
NT = (((1,), (1,)), ((), ()))
TN = (((0,), (0,)), ((), ()))
NN = (((1,), (0,)), ((), ()))


def fits(n_rows, n_ch, arrays):
    images, kernel_one = arrays[0], arrays[3]
    micros, rows_dev, width, in_local = images.shape
    out_local = kernel_one.shape[3]
    return (
        n_ch == 2
        and micros % 2 == 0
        and n_rows >= 4
        and n_rows % min(8, n_rows) == 0
        and n_rows % 4 == 0
        and rows_dev % 8 == 0
        and SHIFT % rows_dev == rows_dev // 2
        and IMG % rows_dev == 0
        and 2 * width == TILE
        and in_local % 16 == 0
        and 2 * in_local < TILE
        and out_local % 32 == 0
        and TILE < 2 * out_local <= 2 * TILE
    )


def dot(left, right, dims=NN):
    return lax.dot_general(left, right, dims, preferred_element_type=F32)


def iota(shape, dim):
    return lax.broadcasted_iota(jnp.int32, shape, dim)


def pieces(row):
    first = row.astype(BF16).astype(F32)
    rest = row - first
    second = rest.astype(BF16).astype(F32)
    third = rest - second
    at = iota((16, row.shape[1]), 0)
    zero = jnp.zeros((16, row.shape[1]), F32)
    stacked = jnp.where(at == 0, first, jnp.where(at == 1, second, jnp.where(at == 2, third, zero)))
    return stacked.astype(BF16)


def total(value):
    return jnp.sum(jnp.sum(value, axis=0, keepdims=True), axis=1, keepdims=True)


def power(vector_row, kernel):
    left = jnp.sum(dot(pieces(vector_row), kernel, NT), axis=0, keepdims=True)
    left = left * lax.rsqrt(total(left * left) + EPS)
    image = jnp.sum(dot(pieces(left), kernel), axis=0, keepdims=True)
    square = total(image * image)
    scale = lax.rsqrt(square + EPS)
    return left, image * scale, square * scale


def slope(value):
    gate = 1.0 / (1.0 + jnp.exp(-value))
    return gate + value * gate * (1.0 - gate)


def fused_kernel(names, n_rows, dims, *refs):
    micros, rows, width, ci, co, lanes_each, bits, share1, share2 = dims
    ref = dict(zip(names, refs))
    half = width // 2
    per = micros // 2
    pairs = rows // 2
    cut = rows // 2
    seg_slots = cut + 3
    seg_out = cut + 1
    pairs_a = cut // 2 + 1
    n_chips = n_rows // 2
    cin, cout = 2 * ci, 2 * co
    op = 2 * TILE
    total_rows = rows * n_rows
    own_px = pairs * half
    all_px = (pairs + 2) * half

    ssem, rsem, lsem = ref["ssem"], ref["rsem"], ref["lsem"]
    me = lax.axis_index("rows")
    c = lax.axis_index("ch")
    o = 1 - c
    core = lax.rem(me, 2)
    mate = me + 1 - 2 * core
    chip = me // 2
    up = lax.rem(me + n_rows - 1, n_rows)
    down = lax.rem(me + 1, n_rows)
    my_id = c * n_chips + chip
    sub = min(4, n_chips)
    cubes = n_chips // sub
    spot_in, cube = lax.rem(chip, sub), chip // sub
    my_id = c * sub + spot_in
    far = []
    for delta in range(1, 2 * sub):
        other = lax.rem(my_id + delta, 2 * sub)
        far.append((2 * (cube * sub + lax.rem(other, sub)) + core, other // sub))
    across = []
    for delta in range(1, cubes):
        across.append((2 * (lax.rem(cube + delta, cubes) * sub + spot_in) + core, c))
    around = []
    for delta in range(1, 2 * sub):
        other = lax.rem(2 * spot_in + core + delta, 2 * sub)
        around.append((2 * cube * sub + other, c))
    near = [(me, o), (mate, c), (up, c), (up, o), (down, c), (down, o)]

    barrier = pltpu.get_barrier_semaphore()
    for device in near + far + across + around:
        pl.semaphore_signal(barrier, inc=1, device_id=device, device_id_type=MESH)

    count = [0]
    sends = []

    def remote(src, dst, device):
        at = count[0]
        count[0] += 1
        return pltpu.make_async_remote_copy(
            src_ref=src,
            dst_ref=dst,
            send_sem=ssem.at[at],
            recv_sem=rsem.at[at],
            device_id=device,
            device_id_type=MESH,
        )

    def begin(*args):
        copy = remote(*args)
        copy.start()
        sends.append(copy)
        return copy

    img, cot, k10, k2 = ref["img_v"], ref["cot_v"], ref["k10_v"], ref["k2_v"]
    n1, n2 = 9 * cin, 9 * cout
    loads = []
    for i, (src, dst) in enumerate(
        [
            (ref["img"], img),
            (ref["k1"], k10.at[0:n1]),
            (ref["k0"], k10.at[n1 : n1 + cin]),
            (ref["k2"], k2.at[0:n2]),
            (ref["cot"], cot),
        ]
    ):
        load = pltpu.make_async_copy(src, dst, lsem.at[i])
        load.start()
        loads.append(load)

    perm_in, perm_x = ref["perm_in"], ref["perm_x"]
    shape = (8 * half, TILE)
    at, lane = iota(shape, 0), iota(shape, 1)
    column = 2 * lax.rem(at, half) + lax.rem(at // half, 4) - 1
    hit = (lane - at // (4 * half) * width == column) & (column >= 0) & (column < width)
    perm_in[...] = jnp.where(hit, 1.0, 0.0).astype(BF16)
    shape = (4 * half, TILE)
    at, lane = iota(shape, 0), iota(shape, 1)
    source = at // (2 * half) * width + 2 * lax.rem(at, half) + lax.rem(at // half, 2)
    perm_x[0 : 4 * half] = jnp.where(lane == source, 1.0, 0.0).astype(BF16)
    shape = (half, TILE)
    at, lane = iota(shape, 0), iota(shape, 1)
    perm_x[4 * half : 5 * half] = jnp.where(lax.rem(lane, width) // 2 == at, 1.0, 0.0).astype(BF16)

    def rem_pos(value, by):
        return lax.rem(lax.rem(value, by) + by, by)

    first_a = rem_pos(me * rows - SHIFT, total_rows)
    first_b = rem_pos(me * rows + cut - SHIFT, total_rows)
    base = [lax.rem(first_a, IMG), lax.rem(first_b, IMG) - cut]
    image_a, image_b = first_a // IMG, first_b // IMG
    keep = jnp.where(base[1] < 0, 0.0, 1.0).astype(F32)
    vh, vw = ref["vh"], ref["vw"]
    high = [[vh[c * per + j, image] for image in (image_a, image_b)] for j in range(per)]
    wide = [[vw[c * per + j, image] for image in (image_a, image_b)] for j in range(per)]

    def choose(seg, two):
        return jnp.where(seg == 0, two[0], two[1])

    vec = ref["vec"]
    vec[c] = jnp.zeros(vec.shape[1:], F32)
    for i, name in enumerate(("q1", "q2", "q0", "b1", "b2")):
        vec[c, i : i + 1, 0:co] = ref[name][...].astype(F32)

    imgr, sendp = ref["imgr"], ref["sendp"]
    loads[0].wait()
    for j in range(per):
        for mine in (False, True):

            def pack(p, carry, j=j, mine=mine):
                m = (c if mine else o) * per + j
                pair = jnp.concatenate([img[m, 2 * p], img[m, 2 * p + 1]], axis=1)
                if mine:
                    imgr[j, c, p + 1] = pair
                else:
                    sendp[j, p] = pair
                return carry

            lax.fori_loop(0, pairs, pack, 0, unroll=4)
    for load in loads[1:]:
        load.wait()

    pl.semaphore_wait(barrier, len(near + far + across + around))

    k10h, k2h, cotr = ref["k10h"], ref["k2h"], ref["cotr"]
    spots = [core] + [lax.rem(me // 2**b, 2) for b in range(1, bits)]
    mates = [mate] + [me + 2**b * (1 - 2 * spots[b]) for b in range(1, bits)]

    def piece(rows_each, level, depth):
        first = 0
        for b in range(depth - level):
            first = first * 2 + spots[b]
        return pl.ds(first * (2**level * rows_each), 2**level * rows_each)

    class Shared:
        def __init__(self, own, got, rows_each, depth):
            self.got, self.rows_each, self.depth, self.level = got, rows_each, depth, 0
            at = piece(rows_each, 0, depth)
            self.copy = begin(own.at[at], got.at[at], (me, o))

        def turn(self):
            self.copy.wait_recv()
            if self.level < self.depth:
                at = piece(self.rows_each, self.level, self.depth)
                device = (mates[self.depth - 1 - self.level], c)
                self.copy = begin(self.got.at[at], self.got.at[at], device)
            self.level += 1

    mine_c, mine_o = pl.ds(c * per, per), pl.ds(o * per, per)
    img_x, img_halo = [], []

    def send_image(j):
        img_x.append(begin(sendp.at[j], imgr.at[j, c, pl.ds(1, pairs)], (me, o)))
        img_halo.append(
            [
                begin(sendp.at[j, 0], imgr.at[j, c, pairs + 1], (up, o)),
                begin(sendp.at[j, pairs - 1], imgr.at[j, c, 0], (down, o)),
                begin(imgr.at[j, c, 1], imgr.at[j, c, pairs + 1], (up, c)),
                begin(imgr.at[j, c, pairs], imgr.at[j, c, 0], (down, c)),
            ]
        )

    vec_x = begin(vec.at[c], vec.at[c], (me, o))
    one = Shared(k10, k10h, share1, 2)
    send_image(0)
    two = Shared(k2, k2h, share2, bits)
    for j in range(1, per):
        send_image(j)
    cot_x = begin(cot.at[mine_o], cotr.at[:, c, pl.ds(1, pairs)], (me, o))
    cot_halo = [
        begin(cot.at[mine_o, 0], cotr.at[:, c, pairs + 1], (up, o)),
        begin(cot.at[mine_o, pairs - 1], cotr.at[:, c, 0], (down, o)),
        begin(cot.at[mine_c, 0], cotr.at[:, c, pairs + 1], (up, c)),
        begin(cot.at[mine_c, pairs - 1], cotr.at[:, c, 0], (down, c)),
    ]

    w1, w2, w0 = ref["w1"], ref["w2"], ref["w0"]

    def place(dst, row, own_part, other_part, padded):
        size = own_part.shape[0]
        first = jnp.where(c == 0, own_part, other_part)
        second = jnp.where(c == 0, other_part, own_part)
        line = jnp.concatenate([first, second, jnp.zeros((size, op - cout), BF16)], axis=1)
        dst[pl.ds(row, size), :] = line
        if padded > size:
            dst[pl.ds(row + size, padded - size), :] = jnp.zeros((padded - size, op), BF16)

    def row_of(i):
        return jnp.concatenate(
            [vec[0, i : i + 1, 0:co], vec[1, i : i + 1, 0:co], jnp.zeros((1, op - cout), F32)], axis=1
        )

    b_in, xp, xb = ref["b_in"], ref["xp"], ref["xb"]
    ones = jnp.where(iota((TILE - cin, TILE), 0) == 0, 1.0, 0.0).astype(BF16)

    def prepare(j):
        img_x[j].wait_recv()
        for copy in img_halo[j]:
            copy.wait_recv()

        def two_pairs(step, carry):
            lane = iota((1, TILE), 1)
            column = lax.rem(lane, width)
            acts, plain, slots = [], [], []
            for k in range(2):
                p = 2 * step + k
                seg = (p >= pairs_a).astype(jnp.int32)
                row = 2 * p - 2 + lane // width
                mask = jnp.where(
                    (choose(seg, base) + row < choose(seg, high[j])) & (column < choose(seg, wide[j])), 1.0, 0.0
                )
                x = jnp.concatenate([imgr[j, 0, p], imgr[j, 1, p]], axis=0).astype(F32) * mask
                act = x / (1.0 + jnp.exp(-x))
                acts += [act.astype(BF16), ones]
                plain += [x.astype(BF16), ones]
                slots.append(2 * p + 2 * seg)
            spread = dot(perm_in[...], jnp.concatenate(acts, axis=0), NT).astype(BF16)
            for k in range(2):
                for a in range(2):
                    for t in range(4):
                        b_in[j, slots[k] + a, :, t * TILE : (t + 1) * TILE] = spread[
                            (4 * a + t) * half : (4 * a + t + 1) * half, k * TILE : (k + 1) * TILE
                        ]
            spread = dot(perm_x[...], jnp.concatenate(plain, axis=0), NT).astype(BF16)
            for k in range(2):
                part = spread[:, k * TILE : (k + 1) * TILE]
                xp[j, 2 * step + k] = part[0 : 4 * half]
                xb[j, 2 * step + k] = part[4 * half : 5 * half]
            return carry

        lax.fori_loop(0, (pairs + 2) // 2, two_pairs, 0, unroll=True)
        b_in[j, seg_slots - 1] = (b_in[j, seg_slots + 1].astype(F32) * keep).astype(BF16)
        b_in[j, seg_slots] = (b_in[j, seg_slots - 2].astype(F32) * keep).astype(BF16)

    raw1, grad1 = ref["raw1"], ref["grad1"]

    def conv_one(j):
        def segment(seg, carry):
            parts = []
            for b in range(2):
                taps = [
                    b_in[j, pl.ds(seg * seg_slots + u, seg_out), :, b * TILE : (b + 3) * TILE].reshape(
                        seg_out * half, 3 * TILE
                    )
                    for u in range(3)
                ]
                parts.append(jnp.concatenate(taps, axis=1))
            result = dot(jnp.concatenate(parts, axis=0), w1[...])
            for b in range(2):
                raw1[j, b, pl.ds(seg * seg_out, seg_out)] = result[
                    b * seg_out * half : (b + 1) * seg_out * half
                ].reshape(seg_out, half, op)
            return carry

        lax.fori_loop(0, 2, segment, 0)

    cols = ref["cols"]
    pixel = iota((half, op), 0)

    def activate(j):
        def line(i, carry):
            seg = (i >= seg_out).astype(jnp.int32)
            broad = jnp.where(choose(seg, base) + i - 1 < choose(seg, high[j]), choose(seg, wide[j]), 0)
            acts = []
            for b in range(2):
                pre = raw1[j, b, i] * scale1 + bias1
                gate = 1.0 / (1.0 + jnp.exp(-pre))
                mask = 2 * pixel + b < broad
                lift = pre * gate
                grad1[j, b, i] = jnp.where(mask, gate + lift * (1.0 - gate), 0.0)
                acts.append(jnp.where(mask, lift, 0.0).astype(BF16).astype(F32))
            even, odd = acts
            before = jnp.where(pixel == 0, 0.0, pltpu.roll(odd, 1, 0))
            after = jnp.where(pixel == half - 1, 0.0, pltpu.roll(even, half - 1, 0))
            cols[j, 0, i] = before + even
            cols[j, 1, i] = even + odd
            cols[j, 2, i] = odd + after
            return carry

        lax.fori_loop(0, 2 * seg_out, line, 0, unroll=2)

    box = ref["box"]

    def boxes(j):
        def line(i, carry):
            above = jnp.where(i == cut // 2, keep, 1.0)
            below = jnp.where(i == cut // 2 - 1, keep, 1.0)
            for w in range(3):
                lines = [cols[j, w, 2 * i + k] for k in range(4)]
                for u in range(3):
                    upper, lower = lines[u], lines[u + 1]
                    if u == 0:
                        upper = upper * above
                    if u == 2:
                        lower = lower * below
                    tap = 3 * u + w
                    box[j, i, :, tap * op : (tap + 1) * op] = (upper + lower).astype(BF16)
            return carry

        lax.fori_loop(0, pairs, line, 0, unroll=2)

    quart = ref["quart"]

    def quarter(j):
        def put(i, own, other):
            first = jnp.where(c == 0, own, other)
            second = jnp.where(c == 0, other, own)
            line = jnp.concatenate([first, second, jnp.zeros((half, op - cout), BF16)], axis=1)
            quart[j, i] = (line.astype(F32) * 0.25).astype(BF16)

        def inner(i, carry):
            put(i + 1, cot[c * per + j, i], cotr[j, o, i + 1])
            return carry

        lax.fori_loop(0, pairs, inner, 0, unroll=4)
        for i in (0, pairs + 1):
            put(i, cotr[j, c, i], cotr[j, o, i])

    def owned(j):
        return quart[j, 1 : pairs + 1].reshape(own_px, op)

    half_rows = co // 2
    kept_rows = pl.ds(core * half_rows, half_rows)
    mate_rows = pl.ds((1 - core) * half_rows, half_rows)

    class Summed:
        def __init__(self, name):
            self.wire, self.got, self.shares, self.landing, self.mine, self.mids, self.result = [
                ref[part + name] for part in ("wire", "got", "shares", "landing", "mine", "mids", "result")
            ]
            self.share = self.result.shape[2]
            self.copies = [begin(self.wire.at[:, mate_rows], self.got, (mate, c))]

        def arrived(self):
            for copy in self.copies:
                copy.wait_recv()

        def to_owners(self):
            self.arrived()
            for ch in range(2):
                value = self.wire[ch, kept_rows].astype(F32) + self.got[ch].astype(F32)
                for at in range(sub):
                    part = value[:, at * self.share : (at + 1) * self.share]
                    self.shares[ch, at] = part.astype(BF16)

                    @pl.when(my_id == ch * sub + at)
                    def _():
                        self.mine[...] = part

            self.copies = []
            for delta in range(1, 2 * sub):
                other = lax.rem(my_id + delta, 2 * sub)
                self.copies.append(
                    begin(
                        self.shares.at[other // sub, lax.rem(other, sub)], self.landing.at[delta - 1], far[delta - 1]
                    )
                )

        def to_cubes(self):
            self.arrived()
            value = self.mine[...]
            for delta in range(1, 2 * sub):
                value = value + self.landing[delta - 1].astype(F32)
            self.mids[cube] = value.astype(BF16)
            self.copies = [begin(self.mids.at[cube], self.mids.at[cube], device) for device in across]

        def to_all(self):
            self.arrived()
            value = self.mids[0].astype(F32)
            for at in range(1, cubes):
                value = value + self.mids[at].astype(F32)
            self.result[spot_in, kept_rows] = value.astype(BF16)
            place_at = self.result.at[spot_in, kept_rows]
            self.copies = [begin(place_at, place_at, device) for device in around]

        def flat(self):
            self.arrived()
            return jnp.concatenate([self.result[at].astype(F32) for at in range(sub)], axis=1)

    one.turn()
    prepare(0)
    one.turn()
    two.turn()
    one.turn()
    vec_x.wait_recv()
    for tap in range(9):
        rows_at = slice(tap * cin, (tap + 1) * cin)
        place(w1, tap * TILE, k10[rows_at], k10h[rows_at], TILE)
    rows_at = slice(n1, n1 + cin)
    place(w0, 0, k10[rows_at], k10h[rows_at], TILE)
    left1, right1, sigma1 = power(row_of(0), w1[...])
    left0, right0, sigma0 = power(row_of(2), w0[...])
    scale1, scale0 = 1.0 / sigma1, 1.0 / sigma0
    bias1, bias2 = row_of(3), row_of(4)
    left1_ref, left2_ref, left0_ref = ref["left1"], ref["left2"], ref["left0"]
    left1_ref[0:1] = left1
    left0_ref[0:1] = left0
    conv_one(0)
    activate(0)
    two.turn()
    boxes(0)
    for j in range(1, per):
        prepare(j)
        conv_one(j)
        if j == 1:
            two.turn()
        activate(j)
        boxes(j)
    cot_x.wait_recv()
    for copy in cot_halo:
        copy.wait_recv()
    for j in range(per):
        quarter(j)

    acc0 = ref["acc0"]
    given = jnp.concatenate([owned(j) for j in range(per)], axis=0)[:, 0:cout]
    turned_quart = jnp.transpose(given)
    group_a = None
    for name, taps in (("a", range(0, 5)), ("b", range(5, 9))):
        lanes = slice(taps[0] * op, (taps[-1] + 1) * op)
        value = dot(turned_quart, box[:, :, :, lanes].reshape(per * own_px, len(taps) * op))
        parts = [value[:, k * op : k * op + cout] for k in range(len(taps))]
        if name == "b":
            skip = dot(turned_quart, xb[:, 1 : pairs + 1].reshape(per * own_px, TILE))
            acc0[...] = skip
            parts.append(skip[:, 0:cin])
        parts.append(jnp.zeros((cout, lanes_each - sum(part.shape[1] for part in parts)), F32))
        flat = jnp.concatenate(parts, axis=1).astype(BF16)
        for ch in range(2):
            ref["wire" + name][ch] = flat[ch * co : (ch + 1) * co]
        if name == "a":
            group_a = Summed("a")
    group_b = Summed("b")
    for turn in range(two.level, bits + 1):
        two.turn()
    for tap in range(9):
        rows_at = slice(tap * cout, (tap + 1) * cout)
        place(w2, tap * op, k2[rows_at], k2h[rows_at], op)
    left2, right2, sigma2 = power(row_of(1), w2[...])
    scale2 = 1.0 / sigma2
    left2_ref[0:1] = left2

    taps_sum = ref["taps_sum"]
    spot = iota((all_px, op), 0)
    at_left = lax.rem(spot, half) == 0
    at_right = lax.rem(spot, half) == half - 1
    g_pre = ref["g_pre"]

    def back_two(j, dot1):
        given = quart[j].reshape(all_px, op)
        for u in range(3):
            t0, t1, t2 = [
                dot(given, w2[(3 * u + w) * op : (3 * u + w + 1) * op], NT) for w in range(3)
            ]
            even = t0 + t1 + jnp.where(at_left, 0.0, pltpu.roll(t2, 1, 0))
            odd = t1 + t2 + jnp.where(at_right, 0.0, pltpu.roll(t0, all_px - 1, 0))
            taps_sum[u, 0] = even.reshape(pairs + 2, half, op)
            taps_sum[u, 1] = odd.reshape(pairs + 2, half, op)

        def line(i, carry):
            hold = jnp.where(i == cut // 2, keep, 1.0)
            own_even = jnp.where(i < pairs, 1.0, 0.0)
            own_odd = jnp.where(i > 0, 1.0, 0.0)
            for b in range(2):
                upper, lower = taps_sum[2, b, i], taps_sum[0, b, i + 1]
                even = lower + taps_sum[1, b, i + 1] + hold * upper
                odd = taps_sum[1, b, i] + upper + hold * lower
                even = (even * scale2 * grad1[j, b, 2 * i + 1]).astype(BF16)
                odd = (odd * scale2 * grad1[j, b, 2 * i]).astype(BF16)
                g_pre[j, b, 2 * i + 1] = even
                g_pre[j, b, 2 * i] = odd
                carry = carry + own_even * even.astype(F32) * raw1[j, b, 2 * i + 1]
                carry = carry + own_odd * odd.astype(F32) * raw1[j, b, 2 * i]
            return carry

        return lax.fori_loop(0, pairs + 1, line, dot1, unroll=3)

    group_a.to_owners()
    group_b.to_owners()
    dot1 = jnp.zeros((half, op), F32)
    for j in range(per):
        dot1 = back_two(j, dot1)

    acc1 = ref["acc1"]

    def kernel_one_grad(step, carry):
        j, seg = step // 2, lax.rem(step, 2)
        value = None
        for b in range(2):
            given = g_pre[j, b, pl.ds(seg * cut + 1, cut)].reshape(cut * half, op)[:, 0:cout]
            taps = [
                b_in[j, pl.ds(seg * (cut + 2) + 1 + u, cut), :, b * TILE : (b + 3) * TILE].reshape(
                    cut * half, 3 * TILE
                )
                for u in range(3)
            ]
            part = dot(given, jnp.concatenate(taps, axis=1), TN)
            value = part if value is None else value + part
        acc1[...] = acc1[...] + value
        return carry

    acc1[...] = jnp.zeros_like(acc1)
    lax.fori_loop(0, 2 * per, kernel_one_grad, 0)
    spare = lanes_each - 9 * cin - 6

    def pair_of(column):
        high_part = column.astype(BF16).astype(F32)
        return [high_part, column - high_part]

    parts = [acc1[:, tap * TILE : tap * TILE + cin] for tap in range(9)]
    parts += pair_of(acc1[:, 4 * TILE + cin : 4 * TILE + cin + 1])
    parts += pair_of(acc0[:, cin : cin + 1])
    parts += pair_of(jnp.broadcast_to(total(dot1), (cout, 1)))
    parts.append(jnp.zeros((cout, spare), F32))
    flat = jnp.concatenate(parts, axis=1).astype(BF16)
    for ch in range(2):
        ref["wirec"][ch] = flat[ch * co : (ch + 1) * co]
    group_c = Summed("c")

    out_b, send_b, got_b = ref["out_b"], ref["send_b"], ref["got_b"]

    def conv_two(j):
        main = dot(box[j].reshape(own_px, 9 * op), w2[...])
        skip = dot(xb[j, 1 : pairs + 1].reshape(own_px, TILE), w0[...])
        value = ((main * scale2 + skip * scale0) * 0.25 + bias2).astype(BF16)
        first, second = value[:, 0:co], value[:, co:cout]
        out_b[c * per + j] = jnp.where(c == 0, first, second).reshape(pairs, half, co)
        send_b[j] = jnp.where(c == 0, second, first).reshape(pairs, half, co)

    taps_in, skip_back = ref["taps_in"], ref["skip_back"]
    pixel_in = iota((half, TILE), 0)
    out_g, send_g, got_g = ref["out_g"], ref["send_g"], ref["got_g"]

    def back_products(j):
        skip_back[...] = (dot(owned(j), w0[...], NT) * scale0).reshape(pairs, half, TILE)

        def some(step, carry):
            b, part = step // 2, lax.rem(step, 2)
            given = g_pre[j, b, pl.ds(part * seg_out, seg_out)].reshape(seg_out * half, op)
            taps_in[b, pl.ds(part * seg_out, seg_out)] = dot(given, w1[...], NT).reshape(
                seg_out, half, 9 * TILE
            )
            return carry

        lax.fori_loop(0, 4, some, 0)

    def input_rows(j):
        def two_rows(p, carry):
            lines = []
            for a in range(2):
                r = 2 * p + a
                hold_up = jnp.where(r == cut - 1, keep, 1.0)
                hold_down = jnp.where(r == cut, keep, 1.0)

                def column_sum(w, s):
                    def of(u, row):
                        at = (3 * u + w) * TILE
                        return taps_in[s, row, :, at : at + TILE]

                    return of(0, r + 2) * hold_up + of(1, r + 1) + of(2, r) * hold_down

                before = pltpu.roll(column_sum(2, 1), 1, 0)
                after = pltpu.roll(column_sum(0, 0), half - 1, 0)
                even = column_sum(0, 1) + column_sum(1, 0) + jnp.where(pixel_in == 0, 0.0, before)
                odd = column_sum(1, 1) + column_sum(2, 0) + jnp.where(pixel_in == half - 1, 0.0, after)
                seg = (r >= cut).astype(jnp.int32)
                broad = jnp.where(choose(seg, base) + r < choose(seg, high[j]), choose(seg, wide[j]), 0)
                for b, value in ((0, even), (1, odd)):
                    at = (2 * a + b) * half
                    x = xp[j, p + 1, at : at + half].astype(F32)
                    mask = 2 * pixel_in + b < broad
                    value = slope(x) * (value * scale1) + skip_back[p]
                    lines.append(jnp.where(mask, value, 0.0).astype(BF16))
            line = dot(jnp.concatenate(lines, axis=0), perm_x[0 : 4 * half], TN).astype(BF16)
            own = jnp.where(c == 0, line[0:ci], line[ci:cin])
            other = jnp.where(c == 0, line[ci:cin], line[0:ci])
            out_g[c * per + j, 2 * p] = own[:, 0:width]
            out_g[c * per + j, 2 * p + 1] = own[:, width:TILE]
            send_g[j, p] = other
            return carry

        lax.fori_loop(0, pairs, two_rows, 0, unroll=4)
        return begin(send_g.at[j], got_g.at[j], (me, o))

    def unpack(j):
        def line(p, carry):
            out_g[o * per + j, 2 * p] = got_g[j, p, :, 0:width]
            out_g[o * per + j, 2 * p + 1] = got_g[j, p, :, width:TILE]
            return carry

        grad_x[j].wait_recv()
        lax.fori_loop(0, pairs, line, 0, unroll=4)

    for j in range(per):
        conv_two(j)
    group_c.to_owners()
    out_x = begin(send_b, got_b, (me, o))
    back_products(0)
    group_a.to_cubes()
    grad_x = [input_rows(0)]
    group_b.to_cubes()
    for j in range(1, per):
        back_products(j)
        if j == 1:
            group_a.to_all()
        grad_x.append(input_rows(j))
    def own_half(row):
        return jnp.where(c == 0, row[:, 0:co], row[:, co:cout])

    def column_of(row):
        row = jnp.concatenate([own_half(row), jnp.zeros((1, TILE - co), F32)], axis=1)
        return jnp.transpose(jnp.broadcast_to(row, (TILE, TILE)))[0:co]

    def compact(row, size, padded):
        return jnp.concatenate([row[:, t * padded : t * padded + size] for t in range(9)], axis=1)

    def turned(part, out, at):
        some = part.shape[1]
        if some < TILE:
            part = jnp.concatenate([part, jnp.zeros((co, TILE - some), F32)], axis=1)
        part = jnp.concatenate([part, jnp.zeros((TILE - co, TILE), F32)], axis=0)
        out[at : at + some] = jnp.transpose(part)[0:some, 0:co]

    def outer(left, right, out):
        columns = column_of(right)
        for at in range(0, left.shape[1], TILE):
            some = min(TILE, left.shape[1] - at)
            turned(columns[:, 0:some] * left[:, at : at + some], out, at)

    corr1, corr2, corr0 = ref["corr1"], ref["corr2"], ref["corr0"]
    group_c.to_cubes()
    group_b.to_all()
    outer(compact(left1_ref[0:1], cin, TILE), right1 * (scale1 * scale1), corr1)
    outer(compact(left2_ref[0:1], cout, op), right2 * scale2, corr2)
    outer(left0_ref[0:1, 0:cin], right0 * scale0, corr0)
    out_k1, out_k2, out_k0 = ref["out_k1"], ref["out_k2"], ref["out_k0"]
    group_c.to_all()
    flat = group_a.flat()
    for at in range(0, 5 * cout, TILE):
        turned(flat[:, at : min(at + TILE, 5 * cout)] * scale2, out_k2, at)
    flat = group_b.flat()
    for at in range(0, 4 * cout, TILE):
        turned(flat[:, at : min(at + TILE, 4 * cout)] * scale2, out_k2, 5 * cout + at)
    turned(flat[:, 4 * cout : 4 * cout + cin] * scale0, out_k0, 0)

    dots = ref["dots"]
    at = iota((8, TILE), 0)
    sum2 = total(out_k2[...] * k2[0:n2].astype(F32))
    sum0 = total(out_k0[...] * k10[n1 : n1 + cin].astype(F32))
    dots[c] = jnp.where(at == 0, sum2, jnp.where(at == 1, sum0, 0.0))
    dots_x = begin(dots.at[c], dots.at[c], (me, o))
    out_x.wait_recv()
    out_b[mine_o] = got_b[...]
    for j in range(per):
        unpack(j)
    dots_x.wait_recv()
    both = dots[0] + dots[1]
    for out, corr, row in ((out_k2, corr2, 0), (out_k0, corr0, 1)):
        out[...] = out[...] - corr[...] * both[row : row + 1, 0:1]
    flat = group_c.flat()
    extra = flat[:, n1 : n1 + 6]
    sum1 = extra[0:1, 4:5] + extra[0:1, 5:6]
    biases = jnp.concatenate([extra, jnp.zeros((co, TILE - 6), F32)], axis=1)
    biases = jnp.transpose(jnp.concatenate([biases, jnp.zeros((TILE - co, TILE), F32)], axis=0))
    ref["out_b1"][...] = biases[0:1, 0:co] + biases[1:2, 0:co]
    ref["out_b2"][...] = biases[2:3, 0:co] + biases[3:4, 0:co]
    for at in range(0, n1, TILE):
        turned(flat[:, at : min(at + TILE, n1)] * scale1, out_k1, at)
    out_k1[...] = out_k1[...] - corr1[...] * sum1

    for copy in sends:
        copy.wait_send()


def hand_over(arrays):
    number = len(arrays)

    def copy_all(*refs):
        sem = refs[-1]
        copies = [pltpu.make_async_copy(refs[i], refs[number + i], sem.at[i]) for i in range(number)]
        for copy in copies:
            copy.start()
        for copy in copies:
            copy.wait()

    return pl.pallas_call(
        copy_all,
        out_shape=[jax.ShapeDtypeStruct(a.shape, a.dtype) for a in arrays],
        in_specs=[pl.BlockSpec(memory_space=pltpu.VMEM)] * number,
        out_specs=[pl.BlockSpec(memory_space=pl.ANY)] * number,
        scratch_shapes=[pltpu.SemaphoreType.DMA((number,))],
        name="hand_over",
    )(*[pltpu.with_memory_space_constraint(a, pltpu.VMEM) for a in arrays])


def fused(n_rows, arrays):
    (images, valid_h, valid_w, kernel_one, kernel_two, kernel_skip, bias_one, bias_two,
     vector_one, vector_two, vector_skip, cotangent) = arrays
    micros, rows, width, ci = images.shape
    co = kernel_one.shape[3]
    per, pairs, half = micros // 2, rows // 2, width // 2
    op = 2 * TILE
    n_chips = n_rows // 2
    cin, cout = 2 * ci, 2 * co
    sub = min(4, n_chips)
    cubes = n_chips // sub
    lanes_each = -(-max(9 * cin + 6, 5 * cout, 4 * cout + cin) // (TILE * sub)) * (TILE * sub)
    seg_out = rows // 2 + 1
    bits = 3 if n_rows % 8 == 0 else 2
    share1 = -(-(10 * cin) // 64) * 16
    share2 = -(-(9 * cout) // (16 * 2**bits)) * 16
    inputs = {
        "vh": valid_h,
        "vw": valid_w,
        "img": jnp.transpose(images, (0, 1, 3, 2)),
        "k1": kernel_one.reshape(9 * cin, co),
        "k2": kernel_two.reshape(9 * cout, co),
        "k0": kernel_skip,
        "b1": bias_one.reshape(1, co),
        "b2": bias_two.reshape(1, co),
        "q1": vector_one.reshape(1, co),
        "q2": vector_two.reshape(1, co),
        "q0": vector_skip.reshape(1, co),
        "cot": cotangent,
    }
    outputs = {
        "out_b": jax.ShapeDtypeStruct(cotangent.shape, BF16),
        "out_g": jax.ShapeDtypeStruct((micros, rows, ci, width), BF16),
        "out_k1": jax.ShapeDtypeStruct((9 * cin, co), F32),
        "out_k2": jax.ShapeDtypeStruct((9 * cout, co), F32),
        "out_k0": jax.ShapeDtypeStruct((cin, co), F32),
        "out_b1": jax.ShapeDtypeStruct((1, co), F32),
        "out_b2": jax.ShapeDtypeStruct((1, co), F32),
    }
    vm = pltpu.VMEM
    scratch = {
        "img_v": vm((micros, rows, ci, width), BF16),
        "cot_v": vm(cotangent.shape, BF16),
        "k10_v": vm((4 * share1, co), BF16),
        "k2_v": vm((2**bits * share2, co), BF16),
        "k10h": vm((4 * share1, co), BF16),
        "k2h": vm((2**bits * share2, co), BF16),
        "imgr": vm((per, 2, pairs + 2, ci, TILE), BF16),
        "sendp": vm((per, pairs, ci, TILE), BF16),
        "vec": vm((2, 8, TILE), F32),
        "cotr": vm((per, 2, pairs + 2, half, co), BF16),
        "perm_in": vm((8 * half, TILE), BF16),
        "perm_x": vm((5 * half, TILE), BF16),
        "w1": vm((9 * TILE, op), BF16),
        "w2": vm((9 * op, op), BF16),
        "w0": vm((TILE, op), BF16),
        "left1": vm((8, 9 * TILE), F32),
        "left2": vm((8, 9 * op), F32),
        "left0": vm((8, TILE), F32),
        "b_in": vm((per, 2 * (rows // 2 + 3), half, 4 * TILE), BF16),
        "xp": vm((per, pairs + 2, 4 * half, TILE), BF16),
        "xb": vm((per, pairs + 2, half, TILE), BF16),
        "raw1": vm((per, 2, 2 * seg_out, half, op), F32),
        "grad1": vm((per, 2, 2 * seg_out, half, op), F32),
        "cols": vm((per, 3, 2 * seg_out, half, op), F32),
        "box": vm((per, pairs, half, 9 * op), BF16),
        "quart": vm((per, pairs + 2, half, op), BF16),
        "acc0": vm((cout, TILE), F32),
        "acc1": vm((cout, 9 * TILE), F32),
        "taps_sum": vm((3, 2, pairs + 2, half, op), F32),
        "g_pre": vm((per, 2, 2 * seg_out, half, op), BF16),
        "taps_in": vm((2, 2 * seg_out, half, 9 * TILE), F32),
        "skip_back": vm((pairs, half, TILE), F32),
        "send_b": vm((per, pairs, half, co), BF16),
        "got_b": vm((per, pairs, half, co), BF16),
        "send_g": vm((per, pairs, ci, TILE), BF16),
        "got_g": vm((per, pairs, ci, TILE), BF16),
    }
    for name, size in (("corr1", 9 * cin), ("corr2", 9 * cout), ("corr0", cin)):
        scratch[name] = vm((size, co), F32)
    share = lanes_each // sub
    for name in ("a", "b", "c"):
        scratch["wire" + name] = vm((2, co, lanes_each), BF16)
        scratch["got" + name] = vm((2, co // 2, lanes_each), BF16)
        scratch["shares" + name] = vm((2, sub, co // 2, share), BF16)
        scratch["landing" + name] = vm((2 * sub - 1, co // 2, share), BF16)
        scratch["mine" + name] = vm((co // 2, share), F32)
        scratch["mids" + name] = vm((cubes, co // 2, share), BF16)
        scratch["result" + name] = vm((sub, co, share), BF16)
    scratch["dots"] = vm((2, 8, TILE), F32)
    copies = 13 + bits + 6 * per + 3 * (1 + 2 * (2 * sub - 1) + cubes - 1)
    scratch["lsem"] = pltpu.SemaphoreType.DMA((5,))
    scratch["ssem"] = pltpu.SemaphoreType.DMA((copies,))
    scratch["rsem"] = pltpu.SemaphoreType.DMA((copies,))
    names = list(inputs) + list(outputs) + list(scratch)
    dims = (micros, rows, width, ci, co, lanes_each, bits, share1, share2)
    smem = pl.BlockSpec(memory_space=pltpu.SMEM)
    vmem = pl.BlockSpec(memory_space=pltpu.VMEM)
    hbm = pl.BlockSpec(memory_space=pltpu.HBM)
    large = ("img", "k1", "k2", "k0", "cot")
    small = ("b1", "b2", "q1", "q2", "q0")
    results = pl.pallas_call(
        functools.partial(fused_kernel, names, n_rows, dims),
        out_shape=[pltpu.VMEM(a.shape, a.dtype) for a in outputs.values()],
        in_specs=[smem, smem] + [vmem if n in small else hbm for n in list(inputs)[2:]],
        out_specs=[vmem] * len(outputs),
        scratch_shapes=list(scratch.values()),
        compiler_params=pltpu.CompilerParams(
            collective_id=0, has_side_effects=True, vmem_limit_bytes=48 * 1024 * 1024
        ),
        name="down_block",
    )(*[pltpu.with_memory_space_constraint(a, pltpu.HBM) if n in large else a for n, a in inputs.items()])
    out_b, out_g, out_k1, out_k2, out_k0, out_b1, out_b2 = hand_over(results)
    return (
        out_b,
        jnp.transpose(out_g, (0, 1, 3, 2)),
        out_k1.reshape(3, 3, cin, co),
        out_k2.reshape(3, 3, cout, co),
        out_k0,
        out_b1.reshape(co),
        out_b2.reshape(co),
    )


def solution(mesh):
    in_specs = (
        P(None, "rows", None, "ch"),
        P(),
        P(),
        P(None, None, None, "ch"),
        P(None, None, None, "ch"),
        P(None, "ch"),
        P("ch"),
        P("ch"),
        P("ch"),
        P("ch"),
        P("ch"),
        P(None, "rows", None, "ch"),
    )
    out_specs = (
        P(None, "rows", None, "ch"),
        P(None, "rows", None, "ch"),
        P(None, None, None, "ch"),
        P(None, None, None, "ch"),
        P(None, "ch"),
        P("ch"),
        P("ch"),
    )

    def step(*arrays):
        if fits(mesh.shape["rows"], mesh.shape["ch"], arrays):
            return fused(mesh.shape["rows"], arrays)
        return shards(*arrays)

    return jax.shard_map(step, mesh=mesh, in_specs=in_specs, out_specs=out_specs, check_vma=False)
```

```python
import functools

import jax
import jax.numpy as jnp
from jax import lax
from jax.experimental import pallas as pl
from jax.experimental.pallas import tpu as pltpu
from jax.sharding import PartitionSpec as P

IMG = 64
SHIFT = 40


EPS = 1e-06
HIGH = lax.Precision.HIGHEST


def extended(cells, sides, width):
    for axis, dim in sides:
        count = lax.axis_size(axis)
        head = lax.slice_in_dim(cells, 0, width, axis=dim)
        tail = lax.slice_in_dim(cells, cells.shape[dim] - width, cells.shape[dim], axis=dim)
        cells = jnp.concatenate(
            [
                lax.ppermute(tail, axis, [(i, (i + 1) % count) for i in range(count)]),
                cells,
                lax.ppermute(head, axis, [((i + 1) % count, i) for i in range(count)]),
            ],
            axis=dim,
        )
    return cells


def conv_rows(rim, kernel, taps):
    slab_rows = taps.shape[1]
    result = None
    for row_tap in range(3):
        part = lax.conv_general_dilated(
            rim[None, row_tap : row_tap + slab_rows],
            kernel[row_tap : row_tap + 1],
            (1, 1),
            ((0, 0), (1, 1)),
            dimension_numbers=("NHWC", "HWIO", "NHWC"),
            preferred_element_type=jnp.float32,
        )
        part = part[0] * taps[row_tap][:, None, None]
        result = part if result is None else result + part
    return result


def flipped(kernel):
    return jnp.transpose(kernel[::-1, ::-1], (0, 1, 3, 2))


def kernel_taps(rim, grad, taps_low):
    slab_rows = grad.shape[0]
    width = grad.shape[1]
    padded = jnp.pad(rim, ((0, 0), (1, 1), (0, 0)))
    stacked = []
    for row_tap in range(3):
        kept_grad = grad * taps_low[row_tap][:, None, None]
        line = []
        for col_tap in range(3):
            window = padded[row_tap : row_tap + slab_rows, col_tap : col_tap + width]
            line.append(
                jnp.einsum("rci,rco->io", window, kept_grad, preferred_element_type=jnp.float32)
            )
        stacked.append(jnp.stack(line))
    return jnp.stack(stacked)


def silu_slope(value):
    gate = jax.nn.sigmoid(value)
    return gate + value * gate * (1.0 - gate)


def shards(
    images,
    valid_h,
    valid_w,
    kernel_one,
    kernel_two,
    kernel_skip,
    bias_one,
    bias_two,
    vector_one,
    vector_two,
    vector_skip,
    cotangent,
):
    micros, rows_dev, width, in_local = images.shape
    out_local = kernel_one.shape[3]
    count_images = valid_h.shape[1]
    total_rows = rows_dev * lax.axis_size("rows")
    slab_start = lax.axis_index("rows") * rows_dev
    rim_global = slab_start - 1 + jnp.arange(rows_dev + 2, dtype=jnp.int32)
    placed = jnp.mod(rim_global - SHIFT, total_rows)
    image_of = placed // IMG
    row_of = placed % IMG
    taps = jnp.stack(
        [image_of[tap : tap + rows_dev] == image_of[1 : rows_dev + 1] for tap in range(3)]
    ).astype(jnp.float32)
    taps_low = taps.astype(jnp.bfloat16)
    owner = image_of[:, None] == jnp.arange(count_images, dtype=jnp.int32)[None, :]
    columns = jnp.arange(width)
    kern_one = kernel_one.astype(jnp.float32)
    kern_two = kernel_two.astype(jnp.float32)
    kern_skip = kernel_skip.astype(jnp.float32).reshape(1, 1, -1, out_local)
    part_one = jnp.einsum("hwio,o->hwi", kern_one, vector_one, precision=HIGH)
    part_two = jnp.einsum("hwio,o->hwi", kern_two, vector_two, precision=HIGH)
    part_skip = jnp.einsum("hwio,o->hwi", kern_skip, vector_skip, precision=HIGH)
    left_one, left_two, left_skip = lax.psum((part_one, part_two, part_skip), "ch")
    left_one = left_one * lax.rsqrt(jnp.sum(left_one * left_one) + EPS)
    left_two = left_two * lax.rsqrt(jnp.sum(left_two * left_two) + EPS)
    left_skip = left_skip * lax.rsqrt(jnp.sum(left_skip * left_skip) + EPS)
    image_one = jnp.einsum("hwio,hwi->o", kern_one, left_one, precision=HIGH)
    image_two = jnp.einsum("hwio,hwi->o", kern_two, left_two, precision=HIGH)
    image_skip = jnp.einsum("hwio,hwi->o", kern_skip, left_skip, precision=HIGH)
    square_one, square_two, square_skip = lax.psum(
        (
            jnp.sum(image_one * image_one),
            jnp.sum(image_two * image_two),
            jnp.sum(image_skip * image_skip),
        ),
        "ch",
    )
    scale_one = lax.rsqrt(square_one + EPS)
    scale_two = lax.rsqrt(square_two + EPS)
    scale_skip = lax.rsqrt(square_skip + EPS)
    right_one = image_one * scale_one
    right_two = image_two * scale_two
    right_skip = image_skip * scale_skip
    sigma_one = square_one * scale_one
    sigma_two = square_two * scale_two
    sigma_skip = square_skip * scale_skip
    eff_one = (kern_one / sigma_one).astype(jnp.bfloat16)
    eff_two = (kern_two / sigma_two).astype(jnp.bfloat16)
    eff_skip_full = (kern_skip / sigma_skip).astype(jnp.bfloat16)
    eff_skip = eff_skip_full[0, 0]
    bias_first = bias_one.astype(jnp.float32)
    bias_second = bias_two.astype(jnp.float32)
    back_two = flipped(eff_two)
    back_one = flipped(eff_one)
    outputs = []
    in_grads = []
    totals = None
    for micro in range(micros):
        height_rows = jnp.sum(jnp.where(owner, valid_h[micro][None, :], 0), axis=1)
        width_rows = jnp.sum(jnp.where(owner, valid_w[micro][None, :], 0), axis=1)
        mask_rim = (
            (row_of < height_rows)[:, None] & (columns[None, :] < width_rows[:, None])
        ).astype(jnp.float32)[:, :, None]
        mask_in = mask_rim[1:-1]
        input_rim = extended(images[micro], (("rows", 0),), 1)
        gathered = lax.all_gather(input_rim, "ch", axis=2, tiled=True)
        masked_rim = gathered * mask_rim.astype(jnp.bfloat16)
        act_in = jax.nn.silu(masked_rim.astype(jnp.float32)).astype(jnp.bfloat16)
        pre_one = conv_rows(act_in, eff_one, taps) + bias_first
        act_one = (jax.nn.silu(pre_one) * mask_in).astype(jnp.bfloat16)
        hidden_rim = extended(act_one, (("rows", 0),), 1)
        hidden_all = lax.all_gather(hidden_rim, "ch", axis=2, tiled=True)
        skip_in = masked_rim[1:-1]
        total = conv_rows(hidden_all, eff_two, taps) + bias_second
        total = total + jnp.einsum(
            "rci,io->rco", skip_in, eff_skip, preferred_element_type=jnp.float32
        )
        pooled = jnp.mean(total.reshape(rows_dev // 2, 2, width // 2, 2, out_local), axis=(1, 3))
        outputs.append(pooled.astype(jnp.bfloat16))
        quarter = cotangent[micro] * 0.25
        grad_total = jnp.broadcast_to(
            quarter[:, None, :, None, :], (rows_dev // 2, 2, width // 2, 2, out_local)
        ).reshape(rows_dev, width, out_local)
        grad_rim = extended(grad_total, (("rows", 0),), 1)
        partial_hidden = conv_rows(grad_rim, back_two, taps)
        grad_act_one = lax.psum_scatter(partial_hidden, "ch", scatter_dimension=2, tiled=True)
        grad_pre_one = (grad_act_one * mask_in * silu_slope(pre_one)).astype(jnp.bfloat16)
        pre_rim = extended(grad_pre_one, (("rows", 0),), 1)
        partial_act = conv_rows(pre_rim, back_one, taps)
        partial_skip = jnp.einsum(
            "rco,io->rci", grad_total, eff_skip, preferred_element_type=jnp.float32
        )
        grad_act_in, grad_skip_in = (
            lax.psum_scatter(partial_act, "ch", scatter_dimension=2, tiled=True),
            lax.psum_scatter(partial_skip, "ch", scatter_dimension=2, tiled=True),
        )
        own_input = images[micro].astype(jnp.float32)
        in_grads.append(
            (mask_in * (silu_slope(own_input) * grad_act_in + grad_skip_in)).astype(jnp.bfloat16)
        )
        grad_one = kernel_taps(act_in, grad_pre_one, taps_low)
        grad_two = kernel_taps(hidden_all, grad_total, taps_low)
        grad_skip = jnp.einsum(
            "rci,rco->io", skip_in, grad_total, preferred_element_type=jnp.float32
        )
        grad_first = jnp.sum(grad_pre_one.astype(jnp.float32), axis=(0, 1))
        grad_second = jnp.sum(grad_total.astype(jnp.float32), axis=(0, 1))
        current = (grad_one, grad_two, grad_skip, grad_first, grad_second)
        if totals is None:
            totals = current
        else:
            totals = tuple((acc + new for acc, new in zip(totals, current)))
    summed = lax.psum((totals[0], totals[1], totals[2], totals[3], totals[4]), "rows")
    sum_one, sum_two, sum_skip, sum_first, sum_second = summed
    sum_skip = sum_skip.reshape(1, 1, -1, out_local)
    dot_one, dot_two, dot_skip = lax.psum(
        (jnp.sum(sum_one * kern_one), jnp.sum(sum_two * kern_two), jnp.sum(sum_skip * kern_skip)),
        "ch",
    )
    final_one = (
        sum_one / sigma_one - dot_one / (sigma_one * sigma_one) * left_one[..., None] * right_one
    )
    final_two = (
        sum_two / sigma_two - dot_two / (sigma_two * sigma_two) * left_two[..., None] * right_two
    )
    final_skip = (
        sum_skip / sigma_skip
        - dot_skip / (sigma_skip * sigma_skip) * left_skip[..., None] * right_skip
    )
    return (
        jnp.stack(outputs),
        jnp.stack(in_grads),
        final_one,
        final_two,
        final_skip[0, 0],
        sum_first,
        sum_second,
    )


F32 = jnp.float32
BF16 = jnp.bfloat16
MESH = pl.DeviceIdType.MESH
TILE = 128
NT = (((1,), (1,)), ((), ()))
TN = (((0,), (0,)), ((), ()))
NN = (((1,), (0,)), ((), ()))


def fits(n_rows, n_ch, arrays):
    images, kernel_one = arrays[0], arrays[3]
    micros, rows_dev, width, in_local = images.shape
    out_local = kernel_one.shape[3]
    return (
        n_ch == 2
        and micros % 2 == 0
        and n_rows >= 4
        and n_rows % min(8, n_rows) == 0
        and n_rows % 4 == 0
        and rows_dev % 8 == 0
        and SHIFT % rows_dev == rows_dev // 2
        and IMG % rows_dev == 0
        and 2 * width == TILE
        and in_local % 16 == 0
        and 2 * in_local < TILE
        and out_local == 3 * TILE // 4
    )


def dot(left, right, dims=NN):
    return lax.dot_general(left, right, dims, preferred_element_type=F32)


def iota(shape, dim):
    return lax.broadcasted_iota(jnp.int32, shape, dim)


def pieces(row):
    first = row.astype(BF16).astype(F32)
    rest = row - first
    second = rest.astype(BF16).astype(F32)
    third = rest - second
    at = iota((16, row.shape[1]), 0)
    zero = jnp.zeros((16, row.shape[1]), F32)
    stacked = jnp.where(at == 0, first, jnp.where(at == 1, second, jnp.where(at == 2, third, zero)))
    return stacked.astype(BF16)


def total(value):
    return jnp.sum(jnp.sum(value, axis=0, keepdims=True), axis=1, keepdims=True)


def power(vector_row, kernel):
    left = jnp.sum(dot(pieces(vector_row), kernel, NT), axis=0, keepdims=True)
    left = left * lax.rsqrt(total(left * left) + EPS)
    image = jnp.sum(dot(pieces(left), kernel), axis=0, keepdims=True)
    square = total(image * image)
    scale = lax.rsqrt(square + EPS)
    return left, image * scale, square * scale


def slope(value):
    gate = 1.0 / (1.0 + jnp.exp(-value))
    return gate + value * gate * (1.0 - gate)


def fused_kernel(names, n_rows, dims, *refs):
    micros, rows, width, ci, co, lanes_each, bits, share1, share2 = dims
    ref = dict(zip(names, refs))
    half = width // 2
    per = micros // 2
    pairs = rows // 2
    cut = rows // 2
    seg_slots = cut + 3
    seg_out = cut + 1
    pairs_a = cut // 2 + 1
    n_chips = n_rows // 2
    cin, cout = 2 * ci, 2 * co
    op = 2 * TILE
    total_rows = rows * n_rows
    own_px = pairs * half
    all_px = (pairs + 2) * half

    ssem, rsem, lsem = ref["ssem"], ref["rsem"], ref["lsem"]
    me = lax.axis_index("rows")
    c = lax.axis_index("ch")
    o = 1 - c
    core = lax.rem(me, 2)
    mate = me + 1 - 2 * core
    chip = me // 2
    up = lax.rem(me + n_rows - 1, n_rows)
    down = lax.rem(me + 1, n_rows)
    my_id = c * n_chips + chip
    sub = min(4, n_chips)
    cubes = n_chips // sub
    spot_in, cube = lax.rem(chip, sub), chip // sub
    my_id = c * sub + spot_in
    far = []
    for delta in range(1, 2 * sub):
        other = lax.rem(my_id + delta, 2 * sub)
        far.append((2 * (cube * sub + lax.rem(other, sub)) + core, other // sub))
    across = []
    for delta in range(1, cubes):
        across.append((2 * (lax.rem(cube + delta, cubes) * sub + spot_in) + core, c))
    around = []
    for delta in range(1, 2 * sub):
        other = lax.rem(2 * spot_in + core + delta, 2 * sub)
        around.append((2 * cube * sub + other, c))
    near = [(me, o), (mate, c), (up, c), (up, o), (down, c), (down, o)]

    barrier = pltpu.get_barrier_semaphore()
    for device in near + far + across + around:
        pl.semaphore_signal(barrier, inc=1, device_id=device, device_id_type=MESH)

    count = [0]
    sends = []

    def remote(src, dst, device):
        at = count[0]
        count[0] += 1
        return pltpu.make_async_remote_copy(
            src_ref=src,
            dst_ref=dst,
            send_sem=ssem.at[at],
            recv_sem=rsem.at[at],
            device_id=device,
            device_id_type=MESH,
        )

    def begin(*args):
        copy = remote(*args)
        copy.start()
        sends.append(copy)
        return copy

    img, cot, k1, k20 = ref["img_v"], ref["cot_v"], ref["k1_v"], ref["k20_v"]
    n1, n2 = 9 * cin, 9 * cout
    loads = []
    for i, (src, dst) in enumerate(
        [
            (ref["img"], img),
            (ref["k1"], k1.at[0:n1]),
            (ref["k0"], k20.at[n2 : n2 + cin]),
            (ref["k2"], k20.at[0:n2]),
            (ref["cot"], cot),
        ]
    ):
        load = pltpu.make_async_copy(src, dst, lsem.at[i])
        load.start()
        loads.append(load)

    perm_in, perm_x = ref["perm_in"], ref["perm_x"]
    shape = (8 * half, TILE)
    at, lane = iota(shape, 0), iota(shape, 1)
    column = 2 * lax.rem(at, half) + lax.rem(at // half, 4) - 1
    hit = (lane - at // (4 * half) * width == column) & (column >= 0) & (column < width)
    perm_in[...] = jnp.where(hit, 1.0, 0.0).astype(BF16)
    shape = (4 * half, TILE)
    at, lane = iota(shape, 0), iota(shape, 1)
    source = at // (2 * half) * width + 2 * lax.rem(at, half) + lax.rem(at // half, 2)
    perm_x[0 : 4 * half] = jnp.where(lane == source, 1.0, 0.0).astype(BF16)
    shape = (half, TILE)
    at, lane = iota(shape, 0), iota(shape, 1)
    perm_x[4 * half : 5 * half] = jnp.where(lax.rem(lane, width) // 2 == at, 1.0, 0.0).astype(BF16)

    def rem_pos(value, by):
        return lax.rem(lax.rem(value, by) + by, by)

    first_a = rem_pos(me * rows - SHIFT, total_rows)
    first_b = rem_pos(me * rows + cut - SHIFT, total_rows)
    base = [lax.rem(first_a, IMG), lax.rem(first_b, IMG) - cut]
    image_a, image_b = first_a // IMG, first_b // IMG
    keep = jnp.where(base[1] < 0, 0.0, 1.0).astype(F32)
    vh, vw = ref["vh"], ref["vw"]
    high = [[vh[c * per + j, image] for image in (image_a, image_b)] for j in range(per)]
    wide = [[vw[c * per + j, image] for image in (image_a, image_b)] for j in range(per)]

    def choose(seg, two):
        return jnp.where(seg == 0, two[0], two[1])

    vec = ref["vec"]
    vec[c] = jnp.zeros(vec.shape[1:], F32)
    for i, name in enumerate(("q1", "q2", "q0", "b1", "b2")):
        vec[c, i : i + 1, 0:co] = ref[name][...].astype(F32)

    imgr, sendp = ref["imgr"], ref["sendp"]
    loads[0].wait()
    for j in range(per):
        for mine in (False, True):

            def pack(p, carry, j=j, mine=mine):
                m = (c if mine else o) * per + j
                pair = jnp.concatenate([img[m, 2 * p], img[m, 2 * p + 1]], axis=1)
                if mine:
                    imgr[j, c, p + 1] = pair
                else:
                    sendp[j, p] = pair
                return carry

            lax.fori_loop(0, pairs, pack, 0, unroll=4)
    for load in loads[1:]:
        load.wait()

    def packed(value):
        kept, strip = 3 * value.shape[-2] // 4, co // 3
        last = value[kept:]
        beside = jnp.concatenate([last[:, k * strip : (k + 1) * strip] for k in range(3)], axis=0)
        return jnp.concatenate([value[:kept], beside], axis=1)

    def unpacked(value):
        part = value.shape[0] // 3
        last = jnp.concatenate([value[k * part : (k + 1) * part, co:] for k in range(3)], axis=1)
        return jnp.concatenate([value[:, :co], last], axis=0)

    k1p, k20p, cotp = ref["k1p"], ref["k20p"], ref["cotp"]
    size1, size20 = 3 * k1.shape[0] // 4, 3 * k20.shape[0] // 4
    k1p[0:size1] = packed(k1[...])
    k20p[0:size20] = packed(k20[...])
    for j in range(per):
        cotp[j] = packed(cot[o * per + j].reshape(own_px, co))

    pl.semaphore_wait(barrier, len(near + far + across + around))

    k1h, k20h, coth, cotr = ref["k1h"], ref["k20h"], ref["coth"], ref["cotr"]
    spots = [core] + [lax.rem(me // 2**b, 2) for b in range(1, bits)]
    mates = [mate] + [me + 2**b * (1 - 2 * spots[b]) for b in range(1, bits)]

    def piece(rows_each, level, depth):
        first = 0
        for b in range(depth - level):
            first = first * 2 + spots[b]
        return pl.ds(first * (2**level * rows_each), 2**level * rows_each)

    class Shared:
        def __init__(self, own, got, rows_each, depth):
            self.got, self.rows_each, self.depth, self.level = got, rows_each, depth, 0
            at = piece(rows_each, 0, depth)
            self.copy = begin(own.at[at], got.at[at], (me, o))

        def turn(self):
            self.copy.wait_recv()
            if self.level < self.depth:
                at = piece(self.rows_each, self.level, self.depth)
                device = (mates[self.depth - 1 - self.level], c)
                self.copy = begin(self.got.at[at], self.got.at[at], device)
            self.level += 1

    mine_c, mine_o = pl.ds(c * per, per), pl.ds(o * per, per)
    img_x, img_halo = [], []

    def send_image(j):
        img_x.append(begin(sendp.at[j], imgr.at[j, c, pl.ds(1, pairs)], (me, o)))
        img_halo.append(
            [
                begin(sendp.at[j, 0], imgr.at[j, c, pairs + 1], (up, o)),
                begin(sendp.at[j, pairs - 1], imgr.at[j, c, 0], (down, o)),
                begin(imgr.at[j, c, 1], imgr.at[j, c, pairs + 1], (up, c)),
                begin(imgr.at[j, c, pairs], imgr.at[j, c, 0], (down, c)),
            ]
        )

    vec_x = begin(vec.at[c], vec.at[c], (me, o))
    one = Shared(k1p, k1h, share1, 2)
    two = Shared(k20p, k20h, share2, bits)
    for j in range(per):
        send_image(j)
    cot_x = [begin(cotp.at[j], coth.at[j], (me, o)) for j in range(per)]
    cot_halo = [
        begin(cot.at[mine_o, 0], cotr.at[:, c, 1], (up, o)),
        begin(cot.at[mine_o, pairs - 1], cotr.at[:, c, 0], (down, o)),
        begin(cot.at[mine_c, 0], cotr.at[:, c, 1], (up, c)),
        begin(cot.at[mine_c, pairs - 1], cotr.at[:, c, 0], (down, c)),
    ]

    w1, w2, w0 = ref["w1"], ref["w2"], ref["w0"]

    def place(dst, row, own_part, other_part, padded):
        size = own_part.shape[0]
        first = jnp.where(c == 0, own_part, other_part)
        second = jnp.where(c == 0, other_part, own_part)
        line = jnp.concatenate([first, second, jnp.zeros((size, op - cout), BF16)], axis=1)
        dst[pl.ds(row, size), :] = line
        if padded > size:
            dst[pl.ds(row + size, padded - size), :] = jnp.zeros((padded - size, op), BF16)

    def row_of(i):
        return jnp.concatenate(
            [vec[0, i : i + 1, 0:co], vec[1, i : i + 1, 0:co], jnp.zeros((1, op - cout), F32)], axis=1
        )

    b_in, xp, xb = ref["b_in"], ref["xp"], ref["xb"]
    ones = jnp.where(iota((TILE - cin, TILE), 0) == 0, 1.0, 0.0).astype(BF16)

    def prepare(j):
        img_x[j].wait_recv()
        for copy in img_halo[j]:
            copy.wait_recv()

        def two_pairs(step, carry):
            lane = iota((1, TILE), 1)
            column = lax.rem(lane, width)
            acts, plain, slots = [], [], []
            for k in range(2):
                p = 2 * step + k
                seg = (p >= pairs_a).astype(jnp.int32)
                row = 2 * p - 2 + lane // width
                mask = jnp.where(
                    (choose(seg, base) + row < choose(seg, high[j])) & (column < choose(seg, wide[j])), 1.0, 0.0
                )
                x = jnp.concatenate([imgr[j, 0, p], imgr[j, 1, p]], axis=0).astype(F32) * mask
                act = x / (1.0 + jnp.exp(-x))
                acts += [act.astype(BF16), ones]
                plain += [x.astype(BF16), ones]
                slots.append(2 * p + 2 * seg)
            spread = dot(perm_in[...], jnp.concatenate(acts, axis=0), NT).astype(BF16)
            for k in range(2):
                for a in range(2):
                    for t in range(4):
                        b_in[j, slots[k] + a, :, t * TILE : (t + 1) * TILE] = spread[
                            (4 * a + t) * half : (4 * a + t + 1) * half, k * TILE : (k + 1) * TILE
                        ]
            spread = dot(perm_x[...], jnp.concatenate(plain, axis=0), NT).astype(BF16)
            for k in range(2):
                part = spread[:, k * TILE : (k + 1) * TILE]
                xp[j, 2 * step + k] = part[0 : 4 * half]
                xb[j, 2 * step + k] = part[4 * half : 5 * half]
            return carry

        lax.fori_loop(0, (pairs + 2) // 2, two_pairs, 0, unroll=True)
        b_in[j, seg_slots - 1] = (b_in[j, seg_slots + 1].astype(F32) * keep).astype(BF16)
        b_in[j, seg_slots] = (b_in[j, seg_slots - 2].astype(F32) * keep).astype(BF16)

    raw1, grad1 = ref["raw1"], ref["grad1"]

    def conv_one(j):
        def segment(seg, carry):
            parts = []
            for b in range(2):
                taps = [
                    b_in[j, pl.ds(seg * seg_slots + u, seg_out), :, b * TILE : (b + 3) * TILE].reshape(
                        seg_out * half, 3 * TILE
                    )
                    for u in range(3)
                ]
                parts.append(jnp.concatenate(taps, axis=1))
            result = dot(jnp.concatenate(parts, axis=0), w1[...])
            for b in range(2):
                raw1[j, b, pl.ds(seg * seg_out, seg_out)] = result[
                    b * seg_out * half : (b + 1) * seg_out * half
                ].reshape(seg_out, half, op)
            return carry

        lax.fori_loop(0, 2, segment, 0)

    cols = ref["cols"]
    pixel = iota((half, op), 0)

    def activate(j):
        def line(i, carry):
            seg = (i >= seg_out).astype(jnp.int32)
            broad = jnp.where(choose(seg, base) + i - 1 < choose(seg, high[j]), choose(seg, wide[j]), 0)
            acts = []
            for b in range(2):
                pre = raw1[j, b, i] * scale1 + bias1
                gate = 1.0 / (1.0 + jnp.exp(-pre))
                mask = 2 * pixel + b < broad
                lift = pre * gate
                grad1[j, b, i] = jnp.where(mask, gate + lift * (1.0 - gate), 0.0)
                acts.append(jnp.where(mask, lift, 0.0).astype(BF16).astype(F32))
            even, odd = acts
            before = jnp.where(pixel == 0, 0.0, pltpu.roll(odd, 1, 0))
            after = jnp.where(pixel == half - 1, 0.0, pltpu.roll(even, half - 1, 0))
            cols[j, 0, i] = before + even
            cols[j, 1, i] = even + odd
            cols[j, 2, i] = odd + after
            return carry

        lax.fori_loop(0, 2 * seg_out, line, 0, unroll=2)

    box = ref["box"]

    def boxes(j):
        def line(i, carry):
            above = jnp.where(i == cut // 2, keep, 1.0)
            below = jnp.where(i == cut // 2 - 1, keep, 1.0)
            for w in range(3):
                lines = [cols[j, w, 2 * i + k] for k in range(4)]
                for u in range(3):
                    upper, lower = lines[u], lines[u + 1]
                    if u == 0:
                        upper = upper * above
                    if u == 2:
                        lower = lower * below
                    tap = 3 * u + w
                    box[j, i, :, tap * op : (tap + 1) * op] = (upper + lower).astype(BF16)
            return carry

        lax.fori_loop(0, pairs, line, 0, unroll=2)

    quart = ref["quart"]

    def quarter(j):
        def put(i, own, other):
            first = jnp.where(c == 0, own, other)
            second = jnp.where(c == 0, other, own)
            size = first.shape[0]
            line = jnp.concatenate([first, second, jnp.zeros((size, op - cout), BF16)], axis=1)
            line = (line.astype(F32) * 0.25).astype(BF16)
            quart[j, pl.ds(i, size // half)] = line.reshape(size // half, half, op)

        put(1, cot[c * per + j].reshape(own_px, co), unpacked(coth[j]))
        for i in (0, 1):
            put(i * (pairs + 1), cotr[j, c, i], cotr[j, o, i])

    def owned(j):
        return quart[j, 1 : pairs + 1].reshape(own_px, op)

    half_rows = co // 2
    kept_rows = pl.ds(core * half_rows, half_rows)
    mate_rows = pl.ds((1 - core) * half_rows, half_rows)

    class Summed:
        def __init__(self, name):
            self.wire, self.got, self.shares, self.landing, self.mine, self.mids, self.result = [
                ref[part + name] for part in ("wire", "got", "shares", "landing", "mine", "mids", "result")
            ]
            self.share = self.result.shape[2]
            self.copies = [begin(self.wire.at[:, mate_rows], self.got, (mate, c))]

        def arrived(self):
            for copy in self.copies:
                copy.wait_recv()

        def to_owners(self):
            self.arrived()
            for ch in range(2):
                value = self.wire[ch, kept_rows].astype(F32) + self.got[ch].astype(F32)
                for at in range(sub):
                    part = value[:, at * self.share : (at + 1) * self.share]
                    self.shares[ch, at] = part.astype(BF16)

                    @pl.when(my_id == ch * sub + at)
                    def _():
                        self.mine[...] = part

            self.copies = []
            for delta in range(1, 2 * sub):
                other = lax.rem(my_id + delta, 2 * sub)
                self.copies.append(
                    begin(
                        self.shares.at[other // sub, lax.rem(other, sub)], self.landing.at[delta - 1], far[delta - 1]
                    )
                )

        def to_cubes(self):
            self.arrived()
            value = self.mine[...]
            for delta in range(1, 2 * sub):
                value = value + self.landing[delta - 1].astype(F32)
            self.mids[cube] = value.astype(BF16)
            self.copies = [begin(self.mids.at[cube], self.mids.at[cube], device) for device in across]

        def to_all(self):
            self.arrived()
            value = self.mids[0].astype(F32)
            for at in range(1, cubes):
                value = value + self.mids[at].astype(F32)
            self.result[spot_in, kept_rows] = value.astype(BF16)
            place_at = self.result.at[spot_in, kept_rows]
            self.copies = [begin(place_at, place_at, device) for device in around]

        def flat(self):
            self.arrived()
            return jnp.concatenate([self.result[at].astype(F32) for at in range(sub)], axis=1)

    one.turn()
    two.turn()
    one.turn()
    prepare(0)
    one.turn()
    vec_x.wait_recv()
    k1o = unpacked(k1h[0:size1])
    for tap in range(9):
        rows_at = slice(tap * cin, (tap + 1) * cin)
        place(w1, tap * TILE, k1[rows_at], k1o[rows_at], TILE)
    left1, right1, sigma1 = power(row_of(0), w1[...])
    scale1 = 1.0 / sigma1
    bias1, bias2 = row_of(3), row_of(4)
    left1_ref, left2_ref, left0_ref = ref["left1"], ref["left2"], ref["left0"]
    left1_ref[0:1] = left1
    conv_one(0)
    two.turn()
    activate(0)
    boxes(0)
    for j in range(1, per):
        prepare(j)
        conv_one(j)
        activate(j)
        boxes(j)
    two.turn()
    for copy in cot_x:
        copy.wait_recv()
    for copy in cot_halo:
        copy.wait_recv()
    for j in range(per):
        quarter(j)

    acc0 = ref["acc0"]
    given = jnp.concatenate([owned(j) for j in range(per)], axis=0)[:, 0:cout]
    turned_quart = jnp.transpose(given)
    group_a = None
    for name, taps in (("a", range(0, 5)), ("b", range(5, 9))):
        lanes = slice(taps[0] * op, (taps[-1] + 1) * op)
        value = dot(turned_quart, box[:, :, :, lanes].reshape(per * own_px, len(taps) * op))
        parts = [value[:, k * op : k * op + cout] for k in range(len(taps))]
        if name == "b":
            skip = dot(turned_quart, xb[:, 1 : pairs + 1].reshape(per * own_px, TILE))
            acc0[...] = skip
            parts.append(skip[:, 0:cin])
        parts.append(jnp.zeros((cout, lanes_each - sum(part.shape[1] for part in parts)), F32))
        flat = jnp.concatenate(parts, axis=1).astype(BF16)
        for ch in range(2):
            ref["wire" + name][ch] = flat[ch * co : (ch + 1) * co]
        if name == "a":
            group_a = Summed("a")
    group_b = Summed("b")
    for turn in range(two.level, bits + 1):
        two.turn()
    k20o = unpacked(k20h[0:size20])
    for tap in range(9):
        rows_at = slice(tap * cout, (tap + 1) * cout)
        place(w2, tap * op, k20[rows_at], k20o[rows_at], op)
    rows_at = slice(n2, n2 + cin)
    place(w0, 0, k20[rows_at], k20o[rows_at], TILE)
    left2, right2, sigma2 = power(row_of(1), w2[...])
    left0, right0, sigma0 = power(row_of(2), w0[...])
    scale2, scale0 = 1.0 / sigma2, 1.0 / sigma0
    left0_ref[0:1] = left0
    left2_ref[0:1] = left2

    taps_sum = ref["taps_sum"]
    spot = iota((all_px, op), 0)
    at_left = lax.rem(spot, half) == 0
    at_right = lax.rem(spot, half) == half - 1
    g_pre = ref["g_pre"]

    def back_two(j, dot1):
        given = quart[j].reshape(all_px, op)
        for u in range(3):
            t0, t1, t2 = [
                dot(given, w2[(3 * u + w) * op : (3 * u + w + 1) * op], NT) for w in range(3)
            ]
            even = t0 + t1 + jnp.where(at_left, 0.0, pltpu.roll(t2, 1, 0))
            odd = t1 + t2 + jnp.where(at_right, 0.0, pltpu.roll(t0, all_px - 1, 0))
            taps_sum[u, 0] = even.reshape(pairs + 2, half, op)
            taps_sum[u, 1] = odd.reshape(pairs + 2, half, op)

        def line(i, carry):
            hold = jnp.where(i == cut // 2, keep, 1.0)
            own_even = jnp.where(i < pairs, 1.0, 0.0)
            own_odd = jnp.where(i > 0, 1.0, 0.0)
            for b in range(2):
                upper, lower = taps_sum[2, b, i], taps_sum[0, b, i + 1]
                even = lower + taps_sum[1, b, i + 1] + hold * upper
                odd = taps_sum[1, b, i] + upper + hold * lower
                even = (even * scale2 * grad1[j, b, 2 * i + 1]).astype(BF16)
                odd = (odd * scale2 * grad1[j, b, 2 * i]).astype(BF16)
                g_pre[j, b, 2 * i + 1] = even
                g_pre[j, b, 2 * i] = odd
                carry = carry + own_even * even.astype(F32) * raw1[j, b, 2 * i + 1]
                carry = carry + own_odd * odd.astype(F32) * raw1[j, b, 2 * i]
            return carry

        return lax.fori_loop(0, pairs + 1, line, dot1, unroll=3)

    group_a.to_owners()
    group_b.to_owners()
    dot1 = jnp.zeros((half, op), F32)
    for j in range(per):
        dot1 = back_two(j, dot1)

    def kernel_one_grad(taps_u):
        value = None
        for b in range(2):
            given, lines = [], []
            for j in range(per):
                for seg in range(2):
                    given.append(g_pre[j, b, seg * cut + 1 : (seg + 1) * cut + 1].reshape(cut * half, op)[:, 0:cout])
                    first = seg * (cut + 2) + 1
                    lines.append(
                        jnp.concatenate(
                            [
                                b_in[j, first + u : first + u + cut, :, b * TILE : (b + 3) * TILE].reshape(
                                    cut * half, 3 * TILE
                                )
                                for u in taps_u
                            ],
                            axis=1,
                        )
                    )
            part = dot(jnp.concatenate(given, axis=0), jnp.concatenate(lines, axis=0), TN)
            value = part if value is None else value + part
        return value

    acc1 = kernel_one_grad(range(3))
    spare = lanes_each - 9 * cin - 6

    def pair_of(column):
        high_part = column.astype(BF16).astype(F32)
        return [high_part, column - high_part]

    parts = [acc1[:, tap * TILE : tap * TILE + cin] for tap in range(9)]
    parts += pair_of(acc1[:, 4 * TILE + cin : 4 * TILE + cin + 1])
    parts += pair_of(acc0[:, cin : cin + 1])
    parts += pair_of(jnp.broadcast_to(total(dot1), (cout, 1)))
    parts.append(jnp.zeros((cout, spare), F32))
    flat = jnp.concatenate(parts, axis=1).astype(BF16)
    for ch in range(2):
        ref["wirec"][ch] = flat[ch * co : (ch + 1) * co]
    group_c = Summed("c")

    out_b, send_b, got_b = ref["out_b"], ref["send_b"], ref["got_b"]

    def conv_two(j):
        main = dot(box[j].reshape(own_px, 9 * op), w2[...])
        skip = dot(xb[j, 1 : pairs + 1].reshape(own_px, TILE), w0[...])
        value = ((main * scale2 + skip * scale0) * 0.25 + bias2).astype(BF16)
        first, second = value[:, 0:co], value[:, co:cout]
        out_b[c * per + j] = jnp.where(c == 0, first, second).reshape(pairs, half, co)
        send_b[j] = jnp.where(c == 0, second, first).reshape(pairs, half, co)

    taps_in, skip_back = ref["taps_in"], ref["skip_back"]
    pixel_in = iota((half, TILE), 0)
    out_g, send_g, got_g = ref["out_g"], ref["send_g"], ref["got_g"]

    def back_products(j):
        skip_back[...] = (dot(owned(j), w0[...], NT) * scale0).reshape(pairs, half, TILE)

        def some(step, carry):
            b, part = step // 2, lax.rem(step, 2)
            given = g_pre[j, b, pl.ds(part * seg_out, seg_out)].reshape(seg_out * half, op)
            taps_in[b, pl.ds(part * seg_out, seg_out)] = dot(given, w1[...], NT).reshape(
                seg_out, half, 9 * TILE
            )
            return carry

        lax.fori_loop(0, 4, some, 0)

    def input_rows(j):
        def two_rows(p, carry):
            lines = []
            for a in range(2):
                r = 2 * p + a
                hold_up = jnp.where(r == cut - 1, keep, 1.0)
                hold_down = jnp.where(r == cut, keep, 1.0)

                def column_sum(w, s):
                    def of(u, row):
                        at = (3 * u + w) * TILE
                        return taps_in[s, row, :, at : at + TILE]

                    return of(0, r + 2) * hold_up + of(1, r + 1) + of(2, r) * hold_down

                before = pltpu.roll(column_sum(2, 1), 1, 0)
                after = pltpu.roll(column_sum(0, 0), half - 1, 0)
                even = column_sum(0, 1) + column_sum(1, 0) + jnp.where(pixel_in == 0, 0.0, before)
                odd = column_sum(1, 1) + column_sum(2, 0) + jnp.where(pixel_in == half - 1, 0.0, after)
                seg = (r >= cut).astype(jnp.int32)
                broad = jnp.where(choose(seg, base) + r < choose(seg, high[j]), choose(seg, wide[j]), 0)
                for b, value in ((0, even), (1, odd)):
                    at = (2 * a + b) * half
                    x = xp[j, p + 1, at : at + half].astype(F32)
                    mask = 2 * pixel_in + b < broad
                    value = slope(x) * (value * scale1) + skip_back[p]
                    lines.append(jnp.where(mask, value, 0.0).astype(BF16))
            line = dot(jnp.concatenate(lines, axis=0), perm_x[0 : 4 * half], TN).astype(BF16)
            own = jnp.where(c == 0, line[0:ci], line[ci:cin])
            other = jnp.where(c == 0, line[ci:cin], line[0:ci])
            out_g[c * per + j, 2 * p] = own[:, 0:width]
            out_g[c * per + j, 2 * p + 1] = own[:, width:TILE]
            send_g[j, p] = other
            return carry

        lax.fori_loop(0, pairs, two_rows, 0, unroll=4)
        return begin(send_g.at[j], got_g.at[j], (me, o))

    def unpack(j):
        def line(p, carry):
            out_g[o * per + j, 2 * p] = got_g[j, p, :, 0:width]
            out_g[o * per + j, 2 * p + 1] = got_g[j, p, :, width:TILE]
            return carry

        grad_x[j].wait_recv()
        lax.fori_loop(0, pairs, line, 0, unroll=4)

    for j in range(per):
        conv_two(j)
    group_c.to_owners()
    out_x = begin(send_b, got_b, (me, o))
    back_products(0)
    group_a.to_cubes()
    grad_x = [input_rows(0)]
    group_b.to_cubes()
    for j in range(1, per):
        back_products(j)
        if j == 1:
            group_a.to_all()
        grad_x.append(input_rows(j))
    def own_half(row):
        return jnp.where(c == 0, row[:, 0:co], row[:, co:cout])

    def column_of(row):
        row = jnp.concatenate([own_half(row), jnp.zeros((1, TILE - co), F32)], axis=1)
        return jnp.transpose(jnp.broadcast_to(row, (TILE, TILE)))[0:co]

    def compact(row, size, padded):
        return jnp.concatenate([row[:, t * padded : t * padded + size] for t in range(9)], axis=1)

    def turned(part, out, at):
        some = part.shape[1]
        if some < TILE:
            part = jnp.concatenate([part, jnp.zeros((co, TILE - some), F32)], axis=1)
        part = jnp.concatenate([part, jnp.zeros((TILE - co, TILE), F32)], axis=0)
        out[at : at + some] = jnp.transpose(part)[0:some, 0:co]

    def outer(left, right, out):
        columns = column_of(right)
        for at in range(0, left.shape[1], TILE):
            some = min(TILE, left.shape[1] - at)
            turned(columns[:, 0:some] * left[:, at : at + some], out, at)

    corr1, corr2, corr0 = ref["corr1"], ref["corr2"], ref["corr0"]
    group_c.to_cubes()
    group_b.to_all()
    outer(compact(left1_ref[0:1], cin, TILE), right1 * (scale1 * scale1), corr1)
    outer(compact(left2_ref[0:1], cout, op), right2 * scale2, corr2)
    outer(left0_ref[0:1, 0:cin], right0 * scale0, corr0)
    out_k1, out_k2, out_k0 = ref["out_k1"], ref["out_k2"], ref["out_k0"]
    group_c.to_all()
    flat = group_a.flat()
    for at in range(0, 5 * cout, TILE):
        turned(flat[:, at : min(at + TILE, 5 * cout)] * scale2, out_k2, at)
    flat = group_b.flat()
    for at in range(0, 4 * cout, TILE):
        turned(flat[:, at : min(at + TILE, 4 * cout)] * scale2, out_k2, 5 * cout + at)
    turned(flat[:, 4 * cout : 4 * cout + cin] * scale0, out_k0, 0)

    dots = ref["dots"]
    at = iota((8, TILE), 0)
    sum2 = total(out_k2[...] * k20[0:n2].astype(F32))
    sum0 = total(out_k0[...] * k20[n2 : n2 + cin].astype(F32))
    dots[c] = jnp.where(at == 0, sum2, jnp.where(at == 1, sum0, 0.0))
    dots_x = begin(dots.at[c], dots.at[c], (me, o))
    out_x.wait_recv()
    out_b[mine_o] = got_b[...]
    for j in range(per):
        unpack(j)
    dots_x.wait_recv()
    both = dots[0] + dots[1]
    for out, corr, row in ((out_k2, corr2, 0), (out_k0, corr0, 1)):
        out[...] = out[...] - corr[...] * both[row : row + 1, 0:1]
    flat = group_c.flat()
    extra = flat[:, n1 : n1 + 6]
    sum1 = extra[0:1, 4:5] + extra[0:1, 5:6]
    biases = jnp.concatenate([extra, jnp.zeros((co, TILE - 6), F32)], axis=1)
    biases = jnp.transpose(jnp.concatenate([biases, jnp.zeros((TILE - co, TILE), F32)], axis=0))
    ref["out_b1"][...] = biases[0:1, 0:co] + biases[1:2, 0:co]
    ref["out_b2"][...] = biases[2:3, 0:co] + biases[3:4, 0:co]
    for at in range(0, n1, TILE):
        turned(flat[:, at : min(at + TILE, n1)] * scale1, out_k1, at)
    out_k1[...] = out_k1[...] - corr1[...] * sum1

    for copy in sends:
        copy.wait_send()


def hand_over(arrays):
    number = len(arrays)

    def copy_all(*refs):
        sem = refs[-1]
        copies = [pltpu.make_async_copy(refs[i], refs[number + i], sem.at[i]) for i in range(number)]
        for copy in copies:
            copy.start()
        for copy in copies:
            copy.wait()

    return pl.pallas_call(
        copy_all,
        out_shape=[jax.ShapeDtypeStruct(a.shape, a.dtype) for a in arrays],
        in_specs=[pl.BlockSpec(memory_space=pltpu.VMEM)] * number,
        out_specs=[pl.BlockSpec(memory_space=pl.ANY)] * number,
        scratch_shapes=[pltpu.SemaphoreType.DMA((number,))],
        name="hand_over",
    )(*[pltpu.with_memory_space_constraint(a, pltpu.VMEM) for a in arrays])


def fused(n_rows, arrays):
    (images, valid_h, valid_w, kernel_one, kernel_two, kernel_skip, bias_one, bias_two,
     vector_one, vector_two, vector_skip, cotangent) = arrays
    micros, rows, width, ci = images.shape
    co = kernel_one.shape[3]
    per, pairs, half = micros // 2, rows // 2, width // 2
    op = 2 * TILE
    n_chips = n_rows // 2
    cin, cout = 2 * ci, 2 * co
    sub = min(4, n_chips)
    cubes = n_chips // sub
    lanes_each = -(-max(9 * cin + 6, 5 * cout, 4 * cout + cin) // (TILE * sub)) * (TILE * sub)
    seg_out = rows // 2 + 1
    bits = 3 if n_rows % 8 == 0 else 2
    size1 = -(-(9 * cin) // 64) * 64
    size20 = -(-(9 * cout + cin) // 64) * 64
    share1 = -(-(3 * size1 // 4) // 64) * 16
    share2 = -(-(3 * size20 // 4) // (16 * 2**bits)) * 16
    inputs = {
        "vh": valid_h,
        "vw": valid_w,
        "img": jnp.transpose(images, (0, 1, 3, 2)),
        "k1": kernel_one.reshape(9 * cin, co),
        "k2": kernel_two.reshape(9 * cout, co),
        "k0": kernel_skip,
        "b1": bias_one.reshape(1, co),
        "b2": bias_two.reshape(1, co),
        "q1": vector_one.reshape(1, co),
        "q2": vector_two.reshape(1, co),
        "q0": vector_skip.reshape(1, co),
        "cot": cotangent,
    }
    outputs = {
        "out_b": jax.ShapeDtypeStruct(cotangent.shape, BF16),
        "out_g": jax.ShapeDtypeStruct((micros, rows, ci, width), BF16),
        "out_k1": jax.ShapeDtypeStruct((9 * cin, co), F32),
        "out_k2": jax.ShapeDtypeStruct((9 * cout, co), F32),
        "out_k0": jax.ShapeDtypeStruct((cin, co), F32),
        "out_b1": jax.ShapeDtypeStruct((1, co), F32),
        "out_b2": jax.ShapeDtypeStruct((1, co), F32),
    }
    vm = pltpu.VMEM
    scratch = {
        "img_v": vm((micros, rows, ci, width), BF16),
        "cot_v": vm(cotangent.shape, BF16),
        "k1_v": vm((size1, co), BF16),
        "k20_v": vm((size20, co), BF16),
        "k1p": vm((4 * share1, TILE), BF16),
        "k20p": vm((2**bits * share2, TILE), BF16),
        "k1h": vm((4 * share1, TILE), BF16),
        "k20h": vm((2**bits * share2, TILE), BF16),
        "cotp": vm((per, 3 * pairs * half // 4, TILE), BF16),
        "coth": vm((per, 3 * pairs * half // 4, TILE), BF16),
        "imgr": vm((per, 2, pairs + 2, ci, TILE), BF16),
        "sendp": vm((per, pairs, ci, TILE), BF16),
        "vec": vm((2, 8, TILE), F32),
        "cotr": vm((per, 2, 2, half, co), BF16),
        "perm_in": vm((8 * half, TILE), BF16),
        "perm_x": vm((5 * half, TILE), BF16),
        "w1": vm((9 * TILE, op), BF16),
        "w2": vm((9 * op, op), BF16),
        "w0": vm((TILE, op), BF16),
        "left1": vm((8, 9 * TILE), F32),
        "left2": vm((8, 9 * op), F32),
        "left0": vm((8, TILE), F32),
        "b_in": vm((per, 2 * (rows // 2 + 3), half, 4 * TILE), BF16),
        "xp": vm((per, pairs + 2, 4 * half, TILE), BF16),
        "xb": vm((per, pairs + 2, half, TILE), BF16),
        "raw1": vm((per, 2, 2 * seg_out, half, op), F32),
        "grad1": vm((per, 2, 2 * seg_out, half, op), F32),
        "cols": vm((per, 3, 2 * seg_out, half, op), F32),
        "box": vm((per, pairs, half, 9 * op), BF16),
        "quart": vm((per, pairs + 2, half, op), BF16),
        "acc0": vm((cout, TILE), F32),
        "taps_sum": vm((3, 2, pairs + 2, half, op), F32),
        "g_pre": vm((per, 2, 2 * seg_out, half, op), BF16),
        "taps_in": vm((2, 2 * seg_out, half, 9 * TILE), F32),
        "skip_back": vm((pairs, half, TILE), F32),
        "send_b": vm((per, pairs, half, co), BF16),
        "got_b": vm((per, pairs, half, co), BF16),
        "send_g": vm((per, pairs, ci, TILE), BF16),
        "got_g": vm((per, pairs, ci, TILE), BF16),
    }
    for name, size in (("corr1", 9 * cin), ("corr2", 9 * cout), ("corr0", cin)):
        scratch[name] = vm((size, co), F32)
    share = lanes_each // sub
    for name in ("a", "b", "c"):
        scratch["wire" + name] = vm((2, co, lanes_each), BF16)
        scratch["got" + name] = vm((2, co // 2, lanes_each), BF16)
        scratch["shares" + name] = vm((2, sub, co // 2, share), BF16)
        scratch["landing" + name] = vm((2 * sub - 1, co // 2, share), BF16)
        scratch["mine" + name] = vm((co // 2, share), F32)
        scratch["mids" + name] = vm((cubes, co // 2, share), BF16)
        scratch["result" + name] = vm((sub, co, share), BF16)
    scratch["dots"] = vm((2, 8, TILE), F32)
    copies = 12 + bits + 7 * per + 3 * (1 + 2 * (2 * sub - 1) + cubes - 1)
    scratch["lsem"] = pltpu.SemaphoreType.DMA((5,))
    scratch["ssem"] = pltpu.SemaphoreType.DMA((copies,))
    scratch["rsem"] = pltpu.SemaphoreType.DMA((copies,))
    names = list(inputs) + list(outputs) + list(scratch)
    dims = (micros, rows, width, ci, co, lanes_each, bits, share1, share2)
    smem = pl.BlockSpec(memory_space=pltpu.SMEM)
    vmem = pl.BlockSpec(memory_space=pltpu.VMEM)
    hbm = pl.BlockSpec(memory_space=pltpu.HBM)
    large = ("img", "k1", "k2", "k0", "cot")
    small = ("b1", "b2", "q1", "q2", "q0")
    results = pl.pallas_call(
        functools.partial(fused_kernel, names, n_rows, dims),
        out_shape=[pltpu.VMEM(a.shape, a.dtype) for a in outputs.values()],
        in_specs=[smem, smem] + [vmem if n in small else hbm for n in list(inputs)[2:]],
        out_specs=[vmem] * len(outputs),
        scratch_shapes=list(scratch.values()),
        compiler_params=pltpu.CompilerParams(
            collective_id=0, has_side_effects=True, vmem_limit_bytes=48 * 1024 * 1024
        ),
        name="down_block",
    )(*[pltpu.with_memory_space_constraint(a, pltpu.HBM) if n in large else a for n, a in inputs.items()])
    out_b, out_g, out_k1, out_k2, out_k0, out_b1, out_b2 = hand_over(results)
    return (
        out_b,
        jnp.transpose(out_g, (0, 1, 3, 2)),
        out_k1.reshape(3, 3, cin, co),
        out_k2.reshape(3, 3, cout, co),
        out_k0,
        out_b1.reshape(co),
        out_b2.reshape(co),
    )


def solution(mesh):
    in_specs = (
        P(None, "rows", None, "ch"),
        P(),
        P(),
        P(None, None, None, "ch"),
        P(None, None, None, "ch"),
        P(None, "ch"),
        P("ch"),
        P("ch"),
        P("ch"),
        P("ch"),
        P("ch"),
        P(None, "rows", None, "ch"),
    )
    out_specs = (
        P(None, "rows", None, "ch"),
        P(None, "rows", None, "ch"),
        P(None, None, None, "ch"),
        P(None, None, None, "ch"),
        P(None, "ch"),
        P("ch"),
        P("ch"),
    )

    def step(*arrays):
        if fits(mesh.shape["rows"], mesh.shape["ch"], arrays):
            return fused(mesh.shape["rows"], arrays)
        return shards(*arrays)

    return jax.shard_map(step, mesh=mesh, in_specs=in_specs, out_specs=out_specs, check_vma=False)
```

```python
import functools

import jax
import jax.numpy as jnp
from jax import lax
from jax.experimental import pallas as pl
from jax.experimental.pallas import tpu as pltpu
from jax.sharding import PartitionSpec as P

IMG = 64
SHIFT = 40


EPS = 1e-06
HIGH = lax.Precision.HIGHEST


def extended(cells, sides, width):
    for axis, dim in sides:
        count = lax.axis_size(axis)
        head = lax.slice_in_dim(cells, 0, width, axis=dim)
        tail = lax.slice_in_dim(cells, cells.shape[dim] - width, cells.shape[dim], axis=dim)
        cells = jnp.concatenate(
            [
                lax.ppermute(tail, axis, [(i, (i + 1) % count) for i in range(count)]),
                cells,
                lax.ppermute(head, axis, [((i + 1) % count, i) for i in range(count)]),
            ],
            axis=dim,
        )
    return cells


def conv_rows(rim, kernel, taps):
    slab_rows = taps.shape[1]
    result = None
    for row_tap in range(3):
        part = lax.conv_general_dilated(
            rim[None, row_tap : row_tap + slab_rows],
            kernel[row_tap : row_tap + 1],
            (1, 1),
            ((0, 0), (1, 1)),
            dimension_numbers=("NHWC", "HWIO", "NHWC"),
            preferred_element_type=jnp.float32,
        )
        part = part[0] * taps[row_tap][:, None, None]
        result = part if result is None else result + part
    return result


def flipped(kernel):
    return jnp.transpose(kernel[::-1, ::-1], (0, 1, 3, 2))


def kernel_taps(rim, grad, taps_low):
    slab_rows = grad.shape[0]
    width = grad.shape[1]
    padded = jnp.pad(rim, ((0, 0), (1, 1), (0, 0)))
    stacked = []
    for row_tap in range(3):
        kept_grad = grad * taps_low[row_tap][:, None, None]
        line = []
        for col_tap in range(3):
            window = padded[row_tap : row_tap + slab_rows, col_tap : col_tap + width]
            line.append(
                jnp.einsum("rci,rco->io", window, kept_grad, preferred_element_type=jnp.float32)
            )
        stacked.append(jnp.stack(line))
    return jnp.stack(stacked)


def silu_slope(value):
    gate = jax.nn.sigmoid(value)
    return gate + value * gate * (1.0 - gate)


def shards(
    images,
    valid_h,
    valid_w,
    kernel_one,
    kernel_two,
    kernel_skip,
    bias_one,
    bias_two,
    vector_one,
    vector_two,
    vector_skip,
    cotangent,
):
    micros, rows_dev, width, in_local = images.shape
    out_local = kernel_one.shape[3]
    count_images = valid_h.shape[1]
    total_rows = rows_dev * lax.axis_size("rows")
    slab_start = lax.axis_index("rows") * rows_dev
    rim_global = slab_start - 1 + jnp.arange(rows_dev + 2, dtype=jnp.int32)
    placed = jnp.mod(rim_global - SHIFT, total_rows)
    image_of = placed // IMG
    row_of = placed % IMG
    taps = jnp.stack(
        [image_of[tap : tap + rows_dev] == image_of[1 : rows_dev + 1] for tap in range(3)]
    ).astype(jnp.float32)
    taps_low = taps.astype(jnp.bfloat16)
    owner = image_of[:, None] == jnp.arange(count_images, dtype=jnp.int32)[None, :]
    columns = jnp.arange(width)
    kern_one = kernel_one.astype(jnp.float32)
    kern_two = kernel_two.astype(jnp.float32)
    kern_skip = kernel_skip.astype(jnp.float32).reshape(1, 1, -1, out_local)
    part_one = jnp.einsum("hwio,o->hwi", kern_one, vector_one, precision=HIGH)
    part_two = jnp.einsum("hwio,o->hwi", kern_two, vector_two, precision=HIGH)
    part_skip = jnp.einsum("hwio,o->hwi", kern_skip, vector_skip, precision=HIGH)
    left_one, left_two, left_skip = lax.psum((part_one, part_two, part_skip), "ch")
    left_one = left_one * lax.rsqrt(jnp.sum(left_one * left_one) + EPS)
    left_two = left_two * lax.rsqrt(jnp.sum(left_two * left_two) + EPS)
    left_skip = left_skip * lax.rsqrt(jnp.sum(left_skip * left_skip) + EPS)
    image_one = jnp.einsum("hwio,hwi->o", kern_one, left_one, precision=HIGH)
    image_two = jnp.einsum("hwio,hwi->o", kern_two, left_two, precision=HIGH)
    image_skip = jnp.einsum("hwio,hwi->o", kern_skip, left_skip, precision=HIGH)
    square_one, square_two, square_skip = lax.psum(
        (
            jnp.sum(image_one * image_one),
            jnp.sum(image_two * image_two),
            jnp.sum(image_skip * image_skip),
        ),
        "ch",
    )
    scale_one = lax.rsqrt(square_one + EPS)
    scale_two = lax.rsqrt(square_two + EPS)
    scale_skip = lax.rsqrt(square_skip + EPS)
    right_one = image_one * scale_one
    right_two = image_two * scale_two
    right_skip = image_skip * scale_skip
    sigma_one = square_one * scale_one
    sigma_two = square_two * scale_two
    sigma_skip = square_skip * scale_skip
    eff_one = (kern_one / sigma_one).astype(jnp.bfloat16)
    eff_two = (kern_two / sigma_two).astype(jnp.bfloat16)
    eff_skip_full = (kern_skip / sigma_skip).astype(jnp.bfloat16)
    eff_skip = eff_skip_full[0, 0]
    bias_first = bias_one.astype(jnp.float32)
    bias_second = bias_two.astype(jnp.float32)
    back_two = flipped(eff_two)
    back_one = flipped(eff_one)
    outputs = []
    in_grads = []
    totals = None
    for micro in range(micros):
        height_rows = jnp.sum(jnp.where(owner, valid_h[micro][None, :], 0), axis=1)
        width_rows = jnp.sum(jnp.where(owner, valid_w[micro][None, :], 0), axis=1)
        mask_rim = (
            (row_of < height_rows)[:, None] & (columns[None, :] < width_rows[:, None])
        ).astype(jnp.float32)[:, :, None]
        mask_in = mask_rim[1:-1]
        input_rim = extended(images[micro], (("rows", 0),), 1)
        gathered = lax.all_gather(input_rim, "ch", axis=2, tiled=True)
        masked_rim = gathered * mask_rim.astype(jnp.bfloat16)
        act_in = jax.nn.silu(masked_rim.astype(jnp.float32)).astype(jnp.bfloat16)
        pre_one = conv_rows(act_in, eff_one, taps) + bias_first
        act_one = (jax.nn.silu(pre_one) * mask_in).astype(jnp.bfloat16)
        hidden_rim = extended(act_one, (("rows", 0),), 1)
        hidden_all = lax.all_gather(hidden_rim, "ch", axis=2, tiled=True)
        skip_in = masked_rim[1:-1]
        total = conv_rows(hidden_all, eff_two, taps) + bias_second
        total = total + jnp.einsum(
            "rci,io->rco", skip_in, eff_skip, preferred_element_type=jnp.float32
        )
        pooled = jnp.mean(total.reshape(rows_dev // 2, 2, width // 2, 2, out_local), axis=(1, 3))
        outputs.append(pooled.astype(jnp.bfloat16))
        quarter = cotangent[micro] * 0.25
        grad_total = jnp.broadcast_to(
            quarter[:, None, :, None, :], (rows_dev // 2, 2, width // 2, 2, out_local)
        ).reshape(rows_dev, width, out_local)
        grad_rim = extended(grad_total, (("rows", 0),), 1)
        partial_hidden = conv_rows(grad_rim, back_two, taps)
        grad_act_one = lax.psum_scatter(partial_hidden, "ch", scatter_dimension=2, tiled=True)
        grad_pre_one = (grad_act_one * mask_in * silu_slope(pre_one)).astype(jnp.bfloat16)
        pre_rim = extended(grad_pre_one, (("rows", 0),), 1)
        partial_act = conv_rows(pre_rim, back_one, taps)
        partial_skip = jnp.einsum(
            "rco,io->rci", grad_total, eff_skip, preferred_element_type=jnp.float32
        )
        grad_act_in, grad_skip_in = (
            lax.psum_scatter(partial_act, "ch", scatter_dimension=2, tiled=True),
            lax.psum_scatter(partial_skip, "ch", scatter_dimension=2, tiled=True),
        )
        own_input = images[micro].astype(jnp.float32)
        in_grads.append(
            (mask_in * (silu_slope(own_input) * grad_act_in + grad_skip_in)).astype(jnp.bfloat16)
        )
        grad_one = kernel_taps(act_in, grad_pre_one, taps_low)
        grad_two = kernel_taps(hidden_all, grad_total, taps_low)
        grad_skip = jnp.einsum(
            "rci,rco->io", skip_in, grad_total, preferred_element_type=jnp.float32
        )
        grad_first = jnp.sum(grad_pre_one.astype(jnp.float32), axis=(0, 1))
        grad_second = jnp.sum(grad_total.astype(jnp.float32), axis=(0, 1))
        current = (grad_one, grad_two, grad_skip, grad_first, grad_second)
        if totals is None:
            totals = current
        else:
            totals = tuple((acc + new for acc, new in zip(totals, current)))
    summed = lax.psum((totals[0], totals[1], totals[2], totals[3], totals[4]), "rows")
    sum_one, sum_two, sum_skip, sum_first, sum_second = summed
    sum_skip = sum_skip.reshape(1, 1, -1, out_local)
    dot_one, dot_two, dot_skip = lax.psum(
        (jnp.sum(sum_one * kern_one), jnp.sum(sum_two * kern_two), jnp.sum(sum_skip * kern_skip)),
        "ch",
    )
    final_one = (
        sum_one / sigma_one - dot_one / (sigma_one * sigma_one) * left_one[..., None] * right_one
    )
    final_two = (
        sum_two / sigma_two - dot_two / (sigma_two * sigma_two) * left_two[..., None] * right_two
    )
    final_skip = (
        sum_skip / sigma_skip
        - dot_skip / (sigma_skip * sigma_skip) * left_skip[..., None] * right_skip
    )
    return (
        jnp.stack(outputs),
        jnp.stack(in_grads),
        final_one,
        final_two,
        final_skip[0, 0],
        sum_first,
        sum_second,
    )


F32 = jnp.float32
BF16 = jnp.bfloat16
MESH = pl.DeviceIdType.MESH
TILE = 128
NT = (((1,), (1,)), ((), ()))
TN = (((0,), (0,)), ((), ()))
NN = (((1,), (0,)), ((), ()))


def fits(n_rows, n_ch, arrays):
    images, kernel_one = arrays[0], arrays[3]
    micros, rows_dev, width, in_local = images.shape
    out_local = kernel_one.shape[3]
    return (
        n_ch == 2
        and micros % 2 == 0
        and n_rows >= 4
        and n_rows % min(8, n_rows) == 0
        and n_rows % 4 == 0
        and rows_dev % 8 == 0
        and SHIFT % rows_dev == rows_dev // 2
        and IMG % rows_dev == 0
        and 2 * width == TILE
        and in_local % 16 == 0
        and 2 * in_local < TILE
        and out_local == 3 * TILE // 4
    )


def dot(left, right, dims=NN):
    return lax.dot_general(left, right, dims, preferred_element_type=F32)


def iota(shape, dim):
    return lax.broadcasted_iota(jnp.int32, shape, dim)


def pieces(row):
    first = row.astype(BF16).astype(F32)
    rest = row - first
    second = rest.astype(BF16).astype(F32)
    third = rest - second
    at = iota((16, row.shape[1]), 0)
    zero = jnp.zeros((16, row.shape[1]), F32)
    stacked = jnp.where(at == 0, first, jnp.where(at == 1, second, jnp.where(at == 2, third, zero)))
    return stacked.astype(BF16)


def total(value):
    return jnp.sum(jnp.sum(value, axis=0, keepdims=True), axis=1, keepdims=True)


def power(vector_row, kernel):
    left = jnp.sum(dot(pieces(vector_row), kernel, NT), axis=0, keepdims=True)
    left = left * lax.rsqrt(total(left * left) + EPS)
    image = jnp.sum(dot(pieces(left), kernel), axis=0, keepdims=True)
    square = total(image * image)
    scale = lax.rsqrt(square + EPS)
    return left, image * scale, square * scale


def slope(value):
    gate = 1.0 / (1.0 + jnp.exp(-value))
    return gate + value * gate * (1.0 - gate)


def fused_kernel(names, n_rows, dims, *refs):
    micros, rows, width, ci, co, lanes_one, lanes_two, bits, share1, share2 = dims
    ref = dict(zip(names, refs))
    half = width // 2
    per = micros // 2
    pairs = rows // 2
    cut = rows // 2
    seg_slots = cut + 3
    seg_out = cut + 1
    pairs_a = cut // 2 + 1
    n_chips = n_rows // 2
    cin, cout = 2 * ci, 2 * co
    op = 2 * TILE
    total_rows = rows * n_rows
    own_px = pairs * half
    all_px = (pairs + 2) * half

    ssem, rsem, lsem = ref["ssem"], ref["rsem"], ref["lsem"]
    me = lax.axis_index("rows")
    c = lax.axis_index("ch")
    o = 1 - c
    core = lax.rem(me, 2)
    mate = me + 1 - 2 * core
    chip = me // 2
    up = lax.rem(me + n_rows - 1, n_rows)
    down = lax.rem(me + 1, n_rows)
    my_id = c * n_chips + chip
    sub = min(4, n_chips)
    cubes = n_chips // sub
    spot_in, cube = lax.rem(chip, sub), chip // sub
    my_id = c * sub + spot_in
    far = []
    for delta in range(1, 2 * sub):
        other = lax.rem(my_id + delta, 2 * sub)
        far.append((2 * (cube * sub + lax.rem(other, sub)) + core, other // sub))
    across = []
    for delta in range(1, cubes):
        across.append((2 * (lax.rem(cube + delta, cubes) * sub + spot_in) + core, c))
    around = []
    for delta in range(1, 2 * sub):
        other = lax.rem(2 * spot_in + core + delta, 2 * sub)
        around.append((2 * cube * sub + other, c))
    near = [(me, o), (mate, c), (up, c), (up, o), (down, c), (down, o)]

    barrier = pltpu.get_barrier_semaphore()
    for device in near + far + across + around:
        pl.semaphore_signal(barrier, inc=1, device_id=device, device_id_type=MESH)

    count = [0]
    sends = []

    def remote(src, dst, device):
        at = count[0]
        count[0] += 1
        return pltpu.make_async_remote_copy(
            src_ref=src,
            dst_ref=dst,
            send_sem=ssem.at[at],
            recv_sem=rsem.at[at],
            device_id=device,
            device_id_type=MESH,
        )

    def begin(*args):
        copy = remote(*args)
        copy.start()
        sends.append(copy)
        return copy

    img, cot, k1, k20 = ref["img_v"], ref["cot_v"], ref["k1_v"], ref["k20_v"]
    n1, n2 = 9 * cin, 9 * cout
    loads = []
    for i, (src, dst) in enumerate(
        [
            (ref["img"], img),
            (ref["k1"], k1.at[0:n1]),
            (ref["k0"], k20.at[n2 : n2 + cin]),
            (ref["k2"], k20.at[0:n2]),
            (ref["cot"], cot),
            (ref["vh"], ref["vh_s"]),
            (ref["vw"], ref["vw_s"]),
            (ref["b1"], ref["b1_v"]),
            (ref["b2"], ref["b2_v"]),
            (ref["q1"], ref["q1_v"]),
            (ref["q2"], ref["q2_v"]),
            (ref["q0"], ref["q0_v"]),
        ]
    ):
        load = pltpu.make_async_copy(src, dst, lsem.at[i])
        load.start()
        loads.append(load)

    perm_in, perm_x = ref["perm_in"], ref["perm_x"]
    shape = (8 * half, TILE)
    at, lane = iota(shape, 0), iota(shape, 1)
    column = 2 * lax.rem(at, half) + lax.rem(at // half, 4) - 1
    hit = (lane - at // (4 * half) * width == column) & (column >= 0) & (column < width)
    perm_in[...] = jnp.where(hit, 1.0, 0.0).astype(BF16)
    shape = (4 * half, TILE)
    at, lane = iota(shape, 0), iota(shape, 1)
    source = at // (2 * half) * width + 2 * lax.rem(at, half) + lax.rem(at // half, 2)
    perm_x[0 : 4 * half] = jnp.where(lane == source, 1.0, 0.0).astype(BF16)
    shape = (half, TILE)
    at, lane = iota(shape, 0), iota(shape, 1)
    perm_x[4 * half : 5 * half] = jnp.where(lax.rem(lane, width) // 2 == at, 1.0, 0.0).astype(BF16)

    eye = ref["eye"]
    shape = (op, op)
    eye[...] = jnp.where(iota(shape, 0) == iota(shape, 1), 1.0, 0.0).astype(BF16)

    def rem_pos(value, by):
        return lax.rem(lax.rem(value, by) + by, by)

    first_a = rem_pos(me * rows - SHIFT, total_rows)
    first_b = rem_pos(me * rows + cut - SHIFT, total_rows)
    base = [lax.rem(first_a, IMG), lax.rem(first_b, IMG) - cut]
    image_a, image_b = first_a // IMG, first_b // IMG
    keep = jnp.where(base[1] < 0, 0.0, 1.0).astype(F32)
    def choose(seg, two):
        return jnp.where(seg == 0, two[0], two[1])

    imgr, sendp = ref["imgr"], ref["sendp"]
    loads[0].wait()
    for j in range(per):
        for mine in (False, True):

            def pack(p, carry, j=j, mine=mine):
                m = (c if mine else o) * per + j
                pair = jnp.concatenate([img[m, 2 * p], img[m, 2 * p + 1]], axis=1)
                if mine:
                    imgr[j, c, p + 1] = pair
                else:
                    sendp[j, p] = pair
                return carry

            lax.fori_loop(0, pairs, pack, 0, unroll=4)
    for load in loads[1:]:
        load.wait()
    vh, vw = ref["vh_s"], ref["vw_s"]
    high = [[vh[c * per + j, image] for image in (image_a, image_b)] for j in range(per)]
    wide = [[vw[c * per + j, image] for image in (image_a, image_b)] for j in range(per)]

    vec = ref["vec"]
    vec[c] = jnp.zeros(vec.shape[1:], F32)
    for i, name in enumerate(("q1", "q2", "q0", "b1", "b2")):
        vec[c, i : i + 1, 0:co] = ref[name + "_v"][...].astype(F32)

    def packed(value):
        kept, strip = 3 * value.shape[-2] // 4, co // 3
        last = value[kept:]
        beside = jnp.concatenate([last[:, k * strip : (k + 1) * strip] for k in range(3)], axis=0)
        return jnp.concatenate([value[:kept], beside], axis=1)

    def unpacked(value):
        part = value.shape[0] // 3
        last = jnp.concatenate([value[k * part : (k + 1) * part, co:] for k in range(3)], axis=1)
        return jnp.concatenate([value[:, :co], last], axis=0)

    k1p, k20p, cotp = ref["k1p"], ref["k20p"], ref["cotp"]
    size1, size20 = 3 * k1.shape[0] // 4, 3 * k20.shape[0] // 4
    k1p[0:size1] = packed(k1[...])
    k20p[0:size20] = packed(k20[...])
    for j in range(per):
        cotp[j] = packed(cot[o * per + j].reshape(own_px, co))

    pl.semaphore_wait(barrier, len(near + far + across + around))

    k1h, k20h, coth, cotr = ref["k1h"], ref["k20h"], ref["coth"], ref["cotr"]
    spots = [core] + [lax.rem(me // 2**b, 2) for b in range(1, bits)]

    def part_of(rows_each, depth, bits_at):
        first = 0
        for b in range(depth):
            first = first * 2 + bits_at[b]
        return pl.ds(first * rows_each, rows_each)

    class Shared:
        def __init__(self, own, got, rows_each, depth):
            self.got, self.rows_each, self.depth, self.level = got, rows_each, depth, 0
            at = part_of(rows_each, depth, spots)
            self.copies = [begin(own.at[at], got.at[at], (me, o))]

        def turn(self):
            for copy in self.copies:
                copy.wait_recv()
            self.copies = []
            if self.level == 0:
                at = self.got.at[part_of(self.rows_each, self.depth, spots)]
                for mask in range(1, 2 ** (self.depth - 1)):
                    other = me
                    for b in range(1, self.depth):
                        if mask >> (b - 1) & 1:
                            other = other + 2**b * (1 - 2 * spots[b])
                    self.copies.append(begin(at, at, (other, c)))
            if self.level == 1:
                size = 2 ** (self.depth - 1) * self.rows_each
                at = self.got.at[pl.ds(core * size, size)]
                self.copies.append(begin(at, at, (mate, c)))
            self.level += 1

    mine_c, mine_o = pl.ds(c * per, per), pl.ds(o * per, per)
    img_x, img_halo = [], []

    def send_image(j):
        img_x.append(begin(sendp.at[j], imgr.at[j, c, pl.ds(1, pairs)], (me, o)))
        img_halo.append(
            [
                begin(sendp.at[j, 0], imgr.at[j, c, pairs + 1], (up, o)),
                begin(sendp.at[j, pairs - 1], imgr.at[j, c, 0], (down, o)),
                begin(imgr.at[j, c, 1], imgr.at[j, c, pairs + 1], (up, c)),
                begin(imgr.at[j, c, pairs], imgr.at[j, c, 0], (down, c)),
            ]
        )

    vec_x = begin(vec.at[c], vec.at[c], (me, o))
    one = Shared(k1p, k1h, share1, 2)
    two = Shared(k20p, k20h, share2, bits)
    for j in range(per):
        send_image(j)
    cot_x = [begin(cotp.at[j], coth.at[j], (me, o)) for j in range(per)]
    cot_halo = [
        begin(cot.at[mine_o, 0], cotr.at[:, c, 1], (up, o)),
        begin(cot.at[mine_o, pairs - 1], cotr.at[:, c, 0], (down, o)),
        begin(cot.at[mine_c, 0], cotr.at[:, c, 1], (up, c)),
        begin(cot.at[mine_c, pairs - 1], cotr.at[:, c, 0], (down, c)),
    ]

    w1, w2, w0 = ref["w1"], ref["w2"], ref["w0"]

    def place(dst, row, own_part, other_part, padded):
        size = own_part.shape[0]
        first = jnp.where(c == 0, own_part, other_part)
        second = jnp.where(c == 0, other_part, own_part)
        line = jnp.concatenate([first, second, jnp.zeros((size, op - cout), BF16)], axis=1)
        dst[pl.ds(row, size), :] = line
        if padded > size:
            dst[pl.ds(row + size, padded - size), :] = jnp.zeros((padded - size, op), BF16)

    def row_of(i):
        return jnp.concatenate(
            [vec[0, i : i + 1, 0:co], vec[1, i : i + 1, 0:co], jnp.zeros((1, op - cout), F32)], axis=1
        )

    b_in, xp, xb = ref["b_in"], ref["xp"], ref["xb"]
    ones = jnp.where(iota((TILE - cin, TILE), 0) == 0, 1.0, 0.0).astype(BF16)

    def prepare(j):
        img_x[j].wait_recv()
        for copy in img_halo[j]:
            copy.wait_recv()

        def two_pairs(step, carry):
            lane = iota((1, TILE), 1)
            column = lax.rem(lane, width)
            acts, plain, slots = [], [], []
            for k in range(2):
                p = 2 * step + k
                seg = (p >= pairs_a).astype(jnp.int32)
                row = 2 * p - 2 + lane // width
                mask = jnp.where(
                    (choose(seg, base) + row < choose(seg, high[j])) & (column < choose(seg, wide[j])), 1.0, 0.0
                )
                x = jnp.concatenate([imgr[j, 0, p], imgr[j, 1, p]], axis=0).astype(F32) * mask
                act = x / (1.0 + jnp.exp(-x))
                acts += [act.astype(BF16), ones]
                plain += [x.astype(BF16), ones]
                slots.append(2 * p + 2 * seg)
            spread = dot(perm_in[...], jnp.concatenate(acts, axis=0), NT).astype(BF16)
            for k in range(2):
                for a in range(2):
                    for t in range(4):
                        b_in[j, slots[k] + a, :, t * TILE : (t + 1) * TILE] = spread[
                            (4 * a + t) * half : (4 * a + t + 1) * half, k * TILE : (k + 1) * TILE
                        ]
            spread = dot(perm_x[...], jnp.concatenate(plain, axis=0), NT).astype(BF16)
            for k in range(2):
                part = spread[:, k * TILE : (k + 1) * TILE]
                xp[j, 2 * step + k] = part[0 : 4 * half]
                xb[j, 2 * step + k] = part[4 * half : 5 * half]
            return carry

        lax.fori_loop(0, (pairs + 2) // 2, two_pairs, 0, unroll=True)
        b_in[j, seg_slots - 1] = (b_in[j, seg_slots + 1].astype(F32) * keep).astype(BF16)
        b_in[j, seg_slots] = (b_in[j, seg_slots - 2].astype(F32) * keep).astype(BF16)

    raw1, grad1, act1 = ref["raw1"], ref["grad1"], ref["act1"]

    def conv_one(j):
        parts = []
        for seg in range(2):
            for b in range(2):
                first = seg * seg_slots
                taps = [
                    b_in[j, first + u : first + u + seg_out, :, b * TILE : (b + 3) * TILE].reshape(
                        seg_out * half, 3 * TILE
                    )
                    for u in range(3)
                ]
                parts.append(jnp.concatenate(taps, axis=1))
        result = dot(jnp.concatenate(parts, axis=0), w1[...]).reshape(2, 2, seg_out, half, op)
        for seg in range(2):
            for b in range(2):
                raw1[j, b, seg * seg_out : (seg + 1) * seg_out] = result[seg, b]

    cols = ref["cols"]
    pixel = iota((half, op), 0)

    def activate(j):
        def line(i, carry):
            seg = (i >= seg_out).astype(jnp.int32)
            broad = jnp.where(choose(seg, base) + i - 1 < choose(seg, high[j]), choose(seg, wide[j]), 0)
            acts = []
            for b in range(2):
                pre = raw1[j, b, i] * scale1 + bias1
                gate = 1.0 / (1.0 + jnp.exp(-pre))
                mask = 2 * pixel + b < broad
                lift = pre * gate
                grad1[j, b, i] = jnp.where(mask, gate + lift * (1.0 - gate), 0.0)
                act = jnp.where(mask, lift, 0.0).astype(BF16)
                act1[j, b, i] = act
                acts.append(act.astype(F32))
            even, odd = acts
            before = jnp.where(pixel == 0, 0.0, pltpu.roll(odd, 1, 0))
            after = jnp.where(pixel == half - 1, 0.0, pltpu.roll(even, half - 1, 0))
            cols[j, 0, i] = before + even
            cols[j, 1, i] = even + odd
            cols[j, 2, i] = odd + after
            return carry

        lax.fori_loop(0, 2 * seg_out, line, 0, unroll=2)

    box = ref["box"]

    def boxes(j):
        def line(i, carry):
            above = jnp.where(i == cut // 2, keep, 1.0)
            below = jnp.where(i == cut // 2 - 1, keep, 1.0)
            for w in range(3):
                lines = [cols[j, w, 2 * i + k] for k in range(4)]
                for u in range(3):
                    upper, lower = lines[u], lines[u + 1]
                    if u == 0:
                        upper = upper * above
                    if u == 2:
                        lower = lower * below
                    tap = 3 * u + w
                    box[j, i, :, tap * op : (tap + 1) * op] = (upper + lower).astype(BF16)
            return carry

        lax.fori_loop(0, pairs, line, 0, unroll=2)

    quart = ref["quart"]

    def quarter(j):
        def put(i, own, other):
            first = jnp.where(c == 0, own, other)
            second = jnp.where(c == 0, other, own)
            size = first.shape[0]
            line = jnp.concatenate([first, second, jnp.zeros((size, op - cout), BF16)], axis=1)
            line = (line.astype(F32) * 0.25).astype(BF16)
            quart[j, pl.ds(i, size // half)] = line.reshape(size // half, half, op)

        put(1, cot[c * per + j].reshape(own_px, co), unpacked(coth[j]))
        for i in (0, 1):
            put(i * (pairs + 1), cotr[j, c, i], cotr[j, o, i])

    def owned(j):
        return quart[j, 1 : pairs + 1].reshape(own_px, op)

    half_rows = co // 2
    kept_rows = pl.ds(core * half_rows, half_rows)
    mate_rows = pl.ds((1 - core) * half_rows, half_rows)

    class Summed:
        def __init__(self, name):
            self.wire, self.got, self.shares, self.landing, self.mine, self.mids, self.result = [
                ref[part + name] for part in ("wire", "got", "shares", "landing", "mine", "mids", "result")
            ]
            self.share = self.result.shape[2]
            self.copies = [begin(self.wire.at[:, mate_rows], self.got, (mate, c))]

        def arrived(self):
            for copy in self.copies:
                copy.wait_recv()

        def to_owners(self):
            self.arrived()
            for ch in range(2):
                value = self.wire[ch, kept_rows].astype(F32) + self.got[ch].astype(F32)
                for at in range(sub):
                    self.shares[ch, at] = value[:, at * self.share : (at + 1) * self.share].astype(BF16)
            lanes = pl.ds(pl.multiple_of(spot_in * self.share, TILE), self.share)
            self.mine[...] = self.wire[c, kept_rows, lanes].astype(F32) + self.got[c, :, lanes].astype(F32)
            self.copies = []
            for delta in range(1, 2 * sub):
                other = lax.rem(my_id + delta, 2 * sub)
                self.copies.append(
                    begin(
                        self.shares.at[other // sub, lax.rem(other, sub)], self.landing.at[delta - 1], far[delta - 1]
                    )
                )

        def to_cubes(self):
            self.arrived()
            value = self.mine[...]
            for delta in range(1, 2 * sub):
                value = value + self.landing[delta - 1].astype(F32)
            self.mids[cube] = value.astype(BF16)
            self.copies = [begin(self.mids.at[cube], self.mids.at[cube], device) for device in across]

        def to_all(self):
            self.arrived()
            value = self.mids[0].astype(F32)
            for at in range(1, cubes):
                value = value + self.mids[at].astype(F32)
            self.result[spot_in, kept_rows] = value.astype(BF16)
            place_at = self.result.at[spot_in, kept_rows]
            self.copies = [begin(place_at, place_at, device) for device in around]

        def turned(self, scale, out, first, size):
            self.arrived()
            for at in range(0, sub * self.share, op):
                piece, lanes = at // self.share, at % self.share
                value = dot(eye[...], self.result[piece, :, lanes : lanes + op], NT)
                some = min(op, size - at)
                if some > 0:
                    out[first + at : first + at + some] = value[0:some] * scale
                if some < op:
                    return value[some:]

    one.turn()
    two.turn()
    one.turn()
    prepare(0)
    one.turn()
    vec_x.wait_recv()
    k1o = unpacked(k1h[0:size1])
    for tap in range(9):
        rows_at = slice(tap * cin, (tap + 1) * cin)
        place(w1, tap * TILE, k1[rows_at], k1o[rows_at], TILE)
    left1, right1, sigma1 = power(row_of(0), w1[...])
    scale1 = 1.0 / sigma1
    bias1, bias2 = row_of(3), row_of(4)
    left1_ref, left2_ref, left0_ref = ref["left1"], ref["left2"], ref["left0"]
    left1_ref[0:1] = left1
    conv_one(0)
    activate(0)
    two.turn()
    boxes(0)
    for j in range(1, per):
        prepare(j)
        conv_one(j)
        activate(j)
        boxes(j)
    for copy in cot_x:
        copy.wait_recv()
    for copy in cot_halo:
        copy.wait_recv()
    for j in range(per):
        quarter(j)

    acc0 = ref["acc0"]
    given = jnp.concatenate([owned(j) for j in range(per)], axis=0)[:, 0:cout]
    turned_quart = jnp.transpose(given)
    sums0 = ref["sums0"]
    group_a = None
    for name, taps in (("a", range(0, 5)), ("b", range(5, 9))):
        lanes = slice(taps[0] * op, (taps[-1] + 1) * op)
        value = dot(turned_quart, box[:, :, :, lanes].reshape(per * own_px, len(taps) * op))
        parts = [value[:, k * op : k * op + cout] for k in range(len(taps))]
        if name == "b":
            skip = dot(turned_quart, xb[:, 1 : pairs + 1].reshape(per * own_px, TILE))
            acc0[...] = skip
            sums0[...] = skip.astype(BF16)
            parts.append(skip[:, 0:cin])
        parts.append(jnp.zeros((cout, lanes_two - sum(part.shape[1] for part in parts)), F32))
        flat = jnp.concatenate(parts, axis=1).astype(BF16)
        for ch in range(2):
            ref["wire" + name][ch] = flat[ch * co : (ch + 1) * co]
        if name == "a":
            group_a = Summed("a")
    group_b = Summed("b")
    two.turn()
    k20o = unpacked(k20h[0:size20])
    for tap in range(9):
        rows_at = slice(tap * cout, (tap + 1) * cout)
        place(w2, tap * op, k20[rows_at], k20o[rows_at], op)
    rows_at = slice(n2, n2 + cin)
    place(w0, 0, k20[rows_at], k20o[rows_at], TILE)
    left2, right2, sigma2 = power(row_of(1), w2[...])
    left0, right0, sigma0 = power(row_of(2), w0[...])
    scale2, scale0 = 1.0 / sigma2, 1.0 / sigma0
    left0_ref[0:1] = left0
    left2_ref[0:1] = left2

    taps_sum = ref["taps_sum"]
    spot = iota((per * all_px, op), 0)
    at_left = lax.rem(spot, half) == 0
    at_right = lax.rem(spot, half) == half - 1
    g_pre = ref["g_pre"]

    def back_taps():
        given = quart[...].reshape(per * all_px, op)
        for u in range(3):
            t0, t1, t2 = [
                dot(given, w2[(3 * u + w) * op : (3 * u + w + 1) * op], NT) for w in range(3)
            ]
            even = t0 + t1 + jnp.where(at_left, 0.0, pltpu.roll(t2, 1, 0))
            odd = t1 + t2 + jnp.where(at_right, 0.0, pltpu.roll(t0, per * all_px - 1, 0))
            taps_sum[u, 0] = even.reshape(per, pairs + 2, half, op)
            taps_sum[u, 1] = odd.reshape(per, pairs + 2, half, op)

    def back_two(j, dots):
        def line(i, carry):
            hold = jnp.where(i == cut // 2, keep, 1.0)
            own_even = jnp.where(i < pairs, 1.0, 0.0)
            own_odd = jnp.where(i > 0, 1.0, 0.0)
            one, two = carry
            for b in range(2):
                upper, lower = taps_sum[2, b, j, i], taps_sum[0, b, j, i + 1]
                even = lower + taps_sum[1, b, j, i + 1] + hold * upper
                odd = taps_sum[1, b, j, i] + upper + hold * lower
                two = two + own_even * even * act1[j, b, 2 * i + 1].astype(F32)
                two = two + own_odd * odd * act1[j, b, 2 * i].astype(F32)
                even = (even * scale2 * grad1[j, b, 2 * i + 1]).astype(BF16)
                odd = (odd * scale2 * grad1[j, b, 2 * i]).astype(BF16)
                g_pre[j, b, 2 * i + 1] = even
                g_pre[j, b, 2 * i] = odd
                one = one + own_even * even.astype(F32) * raw1[j, b, 2 * i + 1]
                one = one + own_odd * odd.astype(F32) * raw1[j, b, 2 * i]
            return one, two

        return lax.fori_loop(0, pairs + 1, line, dots, unroll=3)

    back_taps()
    group_a.to_owners()
    dots = (jnp.zeros((half, op), F32), jnp.zeros((half, op), F32))
    dots = back_two(0, dots)
    group_b.to_owners()
    for j in range(1, per):
        dots = back_two(j, dots)
    dot1, dot2 = dots

    turned_grad = []
    for b in range(2):
        lines = [g_pre[j, b, 1 : rows + 1].reshape(rows * half, op) for j in range(per)]
        turned_grad.append(jnp.concatenate(lines, axis=0)[:, 0:cout])

    def kernel_one_grad(taps):
        value = None
        for b in range(2):
            lines = []
            for j in range(per):
                for seg in range(2):
                    first = seg * (cut + 2) + 1
                    blocks = []
                    for u in range(3):
                        cols_at = [w for w in range(3) if 3 * u + w in taps]
                        if cols_at:
                            block = b_in[
                                j,
                                first + u : first + u + cut,
                                :,
                                (b + cols_at[0]) * TILE : (b + cols_at[-1] + 1) * TILE,
                            ]
                            blocks.append(block.reshape(cut * half, len(cols_at) * TILE))
                    lines.append(jnp.concatenate(blocks, axis=1))
            part = dot(turned_grad[b], jnp.concatenate(lines, axis=0), TN)
            value = part if value is None else value + part
        return value

    def pair_of(column):
        high_part = column.astype(BF16).astype(F32)
        return [high_part, column - high_part]

    def trace_of(partial, kernel):
        product = dot(partial, kernel)
        eye = iota(product.shape, 0) == iota(product.shape, 1)
        return total(jnp.where(eye, product, 0.0))

    def send_one(name, taps, extras):
        value = kernel_one_grad(taps)
        parts = [value[:, k * TILE : k * TILE + cin] for k in range(len(taps))]
        rest = extras(value)
        spare = lanes_one - len(taps) * cin - len(rest)
        parts.append(jnp.concatenate(rest + [jnp.zeros((cout, spare), F32)], axis=1))
        flat = jnp.concatenate(parts, axis=1).astype(BF16)
        for ch in range(2):
            ref["wire" + name][ch] = flat[ch * co : (ch + 1) * co]
        return Summed(name)

    def extras_c(value):
        at = 4 * TILE + cin
        return pair_of(value[:, at : at + 1]) + pair_of(acc0[:, cin : cin + 1])

    def extras_d(value):
        sums_at = [total(dot1), total(dot2), trace_of(sums0[...], w0[...])]
        return [part for at in sums_at for part in pair_of(jnp.broadcast_to(at, (cout, 1)))]

    group_c = send_one("c", range(0, 9), lambda value: extras_c(value) + extras_d(value))

    out_b, send_b, got_b = ref["out_b"], ref["send_b"], ref["got_b"]

    def conv_two(j):
        main = dot(box[j].reshape(own_px, 9 * op), w2[...])
        skip = dot(xb[j, 1 : pairs + 1].reshape(own_px, TILE), w0[...])
        value = ((main * scale2 + skip * scale0) * 0.25 + bias2).astype(BF16)
        first, second = value[:, 0:co], value[:, co:cout]
        out_b[c * per + j] = jnp.where(c == 0, first, second).reshape(pairs, half, co)
        send_b[j] = jnp.where(c == 0, second, first).reshape(pairs, half, co)

    taps_in, skip_back = ref["taps_in"], ref["skip_back"]
    pixel_in = iota((half, TILE), 0)
    out_g, send_g, got_g = ref["out_g"], ref["send_g"], ref["got_g"]

    def back_products(j):
        skip_back[...] = (dot(owned(j), w0[...], NT) * scale0).reshape(pairs, half, TILE)

        given = g_pre[j].reshape(4 * seg_out * half, op)
        taps_in[...] = dot(given, w1[...], NT).reshape(2, 2 * seg_out, half, 9 * TILE)

    def input_rows(j):
        def two_rows(p, carry):
            lines = []
            for a in range(2):
                r = 2 * p + a
                hold_up = jnp.where(r == cut - 1, keep, 1.0)
                hold_down = jnp.where(r == cut, keep, 1.0)

                def column_sum(w, s):
                    def of(u, row):
                        at = (3 * u + w) * TILE
                        return taps_in[s, row, :, at : at + TILE]

                    return of(0, r + 2) * hold_up + of(1, r + 1) + of(2, r) * hold_down

                before = pltpu.roll(column_sum(2, 1), 1, 0)
                after = pltpu.roll(column_sum(0, 0), half - 1, 0)
                even = column_sum(0, 1) + column_sum(1, 0) + jnp.where(pixel_in == 0, 0.0, before)
                odd = column_sum(1, 1) + column_sum(2, 0) + jnp.where(pixel_in == half - 1, 0.0, after)
                seg = (r >= cut).astype(jnp.int32)
                broad = jnp.where(choose(seg, base) + r < choose(seg, high[j]), choose(seg, wide[j]), 0)
                for b, value in ((0, even), (1, odd)):
                    at = (2 * a + b) * half
                    x = xp[j, p + 1, at : at + half].astype(F32)
                    mask = 2 * pixel_in + b < broad
                    value = slope(x) * (value * scale1) + skip_back[p]
                    lines.append(jnp.where(mask, value, 0.0).astype(BF16))
            line = dot(jnp.concatenate(lines, axis=0), perm_x[0 : 4 * half], TN).astype(BF16)
            own = jnp.where(c == 0, line[0:ci], line[ci:cin])
            other = jnp.where(c == 0, line[ci:cin], line[0:ci])
            out_g[c * per + j, 2 * p] = own[:, 0:width]
            out_g[c * per + j, 2 * p + 1] = own[:, width:TILE]
            send_g[j, p] = other
            return carry

        lax.fori_loop(0, pairs, two_rows, 0, unroll=4)
        return begin(send_g.at[j], got_g.at[j], (me, o))

    def unpack(j):
        def line(p, carry):
            out_g[o * per + j, 2 * p] = got_g[j, p, :, 0:width]
            out_g[o * per + j, 2 * p + 1] = got_g[j, p, :, width:TILE]
            return carry

        grad_x[j].wait_recv()
        lax.fori_loop(0, pairs, line, 0, unroll=4)

    conv_two(0)
    for j in range(1, per):
        conv_two(j)
    group_c.to_owners()
    out_x = begin(send_b, got_b, (me, o))
    back_products(0)
    group_a.to_cubes()
    grad_x = [input_rows(0)]
    group_b.to_cubes()
    for j in range(1, per):
        back_products(j)
        if j == 1:
            group_c.to_cubes()
            group_a.to_all()
        grad_x.append(input_rows(j))

    def own_half(row):
        return jnp.where(c == 0, row[:, 0:co], row[:, co:cout])

    def column_of(row):
        row = jnp.concatenate([own_half(row), jnp.zeros((1, TILE - co), F32)], axis=1)
        return jnp.transpose(jnp.broadcast_to(row, (TILE, TILE)))[0:co]

    def compact(row, size, padded):
        return jnp.concatenate([row[:, t * padded : t * padded + size] for t in range(9)], axis=1)

    def turned(part, out, at):
        some = part.shape[1]
        if some < TILE:
            part = jnp.concatenate([part, jnp.zeros((co, TILE - some), F32)], axis=1)
        part = jnp.concatenate([part, jnp.zeros((TILE - co, TILE), F32)], axis=0)
        out[at : at + some] = jnp.transpose(part)[0:some, 0:co]

    def outer(left, right, out):
        columns = column_of(right)
        for at in range(0, left.shape[1], TILE):
            some = min(TILE, left.shape[1] - at)
            turned(columns[:, 0:some] * left[:, at : at + some], out, at)

    corr1, corr2, corr0 = ref["corr1"], ref["corr2"], ref["corr0"]
    group_b.to_all()
    outer(compact(left1_ref[0:1], cin, TILE), right1 * (scale1 * scale1), corr1)
    outer(compact(left2_ref[0:1], cout, op), right2 * (scale2 * scale2), corr2)
    outer(left0_ref[0:1, 0:cin], right0 * (scale0 * scale0), corr0)
    out_k1, out_k2, out_k0 = ref["out_k1"], ref["out_k2"], ref["out_k0"]
    group_c.to_all()
    group_a.turned(scale2, out_k2, 0, 5 * cout)
    out_x.wait_recv()
    out_b[mine_o] = got_b[...]
    unpack(0)
    rest = group_b.turned(scale2, out_k2, 5 * cout, 4 * cout)
    out_k0[...] = rest[0:cin] * scale0
    for j in range(1, per):
        unpack(j)
    extra = group_c.turned(scale1, out_k1, 0, n1)
    ref["out_b1"][...] = extra[0:1] + extra[1:2]
    ref["out_b2"][...] = extra[2:3] + extra[3:4]
    for at, (out, corr) in enumerate(((out_k1, corr1), (out_k2, corr2), (out_k0, corr0))):
        value = extra[4 + 2 * at : 5 + 2 * at, 0:1] + extra[5 + 2 * at : 6 + 2 * at, 0:1]
        out[...] = out[...] - corr[...] * value

    for copy in sends:
        copy.wait_send()


def hand_over(arrays):
    number = len(arrays)

    def copy_all(*refs):
        sem = refs[-1]
        copies = [pltpu.make_async_copy(refs[i], refs[number + i], sem.at[i]) for i in range(number)]
        for copy in copies:
            copy.start()
        for copy in copies:
            copy.wait()

    return pl.pallas_call(
        copy_all,
        out_shape=[jax.ShapeDtypeStruct(a.shape, a.dtype) for a in arrays],
        in_specs=[pl.BlockSpec(memory_space=pltpu.VMEM)] * number,
        out_specs=[pl.BlockSpec(memory_space=pl.ANY)] * number,
        scratch_shapes=[pltpu.SemaphoreType.DMA((number,))],
        name="hand_over",
    )(*[pltpu.with_memory_space_constraint(a, pltpu.VMEM) for a in arrays])


def fused(n_rows, arrays):
    (images, valid_h, valid_w, kernel_one, kernel_two, kernel_skip, bias_one, bias_two,
     vector_one, vector_two, vector_skip, cotangent) = arrays
    micros, rows, width, ci = images.shape
    co = kernel_one.shape[3]
    per, pairs, half = micros // 2, rows // 2, width // 2
    op = 2 * TILE
    n_chips = n_rows // 2
    cin, cout = 2 * ci, 2 * co
    sub = min(4, n_chips)
    cubes = n_chips // sub
    unit = op * sub
    lanes_two = -(-max(5 * cout, 4 * cout + cin) // unit) * unit
    lanes_one = -(-(9 * cin + 10) // unit) * unit
    seg_out = rows // 2 + 1
    bits = 3 if n_rows % 8 == 0 else 2
    size1 = -(-(9 * cin) // 64) * 64
    size20 = -(-(9 * cout + cin) // 64) * 64
    share1 = -(-(3 * size1 // 4) // 64) * 16
    share2 = -(-(3 * size20 // 4) // (16 * 2**bits)) * 16
    inputs = {
        "vh": valid_h,
        "vw": valid_w,
        "img": jnp.transpose(images, (0, 1, 3, 2)),
        "k1": kernel_one.reshape(9 * cin, co),
        "k2": kernel_two.reshape(9 * cout, co),
        "k0": kernel_skip,
        "b1": bias_one.reshape(1, co),
        "b2": bias_two.reshape(1, co),
        "q1": vector_one.reshape(1, co),
        "q2": vector_two.reshape(1, co),
        "q0": vector_skip.reshape(1, co),
        "cot": cotangent,
    }
    outputs = {
        "out_b": jax.ShapeDtypeStruct(cotangent.shape, BF16),
        "out_g": jax.ShapeDtypeStruct((micros, rows, ci, width), BF16),
        "out_k1": jax.ShapeDtypeStruct((9 * cin, co), F32),
        "out_k2": jax.ShapeDtypeStruct((9 * cout, co), F32),
        "out_k0": jax.ShapeDtypeStruct((cin, co), F32),
        "out_b1": jax.ShapeDtypeStruct((1, co), F32),
        "out_b2": jax.ShapeDtypeStruct((1, co), F32),
    }
    vm = pltpu.VMEM
    scratch = {
        "vh_s": pltpu.SMEM(valid_h.shape, jnp.int32),
        "vw_s": pltpu.SMEM(valid_w.shape, jnp.int32),
        "b1_v": vm((1, co), BF16),
        "b2_v": vm((1, co), BF16),
        "q1_v": vm((1, co), F32),
        "q2_v": vm((1, co), F32),
        "q0_v": vm((1, co), F32),
        "img_v": vm((micros, rows, ci, width), BF16),
        "cot_v": vm(cotangent.shape, BF16),
        "k1_v": vm((size1, co), BF16),
        "k20_v": vm((size20, co), BF16),
        "k1p": vm((4 * share1, TILE), BF16),
        "k20p": vm((2**bits * share2, TILE), BF16),
        "k1h": vm((4 * share1, TILE), BF16),
        "k20h": vm((2**bits * share2, TILE), BF16),
        "cotp": vm((per, 3 * pairs * half // 4, TILE), BF16),
        "coth": vm((per, 3 * pairs * half // 4, TILE), BF16),
        "imgr": vm((per, 2, pairs + 2, ci, TILE), BF16),
        "sendp": vm((per, pairs, ci, TILE), BF16),
        "vec": vm((2, 8, TILE), F32),
        "cotr": vm((per, 2, 2, half, co), BF16),
        "eye": vm((op, op), BF16),
        "perm_in": vm((8 * half, TILE), BF16),
        "perm_x": vm((5 * half, TILE), BF16),
        "w1": vm((9 * TILE, op), BF16),
        "w2": vm((9 * op, op), BF16),
        "w0": vm((TILE, op), BF16),
        "left1": vm((8, 9 * TILE), F32),
        "left2": vm((8, 9 * op), F32),
        "left0": vm((8, TILE), F32),
        "b_in": vm((per, 2 * (rows // 2 + 3), half, 4 * TILE), BF16),
        "xp": vm((per, pairs + 2, 4 * half, TILE), BF16),
        "xb": vm((per, pairs + 2, half, TILE), BF16),
        "raw1": vm((per, 2, 2 * seg_out, half, op), F32),
        "grad1": vm((per, 2, 2 * seg_out, half, op), F32),
        "act1": vm((per, 2, 2 * seg_out, half, op), BF16),
        "cols": vm((per, 3, 2 * seg_out, half, op), F32),
        "box": vm((per, pairs, half, 9 * op), BF16),
        "quart": vm((per, pairs + 2, half, op), BF16),
        "acc0": vm((cout, TILE), F32),
        "sums0": vm((cout, TILE), BF16),
        "taps_sum": vm((3, 2, per, pairs + 2, half, op), F32),
        "g_pre": vm((per, 2, 2 * seg_out, half, op), BF16),
        "taps_in": vm((2, 2 * seg_out, half, 9 * TILE), F32),
        "skip_back": vm((pairs, half, TILE), F32),
        "send_b": vm((per, pairs, half, co), BF16),
        "got_b": vm((per, pairs, half, co), BF16),
        "send_g": vm((per, pairs, ci, TILE), BF16),
        "got_g": vm((per, pairs, ci, TILE), BF16),
    }
    for name, size in (("corr1", 9 * cin), ("corr2", 9 * cout), ("corr0", cin)):
        scratch[name] = vm((size, co), F32)
    for name, lanes_each in (("a", lanes_two), ("b", lanes_two), ("c", lanes_one)):
        share = lanes_each // sub
        scratch["wire" + name] = vm((2, co, lanes_each), BF16)
        scratch["got" + name] = vm((2, co // 2, lanes_each), BF16)
        scratch["shares" + name] = vm((2, sub, co // 2, share), BF16)
        scratch["landing" + name] = vm((2 * sub - 1, co // 2, share), BF16)
        scratch["mine" + name] = vm((co // 2, share), F32)
        scratch["mids" + name] = vm((cubes, co // 2, share), BF16)
        scratch["result" + name] = vm((sub, co, share), BF16)
    copies = 11 + 2 ** (bits - 1) + 7 * per + 3 * (1 + 2 * (2 * sub - 1) + cubes - 1)
    scratch["lsem"] = pltpu.SemaphoreType.DMA((12,))
    scratch["ssem"] = pltpu.SemaphoreType.DMA((copies,))
    scratch["rsem"] = pltpu.SemaphoreType.DMA((copies,))
    names = list(inputs) + list(outputs) + list(scratch)
    dims = (micros, rows, width, ci, co, lanes_one, lanes_two, bits, share1, share2)
    vmem = pl.BlockSpec(memory_space=pltpu.VMEM)
    hbm = pl.BlockSpec(memory_space=pltpu.HBM)
    results = pl.pallas_call(
        functools.partial(fused_kernel, names, n_rows, dims),
        out_shape=[pltpu.VMEM(a.shape, a.dtype) for a in outputs.values()],
        in_specs=[hbm] * len(inputs),
        out_specs=[vmem] * len(outputs),
        scratch_shapes=list(scratch.values()),
        compiler_params=pltpu.CompilerParams(
            collective_id=0, has_side_effects=True, vmem_limit_bytes=48 * 1024 * 1024
        ),
        name="down_block",
    )(*[pltpu.with_memory_space_constraint(a, pltpu.HBM) for a in inputs.values()])
    out_b, out_g, out_k1, out_k2, out_k0, out_b1, out_b2 = hand_over(results)
    return (
        out_b,
        jnp.transpose(out_g, (0, 1, 3, 2)),
        out_k1.reshape(3, 3, cin, co),
        out_k2.reshape(3, 3, cout, co),
        out_k0,
        out_b1.reshape(co),
        out_b2.reshape(co),
    )


def solution(mesh):
    in_specs = (
        P(None, "rows", None, "ch"),
        P(),
        P(),
        P(None, None, None, "ch"),
        P(None, None, None, "ch"),
        P(None, "ch"),
        P("ch"),
        P("ch"),
        P("ch"),
        P("ch"),
        P("ch"),
        P(None, "rows", None, "ch"),
    )
    out_specs = (
        P(None, "rows", None, "ch"),
        P(None, "rows", None, "ch"),
        P(None, None, None, "ch"),
        P(None, None, None, "ch"),
        P(None, "ch"),
        P("ch"),
        P("ch"),
    )

    def step(*arrays):
        if fits(mesh.shape["rows"], mesh.shape["ch"], arrays):
            return fused(mesh.shape["rows"], arrays)
        return shards(*arrays)

    return jax.shard_map(step, mesh=mesh, in_specs=in_specs, out_specs=out_specs, check_vma=False)
```

```python
import functools

import jax
import jax.numpy as jnp
from jax import lax
from jax.experimental import pallas as pl
from jax.experimental.pallas import tpu as pltpu
from jax.sharding import PartitionSpec as P

IMG = 64
SHIFT = 40


EPS = 1e-06
HIGH = lax.Precision.HIGHEST


def extended(cells, sides, width):
    for axis, dim in sides:
        count = lax.axis_size(axis)
        head = lax.slice_in_dim(cells, 0, width, axis=dim)
        tail = lax.slice_in_dim(cells, cells.shape[dim] - width, cells.shape[dim], axis=dim)
        cells = jnp.concatenate(
            [
                lax.ppermute(tail, axis, [(i, (i + 1) % count) for i in range(count)]),
                cells,
                lax.ppermute(head, axis, [((i + 1) % count, i) for i in range(count)]),
            ],
            axis=dim,
        )
    return cells


def conv_rows(rim, kernel, taps):
    slab_rows = taps.shape[1]
    result = None
    for row_tap in range(3):
        part = lax.conv_general_dilated(
            rim[None, row_tap : row_tap + slab_rows],
            kernel[row_tap : row_tap + 1],
            (1, 1),
            ((0, 0), (1, 1)),
            dimension_numbers=("NHWC", "HWIO", "NHWC"),
            preferred_element_type=jnp.float32,
        )
        part = part[0] * taps[row_tap][:, None, None]
        result = part if result is None else result + part
    return result


def flipped(kernel):
    return jnp.transpose(kernel[::-1, ::-1], (0, 1, 3, 2))


def kernel_taps(rim, grad, taps_low):
    slab_rows = grad.shape[0]
    width = grad.shape[1]
    padded = jnp.pad(rim, ((0, 0), (1, 1), (0, 0)))
    stacked = []
    for row_tap in range(3):
        kept_grad = grad * taps_low[row_tap][:, None, None]
        line = []
        for col_tap in range(3):
            window = padded[row_tap : row_tap + slab_rows, col_tap : col_tap + width]
            line.append(
                jnp.einsum("rci,rco->io", window, kept_grad, preferred_element_type=jnp.float32)
            )
        stacked.append(jnp.stack(line))
    return jnp.stack(stacked)


def silu_slope(value):
    gate = jax.nn.sigmoid(value)
    return gate + value * gate * (1.0 - gate)


def shards(
    images,
    valid_h,
    valid_w,
    kernel_one,
    kernel_two,
    kernel_skip,
    bias_one,
    bias_two,
    vector_one,
    vector_two,
    vector_skip,
    cotangent,
):
    micros, rows_dev, width, in_local = images.shape
    out_local = kernel_one.shape[3]
    count_images = valid_h.shape[1]
    total_rows = rows_dev * lax.axis_size("rows")
    slab_start = lax.axis_index("rows") * rows_dev
    rim_global = slab_start - 1 + jnp.arange(rows_dev + 2, dtype=jnp.int32)
    placed = jnp.mod(rim_global - SHIFT, total_rows)
    image_of = placed // IMG
    row_of = placed % IMG
    taps = jnp.stack(
        [image_of[tap : tap + rows_dev] == image_of[1 : rows_dev + 1] for tap in range(3)]
    ).astype(jnp.float32)
    taps_low = taps.astype(jnp.bfloat16)
    owner = image_of[:, None] == jnp.arange(count_images, dtype=jnp.int32)[None, :]
    columns = jnp.arange(width)
    kern_one = kernel_one.astype(jnp.float32)
    kern_two = kernel_two.astype(jnp.float32)
    kern_skip = kernel_skip.astype(jnp.float32).reshape(1, 1, -1, out_local)
    part_one = jnp.einsum("hwio,o->hwi", kern_one, vector_one, precision=HIGH)
    part_two = jnp.einsum("hwio,o->hwi", kern_two, vector_two, precision=HIGH)
    part_skip = jnp.einsum("hwio,o->hwi", kern_skip, vector_skip, precision=HIGH)
    left_one, left_two, left_skip = lax.psum((part_one, part_two, part_skip), "ch")
    left_one = left_one * lax.rsqrt(jnp.sum(left_one * left_one) + EPS)
    left_two = left_two * lax.rsqrt(jnp.sum(left_two * left_two) + EPS)
    left_skip = left_skip * lax.rsqrt(jnp.sum(left_skip * left_skip) + EPS)
    image_one = jnp.einsum("hwio,hwi->o", kern_one, left_one, precision=HIGH)
    image_two = jnp.einsum("hwio,hwi->o", kern_two, left_two, precision=HIGH)
    image_skip = jnp.einsum("hwio,hwi->o", kern_skip, left_skip, precision=HIGH)
    square_one, square_two, square_skip = lax.psum(
        (
            jnp.sum(image_one * image_one),
            jnp.sum(image_two * image_two),
            jnp.sum(image_skip * image_skip),
        ),
        "ch",
    )
    scale_one = lax.rsqrt(square_one + EPS)
    scale_two = lax.rsqrt(square_two + EPS)
    scale_skip = lax.rsqrt(square_skip + EPS)
    right_one = image_one * scale_one
    right_two = image_two * scale_two
    right_skip = image_skip * scale_skip
    sigma_one = square_one * scale_one
    sigma_two = square_two * scale_two
    sigma_skip = square_skip * scale_skip
    eff_one = (kern_one / sigma_one).astype(jnp.bfloat16)
    eff_two = (kern_two / sigma_two).astype(jnp.bfloat16)
    eff_skip_full = (kern_skip / sigma_skip).astype(jnp.bfloat16)
    eff_skip = eff_skip_full[0, 0]
    bias_first = bias_one.astype(jnp.float32)
    bias_second = bias_two.astype(jnp.float32)
    back_two = flipped(eff_two)
    back_one = flipped(eff_one)
    outputs = []
    in_grads = []
    totals = None
    for micro in range(micros):
        height_rows = jnp.sum(jnp.where(owner, valid_h[micro][None, :], 0), axis=1)
        width_rows = jnp.sum(jnp.where(owner, valid_w[micro][None, :], 0), axis=1)
        mask_rim = (
            (row_of < height_rows)[:, None] & (columns[None, :] < width_rows[:, None])
        ).astype(jnp.float32)[:, :, None]
        mask_in = mask_rim[1:-1]
        input_rim = extended(images[micro], (("rows", 0),), 1)
        gathered = lax.all_gather(input_rim, "ch", axis=2, tiled=True)
        masked_rim = gathered * mask_rim.astype(jnp.bfloat16)
        act_in = jax.nn.silu(masked_rim.astype(jnp.float32)).astype(jnp.bfloat16)
        pre_one = conv_rows(act_in, eff_one, taps) + bias_first
        act_one = (jax.nn.silu(pre_one) * mask_in).astype(jnp.bfloat16)
        hidden_rim = extended(act_one, (("rows", 0),), 1)
        hidden_all = lax.all_gather(hidden_rim, "ch", axis=2, tiled=True)
        skip_in = masked_rim[1:-1]
        total = conv_rows(hidden_all, eff_two, taps) + bias_second
        total = total + jnp.einsum(
            "rci,io->rco", skip_in, eff_skip, preferred_element_type=jnp.float32
        )
        pooled = jnp.mean(total.reshape(rows_dev // 2, 2, width // 2, 2, out_local), axis=(1, 3))
        outputs.append(pooled.astype(jnp.bfloat16))
        quarter = cotangent[micro] * 0.25
        grad_total = jnp.broadcast_to(
            quarter[:, None, :, None, :], (rows_dev // 2, 2, width // 2, 2, out_local)
        ).reshape(rows_dev, width, out_local)
        grad_rim = extended(grad_total, (("rows", 0),), 1)
        partial_hidden = conv_rows(grad_rim, back_two, taps)
        grad_act_one = lax.psum_scatter(partial_hidden, "ch", scatter_dimension=2, tiled=True)
        grad_pre_one = (grad_act_one * mask_in * silu_slope(pre_one)).astype(jnp.bfloat16)
        pre_rim = extended(grad_pre_one, (("rows", 0),), 1)
        partial_act = conv_rows(pre_rim, back_one, taps)
        partial_skip = jnp.einsum(
            "rco,io->rci", grad_total, eff_skip, preferred_element_type=jnp.float32
        )
        grad_act_in, grad_skip_in = (
            lax.psum_scatter(partial_act, "ch", scatter_dimension=2, tiled=True),
            lax.psum_scatter(partial_skip, "ch", scatter_dimension=2, tiled=True),
        )
        own_input = images[micro].astype(jnp.float32)
        in_grads.append(
            (mask_in * (silu_slope(own_input) * grad_act_in + grad_skip_in)).astype(jnp.bfloat16)
        )
        grad_one = kernel_taps(act_in, grad_pre_one, taps_low)
        grad_two = kernel_taps(hidden_all, grad_total, taps_low)
        grad_skip = jnp.einsum(
            "rci,rco->io", skip_in, grad_total, preferred_element_type=jnp.float32
        )
        grad_first = jnp.sum(grad_pre_one.astype(jnp.float32), axis=(0, 1))
        grad_second = jnp.sum(grad_total.astype(jnp.float32), axis=(0, 1))
        current = (grad_one, grad_two, grad_skip, grad_first, grad_second)
        if totals is None:
            totals = current
        else:
            totals = tuple((acc + new for acc, new in zip(totals, current)))
    summed = lax.psum((totals[0], totals[1], totals[2], totals[3], totals[4]), "rows")
    sum_one, sum_two, sum_skip, sum_first, sum_second = summed
    sum_skip = sum_skip.reshape(1, 1, -1, out_local)
    dot_one, dot_two, dot_skip = lax.psum(
        (jnp.sum(sum_one * kern_one), jnp.sum(sum_two * kern_two), jnp.sum(sum_skip * kern_skip)),
        "ch",
    )
    final_one = (
        sum_one / sigma_one - dot_one / (sigma_one * sigma_one) * left_one[..., None] * right_one
    )
    final_two = (
        sum_two / sigma_two - dot_two / (sigma_two * sigma_two) * left_two[..., None] * right_two
    )
    final_skip = (
        sum_skip / sigma_skip
        - dot_skip / (sigma_skip * sigma_skip) * left_skip[..., None] * right_skip
    )
    return (
        jnp.stack(outputs),
        jnp.stack(in_grads),
        final_one,
        final_two,
        final_skip[0, 0],
        sum_first,
        sum_second,
    )


F32 = jnp.float32
BF16 = jnp.bfloat16
MESH = pl.DeviceIdType.MESH
TILE = 128
NT = (((1,), (1,)), ((), ()))
TN = (((0,), (0,)), ((), ()))
NN = (((1,), (0,)), ((), ()))


def fits(n_rows, n_ch, arrays):
    images, kernel_one = arrays[0], arrays[3]
    micros, rows_dev, width, in_local = images.shape
    out_local = kernel_one.shape[3]
    return (
        n_ch == 2
        and micros % 2 == 0
        and n_rows >= 4
        and n_rows % min(8, n_rows) == 0
        and n_rows % 4 == 0
        and rows_dev % 8 == 0
        and SHIFT % rows_dev == rows_dev // 2
        and IMG % rows_dev == 0
        and 2 * width == TILE
        and in_local % 16 == 0
        and 2 * in_local < TILE
        and out_local == 3 * TILE // 4
    )


def dot(left, right, dims=NN):
    return lax.dot_general(left, right, dims, preferred_element_type=F32)


def iota(shape, dim):
    return lax.broadcasted_iota(jnp.int32, shape, dim)


def pieces(row):
    first = row.astype(BF16).astype(F32)
    rest = row - first
    second = rest.astype(BF16).astype(F32)
    third = rest - second
    at = iota((16, row.shape[1]), 0)
    zero = jnp.zeros((16, row.shape[1]), F32)
    stacked = jnp.where(at == 0, first, jnp.where(at == 1, second, jnp.where(at == 2, third, zero)))
    return stacked.astype(BF16)


def total(value):
    return jnp.sum(jnp.sum(value, axis=0, keepdims=True), axis=1, keepdims=True)


def power(vector_row, kernel):
    left = jnp.sum(dot(pieces(vector_row), kernel, NT), axis=0, keepdims=True)
    left = left * lax.rsqrt(total(left * left) + EPS)
    image = jnp.sum(dot(pieces(left), kernel), axis=0, keepdims=True)
    square = total(image * image)
    scale = lax.rsqrt(square + EPS)
    return left, image * scale, square * scale


def sigmoid(value):
    return 0.5 * jnp.tanh(0.5 * value) + 0.5


def slope(value):
    gate = sigmoid(value)
    return gate + value * gate * (1.0 - gate)


def fused_kernel(names, n_rows, dims, *refs):
    micros, rows, width, ci, co, lanes_one, lanes_two, bits, share1, share2 = dims
    ref = dict(zip(names, refs))
    half = width // 2
    per = micros // 2
    pairs = rows // 2
    cut = rows // 2
    seg_slots = cut + 3
    seg_out = cut + 1
    pairs_a = cut // 2 + 1
    n_chips = n_rows // 2
    cin, cout = 2 * ci, 2 * co
    op = 2 * TILE
    total_rows = rows * n_rows
    own_px = pairs * half
    all_px = (pairs + 2) * half

    ssem, rsem, lsem = ref["ssem"], ref["rsem"], ref["lsem"]
    me = lax.axis_index("rows")
    c = lax.axis_index("ch")
    o = 1 - c
    core = lax.rem(me, 2)
    mate = me + 1 - 2 * core
    chip = me // 2
    up = lax.rem(me + n_rows - 1, n_rows)
    down = lax.rem(me + 1, n_rows)
    my_id = c * n_chips + chip
    sub = min(4, n_chips)
    cubes = n_chips // sub
    spot_in, cube = lax.rem(chip, sub), chip // sub
    my_id = c * sub + spot_in
    far = []
    for delta in range(1, 2 * sub):
        other = lax.rem(my_id + delta, 2 * sub)
        far.append((2 * (cube * sub + lax.rem(other, sub)) + core, other // sub))
    across = []
    for delta in range(1, cubes):
        across.append((2 * (lax.rem(cube + delta, cubes) * sub + spot_in) + core, c))
    around = []
    for delta in range(1, 2 * sub):
        other = lax.rem(2 * spot_in + core + delta, 2 * sub)
        around.append((2 * cube * sub + other, c))
    near = [(me, o), (mate, c), (up, c), (up, o), (down, c), (down, o)]

    barrier = pltpu.get_barrier_semaphore()
    for device in near + far + across + around:
        pl.semaphore_signal(barrier, inc=1, device_id=device, device_id_type=MESH)

    count = [0]
    sends = []

    def remote(src, dst, device):
        at = count[0]
        count[0] += 1
        return pltpu.make_async_remote_copy(
            src_ref=src,
            dst_ref=dst,
            send_sem=ssem.at[at],
            recv_sem=rsem.at[at],
            device_id=device,
            device_id_type=MESH,
        )

    def begin(*args):
        copy = remote(*args)
        copy.start()
        sends.append(copy)
        return copy

    img, cot, k1, k20 = ref["img_v"], ref["cot_v"], ref["k1_v"], ref["k20_v"]
    n1, n2 = 9 * cin, 9 * cout
    loads = []
    for i, (src, dst) in enumerate(
        [
            (ref["img"], img),
            (ref["k1"], k1.at[0:n1]),
            (ref["k0"], k20.at[n2 : n2 + cin]),
            (ref["k2"], k20.at[0:n2]),
            (ref["cot"], cot),
            (ref["vh"], ref["vh_s"]),
            (ref["vw"], ref["vw_s"]),
            (ref["b1"], ref["b1_v"]),
            (ref["b2"], ref["b2_v"]),
            (ref["q1"], ref["q1_v"]),
            (ref["q2"], ref["q2_v"]),
            (ref["q0"], ref["q0_v"]),
        ]
    ):
        load = pltpu.make_async_copy(src, dst, lsem.at[i])
        load.start()
        loads.append(load)

    perm_in, perm_x = ref["perm_in"], ref["perm_x"]
    shape = (8 * half, TILE)
    at, lane = iota(shape, 0), iota(shape, 1)
    column = 2 * lax.rem(at, half) + lax.rem(at // half, 4) - 1
    hit = (lane - at // (4 * half) * width == column) & (column >= 0) & (column < width)
    perm_in[...] = jnp.where(hit, 1.0, 0.0).astype(BF16)
    shape = (4 * half, TILE)
    at, lane = iota(shape, 0), iota(shape, 1)
    source = at // (2 * half) * width + 2 * lax.rem(at, half) + lax.rem(at // half, 2)
    perm_x[0 : 4 * half] = jnp.where(lane == source, 1.0, 0.0).astype(BF16)
    shape = (half, TILE)
    at, lane = iota(shape, 0), iota(shape, 1)
    perm_x[4 * half : 5 * half] = jnp.where(lax.rem(lane, width) // 2 == at, 1.0, 0.0).astype(BF16)

    eye = ref["eye"]
    shape = (op, op)
    eye[...] = jnp.where(iota(shape, 0) == iota(shape, 1), 1.0, 0.0).astype(BF16)

    def rem_pos(value, by):
        return lax.rem(lax.rem(value, by) + by, by)

    first_a = rem_pos(me * rows - SHIFT, total_rows)
    first_b = rem_pos(me * rows + cut - SHIFT, total_rows)
    base = [lax.rem(first_a, IMG), lax.rem(first_b, IMG) - cut]
    image_a, image_b = first_a // IMG, first_b // IMG
    keep = jnp.where(base[1] < 0, 0.0, 1.0).astype(F32)
    def choose(seg, two):
        return jnp.where(seg == 0, two[0], two[1])

    imgr, sendp = ref["imgr"], ref["sendp"]
    loads[0].wait()
    for j in range(per):
        for mine in (False, True):

            def pack(p, carry, j=j, mine=mine):
                m = (c if mine else o) * per + j
                pair = jnp.concatenate([img[m, 2 * p], img[m, 2 * p + 1]], axis=1)
                if mine:
                    imgr[j, c, p + 1] = pair
                else:
                    sendp[j, p] = pair
                return carry

            lax.fori_loop(0, pairs, pack, 0, unroll=4)
    for load in loads[1:]:
        load.wait()
    vh, vw = ref["vh_s"], ref["vw_s"]
    high = [[vh[c * per + j, image] for image in (image_a, image_b)] for j in range(per)]
    wide = [[vw[c * per + j, image] for image in (image_a, image_b)] for j in range(per)]

    vec = ref["vec"]
    vec[c] = jnp.zeros(vec.shape[1:], F32)
    for i, name in enumerate(("q1", "q2", "q0", "b1", "b2")):
        vec[c, i : i + 1, 0:co] = ref[name + "_v"][...].astype(F32)

    def packed(value):
        kept, strip = 3 * value.shape[-2] // 4, co // 3
        last = value[kept:]
        beside = jnp.concatenate([last[:, k * strip : (k + 1) * strip] for k in range(3)], axis=0)
        return jnp.concatenate([value[:kept], beside], axis=1)

    def unpacked(value):
        part = value.shape[0] // 3
        last = jnp.concatenate([value[k * part : (k + 1) * part, co:] for k in range(3)], axis=1)
        return jnp.concatenate([value[:, :co], last], axis=0)

    k1p, k20p, cotp = ref["k1p"], ref["k20p"], ref["cotp"]
    size1, size20 = 3 * k1.shape[0] // 4, 3 * k20.shape[0] // 4
    k1p[0:size1] = packed(k1[...])
    k20p[0:size20] = packed(k20[...])
    for j in range(per):
        cotp[j] = packed(cot[o * per + j].reshape(own_px, co))

    pl.semaphore_wait(barrier, len(near + far + across + around))

    k1h, k20h, coth, cotr = ref["k1h"], ref["k20h"], ref["coth"], ref["cotr"]
    spots = [core] + [lax.rem(me // 2**b, 2) for b in range(1, bits)]

    def part_of(rows_each, depth, bits_at):
        first = 0
        for b in range(depth):
            first = first * 2 + bits_at[b]
        return pl.ds(first * rows_each, rows_each)

    class Shared:
        def __init__(self, own, got, rows_each, depth):
            self.got, self.rows_each, self.depth, self.level = got, rows_each, depth, 0
            at = part_of(rows_each, depth, spots)
            self.copies = [begin(own.at[at], got.at[at], (me, o))]

        def turn(self):
            for copy in self.copies:
                copy.wait_recv()
            self.copies = []
            if self.level == 0:
                at = self.got.at[part_of(self.rows_each, self.depth, spots)]
                for mask in range(1, 2 ** (self.depth - 1)):
                    other = me
                    for b in range(1, self.depth):
                        if mask >> (b - 1) & 1:
                            other = other + 2**b * (1 - 2 * spots[b])
                    self.copies.append(begin(at, at, (other, c)))
            if self.level == 1:
                size = 2 ** (self.depth - 1) * self.rows_each
                at = self.got.at[pl.ds(core * size, size)]
                self.copies.append(begin(at, at, (mate, c)))
            self.level += 1

    mine_c, mine_o = pl.ds(c * per, per), pl.ds(o * per, per)
    img_x, img_halo = [], []

    def send_image(j):
        img_x.append(begin(sendp.at[j], imgr.at[j, c, pl.ds(1, pairs)], (me, o)))
        img_halo.append(
            [
                begin(sendp.at[j, 0], imgr.at[j, c, pairs + 1], (up, o)),
                begin(sendp.at[j, pairs - 1], imgr.at[j, c, 0], (down, o)),
                begin(imgr.at[j, c, 1], imgr.at[j, c, pairs + 1], (up, c)),
                begin(imgr.at[j, c, pairs], imgr.at[j, c, 0], (down, c)),
            ]
        )

    vec_x = begin(vec.at[c], vec.at[c], (me, o))
    one = Shared(k1p, k1h, share1, 2)
    two = Shared(k20p, k20h, share2, bits)
    for j in range(per):
        send_image(j)
    cot_x = [begin(cotp.at[j], coth.at[j], (me, o)) for j in range(per)]
    cot_halo = [
        begin(cot.at[mine_o, 0], cotr.at[:, c, 1], (up, o)),
        begin(cot.at[mine_o, pairs - 1], cotr.at[:, c, 0], (down, o)),
        begin(cot.at[mine_c, 0], cotr.at[:, c, 1], (up, c)),
        begin(cot.at[mine_c, pairs - 1], cotr.at[:, c, 0], (down, c)),
    ]

    w1, w2, w0 = ref["w1"], ref["w2"], ref["w0"]

    def place(dst, row, own_part, other_part, padded):
        size = own_part.shape[0]
        first = jnp.where(c == 0, own_part, other_part)
        second = jnp.where(c == 0, other_part, own_part)
        line = jnp.concatenate([first, second, jnp.zeros((size, op - cout), BF16)], axis=1)
        dst[pl.ds(row, size), :] = line
        if padded > size:
            dst[pl.ds(row + size, padded - size), :] = jnp.zeros((padded - size, op), BF16)

    def row_of(i):
        return jnp.concatenate(
            [vec[0, i : i + 1, 0:co], vec[1, i : i + 1, 0:co], jnp.zeros((1, op - cout), F32)], axis=1
        )

    b_in, xp, xb = ref["b_in"], ref["xp"], ref["xb"]
    ones = jnp.where(iota((TILE - cin, TILE), 0) == 0, 1.0, 0.0).astype(BF16)

    def prepare(j):
        img_x[j].wait_recv()
        for copy in img_halo[j]:
            copy.wait_recv()

        def two_pairs(step, carry):
            lane = iota((1, TILE), 1)
            column = lax.rem(lane, width)
            acts, plain, slots = [], [], []
            for k in range(2):
                p = 2 * step + k
                seg = (p >= pairs_a).astype(jnp.int32)
                row = 2 * p - 2 + lane // width
                mask = jnp.where(
                    (choose(seg, base) + row < choose(seg, high[j])) & (column < choose(seg, wide[j])), 1.0, 0.0
                )
                x = jnp.concatenate([imgr[j, 0, p], imgr[j, 1, p]], axis=0).astype(F32) * mask
                act = x * sigmoid(x)
                acts += [act.astype(BF16), ones]
                plain += [x.astype(BF16), ones]
                slots.append(2 * p + 2 * seg)
            spread = dot(perm_in[...], jnp.concatenate(acts, axis=0), NT).astype(BF16)
            for k in range(2):
                for a in range(2):
                    for t in range(4):
                        b_in[j, slots[k] + a, :, t * TILE : (t + 1) * TILE] = spread[
                            (4 * a + t) * half : (4 * a + t + 1) * half, k * TILE : (k + 1) * TILE
                        ]
            spread = dot(perm_x[...], jnp.concatenate(plain, axis=0), NT).astype(BF16)
            for k in range(2):
                part = spread[:, k * TILE : (k + 1) * TILE]
                xp[j, 2 * step + k] = part[0 : 4 * half]
                xb[j, 2 * step + k] = part[4 * half : 5 * half]
            return carry

        lax.fori_loop(0, (pairs + 2) // 2, two_pairs, 0, unroll=True)
        b_in[j, seg_slots - 1] = (b_in[j, seg_slots + 1].astype(F32) * keep).astype(BF16)
        b_in[j, seg_slots] = (b_in[j, seg_slots - 2].astype(F32) * keep).astype(BF16)

    raw1, grad1, act1 = ref["raw1"], ref["grad1"], ref["act1"]

    def conv_one(j):
        parts = []
        for seg in range(2):
            for b in range(2):
                first = seg * seg_slots
                taps = [
                    b_in[j, first + u : first + u + seg_out, :, b * TILE : (b + 3) * TILE].reshape(
                        seg_out * half, 3 * TILE
                    )
                    for u in range(3)
                ]
                parts.append(jnp.concatenate(taps, axis=1))
        result = dot(jnp.concatenate(parts, axis=0), w1[...]).reshape(2, 2, seg_out, half, op)
        for seg in range(2):
            for b in range(2):
                raw1[j, b, seg * seg_out : (seg + 1) * seg_out] = result[seg, b]

    cols = ref["cols"]
    pixel = iota((half, op), 0)

    def activate(j):
        def line(i, carry):
            seg = (i >= seg_out).astype(jnp.int32)
            broad = jnp.where(choose(seg, base) + i - 1 < choose(seg, high[j]), choose(seg, wide[j]), 0)
            acts = []
            for b in range(2):
                pre = raw1[j, b, i] * scale1 + bias1
                gate = sigmoid(pre)
                mask = 2 * pixel + b < broad
                lift = pre * gate
                grad1[j, b, i] = jnp.where(mask, gate + lift * (1.0 - gate), 0.0)
                act = jnp.where(mask, lift, 0.0).astype(BF16)
                act1[j, b, i] = act
                acts.append(act.astype(F32))
            even, odd = acts
            before = jnp.where(pixel == 0, 0.0, pltpu.roll(odd, 1, 0))
            after = jnp.where(pixel == half - 1, 0.0, pltpu.roll(even, half - 1, 0))
            cols[j, 0, i] = before + even
            cols[j, 1, i] = even + odd
            cols[j, 2, i] = odd + after
            return carry

        lax.fori_loop(0, 2 * seg_out, line, 0, unroll=True)

    box = ref["box"]

    def boxes(j):
        def line(i, carry):
            above = jnp.where(i == cut // 2, keep, 1.0)
            below = jnp.where(i == cut // 2 - 1, keep, 1.0)
            for w in range(3):
                lines = [cols[j, w, 2 * i + k] for k in range(4)]
                for u in range(3):
                    upper, lower = lines[u], lines[u + 1]
                    if u == 0:
                        upper = upper * above
                    if u == 2:
                        lower = lower * below
                    tap = 3 * u + w
                    box[j, i, :, tap * op : (tap + 1) * op] = (upper + lower).astype(BF16)
            return carry

        lax.fori_loop(0, pairs, line, 0, unroll=True)

    quart = ref["quart"]

    def quarter(j):
        def put(i, own, other):
            first = jnp.where(c == 0, own, other)
            second = jnp.where(c == 0, other, own)
            size = first.shape[0]
            line = jnp.concatenate([first, second, jnp.zeros((size, op - cout), BF16)], axis=1)
            line = (line.astype(F32) * 0.25).astype(BF16)
            quart[j, pl.ds(i, size // half)] = line.reshape(size // half, half, op)

        put(1, cot[c * per + j].reshape(own_px, co), unpacked(coth[j]))
        for i in (0, 1):
            put(i * (pairs + 1), cotr[j, c, i], cotr[j, o, i])

    def owned(j):
        return quart[j, 1 : pairs + 1].reshape(own_px, op)

    half_rows = co // 2
    kept_rows = pl.ds(core * half_rows, half_rows)
    mate_rows = pl.ds((1 - core) * half_rows, half_rows)

    class Summed:
        def __init__(self, name):
            self.wire, self.got, self.shares, self.landing, self.mine, self.mids, self.result = [
                ref[part + name] for part in ("wire", "got", "shares", "landing", "mine", "mids", "result")
            ]
            self.share = self.result.shape[2]
            self.copies = [begin(self.wire.at[:, mate_rows], self.got, (mate, c))]

        def arrived(self):
            for copy in self.copies:
                copy.wait_recv()

        def to_owners(self):
            self.arrived()
            for ch in range(2):
                value = self.wire[ch, kept_rows].astype(F32) + self.got[ch].astype(F32)
                for at in range(sub):
                    self.shares[ch, at] = value[:, at * self.share : (at + 1) * self.share].astype(BF16)
            lanes = pl.ds(pl.multiple_of(spot_in * self.share, TILE), self.share)
            self.mine[...] = self.wire[c, kept_rows, lanes].astype(F32) + self.got[c, :, lanes].astype(F32)
            self.copies = []
            for delta in range(1, 2 * sub):
                other = lax.rem(my_id + delta, 2 * sub)
                self.copies.append(
                    begin(
                        self.shares.at[other // sub, lax.rem(other, sub)], self.landing.at[delta - 1], far[delta - 1]
                    )
                )

        def to_cubes(self):
            self.arrived()
            value = self.mine[...]
            for delta in range(1, 2 * sub):
                value = value + self.landing[delta - 1].astype(F32)
            self.mids[cube] = value.astype(BF16)
            self.copies = [begin(self.mids.at[cube], self.mids.at[cube], device) for device in across]

        def to_all(self):
            self.arrived()
            value = self.mids[0].astype(F32)
            for at in range(1, cubes):
                value = value + self.mids[at].astype(F32)
            self.result[spot_in, kept_rows] = value.astype(BF16)
            place_at = self.result.at[spot_in, kept_rows]
            self.copies = [begin(place_at, place_at, device) for device in around]

        def turned(self, scale, out, first, size):
            self.arrived()
            for at in range(0, sub * self.share, op):
                piece, lanes = at // self.share, at % self.share
                value = dot(eye[...], self.result[piece, :, lanes : lanes + op], NT)
                some = min(op, size - at)
                if some > 0:
                    out[first + at : first + at + some] = value[0:some] * scale
                if some < op:
                    return value[some:]

    one.turn()
    two.turn()
    one.turn()
    prepare(0)
    one.turn()
    vec_x.wait_recv()
    k1o = unpacked(k1h[0:size1])
    for tap in range(9):
        rows_at = slice(tap * cin, (tap + 1) * cin)
        place(w1, tap * TILE, k1[rows_at], k1o[rows_at], TILE)
    left1, right1, sigma1 = power(row_of(0), w1[...])
    scale1 = 1.0 / sigma1
    bias1, bias2 = row_of(3), row_of(4)
    left1_ref, left2_ref, left0_ref = ref["left1"], ref["left2"], ref["left0"]
    left1_ref[0:1] = left1
    conv_one(0)
    activate(0)
    two.turn()
    boxes(0)
    for j in range(1, per):
        prepare(j)
        conv_one(j)
        activate(j)
        boxes(j)
    for copy in cot_x:
        copy.wait_recv()
    for copy in cot_halo:
        copy.wait_recv()
    for j in range(per):
        quarter(j)

    acc0 = ref["acc0"]
    given = jnp.concatenate([owned(j) for j in range(per)], axis=0)[:, 0:cout]
    turned_quart = jnp.transpose(given)
    sums0 = ref["sums0"]
    group_a = None
    for name, taps in (("a", range(0, 5)), ("b", range(5, 9))):
        lanes = slice(taps[0] * op, (taps[-1] + 1) * op)
        value = dot(turned_quart, box[:, :, :, lanes].reshape(per * own_px, len(taps) * op))
        parts = [value[:, k * op : k * op + cout] for k in range(len(taps))]
        if name == "b":
            skip = dot(turned_quart, xb[:, 1 : pairs + 1].reshape(per * own_px, TILE))
            acc0[...] = skip
            sums0[...] = skip.astype(BF16)
            parts.append(skip[:, 0:cin])
        parts.append(jnp.zeros((cout, lanes_two - sum(part.shape[1] for part in parts)), F32))
        flat = jnp.concatenate(parts, axis=1).astype(BF16)
        for ch in range(2):
            ref["wire" + name][ch] = flat[ch * co : (ch + 1) * co]
        if name == "a":
            group_a = Summed("a")
    group_b = Summed("b")
    two.turn()
    k20o = unpacked(k20h[0:size20])
    for tap in range(9):
        rows_at = slice(tap * cout, (tap + 1) * cout)
        place(w2, tap * op, k20[rows_at], k20o[rows_at], op)
    rows_at = slice(n2, n2 + cin)
    place(w0, 0, k20[rows_at], k20o[rows_at], TILE)
    left2, right2, sigma2 = power(row_of(1), w2[...])
    left0, right0, sigma0 = power(row_of(2), w0[...])
    scale2, scale0 = 1.0 / sigma2, 1.0 / sigma0
    left0_ref[0:1] = left0
    left2_ref[0:1] = left2

    taps_sum = ref["taps_sum"]
    spot = iota((per * all_px, op), 0)
    at_left = lax.rem(spot, half) == 0
    at_right = lax.rem(spot, half) == half - 1
    g_pre = ref["g_pre"]

    def back_taps():
        given = quart[...].reshape(per * all_px, op)
        for u in range(3):
            t0, t1, t2 = [
                dot(given, w2[(3 * u + w) * op : (3 * u + w + 1) * op], NT) for w in range(3)
            ]
            even = t0 + t1 + jnp.where(at_left, 0.0, pltpu.roll(t2, 1, 0))
            odd = t1 + t2 + jnp.where(at_right, 0.0, pltpu.roll(t0, per * all_px - 1, 0))
            taps_sum[u, 0] = even.reshape(per, pairs + 2, half, op)
            taps_sum[u, 1] = odd.reshape(per, pairs + 2, half, op)

    def back_two(j, dots):
        def line(i, carry):
            hold = jnp.where(i == cut // 2, keep, 1.0)
            own_even = jnp.where(i < pairs, 1.0, 0.0)
            own_odd = jnp.where(i > 0, 1.0, 0.0)
            one, two = carry
            for b in range(2):
                upper, lower = taps_sum[2, b, j, i], taps_sum[0, b, j, i + 1]
                even = lower + taps_sum[1, b, j, i + 1] + hold * upper
                odd = taps_sum[1, b, j, i] + upper + hold * lower
                two = two + own_even * even * act1[j, b, 2 * i + 1].astype(F32)
                two = two + own_odd * odd * act1[j, b, 2 * i].astype(F32)
                even = (even * scale2 * grad1[j, b, 2 * i + 1]).astype(BF16)
                odd = (odd * scale2 * grad1[j, b, 2 * i]).astype(BF16)
                g_pre[j, b, 2 * i + 1] = even
                g_pre[j, b, 2 * i] = odd
                one = one + own_even * even.astype(F32) * raw1[j, b, 2 * i + 1]
                one = one + own_odd * odd.astype(F32) * raw1[j, b, 2 * i]
            return one, two

        return lax.fori_loop(0, pairs + 1, line, dots, unroll=True)

    back_taps()
    group_a.to_owners()
    dots = (jnp.zeros((half, op), F32), jnp.zeros((half, op), F32))
    dots = back_two(0, dots)
    group_b.to_owners()
    for j in range(1, per):
        dots = back_two(j, dots)
    dot1, dot2 = dots

    turned_grad = []
    for b in range(2):
        lines = [g_pre[j, b, 1 : rows + 1].reshape(rows * half, op) for j in range(per)]
        turned_grad.append(jnp.concatenate(lines, axis=0)[:, 0:cout])

    def kernel_one_grad(taps):
        value = None
        for b in range(2):
            lines = []
            for j in range(per):
                for seg in range(2):
                    first = seg * (cut + 2) + 1
                    blocks = []
                    for u in range(3):
                        cols_at = [w for w in range(3) if 3 * u + w in taps]
                        if cols_at:
                            block = b_in[
                                j,
                                first + u : first + u + cut,
                                :,
                                (b + cols_at[0]) * TILE : (b + cols_at[-1] + 1) * TILE,
                            ]
                            blocks.append(block.reshape(cut * half, len(cols_at) * TILE))
                    lines.append(jnp.concatenate(blocks, axis=1))
            part = dot(turned_grad[b], jnp.concatenate(lines, axis=0), TN)
            value = part if value is None else value + part
        return value

    def pair_of(column):
        high_part = column.astype(BF16).astype(F32)
        return [high_part, column - high_part]

    def trace_of(partial, kernel):
        product = dot(partial, kernel)
        eye = iota(product.shape, 0) == iota(product.shape, 1)
        return total(jnp.where(eye, product, 0.0))

    def send_one(name, taps, extras):
        value = kernel_one_grad(taps)
        parts = [value[:, k * TILE : k * TILE + cin] for k in range(len(taps))]
        rest = extras(value)
        spare = lanes_one - len(taps) * cin - len(rest)
        parts.append(jnp.concatenate(rest + [jnp.zeros((cout, spare), F32)], axis=1))
        flat = jnp.concatenate(parts, axis=1).astype(BF16)
        for ch in range(2):
            ref["wire" + name][ch] = flat[ch * co : (ch + 1) * co]
        return Summed(name)

    def extras_c(value):
        at = 4 * TILE + cin
        return pair_of(value[:, at : at + 1]) + pair_of(acc0[:, cin : cin + 1])

    def extras_d(value):
        sums_at = [total(dot1), total(dot2), trace_of(sums0[...], w0[...])]
        return [part for at in sums_at for part in pair_of(jnp.broadcast_to(at, (cout, 1)))]

    group_c = send_one("c", range(0, 9), lambda value: extras_c(value) + extras_d(value))

    out_b, send_b, got_b = ref["out_b"], ref["send_b"], ref["got_b"]

    def conv_two(j):
        main = dot(box[j].reshape(own_px, 9 * op), w2[...])
        skip = dot(xb[j, 1 : pairs + 1].reshape(own_px, TILE), w0[...])
        value = ((main * scale2 + skip * scale0) * 0.25 + bias2).astype(BF16)
        first, second = value[:, 0:co], value[:, co:cout]
        out_b[c * per + j] = jnp.where(c == 0, first, second).reshape(pairs, half, co)
        send_b[j] = jnp.where(c == 0, second, first).reshape(pairs, half, co)

    taps_in, skip_back = ref["taps_in"], ref["skip_back"]
    pixel_in = iota((half, TILE), 0)
    out_g, send_g, got_g = ref["out_g"], ref["send_g"], ref["got_g"]

    def back_products(j):
        skip_back[...] = (dot(owned(j), w0[...], NT) * scale0).reshape(pairs, half, TILE)

        given = g_pre[j].reshape(4 * seg_out * half, op)
        taps_in[...] = dot(given, w1[...], NT).reshape(2, 2 * seg_out, half, 9 * TILE)

    def input_rows(j):
        def two_rows(p, carry):
            lines = []
            for a in range(2):
                r = 2 * p + a
                hold_up = jnp.where(r == cut - 1, keep, 1.0)
                hold_down = jnp.where(r == cut, keep, 1.0)

                def column_sum(w, s):
                    def of(u, row):
                        at = (3 * u + w) * TILE
                        return taps_in[s, row, :, at : at + TILE]

                    return of(0, r + 2) * hold_up + of(1, r + 1) + of(2, r) * hold_down

                before = pltpu.roll(column_sum(2, 1), 1, 0)
                after = pltpu.roll(column_sum(0, 0), half - 1, 0)
                even = column_sum(0, 1) + column_sum(1, 0) + jnp.where(pixel_in == 0, 0.0, before)
                odd = column_sum(1, 1) + column_sum(2, 0) + jnp.where(pixel_in == half - 1, 0.0, after)
                seg = (r >= cut).astype(jnp.int32)
                broad = jnp.where(choose(seg, base) + r < choose(seg, high[j]), choose(seg, wide[j]), 0)
                for b, value in ((0, even), (1, odd)):
                    at = (2 * a + b) * half
                    x = xp[j, p + 1, at : at + half].astype(F32)
                    mask = 2 * pixel_in + b < broad
                    value = slope(x) * (value * scale1) + skip_back[p]
                    lines.append(jnp.where(mask, value, 0.0).astype(BF16))
            line = dot(jnp.concatenate(lines, axis=0), perm_x[0 : 4 * half], TN).astype(BF16)
            own = jnp.where(c == 0, line[0:ci], line[ci:cin])
            other = jnp.where(c == 0, line[ci:cin], line[0:ci])
            out_g[c * per + j, 2 * p] = own[:, 0:width]
            out_g[c * per + j, 2 * p + 1] = own[:, width:TILE]
            send_g[j, p] = other
            return carry

        lax.fori_loop(0, pairs, two_rows, 0, unroll=True)
        return begin(send_g.at[j], got_g.at[j], (me, o))

    def unpack(j):
        def line(p, carry):
            out_g[o * per + j, 2 * p] = got_g[j, p, :, 0:width]
            out_g[o * per + j, 2 * p + 1] = got_g[j, p, :, width:TILE]
            return carry

        grad_x[j].wait_recv()
        lax.fori_loop(0, pairs, line, 0, unroll=4)

    conv_two(0)
    for j in range(1, per):
        conv_two(j)
    group_c.to_owners()
    out_x = begin(send_b, got_b, (me, o))
    back_products(0)
    group_a.to_cubes()
    grad_x = [input_rows(0)]
    group_b.to_cubes()
    for j in range(1, per):
        back_products(j)
        if j == 1:
            group_c.to_cubes()
            group_a.to_all()
        grad_x.append(input_rows(j))

    def own_half(row):
        return jnp.where(c == 0, row[:, 0:co], row[:, co:cout])

    def column_of(row):
        row = jnp.concatenate([own_half(row), jnp.zeros((1, TILE - co), F32)], axis=1)
        return jnp.transpose(jnp.broadcast_to(row, (TILE, TILE)))[0:co]

    def compact(row, size, padded):
        return jnp.concatenate([row[:, t * padded : t * padded + size] for t in range(9)], axis=1)

    def turned(part, out, at):
        some = part.shape[1]
        if some < TILE:
            part = jnp.concatenate([part, jnp.zeros((co, TILE - some), F32)], axis=1)
        part = jnp.concatenate([part, jnp.zeros((TILE - co, TILE), F32)], axis=0)
        out[at : at + some] = jnp.transpose(part)[0:some, 0:co]

    def outer(left, right, out):
        columns = column_of(right)
        for at in range(0, left.shape[1], TILE):
            some = min(TILE, left.shape[1] - at)
            turned(columns[:, 0:some] * left[:, at : at + some], out, at)

    corr1, corr2, corr0 = ref["corr1"], ref["corr2"], ref["corr0"]
    group_b.to_all()
    outer(compact(left1_ref[0:1], cin, TILE), right1 * (scale1 * scale1), corr1)
    outer(compact(left2_ref[0:1], cout, op), right2 * (scale2 * scale2), corr2)
    outer(left0_ref[0:1, 0:cin], right0 * (scale0 * scale0), corr0)
    out_k1, out_k2, out_k0 = ref["out_k1"], ref["out_k2"], ref["out_k0"]
    group_c.to_all()
    group_a.turned(scale2, out_k2, 0, 5 * cout)
    out_x.wait_recv()
    out_b[mine_o] = got_b[...]
    unpack(0)
    rest = group_b.turned(scale2, out_k2, 5 * cout, 4 * cout)
    out_k0[...] = rest[0:cin] * scale0
    for j in range(1, per):
        unpack(j)
    extra = group_c.turned(scale1, out_k1, 0, n1)
    ref["out_b1"][...] = extra[0:1] + extra[1:2]
    ref["out_b2"][...] = extra[2:3] + extra[3:4]
    for at, (out, corr) in enumerate(((out_k1, corr1), (out_k2, corr2), (out_k0, corr0))):
        value = extra[4 + 2 * at : 5 + 2 * at, 0:1] + extra[5 + 2 * at : 6 + 2 * at, 0:1]
        out[...] = out[...] - corr[...] * value

    for copy in sends:
        copy.wait_send()


def hand_over(arrays):
    number = len(arrays)

    def copy_all(*refs):
        sem = refs[-1]
        copies = [pltpu.make_async_copy(refs[i], refs[number + i], sem.at[i]) for i in range(number)]
        for copy in copies:
            copy.start()
        for copy in copies:
            copy.wait()

    return pl.pallas_call(
        copy_all,
        out_shape=[jax.ShapeDtypeStruct(a.shape, a.dtype) for a in arrays],
        in_specs=[pl.BlockSpec(memory_space=pltpu.VMEM)] * number,
        out_specs=[pl.BlockSpec(memory_space=pl.ANY)] * number,
        scratch_shapes=[pltpu.SemaphoreType.DMA((number,))],
        name="hand_over",
    )(*[pltpu.with_memory_space_constraint(a, pltpu.VMEM) for a in arrays])


def fused(n_rows, arrays):
    (images, valid_h, valid_w, kernel_one, kernel_two, kernel_skip, bias_one, bias_two,
     vector_one, vector_two, vector_skip, cotangent) = arrays
    micros, rows, width, ci = images.shape
    co = kernel_one.shape[3]
    per, pairs, half = micros // 2, rows // 2, width // 2
    op = 2 * TILE
    n_chips = n_rows // 2
    cin, cout = 2 * ci, 2 * co
    sub = min(4, n_chips)
    cubes = n_chips // sub
    unit = op * sub
    lanes_two = -(-max(5 * cout, 4 * cout + cin) // unit) * unit
    lanes_one = -(-(9 * cin + 10) // unit) * unit
    seg_out = rows // 2 + 1
    bits = 3 if n_rows % 8 == 0 else 2
    size1 = -(-(9 * cin) // 64) * 64
    size20 = -(-(9 * cout + cin) // 64) * 64
    share1 = -(-(3 * size1 // 4) // 64) * 16
    share2 = -(-(3 * size20 // 4) // (16 * 2**bits)) * 16
    inputs = {
        "vh": valid_h,
        "vw": valid_w,
        "img": jnp.transpose(images, (0, 1, 3, 2)),
        "k1": kernel_one.reshape(9 * cin, co),
        "k2": kernel_two.reshape(9 * cout, co),
        "k0": kernel_skip,
        "b1": bias_one.reshape(1, co),
        "b2": bias_two.reshape(1, co),
        "q1": vector_one.reshape(1, co),
        "q2": vector_two.reshape(1, co),
        "q0": vector_skip.reshape(1, co),
        "cot": cotangent,
    }
    outputs = {
        "out_b": jax.ShapeDtypeStruct(cotangent.shape, BF16),
        "out_g": jax.ShapeDtypeStruct((micros, rows, ci, width), BF16),
        "out_k1": jax.ShapeDtypeStruct((9 * cin, co), F32),
        "out_k2": jax.ShapeDtypeStruct((9 * cout, co), F32),
        "out_k0": jax.ShapeDtypeStruct((cin, co), F32),
        "out_b1": jax.ShapeDtypeStruct((1, co), F32),
        "out_b2": jax.ShapeDtypeStruct((1, co), F32),
    }
    vm = pltpu.VMEM
    scratch = {
        "vh_s": pltpu.SMEM(valid_h.shape, jnp.int32),
        "vw_s": pltpu.SMEM(valid_w.shape, jnp.int32),
        "b1_v": vm((1, co), BF16),
        "b2_v": vm((1, co), BF16),
        "q1_v": vm((1, co), F32),
        "q2_v": vm((1, co), F32),
        "q0_v": vm((1, co), F32),
        "img_v": vm((micros, rows, ci, width), BF16),
        "cot_v": vm(cotangent.shape, BF16),
        "k1_v": vm((size1, co), BF16),
        "k20_v": vm((size20, co), BF16),
        "k1p": vm((4 * share1, TILE), BF16),
        "k20p": vm((2**bits * share2, TILE), BF16),
        "k1h": vm((4 * share1, TILE), BF16),
        "k20h": vm((2**bits * share2, TILE), BF16),
        "cotp": vm((per, 3 * pairs * half // 4, TILE), BF16),
        "coth": vm((per, 3 * pairs * half // 4, TILE), BF16),
        "imgr": vm((per, 2, pairs + 2, ci, TILE), BF16),
        "sendp": vm((per, pairs, ci, TILE), BF16),
        "vec": vm((2, 8, TILE), F32),
        "cotr": vm((per, 2, 2, half, co), BF16),
        "eye": vm((op, op), BF16),
        "perm_in": vm((8 * half, TILE), BF16),
        "perm_x": vm((5 * half, TILE), BF16),
        "w1": vm((9 * TILE, op), BF16),
        "w2": vm((9 * op, op), BF16),
        "w0": vm((TILE, op), BF16),
        "left1": vm((8, 9 * TILE), F32),
        "left2": vm((8, 9 * op), F32),
        "left0": vm((8, TILE), F32),
        "b_in": vm((per, 2 * (rows // 2 + 3), half, 4 * TILE), BF16),
        "xp": vm((per, pairs + 2, 4 * half, TILE), BF16),
        "xb": vm((per, pairs + 2, half, TILE), BF16),
        "raw1": vm((per, 2, 2 * seg_out, half, op), F32),
        "grad1": vm((per, 2, 2 * seg_out, half, op), F32),
        "act1": vm((per, 2, 2 * seg_out, half, op), BF16),
        "cols": vm((per, 3, 2 * seg_out, half, op), F32),
        "box": vm((per, pairs, half, 9 * op), BF16),
        "quart": vm((per, pairs + 2, half, op), BF16),
        "acc0": vm((cout, TILE), F32),
        "sums0": vm((cout, TILE), BF16),
        "taps_sum": vm((3, 2, per, pairs + 2, half, op), F32),
        "g_pre": vm((per, 2, 2 * seg_out, half, op), BF16),
        "taps_in": vm((2, 2 * seg_out, half, 9 * TILE), F32),
        "skip_back": vm((pairs, half, TILE), F32),
        "send_b": vm((per, pairs, half, co), BF16),
        "got_b": vm((per, pairs, half, co), BF16),
        "send_g": vm((per, pairs, ci, TILE), BF16),
        "got_g": vm((per, pairs, ci, TILE), BF16),
    }
    for name, size in (("corr1", 9 * cin), ("corr2", 9 * cout), ("corr0", cin)):
        scratch[name] = vm((size, co), F32)
    for name, lanes_each in (("a", lanes_two), ("b", lanes_two), ("c", lanes_one)):
        share = lanes_each // sub
        scratch["wire" + name] = vm((2, co, lanes_each), BF16)
        scratch["got" + name] = vm((2, co // 2, lanes_each), BF16)
        scratch["shares" + name] = vm((2, sub, co // 2, share), BF16)
        scratch["landing" + name] = vm((2 * sub - 1, co // 2, share), BF16)
        scratch["mine" + name] = vm((co // 2, share), F32)
        scratch["mids" + name] = vm((cubes, co // 2, share), BF16)
        scratch["result" + name] = vm((sub, co, share), BF16)
    copies = 11 + 2 ** (bits - 1) + 7 * per + 3 * (1 + 2 * (2 * sub - 1) + cubes - 1)
    scratch["lsem"] = pltpu.SemaphoreType.DMA((12,))
    scratch["ssem"] = pltpu.SemaphoreType.DMA((copies,))
    scratch["rsem"] = pltpu.SemaphoreType.DMA((copies,))
    names = list(inputs) + list(outputs) + list(scratch)
    dims = (micros, rows, width, ci, co, lanes_one, lanes_two, bits, share1, share2)
    vmem = pl.BlockSpec(memory_space=pltpu.VMEM)
    hbm = pl.BlockSpec(memory_space=pltpu.HBM)
    results = pl.pallas_call(
        functools.partial(fused_kernel, names, n_rows, dims),
        out_shape=[pltpu.VMEM(a.shape, a.dtype) for a in outputs.values()],
        in_specs=[hbm] * len(inputs),
        out_specs=[vmem] * len(outputs),
        scratch_shapes=list(scratch.values()),
        compiler_params=pltpu.CompilerParams(
            collective_id=0, has_side_effects=True, vmem_limit_bytes=48 * 1024 * 1024
        ),
        name="down_block",
    )(*[pltpu.with_memory_space_constraint(a, pltpu.HBM) for a in inputs.values()])
    out_b, out_g, out_k1, out_k2, out_k0, out_b1, out_b2 = hand_over(results)
    return (
        out_b,
        jnp.transpose(out_g, (0, 1, 3, 2)),
        out_k1.reshape(3, 3, cin, co),
        out_k2.reshape(3, 3, cout, co),
        out_k0,
        out_b1.reshape(co),
        out_b2.reshape(co),
    )


def solution(mesh):
    in_specs = (
        P(None, "rows", None, "ch"),
        P(),
        P(),
        P(None, None, None, "ch"),
        P(None, None, None, "ch"),
        P(None, "ch"),
        P("ch"),
        P("ch"),
        P("ch"),
        P("ch"),
        P("ch"),
        P(None, "rows", None, "ch"),
    )
    out_specs = (
        P(None, "rows", None, "ch"),
        P(None, "rows", None, "ch"),
        P(None, None, None, "ch"),
        P(None, None, None, "ch"),
        P(None, "ch"),
        P("ch"),
        P("ch"),
    )

    def step(*arrays):
        if fits(mesh.shape["rows"], mesh.shape["ch"], arrays):
            return fused(mesh.shape["rows"], arrays)
        return shards(*arrays)

    return jax.shard_map(step, mesh=mesh, in_specs=in_specs, out_specs=out_specs, check_vma=False)
```

```python
import functools

import jax
import jax.numpy as jnp
from jax import lax
from jax.experimental import pallas as pl
from jax.experimental.pallas import tpu as pltpu
from jax.sharding import PartitionSpec as P

IMG = 64
SHIFT = 40


EPS = 1e-06
HIGH = lax.Precision.HIGHEST


def extended(cells, sides, width):
    for axis, dim in sides:
        count = lax.axis_size(axis)
        head = lax.slice_in_dim(cells, 0, width, axis=dim)
        tail = lax.slice_in_dim(cells, cells.shape[dim] - width, cells.shape[dim], axis=dim)
        cells = jnp.concatenate(
            [
                lax.ppermute(tail, axis, [(i, (i + 1) % count) for i in range(count)]),
                cells,
                lax.ppermute(head, axis, [((i + 1) % count, i) for i in range(count)]),
            ],
            axis=dim,
        )
    return cells


def conv_rows(rim, kernel, taps):
    slab_rows = taps.shape[1]
    result = None
    for row_tap in range(3):
        part = lax.conv_general_dilated(
            rim[None, row_tap : row_tap + slab_rows],
            kernel[row_tap : row_tap + 1],
            (1, 1),
            ((0, 0), (1, 1)),
            dimension_numbers=("NHWC", "HWIO", "NHWC"),
            preferred_element_type=jnp.float32,
        )
        part = part[0] * taps[row_tap][:, None, None]
        result = part if result is None else result + part
    return result


def flipped(kernel):
    return jnp.transpose(kernel[::-1, ::-1], (0, 1, 3, 2))


def kernel_taps(rim, grad, taps_low):
    slab_rows = grad.shape[0]
    width = grad.shape[1]
    padded = jnp.pad(rim, ((0, 0), (1, 1), (0, 0)))
    stacked = []
    for row_tap in range(3):
        kept_grad = grad * taps_low[row_tap][:, None, None]
        line = []
        for col_tap in range(3):
            window = padded[row_tap : row_tap + slab_rows, col_tap : col_tap + width]
            line.append(
                jnp.einsum("rci,rco->io", window, kept_grad, preferred_element_type=jnp.float32)
            )
        stacked.append(jnp.stack(line))
    return jnp.stack(stacked)


def silu_slope(value):
    gate = jax.nn.sigmoid(value)
    return gate + value * gate * (1.0 - gate)


def shards(
    images,
    valid_h,
    valid_w,
    kernel_one,
    kernel_two,
    kernel_skip,
    bias_one,
    bias_two,
    vector_one,
    vector_two,
    vector_skip,
    cotangent,
):
    micros, rows_dev, width, in_local = images.shape
    out_local = kernel_one.shape[3]
    count_images = valid_h.shape[1]
    total_rows = rows_dev * lax.axis_size("rows")
    slab_start = lax.axis_index("rows") * rows_dev
    rim_global = slab_start - 1 + jnp.arange(rows_dev + 2, dtype=jnp.int32)
    placed = jnp.mod(rim_global - SHIFT, total_rows)
    image_of = placed // IMG
    row_of = placed % IMG
    taps = jnp.stack(
        [image_of[tap : tap + rows_dev] == image_of[1 : rows_dev + 1] for tap in range(3)]
    ).astype(jnp.float32)
    taps_low = taps.astype(jnp.bfloat16)
    owner = image_of[:, None] == jnp.arange(count_images, dtype=jnp.int32)[None, :]
    columns = jnp.arange(width)
    kern_one = kernel_one.astype(jnp.float32)
    kern_two = kernel_two.astype(jnp.float32)
    kern_skip = kernel_skip.astype(jnp.float32).reshape(1, 1, -1, out_local)
    part_one = jnp.einsum("hwio,o->hwi", kern_one, vector_one, precision=HIGH)
    part_two = jnp.einsum("hwio,o->hwi", kern_two, vector_two, precision=HIGH)
    part_skip = jnp.einsum("hwio,o->hwi", kern_skip, vector_skip, precision=HIGH)
    left_one, left_two, left_skip = lax.psum((part_one, part_two, part_skip), "ch")
    left_one = left_one * lax.rsqrt(jnp.sum(left_one * left_one) + EPS)
    left_two = left_two * lax.rsqrt(jnp.sum(left_two * left_two) + EPS)
    left_skip = left_skip * lax.rsqrt(jnp.sum(left_skip * left_skip) + EPS)
    image_one = jnp.einsum("hwio,hwi->o", kern_one, left_one, precision=HIGH)
    image_two = jnp.einsum("hwio,hwi->o", kern_two, left_two, precision=HIGH)
    image_skip = jnp.einsum("hwio,hwi->o", kern_skip, left_skip, precision=HIGH)
    square_one, square_two, square_skip = lax.psum(
        (
            jnp.sum(image_one * image_one),
            jnp.sum(image_two * image_two),
            jnp.sum(image_skip * image_skip),
        ),
        "ch",
    )
    scale_one = lax.rsqrt(square_one + EPS)
    scale_two = lax.rsqrt(square_two + EPS)
    scale_skip = lax.rsqrt(square_skip + EPS)
    right_one = image_one * scale_one
    right_two = image_two * scale_two
    right_skip = image_skip * scale_skip
    sigma_one = square_one * scale_one
    sigma_two = square_two * scale_two
    sigma_skip = square_skip * scale_skip
    eff_one = (kern_one / sigma_one).astype(jnp.bfloat16)
    eff_two = (kern_two / sigma_two).astype(jnp.bfloat16)
    eff_skip_full = (kern_skip / sigma_skip).astype(jnp.bfloat16)
    eff_skip = eff_skip_full[0, 0]
    bias_first = bias_one.astype(jnp.float32)
    bias_second = bias_two.astype(jnp.float32)
    back_two = flipped(eff_two)
    back_one = flipped(eff_one)
    outputs = []
    in_grads = []
    totals = None
    for micro in range(micros):
        height_rows = jnp.sum(jnp.where(owner, valid_h[micro][None, :], 0), axis=1)
        width_rows = jnp.sum(jnp.where(owner, valid_w[micro][None, :], 0), axis=1)
        mask_rim = (
            (row_of < height_rows)[:, None] & (columns[None, :] < width_rows[:, None])
        ).astype(jnp.float32)[:, :, None]
        mask_in = mask_rim[1:-1]
        input_rim = extended(images[micro], (("rows", 0),), 1)
        gathered = lax.all_gather(input_rim, "ch", axis=2, tiled=True)
        masked_rim = gathered * mask_rim.astype(jnp.bfloat16)
        act_in = jax.nn.silu(masked_rim.astype(jnp.float32)).astype(jnp.bfloat16)
        pre_one = conv_rows(act_in, eff_one, taps) + bias_first
        act_one = (jax.nn.silu(pre_one) * mask_in).astype(jnp.bfloat16)
        hidden_rim = extended(act_one, (("rows", 0),), 1)
        hidden_all = lax.all_gather(hidden_rim, "ch", axis=2, tiled=True)
        skip_in = masked_rim[1:-1]
        total = conv_rows(hidden_all, eff_two, taps) + bias_second
        total = total + jnp.einsum(
            "rci,io->rco", skip_in, eff_skip, preferred_element_type=jnp.float32
        )
        pooled = jnp.mean(total.reshape(rows_dev // 2, 2, width // 2, 2, out_local), axis=(1, 3))
        outputs.append(pooled.astype(jnp.bfloat16))
        quarter = cotangent[micro] * 0.25
        grad_total = jnp.broadcast_to(
            quarter[:, None, :, None, :], (rows_dev // 2, 2, width // 2, 2, out_local)
        ).reshape(rows_dev, width, out_local)
        grad_rim = extended(grad_total, (("rows", 0),), 1)
        partial_hidden = conv_rows(grad_rim, back_two, taps)
        grad_act_one = lax.psum_scatter(partial_hidden, "ch", scatter_dimension=2, tiled=True)
        grad_pre_one = (grad_act_one * mask_in * silu_slope(pre_one)).astype(jnp.bfloat16)
        pre_rim = extended(grad_pre_one, (("rows", 0),), 1)
        partial_act = conv_rows(pre_rim, back_one, taps)
        partial_skip = jnp.einsum(
            "rco,io->rci", grad_total, eff_skip, preferred_element_type=jnp.float32
        )
        grad_act_in, grad_skip_in = (
            lax.psum_scatter(partial_act, "ch", scatter_dimension=2, tiled=True),
            lax.psum_scatter(partial_skip, "ch", scatter_dimension=2, tiled=True),
        )
        own_input = images[micro].astype(jnp.float32)
        in_grads.append(
            (mask_in * (silu_slope(own_input) * grad_act_in + grad_skip_in)).astype(jnp.bfloat16)
        )
        grad_one = kernel_taps(act_in, grad_pre_one, taps_low)
        grad_two = kernel_taps(hidden_all, grad_total, taps_low)
        grad_skip = jnp.einsum(
            "rci,rco->io", skip_in, grad_total, preferred_element_type=jnp.float32
        )
        grad_first = jnp.sum(grad_pre_one.astype(jnp.float32), axis=(0, 1))
        grad_second = jnp.sum(grad_total.astype(jnp.float32), axis=(0, 1))
        current = (grad_one, grad_two, grad_skip, grad_first, grad_second)
        if totals is None:
            totals = current
        else:
            totals = tuple((acc + new for acc, new in zip(totals, current)))
    summed = lax.psum((totals[0], totals[1], totals[2], totals[3], totals[4]), "rows")
    sum_one, sum_two, sum_skip, sum_first, sum_second = summed
    sum_skip = sum_skip.reshape(1, 1, -1, out_local)
    dot_one, dot_two, dot_skip = lax.psum(
        (jnp.sum(sum_one * kern_one), jnp.sum(sum_two * kern_two), jnp.sum(sum_skip * kern_skip)),
        "ch",
    )
    final_one = (
        sum_one / sigma_one - dot_one / (sigma_one * sigma_one) * left_one[..., None] * right_one
    )
    final_two = (
        sum_two / sigma_two - dot_two / (sigma_two * sigma_two) * left_two[..., None] * right_two
    )
    final_skip = (
        sum_skip / sigma_skip
        - dot_skip / (sigma_skip * sigma_skip) * left_skip[..., None] * right_skip
    )
    return (
        jnp.stack(outputs),
        jnp.stack(in_grads),
        final_one,
        final_two,
        final_skip[0, 0],
        sum_first,
        sum_second,
    )


F32 = jnp.float32
BF16 = jnp.bfloat16
MESH = pl.DeviceIdType.MESH
TILE = 128
NT = (((1,), (1,)), ((), ()))
TN = (((0,), (0,)), ((), ()))
NN = (((1,), (0,)), ((), ()))


def fits(n_rows, n_ch, arrays):
    images, kernel_one = arrays[0], arrays[3]
    micros, rows_dev, width, in_local = images.shape
    out_local = kernel_one.shape[3]
    return (
        n_ch == 2
        and micros % 2 == 0
        and n_rows >= 4
        and n_rows % min(8, n_rows) == 0
        and n_rows % 4 == 0
        and rows_dev % 8 == 0
        and SHIFT % rows_dev == rows_dev // 2
        and IMG % rows_dev == 0
        and 2 * width == TILE
        and in_local % 16 == 0
        and 2 * in_local < TILE
        and out_local == 3 * TILE // 4
    )


def dot(left, right, dims=NN):
    return lax.dot_general(left, right, dims, preferred_element_type=F32)


def iota(shape, dim):
    return lax.broadcasted_iota(jnp.int32, shape, dim)


def pieces(row):
    first = row.astype(BF16).astype(F32)
    rest = row - first
    second = rest.astype(BF16).astype(F32)
    third = rest - second
    at = iota((16, row.shape[1]), 0)
    zero = jnp.zeros((16, row.shape[1]), F32)
    stacked = jnp.where(at == 0, first, jnp.where(at == 1, second, jnp.where(at == 2, third, zero)))
    return stacked.astype(BF16)


def total(value):
    return jnp.sum(jnp.sum(value, axis=0, keepdims=True), axis=1, keepdims=True)


def power(vector_row, kernel):
    left = jnp.sum(dot(pieces(vector_row), kernel, NT), axis=0, keepdims=True)
    left = left * lax.rsqrt(total(left * left) + EPS)
    image = jnp.sum(dot(pieces(left), kernel), axis=0, keepdims=True)
    square = total(image * image)
    scale = lax.rsqrt(square + EPS)
    return left, image * scale, square * scale


def sigmoid(value):
    return 0.5 * jnp.tanh(0.5 * value) + 0.5


def slope(value):
    gate = sigmoid(value)
    return gate + value * gate * (1.0 - gate)


def fused_kernel(names, n_rows, dims, *refs):
    micros, rows, width, ci, co, lanes_one, lanes_two, bits, share1, share2 = dims
    ref = dict(zip(names, refs))
    half = width // 2
    per = micros // 2
    pairs = rows // 2
    cut = rows // 2
    seg_slots = cut + 3
    seg_out = cut + 1
    pairs_a = cut // 2 + 1
    n_chips = n_rows // 2
    cin, cout = 2 * ci, 2 * co
    op = 2 * TILE
    total_rows = rows * n_rows
    own_px = pairs * half
    all_px = (pairs + 2) * half

    ssem, rsem, lsem = ref["ssem"], ref["rsem"], ref["lsem"]
    me = lax.axis_index("rows")
    c = lax.axis_index("ch")
    o = 1 - c
    core = lax.rem(me, 2)
    mate = me + 1 - 2 * core
    chip = me // 2
    up = lax.rem(me + n_rows - 1, n_rows)
    down = lax.rem(me + 1, n_rows)
    my_id = c * n_chips + chip
    sub = min(4, n_chips)
    cubes = n_chips // sub
    spot_in, cube = lax.rem(chip, sub), chip // sub
    my_id = c * sub + spot_in
    far = []
    for delta in range(1, 2 * sub):
        other = lax.rem(my_id + delta, 2 * sub)
        far.append((2 * (cube * sub + lax.rem(other, sub)) + core, other // sub))
    across = []
    for delta in range(1, cubes):
        across.append((2 * (lax.rem(cube + delta, cubes) * sub + spot_in) + core, c))
    around = []
    for delta in range(1, 2 * sub):
        other = lax.rem(2 * spot_in + core + delta, 2 * sub)
        around.append((2 * cube * sub + other, c))
    same_core = [(2 * (cube * sub + lax.rem(spot_in + delta, sub)) + core, c) for delta in range(1, sub)]
    near = [(me, o), (mate, c), (up, c), (up, o), (down, c), (down, o)]

    barrier = pltpu.get_barrier_semaphore()
    for device in near + far + across + around:
        pl.semaphore_signal(barrier, inc=1, device_id=device, device_id_type=MESH)

    count = [0]
    sends = []

    def remote(src, dst, device):
        at = count[0]
        count[0] += 1
        return pltpu.make_async_remote_copy(
            src_ref=src,
            dst_ref=dst,
            send_sem=ssem.at[at],
            recv_sem=rsem.at[at],
            device_id=device,
            device_id_type=MESH,
        )

    def begin(*args):
        copy = remote(*args)
        copy.start()
        sends.append(copy)
        return copy

    img, cot, k1, k20 = ref["img_v"], ref["cot_v"], ref["k1_v"], ref["k20_v"]
    n1, n2 = 9 * cin, 9 * cout
    loads = []
    for i, (src, dst) in enumerate(
        [
            (ref["img"], img),
            (ref["k1"], k1.at[0:n1]),
            (ref["k0"], k20.at[n2 : n2 + cin]),
            (ref["k2"], k20.at[0:n2]),
            (ref["cot"], cot),
            (ref["vh"], ref["vh_s"]),
            (ref["vw"], ref["vw_s"]),
            (ref["b1"], ref["b1_v"]),
            (ref["b2"], ref["b2_v"]),
            (ref["q1"], ref["q1_v"]),
            (ref["q2"], ref["q2_v"]),
            (ref["q0"], ref["q0_v"]),
        ]
    ):
        load = pltpu.make_async_copy(src, dst, lsem.at[i])
        load.start()
        loads.append(load)

    perm_in, perm_x = ref["perm_in"], ref["perm_x"]
    shape = (8 * half, TILE)
    at, lane = iota(shape, 0), iota(shape, 1)
    column = 2 * lax.rem(at, half) + lax.rem(at // half, 4) - 1
    hit = (lane - at // (4 * half) * width == column) & (column >= 0) & (column < width)
    perm_in[...] = jnp.where(hit, 1.0, 0.0).astype(BF16)
    shape = (4 * half, TILE)
    at, lane = iota(shape, 0), iota(shape, 1)
    source = at // (2 * half) * width + 2 * lax.rem(at, half) + lax.rem(at // half, 2)
    perm_x[0 : 4 * half] = jnp.where(lane == source, 1.0, 0.0).astype(BF16)
    shape = (half, TILE)
    at, lane = iota(shape, 0), iota(shape, 1)
    perm_x[4 * half : 5 * half] = jnp.where(lax.rem(lane, width) // 2 == at, 1.0, 0.0).astype(BF16)

    eye = ref["eye"]
    shape = (op, op)
    eye[...] = jnp.where(iota(shape, 0) == iota(shape, 1), 1.0, 0.0).astype(BF16)

    def rem_pos(value, by):
        return lax.rem(lax.rem(value, by) + by, by)

    first_a = rem_pos(me * rows - SHIFT, total_rows)
    first_b = rem_pos(me * rows + cut - SHIFT, total_rows)
    base = [lax.rem(first_a, IMG), lax.rem(first_b, IMG) - cut]
    image_a, image_b = first_a // IMG, first_b // IMG
    keep = jnp.where(base[1] < 0, 0.0, 1.0).astype(F32)
    def choose(seg, two):
        return jnp.where(seg == 0, two[0], two[1])

    imgr, sendp = ref["imgr"], ref["sendp"]
    loads[0].wait()
    for j in range(per):
        for mine in (False, True):

            def pack(p, carry, j=j, mine=mine):
                m = (c if mine else o) * per + j
                pair = jnp.concatenate([img[m, 2 * p], img[m, 2 * p + 1]], axis=1)
                if mine:
                    imgr[j, c, p + 1] = pair
                else:
                    sendp[j, p] = pair
                return carry

            lax.fori_loop(0, pairs, pack, 0, unroll=4)
    for load in loads[1:]:
        load.wait()
    vh, vw = ref["vh_s"], ref["vw_s"]
    high = [[vh[c * per + j, image] for image in (image_a, image_b)] for j in range(per)]
    wide = [[vw[c * per + j, image] for image in (image_a, image_b)] for j in range(per)]

    vec = ref["vec"]
    vec[c] = jnp.zeros(vec.shape[1:], F32)
    for i, name in enumerate(("q1", "q2", "q0", "b1", "b2")):
        vec[c, i : i + 1, 0:co] = ref[name + "_v"][...].astype(F32)

    def packed(value):
        kept, strip = 3 * value.shape[-2] // 4, co // 3
        last = value[kept:]
        beside = jnp.concatenate([last[:, k * strip : (k + 1) * strip] for k in range(3)], axis=0)
        return jnp.concatenate([value[:kept], beside], axis=1)

    def unpacked(value):
        part = value.shape[0] // 3
        last = jnp.concatenate([value[k * part : (k + 1) * part, co:] for k in range(3)], axis=1)
        return jnp.concatenate([value[:, :co], last], axis=0)

    k1p, k20p, cotp = ref["k1p"], ref["k20p"], ref["cotp"]
    size1, size20 = 3 * k1.shape[0] // 4, 3 * k20.shape[0] // 4
    k1p[0:size1] = packed(k1[...])
    k20p[0:size20] = packed(k20[...])
    for j in range(per):
        cotp[j] = packed(cot[o * per + j].reshape(own_px, co))

    pl.semaphore_wait(barrier, len(near + far + across + around))

    k1h, k20h, coth, cotr = ref["k1h"], ref["k20h"], ref["coth"], ref["cotr"]
    spots = [core] + [lax.rem(me // 2**b, 2) for b in range(1, bits)]

    def part_of(rows_each, depth, bits_at):
        first = 0
        for b in range(depth):
            first = first * 2 + bits_at[b]
        return pl.ds(first * rows_each, rows_each)

    class Shared:
        def __init__(self, own, got, rows_each, depth):
            self.got, self.rows_each, self.depth, self.level = got, rows_each, depth, 0
            at = part_of(rows_each, depth, spots)
            self.copies = [begin(own.at[at], got.at[at], (me, o))]

        def turn(self):
            for copy in self.copies:
                copy.wait_recv()
            self.copies = []
            if self.level == 0:
                at = self.got.at[part_of(self.rows_each, self.depth, spots)]
                for mask in range(1, 2 ** (self.depth - 1)):
                    other = me
                    for b in range(1, self.depth):
                        if mask >> (b - 1) & 1:
                            other = other + 2**b * (1 - 2 * spots[b])
                    self.copies.append(begin(at, at, (other, c)))
            if self.level == 1:
                size = 2 ** (self.depth - 1) * self.rows_each
                at = self.got.at[pl.ds(core * size, size)]
                self.copies.append(begin(at, at, (mate, c)))
            self.level += 1

    mine_c, mine_o = pl.ds(c * per, per), pl.ds(o * per, per)
    img_x, img_halo = [], []

    def send_image(j):
        img_x.append(begin(sendp.at[j], imgr.at[j, c, pl.ds(1, pairs)], (me, o)))
        img_halo.append(
            [
                begin(sendp.at[j, 0], imgr.at[j, c, pairs + 1], (up, o)),
                begin(sendp.at[j, pairs - 1], imgr.at[j, c, 0], (down, o)),
                begin(imgr.at[j, c, 1], imgr.at[j, c, pairs + 1], (up, c)),
                begin(imgr.at[j, c, pairs], imgr.at[j, c, 0], (down, c)),
            ]
        )

    vec_x = begin(vec.at[c], vec.at[c], (me, o))
    one = Shared(k1p, k1h, share1, 2)
    two = Shared(k20p, k20h, share2, bits)
    for j in range(per):
        send_image(j)
    cot_x = [begin(cotp.at[j], coth.at[j], (me, o)) for j in range(per)]
    cot_halo = [
        begin(cot.at[mine_o, 0], cotr.at[:, c, 1], (up, o)),
        begin(cot.at[mine_o, pairs - 1], cotr.at[:, c, 0], (down, o)),
        begin(cot.at[mine_c, 0], cotr.at[:, c, 1], (up, c)),
        begin(cot.at[mine_c, pairs - 1], cotr.at[:, c, 0], (down, c)),
    ]

    w1, w2, w0 = ref["w1"], ref["w2"], ref["w0"]

    def place(dst, row, own_part, other_part, padded):
        size = own_part.shape[0]
        first = jnp.where(c == 0, own_part, other_part)
        second = jnp.where(c == 0, other_part, own_part)
        line = jnp.concatenate([first, second, jnp.zeros((size, op - cout), BF16)], axis=1)
        dst[pl.ds(row, size), :] = line
        if padded > size:
            dst[pl.ds(row + size, padded - size), :] = jnp.zeros((padded - size, op), BF16)

    def row_of(i):
        return jnp.concatenate(
            [vec[0, i : i + 1, 0:co], vec[1, i : i + 1, 0:co], jnp.zeros((1, op - cout), F32)], axis=1
        )

    b_in, xp, xb = ref["b_in"], ref["xp"], ref["xb"]
    ones = jnp.where(iota((TILE - cin, TILE), 0) == 0, 1.0, 0.0).astype(BF16)

    def prepare(j):
        img_x[j].wait_recv()
        for copy in img_halo[j]:
            copy.wait_recv()

        def two_pairs(step, carry):
            lane = iota((1, TILE), 1)
            column = lax.rem(lane, width)
            acts, plain, slots = [], [], []
            for k in range(2):
                p = 2 * step + k
                seg = (p >= pairs_a).astype(jnp.int32)
                row = 2 * p - 2 + lane // width
                mask = jnp.where(
                    (choose(seg, base) + row < choose(seg, high[j])) & (column < choose(seg, wide[j])), 1.0, 0.0
                )
                x = jnp.concatenate([imgr[j, 0, p], imgr[j, 1, p]], axis=0).astype(F32) * mask
                act = x * sigmoid(x)
                acts += [act.astype(BF16), ones]
                plain += [x.astype(BF16), ones]
                slots.append(2 * p + 2 * seg)
            spread = dot(perm_in[...], jnp.concatenate(acts, axis=0), NT).astype(BF16)
            for k in range(2):
                for a in range(2):
                    for t in range(4):
                        b_in[j, slots[k] + a, :, t * TILE : (t + 1) * TILE] = spread[
                            (4 * a + t) * half : (4 * a + t + 1) * half, k * TILE : (k + 1) * TILE
                        ]
            spread = dot(perm_x[...], jnp.concatenate(plain, axis=0), NT).astype(BF16)
            for k in range(2):
                part = spread[:, k * TILE : (k + 1) * TILE]
                xp[j, 2 * step + k] = part[0 : 4 * half]
                xb[j, 2 * step + k] = part[4 * half : 5 * half]
            return carry

        lax.fori_loop(0, (pairs + 2) // 2, two_pairs, 0, unroll=True)
        b_in[j, seg_slots - 1] = (b_in[j, seg_slots + 1].astype(F32) * keep).astype(BF16)
        b_in[j, seg_slots] = (b_in[j, seg_slots - 2].astype(F32) * keep).astype(BF16)

    raw1, grad1, act1 = ref["raw1"], ref["grad1"], ref["act1"]

    def conv_one(j):
        parts = []
        for seg in range(2):
            for b in range(2):
                first = seg * seg_slots
                taps = [
                    b_in[j, first + u : first + u + seg_out, :, b * TILE : (b + 3) * TILE].reshape(
                        seg_out * half, 3 * TILE
                    )
                    for u in range(3)
                ]
                parts.append(jnp.concatenate(taps, axis=1))
        result = dot(jnp.concatenate(parts, axis=0), w1[...]).reshape(2, 2, seg_out, half, op)
        for seg in range(2):
            for b in range(2):
                raw1[j, b, seg * seg_out : (seg + 1) * seg_out] = result[seg, b]

    cols = ref["cols"]
    pixel = iota((half, op), 0)

    def activate(j):
        def line(i, carry):
            seg = (i >= seg_out).astype(jnp.int32)
            broad = jnp.where(choose(seg, base) + i - 1 < choose(seg, high[j]), choose(seg, wide[j]), 0)
            acts = []
            for b in range(2):
                pre = raw1[j, b, i] * scale1 + bias1
                gate = sigmoid(pre)
                mask = 2 * pixel + b < broad
                lift = pre * gate
                grad1[j, b, i] = jnp.where(mask, gate + lift * (1.0 - gate), 0.0)
                act = jnp.where(mask, lift, 0.0).astype(BF16)
                act1[j, b, i] = act
                acts.append(act.astype(F32))
            even, odd = acts
            before = jnp.where(pixel == 0, 0.0, pltpu.roll(odd, 1, 0))
            after = jnp.where(pixel == half - 1, 0.0, pltpu.roll(even, half - 1, 0))
            cols[j, 0, i] = before + even
            cols[j, 1, i] = even + odd
            cols[j, 2, i] = odd + after
            return carry

        lax.fori_loop(0, 2 * seg_out, line, 0, unroll=True)

    box = ref["box"]

    def boxes(j):
        def line(i, carry):
            above = jnp.where(i == cut // 2, keep, 1.0)
            below = jnp.where(i == cut // 2 - 1, keep, 1.0)
            for w in range(3):
                lines = [cols[j, w, 2 * i + k] for k in range(4)]
                for u in range(3):
                    upper, lower = lines[u], lines[u + 1]
                    if u == 0:
                        upper = upper * above
                    if u == 2:
                        lower = lower * below
                    tap = 3 * u + w
                    box[j, i, :, tap * op : (tap + 1) * op] = (upper + lower).astype(BF16)
            return carry

        lax.fori_loop(0, pairs, line, 0, unroll=True)

    quart = ref["quart"]

    def quarter(j):
        def put(i, own, other):
            first = jnp.where(c == 0, own, other)
            second = jnp.where(c == 0, other, own)
            size = first.shape[0]
            line = jnp.concatenate([first, second, jnp.zeros((size, op - cout), BF16)], axis=1)
            line = (line.astype(F32) * 0.25).astype(BF16)
            quart[j, pl.ds(i, size // half)] = line.reshape(size // half, half, op)

        put(1, cot[c * per + j].reshape(own_px, co), unpacked(coth[j]))
        for i in (0, 1):
            put(i * (pairs + 1), cotr[j, c, i], cotr[j, o, i])

    def owned(j):
        return quart[j, 1 : pairs + 1].reshape(own_px, op)

    half_rows = co // 2
    kept_rows = pl.ds(core * half_rows, half_rows)
    mate_rows = pl.ds((1 - core) * half_rows, half_rows)

    class Summed:
        def __init__(self, name):
            self.wire, self.got, self.shares, self.landing, self.mine, self.mids, self.result = [
                ref[part + name] for part in ("wire", "got", "shares", "landing", "mine", "mids", "result")
            ]
            self.share = self.result.shape[2]
            self.copies = [begin(self.wire.at[:, mate_rows], self.got, (mate, c))]

        def arrived(self):
            for copy in self.copies:
                copy.wait_recv()

        def to_owners(self):
            self.arrived()
            for ch in range(2):
                value = self.wire[ch, kept_rows].astype(F32) + self.got[ch].astype(F32)
                for at in range(sub):
                    self.shares[ch, at] = value[:, at * self.share : (at + 1) * self.share].astype(BF16)
            lanes = pl.ds(pl.multiple_of(spot_in * self.share, TILE), self.share)
            self.mine[...] = self.wire[c, kept_rows, lanes].astype(F32) + self.got[c, :, lanes].astype(F32)
            self.copies = []
            for delta in range(1, 2 * sub):
                other = lax.rem(my_id + delta, 2 * sub)
                self.copies.append(
                    begin(
                        self.shares.at[other // sub, lax.rem(other, sub)], self.landing.at[delta - 1], far[delta - 1]
                    )
                )

        def to_cubes(self):
            self.arrived()
            value = self.mine[...]
            for delta in range(1, 2 * sub):
                value = value + self.landing[delta - 1].astype(F32)
            self.mids[cube] = value.astype(BF16)
            self.copies = [begin(self.mids.at[cube], self.mids.at[cube], device) for device in across]

        def forward(self):
            self.arrived()
            place_at = self.result.at[:, kept_rows]
            self.copies = [begin(place_at, place_at, (mate, c))]

        def to_all(self, direct=True):
            self.arrived()
            value = self.mids[0].astype(F32)
            for at in range(1, cubes):
                value = value + self.mids[at].astype(F32)
            self.result[spot_in, kept_rows] = value.astype(BF16)
            place_at = self.result.at[spot_in, kept_rows]
            self.copies = [begin(place_at, place_at, device) for device in (around if direct else same_core)]

        def turned(self, scale, out, first, size):
            self.arrived()
            for at in range(0, sub * self.share, op):
                piece, lanes = at // self.share, at % self.share
                value = dot(eye[...], self.result[piece, :, lanes : lanes + op], NT)
                some = min(op, size - at)
                if some > 0:
                    out[first + at : first + at + some] = value[0:some] * scale
                if some < op:
                    return value[some:]

    one.turn()
    two.turn()
    one.turn()
    prepare(0)
    one.turn()
    vec_x.wait_recv()
    k1o = unpacked(k1h[0:size1])
    for tap in range(9):
        rows_at = slice(tap * cin, (tap + 1) * cin)
        place(w1, tap * TILE, k1[rows_at], k1o[rows_at], TILE)
    left1, right1, sigma1 = power(row_of(0), w1[...])
    scale1 = 1.0 / sigma1
    bias1, bias2 = row_of(3), row_of(4)
    left1_ref, left2_ref, left0_ref = ref["left1"], ref["left2"], ref["left0"]
    left1_ref[0:1] = left1
    conv_one(0)
    activate(0)
    two.turn()
    boxes(0)
    for j in range(1, per):
        prepare(j)
        conv_one(j)
        activate(j)
        boxes(j)
    for copy in cot_x:
        copy.wait_recv()
    for copy in cot_halo:
        copy.wait_recv()
    for j in range(per):
        quarter(j)

    acc0 = ref["acc0"]
    given = jnp.concatenate([owned(j) for j in range(per)], axis=0)[:, 0:cout]
    turned_quart = jnp.transpose(given)
    sums0 = ref["sums0"]
    group_a = None
    for name, taps in (("a", range(0, 5)), ("b", range(5, 9))):
        lanes = slice(taps[0] * op, (taps[-1] + 1) * op)
        value = dot(turned_quart, box[:, :, :, lanes].reshape(per * own_px, len(taps) * op))
        parts = [value[:, k * op : k * op + cout] for k in range(len(taps))]
        if name == "b":
            skip = dot(turned_quart, xb[:, 1 : pairs + 1].reshape(per * own_px, TILE))
            acc0[...] = skip
            sums0[...] = skip.astype(BF16)
            parts.append(skip[:, 0:cin])
        parts.append(jnp.zeros((cout, lanes_two - sum(part.shape[1] for part in parts)), F32))
        flat = jnp.concatenate(parts, axis=1).astype(BF16)
        for ch in range(2):
            ref["wire" + name][ch] = flat[ch * co : (ch + 1) * co]
        if name == "a":
            group_a = Summed("a")
    group_b = Summed("b")
    two.turn()
    k20o = unpacked(k20h[0:size20])
    for tap in range(9):
        rows_at = slice(tap * cout, (tap + 1) * cout)
        place(w2, tap * op, k20[rows_at], k20o[rows_at], op)
    rows_at = slice(n2, n2 + cin)
    place(w0, 0, k20[rows_at], k20o[rows_at], TILE)
    left2, right2, sigma2 = power(row_of(1), w2[...])
    left0, right0, sigma0 = power(row_of(2), w0[...])
    scale2, scale0 = 1.0 / sigma2, 1.0 / sigma0
    left0_ref[0:1] = left0
    left2_ref[0:1] = left2

    taps_sum = ref["taps_sum"]
    spot = iota((per * all_px, op), 0)
    at_left = lax.rem(spot, half) == 0
    at_right = lax.rem(spot, half) == half - 1
    g_pre = ref["g_pre"]

    def back_taps():
        given = quart[...].reshape(per * all_px, op)
        for u in range(3):
            t0, t1, t2 = [
                dot(given, w2[(3 * u + w) * op : (3 * u + w + 1) * op], NT) for w in range(3)
            ]
            even = t0 + t1 + jnp.where(at_left, 0.0, pltpu.roll(t2, 1, 0))
            odd = t1 + t2 + jnp.where(at_right, 0.0, pltpu.roll(t0, per * all_px - 1, 0))
            taps_sum[u, 0] = even.reshape(per, pairs + 2, half, op)
            taps_sum[u, 1] = odd.reshape(per, pairs + 2, half, op)

    def back_two(j, dots):
        def line(i, carry):
            hold = jnp.where(i == cut // 2, keep, 1.0)
            own_even = jnp.where(i < pairs, 1.0, 0.0)
            own_odd = jnp.where(i > 0, 1.0, 0.0)
            one, two = carry
            for b in range(2):
                upper, lower = taps_sum[2, b, j, i], taps_sum[0, b, j, i + 1]
                even = lower + taps_sum[1, b, j, i + 1] + hold * upper
                odd = taps_sum[1, b, j, i] + upper + hold * lower
                two = two + own_even * even * act1[j, b, 2 * i + 1].astype(F32)
                two = two + own_odd * odd * act1[j, b, 2 * i].astype(F32)
                even = (even * scale2 * grad1[j, b, 2 * i + 1]).astype(BF16)
                odd = (odd * scale2 * grad1[j, b, 2 * i]).astype(BF16)
                g_pre[j, b, 2 * i + 1] = even
                g_pre[j, b, 2 * i] = odd
                one = one + own_even * even.astype(F32) * raw1[j, b, 2 * i + 1]
                one = one + own_odd * odd.astype(F32) * raw1[j, b, 2 * i]
            return one, two

        return lax.fori_loop(0, pairs + 1, line, dots, unroll=True)

    back_taps()
    group_a.to_owners()
    dots = (jnp.zeros((half, op), F32), jnp.zeros((half, op), F32))
    dots = back_two(0, dots)
    group_b.to_owners()
    for j in range(1, per):
        dots = back_two(j, dots)
    dot1, dot2 = dots

    turned_grad = []
    for b in range(2):
        lines = [g_pre[j, b, 1 : rows + 1].reshape(rows * half, op) for j in range(per)]
        turned_grad.append(jnp.concatenate(lines, axis=0)[:, 0:cout])

    def kernel_one_grad(taps):
        value = None
        for b in range(2):
            lines = []
            for j in range(per):
                for seg in range(2):
                    first = seg * (cut + 2) + 1
                    blocks = []
                    for u in range(3):
                        cols_at = [w for w in range(3) if 3 * u + w in taps]
                        if cols_at:
                            block = b_in[
                                j,
                                first + u : first + u + cut,
                                :,
                                (b + cols_at[0]) * TILE : (b + cols_at[-1] + 1) * TILE,
                            ]
                            blocks.append(block.reshape(cut * half, len(cols_at) * TILE))
                    lines.append(jnp.concatenate(blocks, axis=1))
            part = dot(turned_grad[b], jnp.concatenate(lines, axis=0), TN)
            value = part if value is None else value + part
        return value

    def pair_of(column):
        high_part = column.astype(BF16).astype(F32)
        return [high_part, column - high_part]

    def trace_of(partial, kernel):
        product = dot(partial, kernel)
        eye = iota(product.shape, 0) == iota(product.shape, 1)
        return total(jnp.where(eye, product, 0.0))

    def send_one(name, taps, extras):
        value = kernel_one_grad(taps)
        parts = [value[:, k * TILE : k * TILE + cin] for k in range(len(taps))]
        rest = extras(value)
        spare = lanes_one - len(taps) * cin - len(rest)
        parts.append(jnp.concatenate(rest + [jnp.zeros((cout, spare), F32)], axis=1))
        flat = jnp.concatenate(parts, axis=1).astype(BF16)
        for ch in range(2):
            ref["wire" + name][ch] = flat[ch * co : (ch + 1) * co]
        return Summed(name)

    def extras_c(value):
        at = 4 * TILE + cin
        return pair_of(value[:, at : at + 1]) + pair_of(acc0[:, cin : cin + 1])

    def extras_d(value):
        sums_at = [total(dot1), total(dot2), trace_of(sums0[...], w0[...])]
        return [part for at in sums_at for part in pair_of(jnp.broadcast_to(at, (cout, 1)))]

    group_c = send_one("c", range(0, 9), lambda value: extras_c(value) + extras_d(value))

    out_b, send_b, got_b = ref["out_b"], ref["send_b"], ref["got_b"]

    def conv_two(j):
        main = dot(box[j].reshape(own_px, 9 * op), w2[...])
        skip = dot(xb[j, 1 : pairs + 1].reshape(own_px, TILE), w0[...])
        value = ((main * scale2 + skip * scale0) * 0.25 + bias2).astype(BF16)
        first, second = value[:, 0:co], value[:, co:cout]
        out_b[c * per + j] = jnp.where(c == 0, first, second).reshape(pairs, half, co)
        send_b[j] = jnp.where(c == 0, second, first).reshape(pairs, half, co)

    taps_in, skip_back = ref["taps_in"], ref["skip_back"]
    pixel_in = iota((half, TILE), 0)
    out_g, send_g, got_g = ref["out_g"], ref["send_g"], ref["got_g"]

    def back_products(j):
        skip_back[...] = (dot(owned(j), w0[...], NT) * scale0).reshape(pairs, half, TILE)

        given = g_pre[j].reshape(4 * seg_out * half, op)
        taps_in[...] = dot(given, w1[...], NT).reshape(2, 2 * seg_out, half, 9 * TILE)

    def input_rows(j):
        def two_rows(p, carry):
            lines = []
            for a in range(2):
                r = 2 * p + a
                hold_up = jnp.where(r == cut - 1, keep, 1.0)
                hold_down = jnp.where(r == cut, keep, 1.0)

                def column_sum(w, s):
                    def of(u, row):
                        at = (3 * u + w) * TILE
                        return taps_in[s, row, :, at : at + TILE]

                    return of(0, r + 2) * hold_up + of(1, r + 1) + of(2, r) * hold_down

                before = pltpu.roll(column_sum(2, 1), 1, 0)
                after = pltpu.roll(column_sum(0, 0), half - 1, 0)
                even = column_sum(0, 1) + column_sum(1, 0) + jnp.where(pixel_in == 0, 0.0, before)
                odd = column_sum(1, 1) + column_sum(2, 0) + jnp.where(pixel_in == half - 1, 0.0, after)
                seg = (r >= cut).astype(jnp.int32)
                broad = jnp.where(choose(seg, base) + r < choose(seg, high[j]), choose(seg, wide[j]), 0)
                for b, value in ((0, even), (1, odd)):
                    at = (2 * a + b) * half
                    x = xp[j, p + 1, at : at + half].astype(F32)
                    mask = 2 * pixel_in + b < broad
                    value = slope(x) * (value * scale1) + skip_back[p]
                    lines.append(jnp.where(mask, value, 0.0).astype(BF16))
            line = dot(jnp.concatenate(lines, axis=0), perm_x[0 : 4 * half], TN).astype(BF16)
            own = jnp.where(c == 0, line[0:ci], line[ci:cin])
            other = jnp.where(c == 0, line[ci:cin], line[0:ci])
            out_g[c * per + j, 2 * p] = own[:, 0:width]
            out_g[c * per + j, 2 * p + 1] = own[:, width:TILE]
            send_g[j, p] = other
            return carry

        lax.fori_loop(0, pairs, two_rows, 0, unroll=True)
        return begin(send_g.at[j], got_g.at[j], (me, o))

    def unpack(j):
        def line(p, carry):
            out_g[o * per + j, 2 * p] = got_g[j, p, :, 0:width]
            out_g[o * per + j, 2 * p + 1] = got_g[j, p, :, width:TILE]
            return carry

        grad_x[j].wait_recv()
        lax.fori_loop(0, pairs, line, 0, unroll=4)

    conv_two(0)
    for j in range(1, per):
        conv_two(j)
    group_c.to_owners()
    back_products(0)
    out_x = begin(send_b, got_b, (me, o))
    group_a.to_cubes()
    grad_x = [input_rows(0)]
    def own_half(row):
        return jnp.where(c == 0, row[:, 0:co], row[:, co:cout])

    def column_of(row):
        row = jnp.concatenate([own_half(row), jnp.zeros((1, TILE - co), F32)], axis=1)
        return jnp.transpose(jnp.broadcast_to(row, (TILE, TILE)))[0:co]

    def compact(row, size, padded):
        return jnp.concatenate([row[:, t * padded : t * padded + size] for t in range(9)], axis=1)

    def turned(part, out, at):
        some = part.shape[1]
        if some < TILE:
            part = jnp.concatenate([part, jnp.zeros((co, TILE - some), F32)], axis=1)
        part = jnp.concatenate([part, jnp.zeros((TILE - co, TILE), F32)], axis=0)
        out[at : at + some] = jnp.transpose(part)[0:some, 0:co]

    def outer(left, right, out):
        columns = column_of(right)
        for at in range(0, left.shape[1], TILE):
            some = min(TILE, left.shape[1] - at)
            turned(columns[:, 0:some] * left[:, at : at + some], out, at)

    corr1, corr2, corr0 = ref["corr1"], ref["corr2"], ref["corr0"]
    outer(compact(left1_ref[0:1], cin, TILE), right1 * (scale1 * scale1), corr1)
    outer(compact(left2_ref[0:1], cout, op), right2 * (scale2 * scale2), corr2)
    outer(left0_ref[0:1, 0:cin], right0 * (scale0 * scale0), corr0)
    for j in range(1, per):
        back_products(j)
        if j == 1:
            group_b.to_cubes()
            group_a.to_all(False)
        grad_x.append(input_rows(j))
    group_c.to_cubes()

    group_b.to_all(False)
    out_k1, out_k2, out_k0 = ref["out_k1"], ref["out_k2"], ref["out_k0"]
    group_a.forward()
    group_c.to_all()
    group_b.forward()
    group_a.turned(scale2, out_k2, 0, 5 * cout)
    out_x.wait_recv()
    out_b[mine_o] = got_b[...]
    unpack(0)
    rest = group_b.turned(scale2, out_k2, 5 * cout, 4 * cout)
    out_k0[...] = rest[0:cin] * scale0
    for j in range(1, per):
        unpack(j)
    extra = group_c.turned(scale1, out_k1, 0, n1)
    ref["out_b1"][...] = extra[0:1] + extra[1:2]
    ref["out_b2"][...] = extra[2:3] + extra[3:4]
    for at, (out, corr) in enumerate(((out_k1, corr1), (out_k2, corr2), (out_k0, corr0))):
        value = extra[4 + 2 * at : 5 + 2 * at, 0:1] + extra[5 + 2 * at : 6 + 2 * at, 0:1]
        out[...] = out[...] - corr[...] * value

    for copy in sends:
        copy.wait_send()


def hand_over(arrays):
    number = len(arrays)

    def copy_all(*refs):
        sem = refs[-1]
        copies = [pltpu.make_async_copy(refs[i], refs[number + i], sem.at[i]) for i in range(number)]
        for copy in copies:
            copy.start()
        for copy in copies:
            copy.wait()

    return pl.pallas_call(
        copy_all,
        out_shape=[jax.ShapeDtypeStruct(a.shape, a.dtype) for a in arrays],
        in_specs=[pl.BlockSpec(memory_space=pltpu.VMEM)] * number,
        out_specs=[pl.BlockSpec(memory_space=pl.ANY)] * number,
        scratch_shapes=[pltpu.SemaphoreType.DMA((number,))],
        name="hand_over",
    )(*[pltpu.with_memory_space_constraint(a, pltpu.VMEM) for a in arrays])


def fused(n_rows, arrays):
    (images, valid_h, valid_w, kernel_one, kernel_two, kernel_skip, bias_one, bias_two,
     vector_one, vector_two, vector_skip, cotangent) = arrays
    micros, rows, width, ci = images.shape
    co = kernel_one.shape[3]
    per, pairs, half = micros // 2, rows // 2, width // 2
    op = 2 * TILE
    n_chips = n_rows // 2
    cin, cout = 2 * ci, 2 * co
    sub = min(4, n_chips)
    cubes = n_chips // sub
    unit = op * sub
    lanes_two = -(-max(5 * cout, 4 * cout + cin) // unit) * unit
    lanes_one = -(-(9 * cin + 10) // unit) * unit
    seg_out = rows // 2 + 1
    bits = 3 if n_rows % 8 == 0 else 2
    size1 = -(-(9 * cin) // 64) * 64
    size20 = -(-(9 * cout + cin) // 64) * 64
    share1 = -(-(3 * size1 // 4) // 64) * 16
    share2 = -(-(3 * size20 // 4) // (16 * 2**bits)) * 16
    inputs = {
        "vh": valid_h,
        "vw": valid_w,
        "img": jnp.transpose(images, (0, 1, 3, 2)),
        "k1": kernel_one.reshape(9 * cin, co),
        "k2": kernel_two.reshape(9 * cout, co),
        "k0": kernel_skip,
        "b1": bias_one.reshape(1, co),
        "b2": bias_two.reshape(1, co),
        "q1": vector_one.reshape(1, co),
        "q2": vector_two.reshape(1, co),
        "q0": vector_skip.reshape(1, co),
        "cot": cotangent,
    }
    outputs = {
        "out_b": jax.ShapeDtypeStruct(cotangent.shape, BF16),
        "out_g": jax.ShapeDtypeStruct((micros, rows, ci, width), BF16),
        "out_k1": jax.ShapeDtypeStruct((9 * cin, co), F32),
        "out_k2": jax.ShapeDtypeStruct((9 * cout, co), F32),
        "out_k0": jax.ShapeDtypeStruct((cin, co), F32),
        "out_b1": jax.ShapeDtypeStruct((1, co), F32),
        "out_b2": jax.ShapeDtypeStruct((1, co), F32),
    }
    vm = pltpu.VMEM
    scratch = {
        "vh_s": pltpu.SMEM(valid_h.shape, jnp.int32),
        "vw_s": pltpu.SMEM(valid_w.shape, jnp.int32),
        "b1_v": vm((1, co), BF16),
        "b2_v": vm((1, co), BF16),
        "q1_v": vm((1, co), F32),
        "q2_v": vm((1, co), F32),
        "q0_v": vm((1, co), F32),
        "img_v": vm((micros, rows, ci, width), BF16),
        "cot_v": vm(cotangent.shape, BF16),
        "k1_v": vm((size1, co), BF16),
        "k20_v": vm((size20, co), BF16),
        "k1p": vm((4 * share1, TILE), BF16),
        "k20p": vm((2**bits * share2, TILE), BF16),
        "k1h": vm((4 * share1, TILE), BF16),
        "k20h": vm((2**bits * share2, TILE), BF16),
        "cotp": vm((per, 3 * pairs * half // 4, TILE), BF16),
        "coth": vm((per, 3 * pairs * half // 4, TILE), BF16),
        "imgr": vm((per, 2, pairs + 2, ci, TILE), BF16),
        "sendp": vm((per, pairs, ci, TILE), BF16),
        "vec": vm((2, 8, TILE), F32),
        "cotr": vm((per, 2, 2, half, co), BF16),
        "eye": vm((op, op), BF16),
        "perm_in": vm((8 * half, TILE), BF16),
        "perm_x": vm((5 * half, TILE), BF16),
        "w1": vm((9 * TILE, op), BF16),
        "w2": vm((9 * op, op), BF16),
        "w0": vm((TILE, op), BF16),
        "left1": vm((8, 9 * TILE), F32),
        "left2": vm((8, 9 * op), F32),
        "left0": vm((8, TILE), F32),
        "b_in": vm((per, 2 * (rows // 2 + 3), half, 4 * TILE), BF16),
        "xp": vm((per, pairs + 2, 4 * half, TILE), BF16),
        "xb": vm((per, pairs + 2, half, TILE), BF16),
        "raw1": vm((per, 2, 2 * seg_out, half, op), F32),
        "grad1": vm((per, 2, 2 * seg_out, half, op), F32),
        "act1": vm((per, 2, 2 * seg_out, half, op), BF16),
        "cols": vm((per, 3, 2 * seg_out, half, op), F32),
        "box": vm((per, pairs, half, 9 * op), BF16),
        "quart": vm((per, pairs + 2, half, op), BF16),
        "acc0": vm((cout, TILE), F32),
        "sums0": vm((cout, TILE), BF16),
        "taps_sum": vm((3, 2, per, pairs + 2, half, op), F32),
        "g_pre": vm((per, 2, 2 * seg_out, half, op), BF16),
        "taps_in": vm((2, 2 * seg_out, half, 9 * TILE), F32),
        "skip_back": vm((pairs, half, TILE), F32),
        "send_b": vm((per, pairs, half, co), BF16),
        "got_b": vm((per, pairs, half, co), BF16),
        "send_g": vm((per, pairs, ci, TILE), BF16),
        "got_g": vm((per, pairs, ci, TILE), BF16),
    }
    for name, size in (("corr1", 9 * cin), ("corr2", 9 * cout), ("corr0", cin)):
        scratch[name] = vm((size, co), F32)
    for name, lanes_each in (("a", lanes_two), ("b", lanes_two), ("c", lanes_one)):
        share = lanes_each // sub
        scratch["wire" + name] = vm((2, co, lanes_each), BF16)
        scratch["got" + name] = vm((2, co // 2, lanes_each), BF16)
        scratch["shares" + name] = vm((2, sub, co // 2, share), BF16)
        scratch["landing" + name] = vm((2 * sub - 1, co // 2, share), BF16)
        scratch["mine" + name] = vm((co // 2, share), F32)
        scratch["mids" + name] = vm((cubes, co // 2, share), BF16)
        scratch["result" + name] = vm((sub, co, share), BF16)
    copies = 11 + 2 ** (bits - 1) + 7 * per + 3 * (1 + 2 * (2 * sub - 1) + cubes - 1)
    scratch["lsem"] = pltpu.SemaphoreType.DMA((12,))
    scratch["ssem"] = pltpu.SemaphoreType.DMA((copies,))
    scratch["rsem"] = pltpu.SemaphoreType.DMA((copies,))
    names = list(inputs) + list(outputs) + list(scratch)
    dims = (micros, rows, width, ci, co, lanes_one, lanes_two, bits, share1, share2)
    vmem = pl.BlockSpec(memory_space=pltpu.VMEM)
    hbm = pl.BlockSpec(memory_space=pltpu.HBM)
    results = pl.pallas_call(
        functools.partial(fused_kernel, names, n_rows, dims),
        out_shape=[pltpu.VMEM(a.shape, a.dtype) for a in outputs.values()],
        in_specs=[hbm] * len(inputs),
        out_specs=[vmem] * len(outputs),
        scratch_shapes=list(scratch.values()),
        compiler_params=pltpu.CompilerParams(
            collective_id=0, has_side_effects=True, vmem_limit_bytes=48 * 1024 * 1024
        ),
        name="down_block",
    )(*[pltpu.with_memory_space_constraint(a, pltpu.HBM) for a in inputs.values()])
    out_b, out_g, out_k1, out_k2, out_k0, out_b1, out_b2 = hand_over(results)
    return (
        out_b,
        jnp.transpose(out_g, (0, 1, 3, 2)),
        out_k1.reshape(3, 3, cin, co),
        out_k2.reshape(3, 3, cout, co),
        out_k0,
        out_b1.reshape(co),
        out_b2.reshape(co),
    )


def solution(mesh):
    in_specs = (
        P(None, "rows", None, "ch"),
        P(),
        P(),
        P(None, None, None, "ch"),
        P(None, None, None, "ch"),
        P(None, "ch"),
        P("ch"),
        P("ch"),
        P("ch"),
        P("ch"),
        P("ch"),
        P(None, "rows", None, "ch"),
    )
    out_specs = (
        P(None, "rows", None, "ch"),
        P(None, "rows", None, "ch"),
        P(None, None, None, "ch"),
        P(None, None, None, "ch"),
        P(None, "ch"),
        P("ch"),
        P("ch"),
    )

    def step(*arrays):
        if fits(mesh.shape["rows"], mesh.shape["ch"], arrays):
            return fused(mesh.shape["rows"], arrays)
        return shards(*arrays)

    return jax.shard_map(step, mesh=mesh, in_specs=in_specs, out_specs=out_specs, check_vma=False)
```

```python
import functools

import jax
import jax.numpy as jnp
from jax import lax
from jax.experimental import pallas as pl
from jax.experimental.pallas import tpu as pltpu
from jax.sharding import PartitionSpec as P

IMG = 64
SHIFT = 40


EPS = 1e-06
HIGH = lax.Precision.HIGHEST


def extended(cells, sides, width):
    for axis, dim in sides:
        count = lax.axis_size(axis)
        head = lax.slice_in_dim(cells, 0, width, axis=dim)
        tail = lax.slice_in_dim(cells, cells.shape[dim] - width, cells.shape[dim], axis=dim)
        cells = jnp.concatenate(
            [
                lax.ppermute(tail, axis, [(i, (i + 1) % count) for i in range(count)]),
                cells,
                lax.ppermute(head, axis, [((i + 1) % count, i) for i in range(count)]),
            ],
            axis=dim,
        )
    return cells


def conv_rows(rim, kernel, taps):
    slab_rows = taps.shape[1]
    result = None
    for row_tap in range(3):
        part = lax.conv_general_dilated(
            rim[None, row_tap : row_tap + slab_rows],
            kernel[row_tap : row_tap + 1],
            (1, 1),
            ((0, 0), (1, 1)),
            dimension_numbers=("NHWC", "HWIO", "NHWC"),
            preferred_element_type=jnp.float32,
        )
        part = part[0] * taps[row_tap][:, None, None]
        result = part if result is None else result + part
    return result


def flipped(kernel):
    return jnp.transpose(kernel[::-1, ::-1], (0, 1, 3, 2))


def kernel_taps(rim, grad, taps_low):
    slab_rows = grad.shape[0]
    width = grad.shape[1]
    padded = jnp.pad(rim, ((0, 0), (1, 1), (0, 0)))
    stacked = []
    for row_tap in range(3):
        kept_grad = grad * taps_low[row_tap][:, None, None]
        line = []
        for col_tap in range(3):
            window = padded[row_tap : row_tap + slab_rows, col_tap : col_tap + width]
            line.append(
                jnp.einsum("rci,rco->io", window, kept_grad, preferred_element_type=jnp.float32)
            )
        stacked.append(jnp.stack(line))
    return jnp.stack(stacked)


def silu_slope(value):
    gate = jax.nn.sigmoid(value)
    return gate + value * gate * (1.0 - gate)


def shards(
    images,
    valid_h,
    valid_w,
    kernel_one,
    kernel_two,
    kernel_skip,
    bias_one,
    bias_two,
    vector_one,
    vector_two,
    vector_skip,
    cotangent,
):
    micros, rows_dev, width, in_local = images.shape
    out_local = kernel_one.shape[3]
    count_images = valid_h.shape[1]
    total_rows = rows_dev * lax.axis_size("rows")
    slab_start = lax.axis_index("rows") * rows_dev
    rim_global = slab_start - 1 + jnp.arange(rows_dev + 2, dtype=jnp.int32)
    placed = jnp.mod(rim_global - SHIFT, total_rows)
    image_of = placed // IMG
    row_of = placed % IMG
    taps = jnp.stack(
        [image_of[tap : tap + rows_dev] == image_of[1 : rows_dev + 1] for tap in range(3)]
    ).astype(jnp.float32)
    taps_low = taps.astype(jnp.bfloat16)
    owner = image_of[:, None] == jnp.arange(count_images, dtype=jnp.int32)[None, :]
    columns = jnp.arange(width)
    kern_one = kernel_one.astype(jnp.float32)
    kern_two = kernel_two.astype(jnp.float32)
    kern_skip = kernel_skip.astype(jnp.float32).reshape(1, 1, -1, out_local)
    part_one = jnp.einsum("hwio,o->hwi", kern_one, vector_one, precision=HIGH)
    part_two = jnp.einsum("hwio,o->hwi", kern_two, vector_two, precision=HIGH)
    part_skip = jnp.einsum("hwio,o->hwi", kern_skip, vector_skip, precision=HIGH)
    left_one, left_two, left_skip = lax.psum((part_one, part_two, part_skip), "ch")
    left_one = left_one * lax.rsqrt(jnp.sum(left_one * left_one) + EPS)
    left_two = left_two * lax.rsqrt(jnp.sum(left_two * left_two) + EPS)
    left_skip = left_skip * lax.rsqrt(jnp.sum(left_skip * left_skip) + EPS)
    image_one = jnp.einsum("hwio,hwi->o", kern_one, left_one, precision=HIGH)
    image_two = jnp.einsum("hwio,hwi->o", kern_two, left_two, precision=HIGH)
    image_skip = jnp.einsum("hwio,hwi->o", kern_skip, left_skip, precision=HIGH)
    square_one, square_two, square_skip = lax.psum(
        (
            jnp.sum(image_one * image_one),
            jnp.sum(image_two * image_two),
            jnp.sum(image_skip * image_skip),
        ),
        "ch",
    )
    scale_one = lax.rsqrt(square_one + EPS)
    scale_two = lax.rsqrt(square_two + EPS)
    scale_skip = lax.rsqrt(square_skip + EPS)
    right_one = image_one * scale_one
    right_two = image_two * scale_two
    right_skip = image_skip * scale_skip
    sigma_one = square_one * scale_one
    sigma_two = square_two * scale_two
    sigma_skip = square_skip * scale_skip
    eff_one = (kern_one / sigma_one).astype(jnp.bfloat16)
    eff_two = (kern_two / sigma_two).astype(jnp.bfloat16)
    eff_skip_full = (kern_skip / sigma_skip).astype(jnp.bfloat16)
    eff_skip = eff_skip_full[0, 0]
    bias_first = bias_one.astype(jnp.float32)
    bias_second = bias_two.astype(jnp.float32)
    back_two = flipped(eff_two)
    back_one = flipped(eff_one)
    outputs = []
    in_grads = []
    totals = None
    for micro in range(micros):
        height_rows = jnp.sum(jnp.where(owner, valid_h[micro][None, :], 0), axis=1)
        width_rows = jnp.sum(jnp.where(owner, valid_w[micro][None, :], 0), axis=1)
        mask_rim = (
            (row_of < height_rows)[:, None] & (columns[None, :] < width_rows[:, None])
        ).astype(jnp.float32)[:, :, None]
        mask_in = mask_rim[1:-1]
        input_rim = extended(images[micro], (("rows", 0),), 1)
        gathered = lax.all_gather(input_rim, "ch", axis=2, tiled=True)
        masked_rim = gathered * mask_rim.astype(jnp.bfloat16)
        act_in = jax.nn.silu(masked_rim.astype(jnp.float32)).astype(jnp.bfloat16)
        pre_one = conv_rows(act_in, eff_one, taps) + bias_first
        act_one = (jax.nn.silu(pre_one) * mask_in).astype(jnp.bfloat16)
        hidden_rim = extended(act_one, (("rows", 0),), 1)
        hidden_all = lax.all_gather(hidden_rim, "ch", axis=2, tiled=True)
        skip_in = masked_rim[1:-1]
        total = conv_rows(hidden_all, eff_two, taps) + bias_second
        total = total + jnp.einsum(
            "rci,io->rco", skip_in, eff_skip, preferred_element_type=jnp.float32
        )
        pooled = jnp.mean(total.reshape(rows_dev // 2, 2, width // 2, 2, out_local), axis=(1, 3))
        outputs.append(pooled.astype(jnp.bfloat16))
        quarter = cotangent[micro] * 0.25
        grad_total = jnp.broadcast_to(
            quarter[:, None, :, None, :], (rows_dev // 2, 2, width // 2, 2, out_local)
        ).reshape(rows_dev, width, out_local)
        grad_rim = extended(grad_total, (("rows", 0),), 1)
        partial_hidden = conv_rows(grad_rim, back_two, taps)
        grad_act_one = lax.psum_scatter(partial_hidden, "ch", scatter_dimension=2, tiled=True)
        grad_pre_one = (grad_act_one * mask_in * silu_slope(pre_one)).astype(jnp.bfloat16)
        pre_rim = extended(grad_pre_one, (("rows", 0),), 1)
        partial_act = conv_rows(pre_rim, back_one, taps)
        partial_skip = jnp.einsum(
            "rco,io->rci", grad_total, eff_skip, preferred_element_type=jnp.float32
        )
        grad_act_in, grad_skip_in = (
            lax.psum_scatter(partial_act, "ch", scatter_dimension=2, tiled=True),
            lax.psum_scatter(partial_skip, "ch", scatter_dimension=2, tiled=True),
        )
        own_input = images[micro].astype(jnp.float32)
        in_grads.append(
            (mask_in * (silu_slope(own_input) * grad_act_in + grad_skip_in)).astype(jnp.bfloat16)
        )
        grad_one = kernel_taps(act_in, grad_pre_one, taps_low)
        grad_two = kernel_taps(hidden_all, grad_total, taps_low)
        grad_skip = jnp.einsum(
            "rci,rco->io", skip_in, grad_total, preferred_element_type=jnp.float32
        )
        grad_first = jnp.sum(grad_pre_one.astype(jnp.float32), axis=(0, 1))
        grad_second = jnp.sum(grad_total.astype(jnp.float32), axis=(0, 1))
        current = (grad_one, grad_two, grad_skip, grad_first, grad_second)
        if totals is None:
            totals = current
        else:
            totals = tuple((acc + new for acc, new in zip(totals, current)))
    summed = lax.psum((totals[0], totals[1], totals[2], totals[3], totals[4]), "rows")
    sum_one, sum_two, sum_skip, sum_first, sum_second = summed
    sum_skip = sum_skip.reshape(1, 1, -1, out_local)
    dot_one, dot_two, dot_skip = lax.psum(
        (jnp.sum(sum_one * kern_one), jnp.sum(sum_two * kern_two), jnp.sum(sum_skip * kern_skip)),
        "ch",
    )
    final_one = (
        sum_one / sigma_one - dot_one / (sigma_one * sigma_one) * left_one[..., None] * right_one
    )
    final_two = (
        sum_two / sigma_two - dot_two / (sigma_two * sigma_two) * left_two[..., None] * right_two
    )
    final_skip = (
        sum_skip / sigma_skip
        - dot_skip / (sigma_skip * sigma_skip) * left_skip[..., None] * right_skip
    )
    return (
        jnp.stack(outputs),
        jnp.stack(in_grads),
        final_one,
        final_two,
        final_skip[0, 0],
        sum_first,
        sum_second,
    )


F32 = jnp.float32
BF16 = jnp.bfloat16
MESH = pl.DeviceIdType.MESH
TILE = 128
NT = (((1,), (1,)), ((), ()))
TN = (((0,), (0,)), ((), ()))
NN = (((1,), (0,)), ((), ()))


def fits(n_rows, n_ch, arrays):
    images, kernel_one = arrays[0], arrays[3]
    micros, rows_dev, width, in_local = images.shape
    out_local = kernel_one.shape[3]
    return (
        n_ch == 2
        and micros % 2 == 0
        and n_rows >= 4
        and n_rows % min(8, n_rows) == 0
        and n_rows % 4 == 0
        and rows_dev % 8 == 0
        and SHIFT % rows_dev == rows_dev // 2
        and IMG % rows_dev == 0
        and 2 * width == TILE
        and in_local % 16 == 0
        and 2 * in_local < TILE
        and out_local == 3 * TILE // 4
    )


def dot(left, right, dims=NN):
    return lax.dot_general(left, right, dims, preferred_element_type=F32)


def iota(shape, dim):
    return lax.broadcasted_iota(jnp.int32, shape, dim)


def pieces(row):
    first = row.astype(BF16).astype(F32)
    rest = row - first
    second = rest.astype(BF16).astype(F32)
    third = rest - second
    at = iota((16, row.shape[1]), 0)
    zero = jnp.zeros((16, row.shape[1]), F32)
    stacked = jnp.where(at == 0, first, jnp.where(at == 1, second, jnp.where(at == 2, third, zero)))
    return stacked.astype(BF16)


def total(value):
    return jnp.sum(jnp.sum(value, axis=0, keepdims=True), axis=1, keepdims=True)


def power(vector_row, kernel):
    left = jnp.sum(dot(pieces(vector_row), kernel, NT), axis=0, keepdims=True)
    left = left * lax.rsqrt(total(left * left) + EPS)
    image = jnp.sum(dot(pieces(left), kernel), axis=0, keepdims=True)
    square = total(image * image)
    scale = lax.rsqrt(square + EPS)
    return left, image * scale, square * scale


def sigmoid(value):
    return 0.5 * jnp.tanh(0.5 * value) + 0.5


def slope(value):
    gate = sigmoid(value)
    return gate + value * gate * (1.0 - gate)


def fused_kernel(names, n_rows, dims, *refs):
    micros, rows, width, ci, co, lanes_one, lanes_two, bits, share1, share2 = dims
    ref = dict(zip(names, refs))
    half = width // 2
    per = micros // 2
    pairs = rows // 2
    cut = rows // 2
    seg_slots = cut + 3
    seg_out = cut + 1
    pairs_a = cut // 2 + 1
    n_chips = n_rows // 2
    cin, cout = 2 * ci, 2 * co
    op = 2 * TILE
    total_rows = rows * n_rows
    own_px = pairs * half
    all_px = (pairs + 2) * half

    ssem, rsem, lsem = ref["ssem"], ref["rsem"], ref["lsem"]
    me = lax.axis_index("rows")
    c = lax.axis_index("ch")
    o = 1 - c
    core = lax.rem(me, 2)
    mate = me + 1 - 2 * core
    chip = me // 2
    up = lax.rem(me + n_rows - 1, n_rows)
    down = lax.rem(me + 1, n_rows)
    my_id = c * n_chips + chip
    sub = min(4, n_chips)
    cubes = n_chips // sub
    spot_in, cube = lax.rem(chip, sub), chip // sub
    my_id = c * sub + spot_in
    far = []
    for delta in range(1, 2 * sub):
        other = lax.rem(my_id + delta, 2 * sub)
        far.append((2 * (cube * sub + lax.rem(other, sub)) + core, other // sub))
    across = []
    for delta in range(1, cubes):
        across.append((2 * (lax.rem(cube + delta, cubes) * sub + spot_in) + core, c))
    around = []
    for delta in range(1, 2 * sub):
        other = lax.rem(2 * spot_in + core + delta, 2 * sub)
        around.append((2 * cube * sub + other, c))
    same_core = [(2 * (cube * sub + lax.rem(spot_in + delta, sub)) + core, c) for delta in range(1, sub)]

    barrier = pltpu.get_barrier_semaphore()
    plane = [(2 * (cube * sub + lax.rem(spot_in + delta, sub)) + core, o) for delta in range(sub)]
    greeted = [(up, o), (down, o), (up, c), (down, c)] + across + plane + around
    for device in greeted:
        pl.semaphore_signal(barrier, inc=1, device_id=device, device_id_type=MESH)

    count = [0]
    sends = []

    def remote(src, dst, device):
        at = count[0]
        count[0] += 1
        return pltpu.make_async_remote_copy(
            src_ref=src,
            dst_ref=dst,
            send_sem=ssem.at[at],
            recv_sem=rsem.at[at],
            device_id=device,
            device_id_type=MESH,
        )

    def begin(*args):
        copy = remote(*args)
        copy.start()
        sends.append(copy)
        return copy

    img, cot, k1, k20 = ref["img_v"], ref["cot_v"], ref["k1_v"], ref["k20_v"]
    n1, n2 = 9 * cin, 9 * cout
    loads = []
    for i, (src, dst) in enumerate(
        [
            (ref["img"], img),
            (ref["k1"], k1.at[0:n1]),
            (ref["k0"], k20.at[n2 : n2 + cin]),
            (ref["k2"], k20.at[0:n2]),
            (ref["cot"], cot),
            (ref["vh"], ref["vh_s"]),
            (ref["vw"], ref["vw_s"]),
            (ref["b1"], ref["b1_v"]),
            (ref["b2"], ref["b2_v"]),
            (ref["q1"], ref["q1_v"]),
            (ref["q2"], ref["q2_v"]),
            (ref["q0"], ref["q0_v"]),
        ]
    ):
        load = pltpu.make_async_copy(src, dst, lsem.at[i])
        load.start()
        loads.append(load)

    perm_in, perm_x = ref["perm_in"], ref["perm_x"]
    shape = (8 * half, TILE)
    at, lane = iota(shape, 0), iota(shape, 1)
    column = 2 * lax.rem(at, half) + lax.rem(at // half, 4) - 1
    hit = (lane - at // (4 * half) * width == column) & (column >= 0) & (column < width)
    perm_in[...] = jnp.where(hit, 1.0, 0.0).astype(BF16)
    shape = (4 * half, TILE)
    at, lane = iota(shape, 0), iota(shape, 1)
    source = at // (2 * half) * width + 2 * lax.rem(at, half) + lax.rem(at // half, 2)
    perm_x[0 : 4 * half] = jnp.where(lane == source, 1.0, 0.0).astype(BF16)
    shape = (half, TILE)
    at, lane = iota(shape, 0), iota(shape, 1)
    perm_x[4 * half : 5 * half] = jnp.where(lax.rem(lane, width) // 2 == at, 1.0, 0.0).astype(BF16)

    eye = ref["eye"]
    shape = (op, op)
    eye[...] = jnp.where(iota(shape, 0) == iota(shape, 1), 1.0, 0.0).astype(BF16)

    def rem_pos(value, by):
        return lax.rem(lax.rem(value, by) + by, by)

    first_a = rem_pos(me * rows - SHIFT, total_rows)
    first_b = rem_pos(me * rows + cut - SHIFT, total_rows)
    base = [lax.rem(first_a, IMG), lax.rem(first_b, IMG) - cut]
    image_a, image_b = first_a // IMG, first_b // IMG
    keep = jnp.where(base[1] < 0, 0.0, 1.0).astype(F32)
    def choose(seg, two):
        return jnp.where(seg == 0, two[0], two[1])

    imgr, sendp = ref["imgr"], ref["sendp"]
    loads[0].wait()
    for j in range(per):
        for mine in (False, True):

            def pack(p, carry, j=j, mine=mine):
                m = (c if mine else o) * per + j
                pair = jnp.concatenate([img[m, 2 * p], img[m, 2 * p + 1]], axis=1)
                if mine:
                    imgr[j, c, p + 1] = pair
                else:
                    sendp[j, p] = pair
                return carry

            lax.fori_loop(0, pairs, pack, 0, unroll=4)
    for load in loads[1:]:
        load.wait()
    vh, vw = ref["vh_s"], ref["vw_s"]
    high = [[vh[c * per + j, image] for image in (image_a, image_b)] for j in range(per)]
    wide = [[vw[c * per + j, image] for image in (image_a, image_b)] for j in range(per)]

    vec = ref["vec"]
    vec[c] = jnp.zeros(vec.shape[1:], F32)
    for i, name in enumerate(("q1", "q2", "q0", "b1", "b2")):
        vec[c, i : i + 1, 0:co] = ref[name + "_v"][...].astype(F32)

    def packed(value):
        kept, strip = 3 * value.shape[-2] // 4, co // 3
        last = value[kept:]
        beside = jnp.concatenate([last[:, k * strip : (k + 1) * strip] for k in range(3)], axis=0)
        return jnp.concatenate([value[:kept], beside], axis=1)

    def unpacked(value):
        part = value.shape[0] // 3
        last = jnp.concatenate([value[k * part : (k + 1) * part, co:] for k in range(3)], axis=1)
        return jnp.concatenate([value[:, :co], last], axis=0)

    k1p, k20p, cotp = ref["k1p"], ref["k20p"], ref["cotp"]
    size1, size20 = 3 * k1.shape[0] // 4, 3 * k20.shape[0] // 4
    k1p[0:size1] = packed(k1[...])
    k20p[0:size20] = packed(k20[...])
    for j in range(per):
        cotp[j] = packed(cot[o * per + j].reshape(own_px, co))

    pl.semaphore_wait(barrier, len(greeted))

    k1h, k20h, coth, cotr = ref["k1h"], ref["k20h"], ref["coth"], ref["cotr"]
    spots = [core] + [lax.rem(me // 2**b, 2) for b in range(1, bits)]

    def part_of(rows_each, depth, bits_at):
        first = 0
        for b in range(depth):
            first = first * 2 + bits_at[b]
        return pl.ds(first * rows_each, rows_each)

    class Shared:
        def __init__(self, own, got, rows_each, depth):
            self.got, self.rows_each, self.depth, self.level = got, rows_each, depth, 0
            at = part_of(rows_each, depth, spots)
            self.copies = [begin(own.at[at], got.at[at], (me, o))]

        def turn(self):
            for copy in self.copies:
                copy.wait_recv()
            self.copies = []
            if self.level == 0:
                at = self.got.at[part_of(self.rows_each, self.depth, spots)]
                for mask in range(1, 2 ** (self.depth - 1)):
                    other = me
                    for b in range(1, self.depth):
                        if mask >> (b - 1) & 1:
                            other = other + 2**b * (1 - 2 * spots[b])
                    self.copies.append(begin(at, at, (other, c)))
            if self.level == 1:
                size = 2 ** (self.depth - 1) * self.rows_each
                at = self.got.at[pl.ds(core * size, size)]
                self.copies.append(begin(at, at, (mate, c)))
            self.level += 1

    mine_c, mine_o = pl.ds(c * per, per), pl.ds(o * per, per)
    img_x, img_halo = [], []

    def send_image(j):
        img_x.append(begin(sendp.at[j], imgr.at[j, c, pl.ds(1, pairs)], (me, o)))
        img_halo.append(
            [
                begin(sendp.at[j, 0], imgr.at[j, c, pairs + 1], (up, o)),
                begin(sendp.at[j, pairs - 1], imgr.at[j, c, 0], (down, o)),
                begin(imgr.at[j, c, 1], imgr.at[j, c, pairs + 1], (up, c)),
                begin(imgr.at[j, c, pairs], imgr.at[j, c, 0], (down, c)),
            ]
        )

    vec_x = begin(vec.at[c], vec.at[c], (me, o))
    one = Shared(k1p, k1h, share1, 2)
    two = Shared(k20p, k20h, share2, bits)
    for j in range(per):
        send_image(j)
    cot_x = [begin(cotp.at[j], coth.at[j], (me, o)) for j in range(per)]
    cot_halo = [
        begin(cot.at[mine_o, 0], cotr.at[:, c, 1], (up, o)),
        begin(cot.at[mine_o, pairs - 1], cotr.at[:, c, 0], (down, o)),
        begin(cot.at[mine_c, 0], cotr.at[:, c, 1], (up, c)),
        begin(cot.at[mine_c, pairs - 1], cotr.at[:, c, 0], (down, c)),
    ]

    w1, w2, w0 = ref["w1"], ref["w2"], ref["w0"]

    def place(dst, row, own_part, other_part, padded):
        size = own_part.shape[0]
        first = jnp.where(c == 0, own_part, other_part)
        second = jnp.where(c == 0, other_part, own_part)
        line = jnp.concatenate([first, second, jnp.zeros((size, op - cout), BF16)], axis=1)
        dst[pl.ds(row, size), :] = line
        if padded > size:
            dst[pl.ds(row + size, padded - size), :] = jnp.zeros((padded - size, op), BF16)

    def row_of(i):
        return jnp.concatenate(
            [vec[0, i : i + 1, 0:co], vec[1, i : i + 1, 0:co], jnp.zeros((1, op - cout), F32)], axis=1
        )

    b_in, xp, xb = ref["b_in"], ref["xp"], ref["xb"]
    ones = jnp.where(iota((TILE - cin, TILE), 0) == 0, 1.0, 0.0).astype(BF16)

    def prepare(j):
        img_x[j].wait_recv()
        for copy in img_halo[j]:
            copy.wait_recv()

        def two_pairs(step, carry):
            lane = iota((1, TILE), 1)
            column = lax.rem(lane, width)
            acts, plain, slots = [], [], []
            for k in range(2):
                p = 2 * step + k
                seg = (p >= pairs_a).astype(jnp.int32)
                row = 2 * p - 2 + lane // width
                mask = jnp.where(
                    (choose(seg, base) + row < choose(seg, high[j])) & (column < choose(seg, wide[j])), 1.0, 0.0
                )
                x = jnp.concatenate([imgr[j, 0, p], imgr[j, 1, p]], axis=0).astype(F32) * mask
                act = x * sigmoid(x)
                acts += [act.astype(BF16), ones]
                plain += [x.astype(BF16), ones]
                slots.append(2 * p + 2 * seg)
            spread = dot(perm_in[...], jnp.concatenate(acts, axis=0), NT).astype(BF16)
            for k in range(2):
                for a in range(2):
                    for t in range(4):
                        b_in[j, slots[k] + a, :, t * TILE : (t + 1) * TILE] = spread[
                            (4 * a + t) * half : (4 * a + t + 1) * half, k * TILE : (k + 1) * TILE
                        ]
            spread = dot(perm_x[...], jnp.concatenate(plain, axis=0), NT).astype(BF16)
            for k in range(2):
                part = spread[:, k * TILE : (k + 1) * TILE]
                xp[j, 2 * step + k] = part[0 : 4 * half]
                xb[j, 2 * step + k] = part[4 * half : 5 * half]
            return carry

        lax.fori_loop(0, (pairs + 2) // 2, two_pairs, 0, unroll=True)
        b_in[j, seg_slots - 1] = (b_in[j, seg_slots + 1].astype(F32) * keep).astype(BF16)
        b_in[j, seg_slots] = (b_in[j, seg_slots - 2].astype(F32) * keep).astype(BF16)

    raw1, grad1, act1 = ref["raw1"], ref["grad1"], ref["act1"]

    def conv_one(j):
        parts = []
        for seg in range(2):
            for b in range(2):
                first = seg * seg_slots
                taps = [
                    b_in[j, first + u : first + u + seg_out, :, b * TILE : (b + 3) * TILE].reshape(
                        seg_out * half, 3 * TILE
                    )
                    for u in range(3)
                ]
                parts.append(jnp.concatenate(taps, axis=1))
        result = dot(jnp.concatenate(parts, axis=0), w1[...]).reshape(2, 2, seg_out, half, op)
        for seg in range(2):
            for b in range(2):
                raw1[j, b, seg * seg_out : (seg + 1) * seg_out] = result[seg, b]

    cols = ref["cols"]
    pixel = iota((half, op), 0)

    def activate(j):
        def line(i, carry):
            seg = (i >= seg_out).astype(jnp.int32)
            broad = jnp.where(choose(seg, base) + i - 1 < choose(seg, high[j]), choose(seg, wide[j]), 0)
            acts = []
            for b in range(2):
                pre = raw1[j, b, i] * scale1 + bias1
                gate = sigmoid(pre)
                mask = 2 * pixel + b < broad
                lift = pre * gate
                grad1[j, b, i] = jnp.where(mask, gate + lift * (1.0 - gate), 0.0)
                act = jnp.where(mask, lift, 0.0).astype(BF16)
                act1[j, b, i] = act
                acts.append(act.astype(F32))
            even, odd = acts
            before = jnp.where(pixel == 0, 0.0, pltpu.roll(odd, 1, 0))
            after = jnp.where(pixel == half - 1, 0.0, pltpu.roll(even, half - 1, 0))
            cols[j, 0, i] = before + even
            cols[j, 1, i] = even + odd
            cols[j, 2, i] = odd + after
            return carry

        lax.fori_loop(0, 2 * seg_out, line, 0, unroll=True)

    box = ref["box"]

    def boxes(j):
        def line(i, carry):
            above = jnp.where(i == cut // 2, keep, 1.0)
            below = jnp.where(i == cut // 2 - 1, keep, 1.0)
            for w in range(3):
                lines = [cols[j, w, 2 * i + k] for k in range(4)]
                for u in range(3):
                    upper, lower = lines[u], lines[u + 1]
                    if u == 0:
                        upper = upper * above
                    if u == 2:
                        lower = lower * below
                    tap = 3 * u + w
                    box[j, i, :, tap * op : (tap + 1) * op] = (upper + lower).astype(BF16)
            return carry

        lax.fori_loop(0, pairs, line, 0, unroll=True)

    quart = ref["quart"]

    def quarter(j):
        def put(i, own, other):
            first = jnp.where(c == 0, own, other)
            second = jnp.where(c == 0, other, own)
            size = first.shape[0]
            line = jnp.concatenate([first, second, jnp.zeros((size, op - cout), BF16)], axis=1)
            line = (line.astype(F32) * 0.25).astype(BF16)
            quart[j, pl.ds(i, size // half)] = line.reshape(size // half, half, op)

        put(1, cot[c * per + j].reshape(own_px, co), unpacked(coth[j]))
        for i in (0, 1):
            put(i * (pairs + 1), cotr[j, c, i], cotr[j, o, i])

    def owned(j):
        return quart[j, 1 : pairs + 1].reshape(own_px, op)

    half_rows = co // 2
    kept_rows = pl.ds(core * half_rows, half_rows)
    mate_rows = pl.ds((1 - core) * half_rows, half_rows)

    class Summed:
        def __init__(self, name):
            self.wire, self.got, self.shares, self.landing, self.mine, self.mids, self.result = [
                ref[part + name] for part in ("wire", "got", "shares", "landing", "mine", "mids", "result")
            ]
            self.share = self.result.shape[2]
            self.copies = [begin(self.wire.at[:, mate_rows], self.got, (mate, c))]

        def arrived(self):
            for copy in self.copies:
                copy.wait_recv()

        def to_owners(self):
            self.arrived()
            for ch in range(2):
                value = self.wire[ch, kept_rows].astype(F32) + self.got[ch].astype(F32)
                for at in range(sub):
                    self.shares[ch, at] = value[:, at * self.share : (at + 1) * self.share].astype(BF16)
            lanes = pl.ds(pl.multiple_of(spot_in * self.share, TILE), self.share)
            self.mine[...] = self.wire[c, kept_rows, lanes].astype(F32) + self.got[c, :, lanes].astype(F32)
            self.copies = []
            for delta in range(1, 2 * sub):
                other = lax.rem(my_id + delta, 2 * sub)
                self.copies.append(
                    begin(
                        self.shares.at[other // sub, lax.rem(other, sub)], self.landing.at[delta - 1], far[delta - 1]
                    )
                )

        def to_cubes(self):
            self.arrived()
            value = self.mine[...]
            for delta in range(1, 2 * sub):
                value = value + self.landing[delta - 1].astype(F32)
            self.mids[cube] = value.astype(BF16)
            self.copies = [begin(self.mids.at[cube], self.mids.at[cube], device) for device in across]

        def forward(self):
            self.arrived()
            place_at = self.result.at[:, kept_rows]
            self.copies = [begin(place_at, place_at, (mate, c))]

        def to_all(self, direct=True):
            self.arrived()
            value = self.mids[0].astype(F32)
            for at in range(1, cubes):
                value = value + self.mids[at].astype(F32)
            self.result[spot_in, kept_rows] = value.astype(BF16)
            place_at = self.result.at[spot_in, kept_rows]
            self.copies = [begin(place_at, place_at, device) for device in (around if direct else same_core)]

        def turned(self, scale, out, first, size):
            self.arrived()
            for at in range(0, sub * self.share, op):
                piece, lanes = at // self.share, at % self.share
                value = dot(eye[...], self.result[piece, :, lanes : lanes + op], NT)
                some = min(op, size - at)
                if some > 0:
                    out[first + at : first + at + some] = value[0:some] * scale
                if some < op:
                    return value[some:]

    one.turn()
    two.turn()
    one.turn()
    prepare(0)
    one.turn()
    vec_x.wait_recv()
    k1o = unpacked(k1h[0:size1])
    for tap in range(9):
        rows_at = slice(tap * cin, (tap + 1) * cin)
        place(w1, tap * TILE, k1[rows_at], k1o[rows_at], TILE)
    left1, right1, sigma1 = power(row_of(0), w1[...])
    scale1 = 1.0 / sigma1
    bias1, bias2 = row_of(3), row_of(4)
    left1_ref, left2_ref, left0_ref = ref["left1"], ref["left2"], ref["left0"]
    left1_ref[0:1] = left1
    conv_one(0)
    activate(0)
    two.turn()
    boxes(0)
    for j in range(1, per):
        prepare(j)
        conv_one(j)
        activate(j)
        boxes(j)
    for copy in cot_x:
        copy.wait_recv()
    for copy in cot_halo:
        copy.wait_recv()
    for j in range(per):
        quarter(j)

    acc0 = ref["acc0"]
    given = jnp.concatenate([owned(j) for j in range(per)], axis=0)[:, 0:cout]
    turned_quart = jnp.transpose(given)
    sums0 = ref["sums0"]
    group_a = None
    for name, taps in (("a", range(0, 5)), ("b", range(5, 9))):
        lanes = slice(taps[0] * op, (taps[-1] + 1) * op)
        value = dot(turned_quart, box[:, :, :, lanes].reshape(per * own_px, len(taps) * op))
        parts = [value[:, k * op : k * op + cout] for k in range(len(taps))]
        if name == "b":
            skip = dot(turned_quart, xb[:, 1 : pairs + 1].reshape(per * own_px, TILE))
            acc0[...] = skip
            sums0[...] = skip.astype(BF16)
            parts.append(skip[:, 0:cin])
        parts.append(jnp.zeros((cout, lanes_two - sum(part.shape[1] for part in parts)), F32))
        flat = jnp.concatenate(parts, axis=1).astype(BF16)
        for ch in range(2):
            ref["wire" + name][ch] = flat[ch * co : (ch + 1) * co]
        if name == "a":
            group_a = Summed("a")
    group_b = Summed("b")
    two.turn()
    k20o = unpacked(k20h[0:size20])
    for tap in range(9):
        rows_at = slice(tap * cout, (tap + 1) * cout)
        place(w2, tap * op, k20[rows_at], k20o[rows_at], op)
    rows_at = slice(n2, n2 + cin)
    place(w0, 0, k20[rows_at], k20o[rows_at], TILE)
    left2, right2, sigma2 = power(row_of(1), w2[...])
    left0, right0, sigma0 = power(row_of(2), w0[...])
    scale2, scale0 = 1.0 / sigma2, 1.0 / sigma0
    left0_ref[0:1] = left0
    left2_ref[0:1] = left2

    taps_sum = ref["taps_sum"]
    spot = iota((per * all_px, op), 0)
    at_left = lax.rem(spot, half) == 0
    at_right = lax.rem(spot, half) == half - 1
    g_pre = ref["g_pre"]

    def back_taps():
        given = quart[...].reshape(per * all_px, op)
        for u in range(3):
            t0, t1, t2 = [
                dot(given, w2[(3 * u + w) * op : (3 * u + w + 1) * op], NT) for w in range(3)
            ]
            even = t0 + t1 + jnp.where(at_left, 0.0, pltpu.roll(t2, 1, 0))
            odd = t1 + t2 + jnp.where(at_right, 0.0, pltpu.roll(t0, per * all_px - 1, 0))
            taps_sum[u, 0] = even.reshape(per, pairs + 2, half, op)
            taps_sum[u, 1] = odd.reshape(per, pairs + 2, half, op)

    def back_two(j, dots):
        def line(i, carry):
            hold = jnp.where(i == cut // 2, keep, 1.0)
            own_even = jnp.where(i < pairs, 1.0, 0.0)
            own_odd = jnp.where(i > 0, 1.0, 0.0)
            one, two = carry
            for b in range(2):
                upper, lower = taps_sum[2, b, j, i], taps_sum[0, b, j, i + 1]
                even = lower + taps_sum[1, b, j, i + 1] + hold * upper
                odd = taps_sum[1, b, j, i] + upper + hold * lower
                two = two + own_even * even * act1[j, b, 2 * i + 1].astype(F32)
                two = two + own_odd * odd * act1[j, b, 2 * i].astype(F32)
                even = (even * scale2 * grad1[j, b, 2 * i + 1]).astype(BF16)
                odd = (odd * scale2 * grad1[j, b, 2 * i]).astype(BF16)
                g_pre[j, b, 2 * i + 1] = even
                g_pre[j, b, 2 * i] = odd
                one = one + own_even * even.astype(F32) * raw1[j, b, 2 * i + 1]
                one = one + own_odd * odd.astype(F32) * raw1[j, b, 2 * i]
            return one, two

        return lax.fori_loop(0, pairs + 1, line, dots, unroll=True)

    back_taps()
    group_a.to_owners()
    dots = (jnp.zeros((half, op), F32), jnp.zeros((half, op), F32))
    dots = back_two(0, dots)
    group_b.to_owners()
    for j in range(1, per):
        dots = back_two(j, dots)
    dot1, dot2 = dots

    turned_grad = []
    for b in range(2):
        lines = [g_pre[j, b, 1 : rows + 1].reshape(rows * half, op) for j in range(per)]
        turned_grad.append(jnp.concatenate(lines, axis=0)[:, 0:cout])

    def kernel_one_grad(taps):
        value = None
        for b in range(2):
            lines = []
            for j in range(per):
                for seg in range(2):
                    first = seg * (cut + 2) + 1
                    blocks = []
                    for u in range(3):
                        cols_at = [w for w in range(3) if 3 * u + w in taps]
                        if cols_at:
                            block = b_in[
                                j,
                                first + u : first + u + cut,
                                :,
                                (b + cols_at[0]) * TILE : (b + cols_at[-1] + 1) * TILE,
                            ]
                            blocks.append(block.reshape(cut * half, len(cols_at) * TILE))
                    lines.append(jnp.concatenate(blocks, axis=1))
            part = dot(turned_grad[b], jnp.concatenate(lines, axis=0), TN)
            value = part if value is None else value + part
        return value

    def pair_of(column):
        high_part = column.astype(BF16).astype(F32)
        return [high_part, column - high_part]

    def trace_of(partial, kernel):
        product = dot(partial, kernel)
        eye = iota(product.shape, 0) == iota(product.shape, 1)
        return total(jnp.where(eye, product, 0.0))

    def send_one(name, taps, extras):
        value = kernel_one_grad(taps)
        parts = [value[:, k * TILE : k * TILE + cin] for k in range(len(taps))]
        rest = extras(value)
        spare = lanes_one - len(taps) * cin - len(rest)
        parts.append(jnp.concatenate(rest + [jnp.zeros((cout, spare), F32)], axis=1))
        flat = jnp.concatenate(parts, axis=1).astype(BF16)
        for ch in range(2):
            ref["wire" + name][ch] = flat[ch * co : (ch + 1) * co]
        return Summed(name)

    def extras_c(value):
        at = 4 * TILE + cin
        return pair_of(value[:, at : at + 1]) + pair_of(acc0[:, cin : cin + 1])

    def extras_d(value):
        sums_at = [total(dot1), total(dot2), trace_of(sums0[...], w0[...])]
        return [part for at in sums_at for part in pair_of(jnp.broadcast_to(at, (cout, 1)))]

    group_c = send_one("c", range(0, 9), lambda value: extras_c(value) + extras_d(value))

    out_b, send_b, got_b = ref["out_b"], ref["send_b"], ref["got_b"]

    def conv_two(j):
        main = dot(box[j].reshape(own_px, 9 * op), w2[...])
        skip = dot(xb[j, 1 : pairs + 1].reshape(own_px, TILE), w0[...])
        value = ((main * scale2 + skip * scale0) * 0.25 + bias2).astype(BF16)
        first, second = value[:, 0:co], value[:, co:cout]
        out_b[c * per + j] = jnp.where(c == 0, first, second).reshape(pairs, half, co)
        send_b[j] = jnp.where(c == 0, second, first).reshape(pairs, half, co)

    taps_in, skip_back = ref["taps_in"], ref["skip_back"]
    pixel_in = iota((half, TILE), 0)
    out_g, send_g, got_g = ref["out_g"], ref["send_g"], ref["got_g"]

    def back_products(j):
        skip_back[...] = (dot(owned(j), w0[...], NT) * scale0).reshape(pairs, half, TILE)

        given = g_pre[j].reshape(4 * seg_out * half, op)
        taps_in[...] = dot(given, w1[...], NT).reshape(2, 2 * seg_out, half, 9 * TILE)

    def input_rows(j):
        def two_rows(p, carry):
            lines = []
            for a in range(2):
                r = 2 * p + a
                hold_up = jnp.where(r == cut - 1, keep, 1.0)
                hold_down = jnp.where(r == cut, keep, 1.0)

                def column_sum(w, s):
                    def of(u, row):
                        at = (3 * u + w) * TILE
                        return taps_in[s, row, :, at : at + TILE]

                    return of(0, r + 2) * hold_up + of(1, r + 1) + of(2, r) * hold_down

                before = pltpu.roll(column_sum(2, 1), 1, 0)
                after = pltpu.roll(column_sum(0, 0), half - 1, 0)
                even = column_sum(0, 1) + column_sum(1, 0) + jnp.where(pixel_in == 0, 0.0, before)
                odd = column_sum(1, 1) + column_sum(2, 0) + jnp.where(pixel_in == half - 1, 0.0, after)
                seg = (r >= cut).astype(jnp.int32)
                broad = jnp.where(choose(seg, base) + r < choose(seg, high[j]), choose(seg, wide[j]), 0)
                for b, value in ((0, even), (1, odd)):
                    at = (2 * a + b) * half
                    x = xp[j, p + 1, at : at + half].astype(F32)
                    mask = 2 * pixel_in + b < broad
                    value = slope(x) * (value * scale1) + skip_back[p]
                    lines.append(jnp.where(mask, value, 0.0).astype(BF16))
            line = dot(jnp.concatenate(lines, axis=0), perm_x[0 : 4 * half], TN).astype(BF16)
            own = jnp.where(c == 0, line[0:ci], line[ci:cin])
            other = jnp.where(c == 0, line[ci:cin], line[0:ci])
            out_g[c * per + j, 2 * p] = own[:, 0:width]
            out_g[c * per + j, 2 * p + 1] = own[:, width:TILE]
            send_g[j, p] = other
            return carry

        lax.fori_loop(0, pairs, two_rows, 0, unroll=True)
        return begin(send_g.at[j], got_g.at[j], (me, o))

    def unpack(j):
        def line(p, carry):
            out_g[o * per + j, 2 * p] = got_g[j, p, :, 0:width]
            out_g[o * per + j, 2 * p + 1] = got_g[j, p, :, width:TILE]
            return carry

        grad_x[j].wait_recv()
        lax.fori_loop(0, pairs, line, 0, unroll=4)

    conv_two(0)
    for j in range(1, per):
        conv_two(j)
    group_c.to_owners()
    back_products(0)
    out_x = begin(send_b, got_b, (me, o))
    group_a.to_cubes()
    grad_x = [input_rows(0)]
    def own_half(row):
        return jnp.where(c == 0, row[:, 0:co], row[:, co:cout])

    def column_of(row):
        row = jnp.concatenate([own_half(row), jnp.zeros((1, TILE - co), F32)], axis=1)
        return jnp.transpose(jnp.broadcast_to(row, (TILE, TILE)))[0:co]

    def compact(row, size, padded):
        return jnp.concatenate([row[:, t * padded : t * padded + size] for t in range(9)], axis=1)

    def turned(part, out, at):
        some = part.shape[1]
        if some < TILE:
            part = jnp.concatenate([part, jnp.zeros((co, TILE - some), F32)], axis=1)
        part = jnp.concatenate([part, jnp.zeros((TILE - co, TILE), F32)], axis=0)
        out[at : at + some] = jnp.transpose(part)[0:some, 0:co]

    def outer(left, right, out):
        columns = column_of(right)
        for at in range(0, left.shape[1], TILE):
            some = min(TILE, left.shape[1] - at)
            turned(columns[:, 0:some] * left[:, at : at + some], out, at)

    corr1, corr2, corr0 = ref["corr1"], ref["corr2"], ref["corr0"]
    outer(compact(left1_ref[0:1], cin, TILE), right1 * (scale1 * scale1), corr1)
    outer(compact(left2_ref[0:1], cout, op), right2 * (scale2 * scale2), corr2)
    outer(left0_ref[0:1, 0:cin], right0 * (scale0 * scale0), corr0)
    for j in range(1, per):
        back_products(j)
        if j == 1:
            group_b.to_cubes()
            group_a.to_all(False)
        grad_x.append(input_rows(j))
    group_c.to_cubes()

    group_b.to_all(False)
    out_k1, out_k2, out_k0 = ref["out_k1"], ref["out_k2"], ref["out_k0"]
    group_a.forward()
    group_c.to_all()
    group_b.forward()
    group_a.turned(scale2, out_k2, 0, 5 * cout)
    out_x.wait_recv()
    out_b[mine_o] = got_b[...]
    unpack(0)
    rest = group_b.turned(scale2, out_k2, 5 * cout, 4 * cout)
    out_k0[...] = rest[0:cin] * scale0
    for j in range(1, per):
        unpack(j)
    extra = group_c.turned(scale1, out_k1, 0, n1)
    ref["out_b1"][...] = extra[0:1] + extra[1:2]
    ref["out_b2"][...] = extra[2:3] + extra[3:4]
    for at, (out, corr) in enumerate(((out_k1, corr1), (out_k2, corr2), (out_k0, corr0))):
        value = extra[4 + 2 * at : 5 + 2 * at, 0:1] + extra[5 + 2 * at : 6 + 2 * at, 0:1]
        out[...] = out[...] - corr[...] * value

    for copy in sends:
        copy.wait_send()


def hand_over(arrays):
    number = len(arrays)

    def copy_all(*refs):
        sem = refs[-1]
        copies = [pltpu.make_async_copy(refs[i], refs[number + i], sem.at[i]) for i in range(number)]
        for copy in copies:
            copy.start()
        for copy in copies:
            copy.wait()

    return pl.pallas_call(
        copy_all,
        out_shape=[jax.ShapeDtypeStruct(a.shape, a.dtype) for a in arrays],
        in_specs=[pl.BlockSpec(memory_space=pltpu.VMEM)] * number,
        out_specs=[pl.BlockSpec(memory_space=pl.ANY)] * number,
        scratch_shapes=[pltpu.SemaphoreType.DMA((number,))],
        name="hand_over",
    )(*[pltpu.with_memory_space_constraint(a, pltpu.VMEM) for a in arrays])


def fused(n_rows, arrays):
    (images, valid_h, valid_w, kernel_one, kernel_two, kernel_skip, bias_one, bias_two,
     vector_one, vector_two, vector_skip, cotangent) = arrays
    micros, rows, width, ci = images.shape
    co = kernel_one.shape[3]
    per, pairs, half = micros // 2, rows // 2, width // 2
    op = 2 * TILE
    n_chips = n_rows // 2
    cin, cout = 2 * ci, 2 * co
    sub = min(4, n_chips)
    cubes = n_chips // sub
    unit = op * sub
    lanes_two = -(-max(5 * cout, 4 * cout + cin) // unit) * unit
    lanes_one = -(-(9 * cin + 10) // unit) * unit
    seg_out = rows // 2 + 1
    bits = 3 if n_rows % 8 == 0 else 2
    size1 = -(-(9 * cin) // 64) * 64
    size20 = -(-(9 * cout + cin) // 64) * 64
    share1 = -(-(3 * size1 // 4) // 64) * 16
    share2 = -(-(3 * size20 // 4) // (16 * 2**bits)) * 16
    inputs = {
        "vh": valid_h,
        "vw": valid_w,
        "img": jnp.transpose(images, (0, 1, 3, 2)),
        "k1": kernel_one.reshape(9 * cin, co),
        "k2": kernel_two.reshape(9 * cout, co),
        "k0": kernel_skip,
        "b1": bias_one.reshape(1, co),
        "b2": bias_two.reshape(1, co),
        "q1": vector_one.reshape(1, co),
        "q2": vector_two.reshape(1, co),
        "q0": vector_skip.reshape(1, co),
        "cot": cotangent,
    }
    outputs = {
        "out_b": jax.ShapeDtypeStruct(cotangent.shape, BF16),
        "out_g": jax.ShapeDtypeStruct((micros, rows, ci, width), BF16),
        "out_k1": jax.ShapeDtypeStruct((9 * cin, co), F32),
        "out_k2": jax.ShapeDtypeStruct((9 * cout, co), F32),
        "out_k0": jax.ShapeDtypeStruct((cin, co), F32),
        "out_b1": jax.ShapeDtypeStruct((1, co), F32),
        "out_b2": jax.ShapeDtypeStruct((1, co), F32),
    }
    vm = pltpu.VMEM
    scratch = {
        "vh_s": pltpu.SMEM(valid_h.shape, jnp.int32),
        "vw_s": pltpu.SMEM(valid_w.shape, jnp.int32),
        "b1_v": vm((1, co), BF16),
        "b2_v": vm((1, co), BF16),
        "q1_v": vm((1, co), F32),
        "q2_v": vm((1, co), F32),
        "q0_v": vm((1, co), F32),
        "img_v": vm((micros, rows, ci, width), BF16),
        "cot_v": vm(cotangent.shape, BF16),
        "k1_v": vm((size1, co), BF16),
        "k20_v": vm((size20, co), BF16),
        "k1p": vm((4 * share1, TILE), BF16),
        "k20p": vm((2**bits * share2, TILE), BF16),
        "k1h": vm((4 * share1, TILE), BF16),
        "k20h": vm((2**bits * share2, TILE), BF16),
        "cotp": vm((per, 3 * pairs * half // 4, TILE), BF16),
        "coth": vm((per, 3 * pairs * half // 4, TILE), BF16),
        "imgr": vm((per, 2, pairs + 2, ci, TILE), BF16),
        "sendp": vm((per, pairs, ci, TILE), BF16),
        "vec": vm((2, 8, TILE), F32),
        "cotr": vm((per, 2, 2, half, co), BF16),
        "eye": vm((op, op), BF16),
        "perm_in": vm((8 * half, TILE), BF16),
        "perm_x": vm((5 * half, TILE), BF16),
        "w1": vm((9 * TILE, op), BF16),
        "w2": vm((9 * op, op), BF16),
        "w0": vm((TILE, op), BF16),
        "left1": vm((8, 9 * TILE), F32),
        "left2": vm((8, 9 * op), F32),
        "left0": vm((8, TILE), F32),
        "b_in": vm((per, 2 * (rows // 2 + 3), half, 4 * TILE), BF16),
        "xp": vm((per, pairs + 2, 4 * half, TILE), BF16),
        "xb": vm((per, pairs + 2, half, TILE), BF16),
        "raw1": vm((per, 2, 2 * seg_out, half, op), F32),
        "grad1": vm((per, 2, 2 * seg_out, half, op), F32),
        "act1": vm((per, 2, 2 * seg_out, half, op), BF16),
        "cols": vm((per, 3, 2 * seg_out, half, op), F32),
        "box": vm((per, pairs, half, 9 * op), BF16),
        "quart": vm((per, pairs + 2, half, op), BF16),
        "acc0": vm((cout, TILE), F32),
        "sums0": vm((cout, TILE), BF16),
        "taps_sum": vm((3, 2, per, pairs + 2, half, op), F32),
        "g_pre": vm((per, 2, 2 * seg_out, half, op), BF16),
        "taps_in": vm((2, 2 * seg_out, half, 9 * TILE), F32),
        "skip_back": vm((pairs, half, TILE), F32),
        "send_b": vm((per, pairs, half, co), BF16),
        "got_b": vm((per, pairs, half, co), BF16),
        "send_g": vm((per, pairs, ci, TILE), BF16),
        "got_g": vm((per, pairs, ci, TILE), BF16),
    }
    for name, size in (("corr1", 9 * cin), ("corr2", 9 * cout), ("corr0", cin)):
        scratch[name] = vm((size, co), F32)
    for name, lanes_each in (("a", lanes_two), ("b", lanes_two), ("c", lanes_one)):
        share = lanes_each // sub
        scratch["wire" + name] = vm((2, co, lanes_each), BF16)
        scratch["got" + name] = vm((2, co // 2, lanes_each), BF16)
        scratch["shares" + name] = vm((2, sub, co // 2, share), BF16)
        scratch["landing" + name] = vm((2 * sub - 1, co // 2, share), BF16)
        scratch["mine" + name] = vm((co // 2, share), F32)
        scratch["mids" + name] = vm((cubes, co // 2, share), BF16)
        scratch["result" + name] = vm((sub, co, share), BF16)
    copies = 11 + 2 ** (bits - 1) + 7 * per + 3 * (1 + 2 * (2 * sub - 1) + cubes - 1)
    scratch["lsem"] = pltpu.SemaphoreType.DMA((12,))
    scratch["ssem"] = pltpu.SemaphoreType.DMA((copies,))
    scratch["rsem"] = pltpu.SemaphoreType.DMA((copies,))
    names = list(inputs) + list(outputs) + list(scratch)
    dims = (micros, rows, width, ci, co, lanes_one, lanes_two, bits, share1, share2)
    vmem = pl.BlockSpec(memory_space=pltpu.VMEM)
    hbm = pl.BlockSpec(memory_space=pltpu.HBM)
    results = pl.pallas_call(
        functools.partial(fused_kernel, names, n_rows, dims),
        out_shape=[pltpu.VMEM(a.shape, a.dtype) for a in outputs.values()],
        in_specs=[hbm] * len(inputs),
        out_specs=[vmem] * len(outputs),
        scratch_shapes=list(scratch.values()),
        compiler_params=pltpu.CompilerParams(
            collective_id=0, has_side_effects=True, vmem_limit_bytes=48 * 1024 * 1024
        ),
        name="down_block",
    )(*[pltpu.with_memory_space_constraint(a, pltpu.HBM) for a in inputs.values()])
    out_b, out_g, out_k1, out_k2, out_k0, out_b1, out_b2 = hand_over(results)
    return (
        out_b,
        jnp.transpose(out_g, (0, 1, 3, 2)),
        out_k1.reshape(3, 3, cin, co),
        out_k2.reshape(3, 3, cout, co),
        out_k0,
        out_b1.reshape(co),
        out_b2.reshape(co),
    )


def solution(mesh):
    in_specs = (
        P(None, "rows", None, "ch"),
        P(),
        P(),
        P(None, None, None, "ch"),
        P(None, None, None, "ch"),
        P(None, "ch"),
        P("ch"),
        P("ch"),
        P("ch"),
        P("ch"),
        P("ch"),
        P(None, "rows", None, "ch"),
    )
    out_specs = (
        P(None, "rows", None, "ch"),
        P(None, "rows", None, "ch"),
        P(None, None, None, "ch"),
        P(None, None, None, "ch"),
        P(None, "ch"),
        P("ch"),
        P("ch"),
    )

    def step(*arrays):
        if fits(mesh.shape["rows"], mesh.shape["ch"], arrays):
            return fused(mesh.shape["rows"], arrays)
        return shards(*arrays)

    return jax.shard_map(step, mesh=mesh, in_specs=in_specs, out_specs=out_specs, check_vma=False)
```
